32 devices in a mesh: grp: 4 (over y, x), frm: 8 (over z, core).
Axes of the slice: x: 2, y: 2, z: 4, core: 2. Of those that a mesh axis runs over, the one named last changes fastest.
Arguments:
- query_in: bfloat16 [8, 128, 2048], P(None, ('grp', 'frm')), may hold values from -32 to 32
- key_in: bfloat16 [8, 128, 2048], P(None, ('grp', 'frm')), may hold values from -32 to 32
- value_in: bfloat16 [8, 128, 2048], P(None, ('grp', 'frm')), may hold values from -6 to 6
- cotangent: bfloat16 [8, 128, 2048], P('frm', 'grp'), may hold values from -6 to 6
- w_in: bfloat16 [4, 2048, 4096], P('grp', None, 'frm'), may hold values from -0.1875 to 0.1875
- w_out: bfloat16 [4, 4096, 2048], P('grp', 'frm'), may hold values from -0.125 to 0.125
- gate_probs: float32 [2, 32], replicated, may hold values from 0.5 to 1
- chosen: int32 [2, 32], replicated, may hold values from 0 to 1023, as said below
Outputs:
- grad_query: bfloat16 [8, 128, 2048], P(None, ('grp', 'frm'))
- grad_key: bfloat16 [8, 128, 2048], P(None, ('grp', 'frm'))
- grad_value: bfloat16 [8, 128, 2048], P(None, ('grp', 'frm'))
The draws below stay inside these ranges and needn't reach their ends.
Inputs may be any that keep to these rules, and one draw needn't show every extreme that they name: `chosen`: row e lists 32 distinct tokens, token t = frame * 128 + patch. Call the tokens of 4 consecutive patches starting at a multiple of 4, over all frames, a block: an expert takes at most 2 tokens of a block, and exactly 2 of some block in every row.
All inputs are finite; a program needn't handle non-finite values.
Results may differ from the reference program's by a relative error of at most 0.025.
Values may be sent and summed in bfloat16 or wider, within the bound.
No kernel may reach another device: no remote copies, remote signals or barrier semaphores. Data moves between devices by JAX's collectives and lax.ppermute only.
A program may use at most 64 MiB of HBM per device.

```python
import math
import jax
import jax.numpy as jnp
from jax import lax

D = 2048
F = 8192
HEADS = 16
MOST = 2
PB = 4
FRAMES = 8
PATCHES = 128
EXPERTS = 2
CAP = 32
N_FRM = 8


def draw_query_in(key, part):
    drawn = jax.random.truncated_normal(jax.random.fold_in(key, 1), -4.0, 4.0, (FRAMES, PATCHES, HEADS, D // HEADS), jnp.float32)
    return drawn.reshape(FRAMES, PATCHES, D).astype(jnp.bfloat16)


def draw_key_in(key, part):
    drawn = jax.random.truncated_normal(jax.random.fold_in(key, 2), -4.0, 4.0, (FRAMES, PATCHES, HEADS, D // HEADS), jnp.float32)
    return drawn.reshape(FRAMES, PATCHES, D).astype(jnp.bfloat16)


def draw_chosen(key, part):
    base = jax.random.fold_in(key, 3)
    streams = jax.random.split(base, 3)
    block_total = PATCHES // PB
    local_rows = FRAMES * PB
    noise = jax.random.randint(streams[0], (EXPERTS, block_total), 0, 1 << 20) * block_total + jnp.arange(block_total)[None, :]
    ranking = jnp.argsort(jnp.argsort(noise, axis=1), axis=1)
    doubled = jax.random.randint(streams[1], (EXPERTS, 1), 1, block_total // 2 + 1)
    counts = 1 + (ranking < doubled).astype(jnp.int32) - ((ranking >= doubled) & (ranking < 2 * doubled)).astype(jnp.int32)
    spread = jax.random.randint(streams[2], (EXPERTS, block_total, local_rows), 0, 1 << 16) * local_rows + jnp.arange(local_rows)[None, None, :]
    locals_picked = jnp.argsort(spread, axis=2)[:, :, :MOST]
    frame_of = locals_picked // PB
    within = locals_picked % PB
    token_ids = frame_of * PATCHES + jnp.arange(block_total)[None, :, None] * PB + within
    alive = jnp.arange(MOST)[None, None, :] < counts[:, :, None]
    flat_tokens = token_ids.reshape(EXPERTS, block_total * MOST)
    flat_alive = alive.reshape(EXPERTS, block_total * MOST).astype(jnp.int32)
    sort_keys = (1 - flat_alive) * (block_total * MOST) + jnp.arange(block_total * MOST)[None, :]
    keeping = jnp.argsort(sort_keys, axis=1)[:, :CAP]
    return jnp.take_along_axis(flat_tokens, keeping, axis=1).astype(jnp.int32)


def strengthened(drawn, own_key, source, target, blocks, factor):
    def block_of(axis_at):
        return (jnp.arange(drawn.shape[axis_at]) // (drawn.shape[axis_at] // blocks)).reshape((-1,) + (1,) * (drawn.ndim - 1 - axis_at))

    one_side = jax.random.permutation(own_key, blocks)[block_of(target)]
    second = (block_of(target) + blocks // 2) % blocks
    return jnp.where((block_of(source) == one_side) | (block_of(source) == second), factor * drawn, drawn)


def steps_of(own_key, extent, cuts, low, top_value):
    def one(dim, parts):
        steps = jax.random.uniform(jax.random.fold_in(jax.random.fold_in(own_key, 6), dim), (parts,), jnp.float32, low / len(cuts), top_value / len(cuts))
        return jnp.repeat(jnp.exp(steps), extent[dim] // parts).reshape((-1,) + (1,) * (len(extent) - dim - 1))

    loudness = one(*cuts[0])
    for cut in cuts[1:]:
        loudness = loudness * one(*cut)
    return loudness


def bell_draw(stream_key, extent, scale, reach, cuts=(), kind=jnp.bfloat16):
    array = jax.random.normal(stream_key, extent, jnp.float32) * scale
    if len(cuts) > 0:
        array = steps_of(stream_key, extent, cuts, -0.22, 0.18) * array
    return jnp.clip(array, min=-reach, max=reach).astype(kind)


def noise_with(own_key, extent, scale, bound, cuts, heavy, kind=jnp.bfloat16):
    array = scale * jax.random.normal(own_key, extent, jnp.float32)
    if cuts:
        array = array * steps_of(own_key, extent, cuts, -0.22, 0.18)
    return jnp.clip(strengthened(array, jax.random.fold_in(own_key, 3), *heavy), -bound, bound).astype(kind)


def setup_inputs(seed: int = 0) -> dict:
    key_of = jax.random.split(jax.random.key(seed), 9)
    query_in = draw_query_in(jax.random.fold_in(key_of[8], 71), 0)
    key_in = draw_key_in(jax.random.fold_in(key_of[8], 71), 0)
    value_in = bell_draw(key_of[2], (FRAMES, PATCHES, D), 1.0, 6.0, ((1, 32),))
    cotangent = bell_draw(key_of[3], (FRAMES, PATCHES, D), 1.0, 6.0, ((0, 8), (1, 4)))
    w_in = noise_with(key_of[4], (2 * EXPERTS, D, F // 2), D ** -0.5, 0.1875, ((0, 4), (2, 8)), (2, 1, 8, 2.0))
    w_out = bell_draw(key_of[5], (2 * EXPERTS, F // 2, D), D ** -0.5, 0.125, ((0, 4), (1, 8)))
    gate_probs = jnp.clip(jax.random.uniform(key_of[6], (EXPERTS, CAP), jnp.float32, 0.5, 1.0), 0.5, 1.0)
    chosen = draw_chosen(jax.random.fold_in(key_of[8], 71), 0)
    return dict(query_in=query_in, key_in=key_in, value_in=value_in, cotangent=cotangent, w_in=w_in, w_out=w_out, gate_probs=gate_probs, chosen=chosen)


root_half = 0.7071067811865476
inv_root_tau = 0.3989422804014327

def gelu_slope(pre_act):
    normal_cdf = 0.5 * (1.0 + jax.scipy.special.erf(pre_act * root_half))
    density = jnp.exp(-0.5 * pre_act * pre_act) * inv_root_tau
    return normal_cdf + pre_act * density

def softmax_rows(scores):
    highest = lax.optimization_barrier(jnp.max(scores, axis=-1, keepdims=True))
    raised = jnp.exp(scores - highest)
    return raised / lax.optimization_barrier(jnp.sum(raised, axis=-1, keepdims=True))

def round_half(values):
    return lax.optimization_barrier(values.astype(jnp.bfloat16)).astype(jnp.float32)

def reference(query_in, key_in, value_in, cotangent, w_in, w_out, gate_probs, chosen):
    frames, patches, features = query_in.shape
    head_dim = features // HEADS
    scaling = head_dim ** (-0.5)
    tokens = frames * patches
    block_size = math.gcd(patches, 64)
    block_count = patches // block_size

    def to_blocks(values):
        return values.reshape(frames, block_count, block_size, HEADS, head_dim).transpose(1, 0, 2, 3, 4)

    def from_blocks(values):
        return values.transpose(1, 0, 2, 3, 4).reshape(frames, patches, features)
    query_blocks = to_blocks(query_in)
    key_blocks = to_blocks(key_in)
    value_blocks = to_blocks(value_in)

    def probabilities(query_part, key_part):
        scores = jnp.einsum('fphd,gphd->phfg', query_part.astype(jnp.float32), key_part.astype(jnp.float32)) * scaling
        return softmax_rows(scores)

    def forward(operands):
        query_part, key_part, value_part = operands
        weights = round_half(probabilities(query_part, key_part))
        mixed = jnp.einsum('phfg,gphd->fphd', weights, value_part.astype(jnp.float32))
        return mixed.astype(jnp.bfloat16)
    attn_out = from_blocks(lax.map(forward, (query_blocks, key_blocks, value_blocks))).reshape(tokens, features)
    cot_flat = cotangent.reshape(tokens, features)
    slices = 2 * N_FRM
    slice_width = w_in.shape[2] // N_FRM
    pair_in = w_in.reshape(EXPERTS, 2, features, w_in.shape[2])
    pair_out = w_out.reshape(EXPERTS, 2, w_out.shape[1], features)

    def expert_grad(operands):
        halves_in, halves_out, probs_row, picked = operands
        hidden_in = jnp.concatenate([halves_in[0], halves_in[1]], axis=1)
        hidden_out = jnp.concatenate([halves_out[0], halves_out[1]], axis=0)
        picked = picked.astype(jnp.int32)
        rows_in = attn_out[picked]
        rows_cot = cot_flat[picked]
        scaled = (probs_row[:, None] * rows_cot.astype(jnp.float32)).astype(jnp.bfloat16)
        pre_act = jnp.dot(rows_in, hidden_in, preferred_element_type=jnp.float32)
        back_act = jnp.dot(scaled, hidden_out.T, preferred_element_type=jnp.float32)
        slope = (back_act * gelu_slope(pre_act)).astype(jnp.bfloat16)
        row_count = picked.shape[0]
        products = jnp.einsum('rsk,dsk->srd', slope.reshape(row_count, slices, slice_width).astype(jnp.float32), hidden_in.reshape(features, slices, slice_width).astype(jnp.float32))
        products = round_half(products)
        halves = lax.optimization_barrier(jnp.sum(products.reshape(2, N_FRM, row_count, features), axis=1))
        halves = round_half(halves)
        return halves[0] + halves[1]
    added = lax.map(expert_grad, (pair_in, pair_out, gate_probs, chosen))
    stream = cot_flat.astype(jnp.float32).at[chosen.reshape(-1).astype(jnp.int32)].add(added.reshape(-1, features))
    stream = stream.astype(jnp.bfloat16)
    stream_blocks = to_blocks(stream.reshape(frames, patches, features))

    def backward(operands):
        query_part, key_part, value_part, grad_part = operands
        attn_probs = probabilities(query_part, key_part)
        weights = round_half(attn_probs)
        grad_heads = grad_part.astype(jnp.float32)
        grad_value = jnp.einsum('phfg,fphd->gphd', weights, grad_heads).astype(jnp.bfloat16)
        grad_prob = jnp.einsum('fphd,gphd->phfg', grad_heads, value_part.astype(jnp.float32))
        centre = lax.optimization_barrier(jnp.sum(attn_probs * grad_prob, axis=-1, keepdims=True))
        grad_score = round_half(attn_probs * (grad_prob - centre))
        grad_query = (jnp.einsum('phfg,gphd->fphd', grad_score, key_part.astype(jnp.float32)) * scaling).astype(jnp.bfloat16)
        grad_key = (jnp.einsum('phfg,fphd->gphd', grad_score, query_part.astype(jnp.float32)) * scaling).astype(jnp.bfloat16)
        return (grad_query, grad_key, grad_value)
    grad_query, grad_key, grad_value = lax.map(backward, (query_blocks, key_blocks, value_blocks, stream_blocks))
    return (from_blocks(grad_query), from_blocks(grad_key), from_blocks(grad_value))
```

```python
import jax
import jax.numpy as jnp
from jax import lax
from jax.sharding import PartitionSpec as P

HEADS = 16
MOST = 2


root_half = 0.7071067811865476
inv_root_tau = 0.3989422804014327


def gelu_slope(pre_act):
    normal_cdf = 0.5 * (1.0 + jax.scipy.special.erf(pre_act * root_half))
    density = jnp.exp(-0.5 * pre_act * pre_act) * inv_root_tau
    return normal_cdf + pre_act * density


def body(query_in, key_in, value_in, cotangent, w_in, w_out, gate_probs, chosen):
    frames, blocks, features = query_in.shape
    head_dim = features // HEADS
    scaling = head_dim ** (-0.5)
    groups = lax.axis_size("grp")
    columns = lax.axis_size("frm")
    experts = gate_probs.shape[0]
    local_rows = frames * blocks
    cot_patch = lax.all_to_all(cotangent, "frm", split_axis=1, concat_axis=0, tiled=True)
    cot_flat = cot_patch.reshape(local_rows, features)
    query_heads = query_in.reshape(frames, blocks, HEADS, head_dim)
    key_heads = key_in.reshape(frames, blocks, HEADS, head_dim)
    value_heads = value_in.reshape(frames, blocks, HEADS, head_dim)
    scores = (
        jnp.einsum("fphd,gphd->phfg", query_heads, key_heads, preferred_element_type=jnp.float32)
        * scaling
    )
    highest = jnp.max(scores, axis=-1, keepdims=True)
    raised = jnp.exp(scores - highest)
    attn_probs = raised / jnp.sum(raised, axis=-1, keepdims=True)
    weights = attn_probs.astype(jnp.bfloat16)
    attn_out = jnp.einsum(
        "phfg,gphd->fphd", weights, value_heads, preferred_element_type=jnp.float32
    )
    attn_out = attn_out.astype(jnp.bfloat16).reshape(local_rows, features)
    patches_all = blocks * groups * columns
    frame_of = chosen // patches_all
    patch_of = chosen % patches_all
    holder = patch_of // blocks
    position = frame_of * blocks + patch_of % blocks
    myself = lax.axis_index("grp") * columns + lax.axis_index("frm")
    owned_here = (holder == myself).astype(jnp.int32)
    ranking = jnp.cumsum(owned_here, axis=1) - 1
    slot_ids = jnp.arange(MOST, dtype=jnp.int32)
    selected = owned_here[:, None, :] * (ranking[:, None, :] == slot_ids[None, :, None]).astype(
        jnp.int32
    )
    position_at = jnp.sum(selected * position[:, None, :], axis=2)
    filled = jnp.sum(selected, axis=2)
    weight_at = jnp.sum(selected.astype(jnp.float32) * gate_probs[:, None, :], axis=2)
    row_ids = jnp.arange(local_rows, dtype=jnp.int32)
    onehot = (
        (position_at[:, :, None] == row_ids[None, None, :]) & (filled[:, :, None] > 0)
    ).astype(jnp.bfloat16)
    picked_in = jnp.einsum(
        "eml,ld->emd", onehot, attn_out, preferred_element_type=jnp.float32
    ).astype(jnp.bfloat16)
    picked_cot = jnp.einsum(
        "eml,ld->emd",
        onehot,
        cot_patch.reshape(local_rows, features),
        preferred_element_type=jnp.float32,
    )
    scaled = (weight_at[:, :, None] * picked_cot).astype(jnp.bfloat16)
    stacked = jnp.stack([picked_in, scaled], axis=2)
    own_in = w_in[0]
    own_out = w_out[0]
    devices = groups * columns
    share = devices // experts
    outgoing = jnp.broadcast_to(
        stacked.reshape(experts, 1, MOST * 2, features), (experts, share, MOST * 2, features)
    ).reshape(devices, MOST * 2, features)
    arrived = lax.all_to_all(outgoing, ("grp", "frm"), split_axis=0, concat_axis=0, tiled=True)
    shard_rows = arrived.reshape(devices * MOST, 2, features)
    pre_act = jnp.dot(shard_rows[:, 0, :], own_in, preferred_element_type=jnp.float32)
    back_act = lax.dot_general(
        shard_rows[:, 1, :], own_out, (((1,), (1,)), ((), ())), preferred_element_type=jnp.float32
    )
    slope = (back_act * gelu_slope(pre_act)).astype(jnp.bfloat16)
    product = lax.dot_general(
        slope, own_in, (((1,), (1,)), ((), ())), preferred_element_type=jnp.float32
    ).astype(jnp.bfloat16)
    returned = lax.all_to_all(
        product.reshape(devices, MOST, features),
        ("grp", "frm"),
        split_axis=0,
        concat_axis=0,
        tiled=True,
    )
    summed = jnp.sum(
        returned.reshape(experts, share, MOST, features).astype(jnp.float32), axis=1
    )
    added = jnp.einsum(
        "eml,emd->ld",
        onehot.astype(jnp.float32),
        summed,
        preferred_element_type=jnp.float32,
        precision=lax.Precision.HIGHEST,
    )
    grad_stream = (cot_flat.astype(jnp.float32) + added).astype(jnp.bfloat16)
    grad_heads = grad_stream.reshape(frames, blocks, HEADS, head_dim)
    grad_value = jnp.einsum(
        "phfg,fphd->gphd", weights, grad_heads, preferred_element_type=jnp.float32
    ).astype(jnp.bfloat16)
    grad_prob = jnp.einsum(
        "fphd,gphd->phfg", grad_heads, value_heads, preferred_element_type=jnp.float32
    )
    centre = jnp.sum(attn_probs * grad_prob, axis=-1, keepdims=True)
    grad_score = (attn_probs * (grad_prob - centre)).astype(jnp.bfloat16)
    grad_query = (
        jnp.einsum("phfg,gphd->fphd", grad_score, key_heads, preferred_element_type=jnp.float32)
        * scaling
    ).astype(jnp.bfloat16)
    grad_key = (
        jnp.einsum("phfg,fphd->gphd", grad_score, query_heads, preferred_element_type=jnp.float32)
        * scaling
    ).astype(jnp.bfloat16)
    return (
        grad_query.reshape(frames, blocks, features),
        grad_key.reshape(frames, blocks, features),
        grad_value.reshape(frames, blocks, features),
    )


def solution(mesh):
    return jax.shard_map(
        body,
        mesh=mesh,
        in_specs=(
            P(None, ("grp", "frm"), None),
            P(None, ("grp", "frm"), None),
            P(None, ("grp", "frm"), None),
            P("frm", "grp", None),
            P("grp", None, "frm"),
            P("grp", "frm", None),
            P(),
            P(),
        ),
        out_specs=(
            P(None, ("grp", "frm"), None),
            P(None, ("grp", "frm"), None),
            P(None, ("grp", "frm"), None),
        ),
        check_vma=False,
    )
```

```python
import jax
import jax.numpy as jnp
from jax import lax
from jax.sharding import PartitionSpec as P

HEADS = 16
MOST = 2
CORES = 2


root_half = 0.7071067811865476
inv_root_tau = 0.3989422804014327


def gelu_slope(pre_act):
    normal_cdf = 0.5 * (1.0 + jax.scipy.special.erf(pre_act * root_half))
    density = jnp.exp(-0.5 * pre_act * pre_act) * inv_root_tau
    return normal_cdf + pre_act * density


def body(query_in, key_in, value_in, cotangent, w_in, w_out, gate_probs, chosen):
    frames, blocks, features = query_in.shape
    head_dim = features // HEADS
    scaling = head_dim ** (-0.5)
    groups = lax.axis_size("grp")
    columns = lax.axis_size("frm")
    experts = gate_probs.shape[0]
    local_rows = frames * blocks
    cot_patch = lax.all_to_all(cotangent, "frm", split_axis=1, concat_axis=0, tiled=True)
    cot_flat = cot_patch.reshape(local_rows, features)
    query_heads = query_in.reshape(frames, blocks, HEADS, head_dim)
    key_heads = key_in.reshape(frames, blocks, HEADS, head_dim)
    value_heads = value_in.reshape(frames, blocks, HEADS, head_dim)
    scores = (
        jnp.einsum("fphd,gphd->phfg", query_heads, key_heads, preferred_element_type=jnp.float32)
        * scaling
    )
    highest = jnp.max(scores, axis=-1, keepdims=True)
    raised = jnp.exp(scores - highest)
    attn_probs = raised / jnp.sum(raised, axis=-1, keepdims=True)
    weights = attn_probs.astype(jnp.bfloat16)
    attn_out = jnp.einsum(
        "phfg,gphd->fphd", weights, value_heads, preferred_element_type=jnp.float32
    )
    attn_out = attn_out.astype(jnp.bfloat16).reshape(local_rows, features)
    patches_all = blocks * groups * columns
    frame_of = chosen // patches_all
    patch_of = chosen % patches_all
    holder = patch_of // blocks
    position = frame_of * blocks + patch_of % blocks
    myself = lax.axis_index("grp") * columns + lax.axis_index("frm")
    owned_here = (holder == myself).astype(jnp.int32)
    ranking = jnp.cumsum(owned_here, axis=1) - 1
    slot_ids = jnp.arange(MOST, dtype=jnp.int32)
    selected = owned_here[:, None, :] * (ranking[:, None, :] == slot_ids[None, :, None]).astype(
        jnp.int32
    )
    position_at = jnp.sum(selected * position[:, None, :], axis=2)
    filled = jnp.sum(selected, axis=2)
    weight_at = jnp.sum(selected.astype(jnp.float32) * gate_probs[:, None, :], axis=2)
    row_ids = jnp.arange(local_rows, dtype=jnp.int32)
    onehot = (
        (position_at[:, :, None] == row_ids[None, None, :]) & (filled[:, :, None] > 0)
    ).astype(jnp.bfloat16)
    per_expert = groups // experts
    levels = columns // CORES
    expert_here = lax.axis_index("grp") // per_expert
    order = expert_here ^ jnp.arange(experts, dtype=jnp.int32)
    onehot = onehot[order]
    weight_at = weight_at[order]
    picked_in = jnp.einsum(
        "eml,ld->emd", onehot, attn_out, preferred_element_type=jnp.float32
    ).astype(jnp.bfloat16)
    picked_cot = jnp.einsum(
        "eml,ld->emd", onehot, cot_flat, preferred_element_type=jnp.float32
    )
    scaled = (weight_at[:, :, None] * picked_cot).astype(jnp.bfloat16)
    stacked = jnp.concatenate([picked_in, scaled], axis=1)
    own_in = w_in[0]
    own_out = w_out[0]

    def swap(values, axis, step):
        size = lax.axis_size(axis)
        return lax.ppermute(values, axis, [(i, i ^ step) for i in range(size)])

    row = jnp.stack(
        [stacked[0]] + [swap(stacked[k // per_expert], "grp", k) for k in range(1, groups)]
    )
    plane = jnp.stack([row] + [swap(row, "frm", CORES * k) for k in range(1, levels)])
    other = swap(plane, "frm", 1)

    def expert(rows):
        rows = rows.reshape(levels * groups, 2, MOST, features)
        pre_act = jnp.dot(
            rows[:, 0].reshape(-1, features), own_in, preferred_element_type=jnp.float32
        )
        back_act = lax.dot_general(
            rows[:, 1].reshape(-1, features),
            own_out,
            (((1,), (1,)), ((), ())),
            preferred_element_type=jnp.float32,
        )
        slope = (back_act * gelu_slope(pre_act)).astype(jnp.bfloat16)
        return lax.dot_general(
            slope, own_in, (((1,), (1,)), ((), ())), preferred_element_type=jnp.float32
        )

    back = swap(expert(other).astype(jnp.bfloat16), "frm", 1)
    mine = (expert(plane) + back.astype(jnp.float32)).astype(jnp.bfloat16)
    mine = mine.reshape(levels, groups, MOST, features)
    over_z = mine[0].astype(jnp.float32)
    for k in range(1, levels):
        over_z = over_z + swap(mine[k], "frm", CORES * k).astype(jnp.float32)
    over_z = over_z.astype(jnp.bfloat16)
    summed = jnp.stack(
        [over_z[0]] + [swap(over_z[k], "grp", k) for k in range(1, groups)]
    )
    summed = jnp.sum(
        summed.reshape(experts, per_expert, MOST, features).astype(jnp.float32), axis=1
    )
    added = jnp.einsum(
        "eml,emd->ld",
        onehot.astype(jnp.float32),
        summed,
        preferred_element_type=jnp.float32,
        precision=lax.Precision.HIGHEST,
    )
    grad_stream = (cot_flat.astype(jnp.float32) + added).astype(jnp.bfloat16)
    grad_heads = grad_stream.reshape(frames, blocks, HEADS, head_dim)
    grad_value = jnp.einsum(
        "phfg,fphd->gphd", weights, grad_heads, preferred_element_type=jnp.float32
    ).astype(jnp.bfloat16)
    grad_prob = jnp.einsum(
        "fphd,gphd->phfg", grad_heads, value_heads, preferred_element_type=jnp.float32
    )
    centre = jnp.sum(attn_probs * grad_prob, axis=-1, keepdims=True)
    grad_score = (attn_probs * (grad_prob - centre)).astype(jnp.bfloat16)
    grad_query = (
        jnp.einsum("phfg,gphd->fphd", grad_score, key_heads, preferred_element_type=jnp.float32)
        * scaling
    ).astype(jnp.bfloat16)
    grad_key = (
        jnp.einsum("phfg,fphd->gphd", grad_score, query_heads, preferred_element_type=jnp.float32)
        * scaling
    ).astype(jnp.bfloat16)
    return (
        grad_query.reshape(frames, blocks, features),
        grad_key.reshape(frames, blocks, features),
        grad_value.reshape(frames, blocks, features),
    )


def solution(mesh):
    return jax.shard_map(
        body,
        mesh=mesh,
        in_specs=(
            P(None, ("grp", "frm"), None),
            P(None, ("grp", "frm"), None),
            P(None, ("grp", "frm"), None),
            P("frm", "grp", None),
            P("grp", None, "frm"),
            P("grp", "frm", None),
            P(),
            P(),
        ),
        out_specs=(
            P(None, ("grp", "frm"), None),
            P(None, ("grp", "frm"), None),
            P(None, ("grp", "frm"), None),
        ),
        check_vma=False,
    )
```

```python
import functools

import jax
import jax.numpy as jnp
from jax import lax
from jax.experimental import pallas as pl
from jax.experimental.pallas import tpu as pltpu
from jax.sharding import PartitionSpec as P

HEADS = 16
MOST = 2
CORES = 2
SUBLANES = 8

root_half = 0.7071067811865476
inv_root_tau = 0.3989422804014327

LANES_BOTH = (((1,), (1,)), ((), ()))


def gelu_slope(pre_act):
    normal_cdf = 0.5 * (1.0 + lax.erf(pre_act * root_half))
    density = jnp.exp(-0.5 * pre_act * pre_act) * inv_root_tau
    return normal_cdf + pre_act * density


def dot(a, b):
    return jnp.dot(a, b, preferred_element_type=jnp.float32)


def dot_lanes(a, b):
    return lax.dot_general(a, b, LANES_BOTH, preferred_element_type=jnp.float32)


def over_frames(values, op, blocks):
    rows = values.shape[0]
    total = values[:SUBLANES]
    for start in range(SUBLANES, rows, SUBLANES):
        total = op(total, values[start : start + SUBLANES])
    step = blocks
    while step < SUBLANES:
        total = op(total, pltpu.roll(total, step, 0))
        step *= 2
    return jnp.concatenate([total] * (rows // SUBLANES), axis=0)


def heads_of(values):
    width = values.shape[1] // HEADS
    return [values[:, h * width : (h + 1) * width] for h in range(HEADS)]


def turn_kernel(blocks, pieces, place_ref, cot_ref, *out_refs):
    rows = cot_ref.shape[1]
    want = lax.broadcasted_iota(jnp.int32, (rows, rows), 0)
    have = lax.broadcasted_iota(jnp.int32, (rows, rows), 1)
    source = ((want // blocks) ^ place_ref[0]) * blocks + want % blocks
    turned = dot((source == have).astype(jnp.bfloat16), cot_ref[0]).astype(jnp.bfloat16)
    size = rows // pieces
    for i, out_ref in enumerate(out_refs):
        out_ref[...] = turned[i * size : (i + 1) * size]


def forward_kernel(
    experts, patches_all, place_ref, query_ref, key_ref, value_ref, chosen_ref, gate_ref,
    probs_ref, picked_ref, here_ref, weight_ref,
):
    frames, blocks, features = query_ref.shape
    rows = frames * blocks
    scaling = (features // HEADS) ** (-0.5)
    query = query_ref[...].reshape(rows, features)
    key = key_ref[...].reshape(rows, features)
    value = value_ref[...].reshape(rows, features)
    scores = jnp.concatenate(
        [dot_lanes(k, q) for k, q in zip(heads_of(key), heads_of(query))], axis=1
    )
    scores = scores * scaling
    raised = jnp.exp(scores - over_frames(scores, jnp.maximum, blocks))
    probs = raised / over_frames(raised, jnp.add, blocks)
    patch_in = lax.broadcasted_iota(jnp.int32, probs.shape, 0) % blocks
    patch_out = lax.broadcasted_iota(jnp.int32, probs.shape, 1) % blocks
    probs = jnp.where(patch_in == patch_out, probs, 0.0)
    probs_ref[...] = probs
    weights = probs.T.astype(jnp.bfloat16)
    mixed = jnp.concatenate(
        [dot(weights[h * rows : (h + 1) * rows], v) for h, v in enumerate(heads_of(value))],
        axis=1,
    ).astype(jnp.bfloat16)

    myself = place_ref[1]
    expert_here = place_ref[2]
    cap = chosen_ref.shape[1]
    before = (
        lax.broadcasted_iota(jnp.int32, (cap, cap), 0)
        < lax.broadcasted_iota(jnp.int32, (cap, cap), 1)
    ).astype(jnp.bfloat16)
    slot = lax.broadcasted_iota(jnp.int32, (SUBLANES, cap), 0)
    row_at = lax.broadcasted_iota(jnp.int32, (rows, cap), 0)
    found = []
    for k in range(experts):
        tokens = chosen_ref[pl.ds(expert_here ^ k, 1), :]
        gates = gate_ref[pl.ds(expert_here ^ k, 1), :]
        patch = tokens % patches_all
        owned = jnp.broadcast_to((patch // blocks == myself).astype(jnp.float32), slot.shape)
        rank = dot(owned.astype(jnp.bfloat16), before)
        taken = jnp.where((rank == slot.astype(jnp.float32)) & (owned > 0.0), 1.0, 0.0)
        position = (tokens // patches_all) * blocks + patch % blocks
        at_row = (row_at == position).astype(jnp.bfloat16)
        here = dot_lanes(taken.astype(jnp.bfloat16), at_row)
        weight = jnp.sum(taken * gates, axis=1, keepdims=True)
        here_ref[k * MOST : (k + 1) * MOST, :] = here[:MOST]
        weight_ref[k * MOST : (k + 1) * MOST, :] = jnp.broadcast_to(
            weight[:MOST], (MOST, weight_ref.shape[1])
        )
        found.append(here[:MOST])
    here = jnp.concatenate(found, axis=0).astype(jnp.bfloat16)
    picked_ref[...] = dot(here, mixed).astype(jnp.bfloat16)


def gather_kernel(blocks, place_ref, *refs):
    *part_refs, other_ref, cot_ref = refs
    rows = cot_ref.shape[0]
    mine = jnp.concatenate([part_ref[:blocks] for part_ref in part_refs], axis=0)
    half = rows // CORES
    want = lax.broadcasted_iota(jnp.int32, (rows, half), 0)
    have = lax.broadcasted_iota(jnp.int32, (rows, half), 1)
    step = (want // blocks) ^ place_ref[0]
    level = (step // CORES) * blocks + want % blocks
    near = ((level == have) & (step % CORES == 0)).astype(jnp.bfloat16)
    far = ((level == have) & (step % CORES == 1)).astype(jnp.bfloat16)
    cot_ref[...] = (dot(near, mine) + dot(far, other_ref[...])).astype(jnp.bfloat16)


def pick_kernel(experts, here_ref, weight_ref, picked_ref, cot_ref, *out_refs):
    rows = dot(here_ref[...].astype(jnp.bfloat16), cot_ref[...])
    rows = (rows * weight_ref[:, :1]).astype(jnp.bfloat16)
    for k, out_ref in enumerate(out_refs):
        out_ref[0] = picked_ref[k * MOST : (k + 1) * MOST]
        out_ref[1] = rows[k * MOST : (k + 1) * MOST]


def expert_kernel(mine_ref, other_ref, w_in_ref, w_out_ref, kept_ref, sent_ref):
    half = mine_ref.shape[1]
    w_in = w_in_ref[0]
    rows_in = jnp.concatenate([mine_ref[0], other_ref[0]], axis=0)
    rows_cot = jnp.concatenate([mine_ref[1], other_ref[1]], axis=0)
    pre_act = dot(rows_in, w_in)
    back_act = dot_lanes(rows_cot, w_out_ref[0])
    slope = (back_act * gelu_slope(pre_act)).astype(jnp.bfloat16)
    product = dot_lanes(slope, w_in)
    kept_ref[...] = product[:half]
    sent_ref[...] = product[half:].astype(jnp.bfloat16)


def backward_kernel(
    here_ref, cot_ref, probs_ref, query_ref, key_ref, value_ref, *refs
):
    *sum_refs, grad_query_ref, grad_key_ref, grad_value_ref = refs
    frames, blocks, features = query_ref.shape
    rows = frames * blocks
    scaling = (features // HEADS) ** (-0.5)
    query = query_ref[...].reshape(rows, features)
    key = key_ref[...].reshape(rows, features)
    value = value_ref[...].reshape(rows, features)
    sums = jnp.concatenate([sum_ref[...] for sum_ref in sum_refs], axis=0)
    added = lax.dot_general(
        here_ref[...].astype(jnp.bfloat16),
        sums,
        (((0,), (0,)), ((), ())),
        preferred_element_type=jnp.float32,
    )
    stream = (cot_ref[...].astype(jnp.float32) + added).astype(jnp.bfloat16)
    probs = probs_ref[...]
    grad_prob = jnp.concatenate(
        [dot_lanes(v, g) for v, g in zip(heads_of(value), heads_of(stream))], axis=1
    )
    centre = over_frames(probs * grad_prob, jnp.add, blocks)
    grad_score = probs * (grad_prob - centre)
    turned = grad_score.T.astype(jnp.bfloat16)
    grad_score = grad_score.astype(jnp.bfloat16)
    weights = probs.astype(jnp.bfloat16)

    def joined(parts):
        return jnp.concatenate(parts, axis=1).astype(jnp.bfloat16).reshape(frames, blocks, features)

    grad_value_ref[...] = joined(
        [dot(w, g) for w, g in zip(heads_of(weights), heads_of(stream))]
    )
    grad_key_ref[...] = joined(
        [dot(s, q) * scaling for s, q in zip(heads_of(grad_score), heads_of(query))]
    )
    grad_query_ref[...] = joined(
        [dot(turned[h * rows : (h + 1) * rows], k) * scaling for h, k in enumerate(heads_of(key))]
    )


def call(kernel, outs, scalars=0, flops=0, moved=0):
    smem = pl.BlockSpec(memory_space=pltpu.SMEM)
    vmem = pl.BlockSpec(memory_space=pltpu.VMEM)

    def run(*operands):
        return pl.pallas_call(
            kernel,
            out_shape=[jax.ShapeDtypeStruct(shape, dtype) for shape, dtype in outs],
            in_specs=[smem] * scalars + [vmem] * (len(operands) - scalars),
            out_specs=[vmem] * len(outs),
            cost_estimate=pl.CostEstimate(
                flops=flops, bytes_accessed=moved, transcendentals=0
            ),
            compiler_params=pltpu.CompilerParams(vmem_limit_bytes=40 * 1024 * 1024),
        )(*operands)

    return run


def swap(values, axis, step):
    size = lax.axis_size(axis)
    return lax.ppermute(values, axis, [(i, i ^ step) for i in range(size)])


def body(query_in, key_in, value_in, cotangent, w_in, w_out, gate_probs, chosen):
    bf16, f32 = jnp.bfloat16, jnp.float32
    frames, blocks, features = query_in.shape
    groups = lax.axis_size("grp")
    columns = lax.axis_size("frm")
    experts = gate_probs.shape[0]
    rows = frames * blocks
    patches_all = blocks * groups * columns
    per_expert = groups // experts
    levels = columns // CORES
    group, column = lax.axis_index("grp"), lax.axis_index("frm")
    place = jnp.stack([column, group * columns + column, group // per_expert])
    place = place.astype(jnp.int32)
    slots = experts * MOST

    span = cotangent.shape[1] // levels
    parts = call(
        functools.partial(turn_kernel, blocks, levels),
        [((span, features), bf16)] * levels,
        scalars=1,
    )(place, cotangent)
    arrived = [parts[0]] + [swap(parts[k], "frm", CORES * k) for k in range(1, levels)]
    probs, picked, here, weight = call(
        functools.partial(forward_kernel, experts, patches_all),
        [
            ((rows, HEADS * rows), f32),
            ((slots, features), bf16),
            ((slots, rows), f32),
            ((slots, 128), f32),
        ],
        scalars=1,
    )(place, query_in, key_in, value_in, chosen, gate_probs)
    away = swap(jnp.concatenate([part[blocks:] for part in arrived], axis=0), "frm", 1)
    (cot,) = call(
        functools.partial(gather_kernel, blocks), [((rows, features), bf16)], scalars=1
    )(place, *arrived, away)
    outgoing = call(
        functools.partial(pick_kernel, experts), [((2, MOST, features), bf16)] * experts
    )(here, weight, picked, cot)

    held = [outgoing[0]]
    held += [swap(outgoing[k], "grp", k * per_expert) for k in range(1, experts)]
    held = jnp.concatenate(held, axis=1)
    held = jnp.concatenate(
        [held] + [swap(held, "frm", CORES * k) for k in range(1, levels)], axis=1
    )
    held = jnp.concatenate(
        [held] + [swap(held, "grp", k) for k in range(1, per_expert)], axis=1
    )
    other = swap(held, "frm", 1)
    count = held.shape[1]
    kept, sent = call(
        expert_kernel, [((count, features), f32), ((count, features), bf16)]
    )(held, other, w_in, w_out)

    total = kept + swap(sent, "frm", 1).astype(f32)
    total = total.reshape(per_expert, count // per_expert, features)
    over_x = total[0]
    for k in range(1, per_expert):
        over_x = over_x + swap(total[k].astype(bf16), "grp", k).astype(f32)
    over_x = over_x.reshape(levels, slots, features)
    over_z = over_x[0]
    for k in range(1, levels):
        over_z = over_z + swap(over_x[k].astype(bf16), "frm", CORES * k).astype(f32)
    over_z = over_z.astype(bf16).reshape(experts, MOST, features)
    sums = [over_z[0]] + [swap(over_z[k], "grp", k * per_expert) for k in range(1, experts)]
    return call(backward_kernel, [((frames, blocks, features), bf16)] * 3)(
        here, cot, probs, query_in, key_in, value_in, *sums
    )


def solution(mesh):
    return jax.shard_map(
        body,
        mesh=mesh,
        in_specs=(
            P(None, ("grp", "frm"), None),
            P(None, ("grp", "frm"), None),
            P(None, ("grp", "frm"), None),
            P("frm", "grp", None),
            P("grp", None, "frm"),
            P("grp", "frm", None),
            P(),
            P(),
        ),
        out_specs=(
            P(None, ("grp", "frm"), None),
            P(None, ("grp", "frm"), None),
            P(None, ("grp", "frm"), None),
        ),
        check_vma=False,
    )
```

```python
import functools

import jax
import jax.numpy as jnp
from jax import lax
from jax.experimental import pallas as pl
from jax.experimental.pallas import tpu as pltpu
from jax.sharding import PartitionSpec as P

HEADS = 16
MOST = 2
CORES = 2
SUBLANES = 8

root_half = 0.7071067811865476
inv_root_tau = 0.3989422804014327

LANES_BOTH = (((1,), (1,)), ((), ()))
FIRST_BOTH = (((0,), (0,)), ((), ()))


def gelu_slope(pre_act):
    normal_cdf = 0.5 * (1.0 + lax.erf(pre_act * root_half))
    density = jnp.exp(-0.5 * pre_act * pre_act) * inv_root_tau
    return normal_cdf + pre_act * density


def dot(a, b):
    return jnp.dot(a, b, preferred_element_type=jnp.float32)


def dot_lanes(a, b):
    return lax.dot_general(a, b, LANES_BOTH, preferred_element_type=jnp.float32)


def over_frames(values, op, blocks):
    rows = values.shape[0]
    total = values[:SUBLANES]
    for start in range(SUBLANES, rows, SUBLANES):
        total = op(total, values[start : start + SUBLANES])
    step = blocks
    while step < SUBLANES:
        total = op(total, pltpu.roll(total, step, 0))
        step *= 2
    return jnp.concatenate([total] * (rows // SUBLANES), axis=0)


def heads_of(values):
    width = values.shape[1] // HEADS
    return [values[:, h * width : (h + 1) * width] for h in range(HEADS)]


def turn_kernel(cot_ref, out_ref):
    out_ref[...] = cot_ref[...].reshape(out_ref.shape)


def forward_kernel(
    patches_all, share, place_ref, query_hbm, key_hbm, value_hbm, chosen_ref, gate_ref,
    probs_ref, picked_ref, here_ref, weight_ref, spread_ref,
    query_ref, key_ref, value_ref, sems,
):
    copies = [
        pltpu.make_async_copy(source, target, sems.at[i])
        for i, (source, target) in enumerate(
            [(query_hbm, query_ref), (key_hbm, key_ref), (value_hbm, value_ref)]
        )
    ]
    for copy in copies:
        copy.start()
    frames, blocks, features = query_ref.shape
    rows = frames * blocks
    scaling = (features // HEADS) ** (-0.5)

    experts, cap = chosen_ref.shape
    myself = place_ref[0]
    before = (
        lax.broadcasted_iota(jnp.int32, (cap, cap), 0)
        < lax.broadcasted_iota(jnp.int32, (cap, cap), 1)
    ).astype(jnp.bfloat16)
    slot = lax.broadcasted_iota(jnp.int32, (SUBLANES, cap), 0)
    row_at = lax.broadcasted_iota(jnp.int32, (rows, cap), 0)
    found = []
    for e in range(experts):
        tokens = chosen_ref[e : e + 1, :]
        gates = gate_ref[e : e + 1, :]
        patch = tokens % patches_all
        owned = jnp.broadcast_to((patch // blocks == myself).astype(jnp.float32), slot.shape)
        rank = dot(owned.astype(jnp.bfloat16), before)
        taken = jnp.where((rank == slot.astype(jnp.float32)) & (owned > 0.0), 1.0, 0.0)
        position = (tokens // patches_all) * blocks + patch % blocks
        at_row = (row_at == position).astype(jnp.bfloat16)
        here = dot_lanes(taken.astype(jnp.bfloat16), at_row)
        weight = jnp.sum(taken * gates, axis=1, keepdims=True)
        here_ref[e * MOST : (e + 1) * MOST, :] = here[:MOST]
        weight_ref[e * MOST : (e + 1) * MOST, :] = jnp.broadcast_to(
            weight[:MOST], (MOST, weight_ref.shape[1])
        )
        found.append(here[:MOST])
    here = jnp.concatenate(found, axis=0).astype(jnp.bfloat16)
    cores, _, returns = spread_ref.shape
    slot_at = lax.broadcasted_iota(jnp.int32, (experts * MOST, returns), 0)
    back_at = lax.broadcasted_iota(jnp.int32, (experts * MOST, returns), 1)
    sender = back_at // MOST
    same = (sender // share == slot_at // MOST) & (back_at % MOST == slot_at % MOST)
    for c in range(cores):
        spread_ref[c] = lax.dot_general(
            here,
            (same & (sender % cores == c)).astype(jnp.bfloat16),
            FIRST_BOTH,
            preferred_element_type=jnp.float32,
        ).astype(jnp.bfloat16)

    for copy in copies:
        copy.wait()
    query = query_ref[...].reshape(rows, features)
    key = key_ref[...].reshape(rows, features)
    value = value_ref[...].reshape(rows, features)
    scores = jnp.concatenate(
        [dot_lanes(k, q) for k, q in zip(heads_of(key), heads_of(query))], axis=1
    )
    scores = scores * scaling
    raised = jnp.exp(scores - over_frames(scores, jnp.maximum, blocks))
    probs = raised / over_frames(raised, jnp.add, blocks)
    patch_in = lax.broadcasted_iota(jnp.int32, probs.shape, 0) % blocks
    patch_out = lax.broadcasted_iota(jnp.int32, probs.shape, 1) % blocks
    probs = jnp.where(patch_in == patch_out, probs, 0.0)
    probs_ref[...] = probs
    weights = probs.T.astype(jnp.bfloat16)
    mixed = jnp.concatenate(
        [dot(weights[h * rows : (h + 1) * rows], v) for h, v in enumerate(heads_of(value))],
        axis=1,
    ).astype(jnp.bfloat16)
    picked_ref[...] = dot(here, mixed).astype(jnp.bfloat16)


def pick_kernel(share, here_ref, weight_ref, picked_ref, cot_ref, out_ref):
    frames, blocks, features = cot_ref.shape
    rows = dot(here_ref[...].astype(jnp.bfloat16), cot_ref[...].reshape(frames * blocks, features))
    rows = (rows * weight_ref[:, :1]).astype(jnp.bfloat16)
    part = features // CORES
    for e in range(out_ref.shape[0] // share):
        slots = slice(e * MOST, (e + 1) * MOST)
        both = jnp.concatenate([picked_ref[slots], rows[slots]], axis=0)
        for i in range(share):
            c = i % CORES
            out_ref[e * share + i] = both[:, c * part : (c + 1) * part]


def half_expert(part, rows_ref, w_in_ref, w_out_hbm, held_ref, sem):
    width = rows_ref.shape[2]
    start = pl.multiple_of(part * width, width)
    copy = pltpu.make_async_copy(w_out_hbm.at[0, :, pl.ds(start, width)], held_ref, sem)
    copy.start()
    rows = rows_ref[...].reshape(-1, width)
    pre_act = dot(rows, w_in_ref[0, pl.ds(start, width), :])
    copy.wait()
    return pre_act, dot_lanes(rows, held_ref[...])


def first_kernel(place_ref, rows_ref, w_in_ref, w_out_hbm, pre_ref, back_ref, held_ref, sem):
    pre_ref[...], back_ref[...] = half_expert(
        place_ref[1], rows_ref, w_in_ref, w_out_hbm, held_ref, sem
    )


def second_kernel(
    place_ref, rows_ref, pre_ref, back_ref, w_in_ref, w_out_hbm, kept_ref, sent_ref, held_ref, sem
):
    mine = place_ref[1]
    pre_act, back_act = half_expert(
        1 - mine, rows_ref, w_in_ref, w_out_hbm, held_ref, sem
    )
    pre_act = pre_act + pre_ref[...]
    back_act = back_act + back_ref[...]
    count = pre_act.shape[0]
    back_act = pltpu.roll(back_act, count - MOST, 0)
    slope = (back_act * gelu_slope(pre_act)).astype(jnp.bfloat16)
    want = lax.broadcasted_iota(jnp.int32, (count // 2, count), 0)
    have = lax.broadcasted_iota(jnp.int32, (count // 2, count), 1)
    chosen = (have == (want // MOST) * (2 * MOST) + want % MOST).astype(jnp.bfloat16)
    slope = dot(chosen, slope).astype(jnp.bfloat16)
    width = rows_ref.shape[2]
    here = pl.multiple_of(mine * width, width)
    there = pl.multiple_of((1 - mine) * width, width)
    sent = dot_lanes(slope, w_in_ref[0, pl.ds(there, width), :])
    sent_ref[...] = sent.astype(jnp.bfloat16).reshape(sent_ref.shape)
    kept = dot_lanes(slope, w_in_ref[0, pl.ds(here, width), :])
    kept_ref[...] = kept.reshape(kept_ref.shape)


def backward_kernel(
    spread_ref, back_ref, cot_ref, probs_ref, query_ref, key_ref, value_ref,
    grad_query_ref, grad_key_ref, grad_value_ref,
):
    frames, blocks, features = query_ref.shape
    rows = frames * blocks
    scaling = (features // HEADS) ** (-0.5)
    query = query_ref[...].reshape(rows, features)
    key = key_ref[...].reshape(rows, features)
    value = value_ref[...].reshape(rows, features)
    back = back_ref[...].reshape(-1, back_ref.shape[2])
    added = jnp.concatenate([dot(spread_ref[c], back) for c in range(CORES)], axis=1)
    cot = cot_ref[...].reshape(rows, features)
    stream = (cot.astype(jnp.float32) + added).astype(jnp.bfloat16)
    probs = probs_ref[...]
    grad_prob = jnp.concatenate(
        [dot_lanes(v, g) for v, g in zip(heads_of(value), heads_of(stream))], axis=1
    )
    centre = over_frames(probs * grad_prob, jnp.add, blocks)
    grad_score = probs * (grad_prob - centre)
    turned = grad_score.T.astype(jnp.bfloat16)
    grad_score = grad_score.astype(jnp.bfloat16)
    weights = probs.astype(jnp.bfloat16)

    def joined(parts):
        return jnp.concatenate(parts, axis=1).astype(jnp.bfloat16).reshape(frames, blocks, features)

    grad_value_ref[...] = joined(
        [dot(w, g) for w, g in zip(heads_of(weights), heads_of(stream))]
    )
    grad_key_ref[...] = joined(
        [dot(s, q) * scaling for s, q in zip(heads_of(grad_score), heads_of(query))]
    )
    grad_query_ref[...] = joined(
        [dot(turned[h * rows : (h + 1) * rows], k) * scaling for h, k in enumerate(heads_of(key))]
    )


def call(kernel, outs, operands, places, scratch=()):
    smem, vmem, hbm = (
        pl.BlockSpec(memory_space=space) for space in (pltpu.SMEM, pltpu.VMEM, pltpu.HBM)
    )
    spaces = {"s": smem, "v": vmem, "h": hbm}
    return pl.pallas_call(
        kernel,
        out_shape=[jax.ShapeDtypeStruct(shape, dtype) for shape, dtype in outs],
        in_specs=[spaces[place] for place in places],
        out_specs=[vmem] * len(outs),
        scratch_shapes=list(scratch),
        compiler_params=pltpu.CompilerParams(vmem_limit_bytes=40 * 1024 * 1024),
    )(*operands)


def body(query_in, key_in, value_in, cotangent, w_in, w_out, gate_probs, chosen):
    bf16, f32 = jnp.bfloat16, jnp.float32
    frames, blocks, features = query_in.shape
    groups = lax.axis_size("grp")
    columns = lax.axis_size("frm")
    experts = gate_probs.shape[0]
    devices = groups * columns
    share = devices // experts
    rows = frames * blocks
    slots = experts * MOST
    part = features // CORES
    hidden = w_in.shape[2]
    column = lax.axis_index("frm")
    place = jnp.stack([lax.axis_index("grp") * columns + column, column % CORES])
    place = place.astype(jnp.int32)
    everyone = ("grp", "frm")

    def swap(values):
        return lax.ppermute(values, "frm", [(i, i ^ 1) for i in range(columns)])

    (turned,) = call(
        turn_kernel, [((columns, blocks, features), bf16)], [cotangent], "v"
    )
    cot = lax.all_to_all(turned, "frm", split_axis=0, concat_axis=0, tiled=True)
    probs, picked, here, weight, spread = call(
        functools.partial(forward_kernel, blocks * devices, share),
        [
            ((rows, HEADS * rows), f32),
            ((slots, features), bf16),
            ((slots, rows), f32),
            ((slots, 128), f32),
            ((CORES, rows, devices * MOST), bf16),
        ],
        [place, query_in, key_in, value_in, chosen, gate_probs],
        "shhhvv",
        [pltpu.VMEM(query_in.shape, bf16)] * 3 + [pltpu.SemaphoreType.DMA((3,))],
    )
    (outgoing,) = call(
        functools.partial(pick_kernel, share),
        [((devices, 2 * MOST, part), bf16)],
        [here, weight, picked, cot],
        "vvvv",
    )
    held = lax.all_to_all(outgoing, everyone, split_axis=0, concat_axis=0, tiled=True)
    other = swap(held)
    acts = ((devices * 2 * MOST, hidden), f32)
    scratch = [pltpu.VMEM((hidden, part), bf16), pltpu.SemaphoreType.DMA]
    pre_act, back_act = call(
        first_kernel, [acts, acts], [place, held, w_in, w_out], "svvh", scratch
    )
    piece = (devices, MOST, part)
    kept, sent = call(
        second_kernel,
        [(piece, f32), (piece, bf16)],
        [place, other, pre_act, back_act, w_in, w_out],
        "svvvvh",
        scratch,
    )
    total = (kept + swap(sent).astype(f32)).astype(bf16)
    back = lax.all_to_all(total, everyone, split_axis=0, concat_axis=0, tiled=True)
    return call(
        backward_kernel,
        [((frames, blocks, features), bf16)] * 3,
        [spread, back, cot, probs, query_in, key_in, value_in],
        "vvvvvvv",
    )


def solution(mesh):
    return jax.shard_map(
        body,
        mesh=mesh,
        in_specs=(
            P(None, ("grp", "frm"), None),
            P(None, ("grp", "frm"), None),
            P(None, ("grp", "frm"), None),
            P("frm", "grp", None),
            P("grp", None, "frm"),
            P("grp", "frm", None),
            P(),
            P(),
        ),
        out_specs=(
            P(None, ("grp", "frm"), None),
            P(None, ("grp", "frm"), None),
            P(None, ("grp", "frm"), None),
        ),
        check_vma=False,
    )
```

```python
import functools

import jax
import jax.numpy as jnp
from jax import lax
from jax.experimental import pallas as pl
from jax.experimental.pallas import tpu as pltpu
from jax.sharding import PartitionSpec as P

HEADS = 16
MOST = 2
CORES = 2
SUBLANES = 8
LANES = 128

root_half = 0.7071067811865476
inv_root_tau = 0.3989422804014327

LANES_BOTH = (((1,), (1,)), ((), ()))
FIRST_BOTH = (((0,), (0,)), ((), ()))


def gelu_slope(pre_act):
    normal_cdf = 0.5 * (1.0 + lax.erf(pre_act * root_half))
    density = jnp.exp(-0.5 * pre_act * pre_act) * inv_root_tau
    return normal_cdf + pre_act * density


def dot(a, b):
    return jnp.dot(a, b, preferred_element_type=jnp.float32)


def dot_lanes(a, b):
    return lax.dot_general(a, b, LANES_BOTH, preferred_element_type=jnp.float32)


def over_frames(values, op, blocks):
    rows = values.shape[0]
    total = values[:SUBLANES]
    for start in range(SUBLANES, rows, SUBLANES):
        total = op(total, values[start : start + SUBLANES])
    step = blocks
    while step < SUBLANES:
        total = op(total, pltpu.roll(total, step, 0))
        step *= 2
    return jnp.concatenate([total] * (rows // SUBLANES), axis=0)


def heads_of(values):
    width = values.shape[1] // HEADS
    return [values[:, h * width : (h + 1) * width] for h in range(HEADS)]


def turn_kernel(cot_hbm, out_ref, cot_ref, sem):
    copy = pltpu.make_async_copy(cot_hbm, cot_ref, sem)
    copy.start()
    copy.wait()
    out_ref[...] = cot_ref[...].reshape(out_ref.shape)


def forward_kernel(
    patches_all, share, place_ref,
    chosen_hbm, gate_hbm, query_hbm, key_hbm, value_hbm, w_in_hbm, w_out_hbm,
    query_ref, key_ref, value_ref, w_in_ref, w_out_ref,
    probs_ref, picked_ref, here_ref, weight_ref, spread_ref,
    chosen_ref, gate_ref, sems,
):
    sources = [chosen_hbm, gate_hbm, query_hbm, key_hbm, value_hbm, w_in_hbm, w_out_hbm]
    targets = [chosen_ref, gate_ref, query_ref, key_ref, value_ref, w_in_ref, w_out_ref]
    copies = [
        pltpu.make_async_copy(source, target, sems.at[i])
        for i, (source, target) in enumerate(zip(sources, targets))
    ]
    for copy in copies:
        copy.start()
    frames, blocks, features = query_ref.shape
    rows = frames * blocks
    scaling = (features // HEADS) ** (-0.5)

    for copy in copies[:2]:
        copy.wait()
    experts, cap = chosen_ref.shape
    myself = place_ref[0]
    before = (
        lax.broadcasted_iota(jnp.int32, (cap, cap), 0)
        < lax.broadcasted_iota(jnp.int32, (cap, cap), 1)
    ).astype(jnp.bfloat16)
    slot = lax.broadcasted_iota(jnp.int32, (SUBLANES, cap), 0)
    row_at = lax.broadcasted_iota(jnp.int32, (rows, cap), 0)
    found = []
    for e in range(experts):
        tokens = chosen_ref[e : e + 1, :]
        gates = gate_ref[e : e + 1, :]
        patch = tokens % patches_all
        owned = jnp.broadcast_to((patch // blocks == myself).astype(jnp.float32), slot.shape)
        rank = dot(owned.astype(jnp.bfloat16), before)
        taken = jnp.where((rank == slot.astype(jnp.float32)) & (owned > 0.0), 1.0, 0.0)
        position = (tokens // patches_all) * blocks + patch % blocks
        at_row = (row_at == position).astype(jnp.bfloat16)
        here = dot_lanes(taken.astype(jnp.bfloat16), at_row)
        weight = jnp.sum(taken * gates, axis=1, keepdims=True)
        here_ref[e * MOST : (e + 1) * MOST, :] = here[:MOST]
        weight_ref[e * MOST : (e + 1) * MOST, :] = jnp.broadcast_to(
            weight[:MOST], (MOST, weight_ref.shape[1])
        )
        found.append(here[:MOST])
    here = jnp.concatenate(found, axis=0).astype(jnp.bfloat16)
    cores, _, returns = spread_ref.shape
    slot_at = lax.broadcasted_iota(jnp.int32, (experts * MOST, returns), 0)
    back_at = lax.broadcasted_iota(jnp.int32, (experts * MOST, returns), 1)
    sender = back_at // MOST
    same = (sender // share == slot_at // MOST) & (back_at % MOST == slot_at % MOST)
    for c in range(cores):
        spread_ref[c] = lax.dot_general(
            here,
            (same & (sender % cores == c)).astype(jnp.bfloat16),
            FIRST_BOTH,
            preferred_element_type=jnp.float32,
        ).astype(jnp.bfloat16)

    for copy in copies[2:5]:
        copy.wait()
    query = query_ref[...].reshape(rows, features)
    key = key_ref[...].reshape(rows, features)
    value = value_ref[...].reshape(rows, features)
    scores = jnp.concatenate(
        [dot_lanes(k, q) for k, q in zip(heads_of(key), heads_of(query))], axis=1
    )
    scores = scores * scaling
    raised = jnp.exp(scores - over_frames(scores, jnp.maximum, blocks))
    probs = raised / over_frames(raised, jnp.add, blocks)
    patch_in = lax.broadcasted_iota(jnp.int32, probs.shape, 0) % blocks
    patch_out = lax.broadcasted_iota(jnp.int32, probs.shape, 1) % blocks
    probs = jnp.where(patch_in == patch_out, probs, 0.0)
    probs_ref[...] = probs
    weights = probs.T.astype(jnp.bfloat16)
    mixed = jnp.concatenate(
        [dot(weights[h * rows : (h + 1) * rows], v) for h, v in enumerate(heads_of(value))],
        axis=1,
    ).astype(jnp.bfloat16)
    picked_ref[...] = dot(here, mixed).astype(jnp.bfloat16)
    for copy in copies[5:]:
        copy.wait()


def pick_kernel(share, here_ref, weight_ref, picked_ref, cot_ref, out_ref):
    frames, blocks, features = cot_ref.shape
    rows = dot(here_ref[...].astype(jnp.bfloat16), cot_ref[...].reshape(frames * blocks, features))
    rows = (rows * weight_ref[:, :1]).astype(jnp.bfloat16)
    part = features // CORES
    for e in range(out_ref.shape[0] // share):
        slots = slice(e * MOST, (e + 1) * MOST)
        both = jnp.concatenate([picked_ref[slots], rows[slots]], axis=0)
        for i in range(share):
            c = i % CORES
            out_ref[e * share + i] = both[:, c * part : (c + 1) * part]


def half_expert(part, rows_ref, w_in_ref, w_out_ref, pre_ref, back_ref):
    width = rows_ref.shape[2]
    start = pl.multiple_of(part * width, width)
    rows = rows_ref[...].reshape(-1, width)
    pre_act = dot(rows, w_in_ref[0, pl.ds(start, width), :])
    back_act = dot_lanes(rows, w_out_ref[0, :, pl.ds(start, width)])
    for i in range(pre_ref.shape[0]):
        pre_ref[i] = pre_act[:, i * LANES : (i + 1) * LANES]
        back_ref[i] = back_act[:, i * LANES : (i + 1) * LANES]


def first_kernel(place_ref, rows_ref, w_in_ref, w_out_ref, pre_ref, back_ref):
    half_expert(place_ref[1], rows_ref, w_in_ref, w_out_ref, pre_ref, back_ref)


def second_kernel(
    place_ref, rows_ref, pre_ref, back_ref, w_in_ref, w_out_ref,
    kept_ref, sent_ref, more_pre_ref, more_back_ref,
):
    mine = place_ref[1]
    half_expert(1 - mine, rows_ref, w_in_ref, w_out_ref, more_pre_ref, more_back_ref)
    devices, stride, width = rows_ref.shape

    def every(start, *refs):
        parts = [
            sum(ref[i, pl.ds(start, devices, stride=stride), :] for ref in refs)
            for i in range(refs[0].shape[0])
        ]
        return jnp.concatenate(parts, axis=1)

    slope = jnp.concatenate(
        [
            every(MOST + m, back_ref, more_back_ref) * gelu_slope(every(m, pre_ref, more_pre_ref))
            for m in range(MOST)
        ],
        axis=0,
    ).astype(jnp.bfloat16)
    want = lax.broadcasted_iota(jnp.int32, (devices * MOST, devices * MOST), 0)
    have = lax.broadcasted_iota(jnp.int32, (devices * MOST, devices * MOST), 1)
    order = (have == (want % MOST) * devices + want // MOST).astype(jnp.bfloat16)
    slope = dot(order, slope).astype(jnp.bfloat16)
    here = pl.multiple_of(mine * width, width)
    there = pl.multiple_of((1 - mine) * width, width)
    sent = dot_lanes(slope, w_in_ref[0, pl.ds(there, width), :])
    sent_ref[...] = sent.astype(jnp.bfloat16).reshape(sent_ref.shape)
    kept = dot_lanes(slope, w_in_ref[0, pl.ds(here, width), :])
    kept_ref[...] = kept.reshape(kept_ref.shape)


def backward_kernel(
    spread_ref, back_ref, cot_ref, probs_ref, query_ref, key_ref, value_ref,
    grad_query_ref, grad_key_ref, grad_value_ref,
):
    frames, blocks, features = query_ref.shape
    rows = frames * blocks
    scaling = (features // HEADS) ** (-0.5)
    query = query_ref[...].reshape(rows, features)
    key = key_ref[...].reshape(rows, features)
    value = value_ref[...].reshape(rows, features)
    back = back_ref[...].reshape(-1, back_ref.shape[2])
    added = jnp.concatenate([dot(spread_ref[c], back) for c in range(CORES)], axis=1)
    cot = cot_ref[...].reshape(rows, features)
    stream = (cot.astype(jnp.float32) + added).astype(jnp.bfloat16)
    probs = probs_ref[...]
    grad_prob = jnp.concatenate(
        [dot_lanes(v, g) for v, g in zip(heads_of(value), heads_of(stream))], axis=1
    )
    centre = over_frames(probs * grad_prob, jnp.add, blocks)
    grad_score = probs * (grad_prob - centre)
    turned = grad_score.T.astype(jnp.bfloat16)
    grad_score = grad_score.astype(jnp.bfloat16)
    weights = probs.astype(jnp.bfloat16)

    def joined(parts):
        return jnp.concatenate(parts, axis=1).astype(jnp.bfloat16).reshape(frames, blocks, features)

    grad_value_ref[...] = joined(
        [dot(w, g) for w, g in zip(heads_of(weights), heads_of(stream))]
    )
    grad_key_ref[...] = joined(
        [dot(s, q) * scaling for s, q in zip(heads_of(grad_score), heads_of(query))]
    )
    grad_query_ref[...] = joined(
        [dot(turned[h * rows : (h + 1) * rows], k) * scaling for h, k in enumerate(heads_of(key))]
    )


def call(kernel, outs, operands, places, scratch=()):
    smem, vmem, hbm = (
        pl.BlockSpec(memory_space=space) for space in (pltpu.SMEM, pltpu.VMEM, pltpu.HBM)
    )
    spaces = {"s": smem, "v": vmem, "h": hbm}
    return pl.pallas_call(
        kernel,
        out_shape=[jax.ShapeDtypeStruct(shape, dtype) for shape, dtype in outs],
        in_specs=[spaces[place] for place in places],
        out_specs=[vmem] * len(outs),
        scratch_shapes=list(scratch),
        compiler_params=pltpu.CompilerParams(vmem_limit_bytes=32 * 1024 * 1024),
    )(*[
        pltpu.with_memory_space_constraint(operand, pltpu.HBM) if place == "h" else operand
        for operand, place in zip(operands, places)
    ])


def body(query_in, key_in, value_in, cotangent, w_in, w_out, gate_probs, chosen):
    bf16, f32 = jnp.bfloat16, jnp.float32
    frames, blocks, features = query_in.shape
    groups = lax.axis_size("grp")
    columns = lax.axis_size("frm")
    experts = gate_probs.shape[0]
    devices = groups * columns
    share = devices // experts
    rows = frames * blocks
    slots = experts * MOST
    part = features // CORES
    hidden = w_in.shape[2]
    column = lax.axis_index("frm")
    place = jnp.stack([lax.axis_index("grp") * columns + column, column % CORES])
    place = place.astype(jnp.int32)
    everyone = ("grp", "frm")

    def swap(values):
        return lax.ppermute(values, "frm", [(i, i ^ 1) for i in range(columns)])

    (turned,) = call(
        turn_kernel, [((columns, blocks, features), bf16)], [cotangent], "h",
        [pltpu.VMEM(cotangent.shape, bf16), pltpu.SemaphoreType.DMA],
    )
    cot = lax.all_to_all(turned, "frm", split_axis=0, concat_axis=0, tiled=True)
    query, key, value, w_in_near, w_out_near, probs, picked, here, weight, spread = call(
        functools.partial(forward_kernel, blocks * devices, share),
        [
            *[(array.shape, bf16) for array in (query_in, key_in, value_in, w_in, w_out)],
            ((rows, HEADS * rows), f32),
            ((slots, features), bf16),
            ((slots, rows), f32),
            ((slots, LANES), f32),
            ((CORES, rows, devices * MOST), bf16),
        ],
        [place, chosen, gate_probs, query_in, key_in, value_in, w_in, w_out],
        "shhhhhhh",
        [
            pltpu.VMEM(chosen.shape, jnp.int32),
            pltpu.VMEM(gate_probs.shape, f32),
            pltpu.SemaphoreType.DMA((7,)),
        ],
    )
    (outgoing,) = call(
        functools.partial(pick_kernel, share),
        [((devices, 2 * MOST, part), bf16)],
        [here, weight, picked, cot],
        "vvvv",
    )
    held = lax.all_to_all(outgoing, everyone, split_axis=0, concat_axis=0, tiled=True)
    other = swap(held)
    acts = (hidden // LANES, devices * 2 * MOST, LANES)
    pre_act, back_act = call(
        first_kernel, [(acts, f32), (acts, f32)], [place, held, w_in_near, w_out_near], "svvv"
    )
    piece = (devices, MOST, part)
    kept, sent = call(
        second_kernel,
        [(piece, f32), (piece, bf16)],
        [place, other, pre_act, back_act, w_in_near, w_out_near],
        "svvvvv",
        [pltpu.VMEM(acts, f32), pltpu.VMEM(acts, f32)],
    )
    total = (kept + swap(sent).astype(f32)).astype(bf16)
    back = lax.all_to_all(total, everyone, split_axis=0, concat_axis=0, tiled=True)
    return call(
        backward_kernel,
        [((frames, blocks, features), bf16)] * 3,
        [spread, back, cot, probs, query, key, value],
        "vvvvvvv",
    )


def solution(mesh):
    return jax.shard_map(
        body,
        mesh=mesh,
        in_specs=(
            P(None, ("grp", "frm"), None),
            P(None, ("grp", "frm"), None),
            P(None, ("grp", "frm"), None),
            P("frm", "grp", None),
            P("grp", None, "frm"),
            P("grp", "frm", None),
            P(),
            P(),
        ),
        out_specs=(
            P(None, ("grp", "frm"), None),
            P(None, ("grp", "frm"), None),
            P(None, ("grp", "frm"), None),
        ),
        check_vma=False,
    )
```

```python
import functools

import jax
import jax.numpy as jnp
from jax import lax
from jax.experimental import pallas as pl
from jax.experimental.pallas import tpu as pltpu
from jax.sharding import PartitionSpec as P

HEADS = 16
MOST = 2
CORES = 2
SUBLANES = 8
LANES = 128
TILE = 16

root_half = 0.7071067811865476
inv_root_tau = 0.3989422804014327

LANES_BOTH = (((1,), (1,)), ((), ()))
FIRST_BOTH = (((0,), (0,)), ((), ()))


def gelu_slope(pre_act):
    normal_cdf = 0.5 * (1.0 + lax.erf(pre_act * root_half))
    density = jnp.exp(-0.5 * pre_act * pre_act) * inv_root_tau
    return normal_cdf + pre_act * density


def dot(a, b):
    return jnp.dot(a, b, preferred_element_type=jnp.float32)


def dot_lanes(a, b):
    return lax.dot_general(a, b, LANES_BOTH, preferred_element_type=jnp.float32)


def over_frames(values, op, blocks):
    rows = values.shape[0]
    total = values[:SUBLANES]
    for start in range(SUBLANES, rows, SUBLANES):
        total = op(total, values[start : start + SUBLANES])
    step = blocks
    while step < SUBLANES:
        total = op(total, pltpu.roll(total, step, 0))
        step *= 2
    return jnp.concatenate([total] * (rows // SUBLANES), axis=0)


def heads_of(values):
    width = values.shape[1] // HEADS
    return [values[:, h * width : (h + 1) * width] for h in range(HEADS)]


def turn_kernel(cot_hbm, out_hbm, cot_ref, turned_ref, sems):
    _, rows, _ = cot_ref.shape
    columns, blocks, features = turned_ref.shape
    pieces = rows // TILE
    span = columns // pieces
    arrivals = [
        pltpu.make_async_copy(
            cot_hbm.at[:, pl.ds(i * TILE, TILE)], cot_ref.at[:, pl.ds(i * TILE, TILE)], sems.at[0, i]
        )
        for i in range(pieces)
    ]
    for copy in arrivals:
        copy.start()
    leaving = []
    for i, copy in enumerate(arrivals):
        copy.wait()
        part = slice(i * span, (i + 1) * span)
        turned_ref[part] = cot_ref[0, i * TILE : (i + 1) * TILE, :].reshape(span, blocks, features)
        copy = pltpu.make_async_copy(
            turned_ref.at[pl.ds(i * span, span)], out_hbm.at[pl.ds(i * span, span)], sems.at[1, i]
        )
        copy.start()
        leaving.append(copy)
    for copy in leaving:
        copy.wait()


def forward_kernel(
    patches_all, share, place_ref,
    chosen_hbm, gate_hbm, query_hbm, key_hbm, value_hbm, w_in_hbm,
    query_ref, key_ref, value_ref, w_in_ref,
    probs_ref, picked_ref, here_ref, weight_ref, spread_ref,
    chosen_ref, gate_ref, sems,
):
    sources = [chosen_hbm, gate_hbm, query_hbm, key_hbm, value_hbm, w_in_hbm]
    targets = [chosen_ref, gate_ref, query_ref, key_ref, value_ref, w_in_ref]
    copies = [
        pltpu.make_async_copy(source, target, sems.at[i])
        for i, (source, target) in enumerate(zip(sources, targets))
    ]
    for copy in copies:
        copy.start()
    frames, blocks, features = query_ref.shape
    rows = frames * blocks
    scaling = (features // HEADS) ** (-0.5)

    for copy in copies[:2]:
        copy.wait()
    experts, cap = chosen_ref.shape
    myself = place_ref[0]
    before = (
        lax.broadcasted_iota(jnp.int32, (cap, cap), 0)
        < lax.broadcasted_iota(jnp.int32, (cap, cap), 1)
    ).astype(jnp.bfloat16)
    slot = lax.broadcasted_iota(jnp.int32, (SUBLANES, cap), 0)
    row_at = lax.broadcasted_iota(jnp.int32, (rows, cap), 0)
    found = []
    for e in range(experts):
        tokens = chosen_ref[e : e + 1, :]
        gates = gate_ref[e : e + 1, :]
        patch = tokens % patches_all
        owned = jnp.broadcast_to((patch // blocks == myself).astype(jnp.float32), slot.shape)
        rank = dot(owned.astype(jnp.bfloat16), before)
        taken = jnp.where((rank == slot.astype(jnp.float32)) & (owned > 0.0), 1.0, 0.0)
        position = (tokens // patches_all) * blocks + patch % blocks
        at_row = (row_at == position).astype(jnp.bfloat16)
        here = dot_lanes(taken.astype(jnp.bfloat16), at_row)
        weight = jnp.sum(taken * gates, axis=1, keepdims=True)
        here_ref[e * MOST : (e + 1) * MOST, :] = here[:MOST]
        weight_ref[e * MOST : (e + 1) * MOST, :] = jnp.broadcast_to(
            weight[:MOST], (MOST, weight_ref.shape[1])
        )
        found.append(here[:MOST])
    here = jnp.concatenate(found, axis=0).astype(jnp.bfloat16)
    cores, _, returns = spread_ref.shape
    slot_at = lax.broadcasted_iota(jnp.int32, (experts * MOST, returns), 0)
    back_at = lax.broadcasted_iota(jnp.int32, (experts * MOST, returns), 1)
    sender = back_at // MOST
    same = (sender // share == slot_at // MOST) & (back_at % MOST == slot_at % MOST)
    for c in range(cores):
        spread_ref[c] = lax.dot_general(
            here,
            (same & (sender % cores == c)).astype(jnp.bfloat16),
            FIRST_BOTH,
            preferred_element_type=jnp.float32,
        ).astype(jnp.bfloat16)

    for copy in copies[2:5]:
        copy.wait()
    query = query_ref[...].reshape(rows, features)
    key = key_ref[...].reshape(rows, features)
    value = value_ref[...].reshape(rows, features)
    scores = jnp.concatenate(
        [dot_lanes(k, q) for k, q in zip(heads_of(key), heads_of(query))], axis=1
    )
    scores = scores * scaling
    raised = jnp.exp(scores - over_frames(scores, jnp.maximum, blocks))
    probs = raised / over_frames(raised, jnp.add, blocks)
    patch_in = lax.broadcasted_iota(jnp.int32, probs.shape, 0) % blocks
    patch_out = lax.broadcasted_iota(jnp.int32, probs.shape, 1) % blocks
    probs = jnp.where(patch_in == patch_out, probs, 0.0)
    probs_ref[...] = probs
    weights = probs.T.astype(jnp.bfloat16)
    mixed = jnp.concatenate(
        [dot(weights[h * rows : (h + 1) * rows], v) for h, v in enumerate(heads_of(value))],
        axis=1,
    ).astype(jnp.bfloat16)
    picked_ref[...] = dot(here, mixed).astype(jnp.bfloat16)
    for copy in copies[5:]:
        copy.wait()


def pick_kernel(share, here_ref, weight_ref, picked_ref, cot_ref, out_ref):
    frames, blocks, features = cot_ref.shape
    rows = dot(here_ref[...].astype(jnp.bfloat16), cot_ref[...].reshape(frames * blocks, features))
    rows = (rows * weight_ref[:, :1]).astype(jnp.bfloat16)
    part = features // CORES
    for e in range(out_ref.shape[0] // share):
        slots = slice(e * MOST, (e + 1) * MOST)
        both = jnp.concatenate([picked_ref[slots], rows[slots]], axis=0)
        for i in range(share):
            c = i % CORES
            out_ref[e * share + i] = both[:, c * part : (c + 1) * part]


def put_tiles(ref, values):
    for i in range(ref.shape[0]):
        ref[i] = values[:, i * LANES : (i + 1) * LANES]


def take_tiles(ref):
    return jnp.concatenate([ref[i] for i in range(ref.shape[0])], axis=1)


def part_of(part, width):
    return pl.ds(pl.multiple_of(part * width, width), width)


def first_kernel(
    place_ref, rows_ref, w_in_ref, w_out_hbm, pre_ref, back_ref, far_ref, near_ref, sems
):
    width = rows_ref.shape[2]
    mine = place_ref[1]
    copies = [
        pltpu.make_async_copy(
            w_out_hbm.at[0, :, part_of(part, width)], target, sems.at[i]
        )
        for i, (part, target) in enumerate([(mine, near_ref), (1 - mine, far_ref)])
    ]
    for copy in copies:
        copy.start()
    rows = rows_ref[...].reshape(-1, width)
    put_tiles(pre_ref, dot(rows, w_in_ref[0, part_of(mine, width), :]))
    copies[0].wait()
    put_tiles(back_ref, dot_lanes(rows, near_ref[...]))
    copies[1].wait()


def second_kernel(
    place_ref, rows_ref, pre_ref, back_ref, w_in_ref, far_ref,
    slope_ref, sent_ref, more_pre_ref, more_back_ref, mixed_ref,
):
    devices, stride, width = rows_ref.shape
    other = part_of(1 - place_ref[1], width)
    rows = rows_ref[...].reshape(-1, width)
    put_tiles(more_pre_ref, dot(rows, w_in_ref[0, other, :]))
    put_tiles(more_back_ref, dot_lanes(rows, far_ref[...]))
    for i in range(pre_ref.shape[0]):
        for m in range(MOST):
            at_in = pl.ds(m, devices, stride=stride)
            at_cot = pl.ds(MOST + m, devices, stride=stride)
            pre_act = pre_ref[i, at_in, :] + more_pre_ref[i, at_in, :]
            back_act = back_ref[i, at_cot, :] + more_back_ref[i, at_cot, :]
            mixed_ref[i, pl.ds(m, devices, stride=MOST), :] = back_act * gelu_slope(pre_act)
    slope = take_tiles(mixed_ref).astype(jnp.bfloat16)
    slope_ref[...] = slope
    sent_ref[...] = dot_lanes(slope, w_in_ref[0, other, :]).astype(jnp.bfloat16)


def third_kernel(place_ref, slope_ref, w_in_ref, kept_ref):
    width = kept_ref.shape[1]
    kept_ref[...] = dot_lanes(slope_ref[...], w_in_ref[0, part_of(place_ref[1], width), :])


def sum_kernel(kept_ref, came_ref, out_ref):
    total = kept_ref[...] + came_ref[...].astype(jnp.float32)
    out_ref[...] = total.astype(jnp.bfloat16).reshape(out_ref.shape)


def backward_kernel(
    spread_ref, back_ref, cot_ref, probs_ref, query_ref, key_ref, value_ref,
    grad_query_hbm, grad_key_hbm, grad_value_hbm,
    grad_query_ref, grad_key_ref, grad_value_ref, sems,
):
    frames, blocks, features = query_ref.shape
    rows = frames * blocks
    scaling = (features // HEADS) ** (-0.5)
    query = query_ref[...].reshape(rows, features)
    key = key_ref[...].reshape(rows, features)
    value = value_ref[...].reshape(rows, features)
    back = back_ref[...].reshape(-1, back_ref.shape[2])
    added = jnp.concatenate([dot(spread_ref[c], back) for c in range(CORES)], axis=1)
    cot = cot_ref[...].reshape(rows, features)
    stream = (cot.astype(jnp.float32) + added).astype(jnp.bfloat16)
    probs = probs_ref[...]
    weights = probs.astype(jnp.bfloat16)
    copies = []

    def put(ref, hbm, parts):
        joined = jnp.concatenate(parts, axis=1).astype(jnp.bfloat16)
        ref[...] = joined.reshape(frames, blocks, features)
        copy = pltpu.make_async_copy(ref, hbm, sems.at[len(copies)])
        copy.start()
        copies.append(copy)

    put(
        grad_value_ref,
        grad_value_hbm,
        [dot(w, g) for w, g in zip(heads_of(weights), heads_of(stream))],
    )
    grad_prob = jnp.concatenate(
        [dot_lanes(v, g) for v, g in zip(heads_of(value), heads_of(stream))], axis=1
    )
    centre = over_frames(probs * grad_prob, jnp.add, blocks)
    grad_score = probs * (grad_prob - centre)
    turned = grad_score.T.astype(jnp.bfloat16)
    grad_score = grad_score.astype(jnp.bfloat16)
    put(
        grad_key_ref,
        grad_key_hbm,
        [dot(s, q) * scaling for s, q in zip(heads_of(grad_score), heads_of(query))],
    )
    put(
        grad_query_ref,
        grad_query_hbm,
        [dot(turned[h * rows : (h + 1) * rows], k) * scaling for h, k in enumerate(heads_of(key))],
    )
    for copy in copies:
        copy.wait()


def call(kernel, outs, operands, places, scratch=(), results="v"):
    smem, vmem, hbm = (
        pl.BlockSpec(memory_space=space) for space in (pltpu.SMEM, pltpu.VMEM, pl.ANY)
    )
    spaces = {"s": smem, "v": vmem, "h": hbm}
    return pl.pallas_call(
        kernel,
        out_shape=[jax.ShapeDtypeStruct(shape, dtype) for shape, dtype in outs],
        in_specs=[spaces[place] for place in places],
        out_specs=[spaces[results]] * len(outs),
        scratch_shapes=list(scratch),
        compiler_params=pltpu.CompilerParams(vmem_limit_bytes=32 * 1024 * 1024),
    )(*[
        pltpu.with_memory_space_constraint(operand, pltpu.HBM) if place == "h" else operand
        for operand, place in zip(operands, places)
    ])


def body(query_in, key_in, value_in, cotangent, w_in, w_out, gate_probs, chosen):
    bf16, f32 = jnp.bfloat16, jnp.float32
    frames, blocks, features = query_in.shape
    groups = lax.axis_size("grp")
    columns = lax.axis_size("frm")
    experts = gate_probs.shape[0]
    devices = groups * columns
    share = devices // experts
    rows = frames * blocks
    slots = experts * MOST
    part = features // CORES
    hidden = w_in.shape[2]
    column = lax.axis_index("frm")
    place = jnp.stack([lax.axis_index("grp") * columns + column, column % CORES])
    place = place.astype(jnp.int32)
    everyone = ("grp", "frm")

    def swap(values):
        return lax.ppermute(values, "frm", [(i, i ^ 1) for i in range(columns)])

    (turned,) = call(
        turn_kernel, [((columns, blocks, features), bf16)], [cotangent], "h",
        [
            pltpu.VMEM(cotangent.shape, bf16),
            pltpu.VMEM((columns, blocks, features), bf16),
            pltpu.SemaphoreType.DMA((2, cotangent.shape[1] // TILE)),
        ],
        "h",
    )
    cot = lax.all_to_all(turned, "frm", split_axis=0, concat_axis=0, tiled=True)
    query, key, value, w_in_near, probs, picked, here, weight, spread = call(
        functools.partial(forward_kernel, blocks * devices, share),
        [
            *[(array.shape, bf16) for array in (query_in, key_in, value_in, w_in)],
            ((rows, HEADS * rows), f32),
            ((slots, features), bf16),
            ((slots, rows), f32),
            ((slots, LANES), f32),
            ((CORES, rows, devices * MOST), bf16),
        ],
        [place, chosen, gate_probs, query_in, key_in, value_in, w_in],
        "shhhhhh",
        [
            pltpu.VMEM(chosen.shape, jnp.int32),
            pltpu.VMEM(gate_probs.shape, f32),
            pltpu.SemaphoreType.DMA((6,)),
        ],
    )
    (outgoing,) = call(
        functools.partial(pick_kernel, share),
        [((devices, 2 * MOST, part), bf16)],
        [here, weight, picked, cot],
        "vvvv",
    )
    held = lax.all_to_all(outgoing, everyone, split_axis=0, concat_axis=0, tiled=True)
    other = swap(held)
    acts = (hidden // LANES, devices * 2 * MOST, LANES)
    half = (hidden, part)
    pre_act, back_act, w_out_far = call(
        first_kernel,
        [(acts, f32), (acts, f32), (half, bf16)],
        [place, held, w_in_near, w_out],
        "svvh",
        [pltpu.VMEM(half, bf16), pltpu.SemaphoreType.DMA((2,))],
    )
    slope, sent = call(
        second_kernel,
        [((devices * MOST, hidden), bf16), ((devices * MOST, part), bf16)],
        [place, other, pre_act, back_act, w_in_near, w_out_far],
        "svvvvv",
        [
            pltpu.VMEM(acts, f32),
            pltpu.VMEM(acts, f32),
            pltpu.VMEM((hidden // LANES, devices * MOST, LANES), f32),
        ],
    )
    came = swap(sent)
    (kept,) = call(
        third_kernel, [((devices * MOST, part), f32)], [place, slope, w_in_near], "svv"
    )
    (total,) = call(sum_kernel, [((devices, MOST, part), bf16)], [kept, came], "vv")
    back = lax.all_to_all(total, everyone, split_axis=0, concat_axis=0, tiled=True)
    return call(
        backward_kernel,
        [((frames, blocks, features), bf16)] * 3,
        [spread, back, cot, probs, query, key, value],
        "vvvvvvv",
        [pltpu.VMEM((frames, blocks, features), bf16)] * 3 + [pltpu.SemaphoreType.DMA((3,))],
        "h",
    )


def solution(mesh):
    return jax.shard_map(
        body,
        mesh=mesh,
        in_specs=(
            P(None, ("grp", "frm"), None),
            P(None, ("grp", "frm"), None),
            P(None, ("grp", "frm"), None),
            P("frm", "grp", None),
            P("grp", None, "frm"),
            P("grp", "frm", None),
            P(),
            P(),
        ),
        out_specs=(
            P(None, ("grp", "frm"), None),
            P(None, ("grp", "frm"), None),
            P(None, ("grp", "frm"), None),
        ),
        check_vma=False,
    )
```

```python
import functools

import jax
import jax.numpy as jnp
from jax import lax
from jax.experimental import pallas as pl
from jax.experimental.pallas import tpu as pltpu
from jax.sharding import PartitionSpec as P

HEADS = 16
MOST = 2
CORES = 2
SUBLANES = 8
LANES = 128
TILE = 16

root_half = 0.7071067811865476
inv_root_tau = 0.3989422804014327

LANES_BOTH = (((1,), (1,)), ((), ()))
FIRST_BOTH = (((0,), (0,)), ((), ()))


def gelu_slope(pre_act):
    normal_cdf = 0.5 * (1.0 + lax.erf(pre_act * root_half))
    density = jnp.exp(-0.5 * pre_act * pre_act) * inv_root_tau
    return normal_cdf + pre_act * density


def dot(a, b):
    return jnp.dot(a, b, preferred_element_type=jnp.float32)


def dot_lanes(a, b):
    return lax.dot_general(a, b, LANES_BOTH, preferred_element_type=jnp.float32)


def over_frames(values, op, blocks):
    rows = values.shape[0]
    total = values[:SUBLANES]
    for start in range(SUBLANES, rows, SUBLANES):
        total = op(total, values[start : start + SUBLANES])
    step = blocks
    while step < SUBLANES:
        total = op(total, pltpu.roll(total, step, 0))
        step *= 2
    return jnp.concatenate([total] * (rows // SUBLANES), axis=0)


def heads_of(values):
    width = values.shape[1] // HEADS
    return [values[:, h * width : (h + 1) * width] for h in range(HEADS)]


def turn_kernel(cot_hbm, out_hbm, cot_ref, turned_ref, sems):
    _, rows, _ = cot_ref.shape
    columns, blocks, features = turned_ref.shape
    pieces = rows // TILE
    span = columns // pieces
    arrivals = [
        pltpu.make_async_copy(
            cot_hbm.at[:, pl.ds(i * TILE, TILE)], cot_ref.at[:, pl.ds(i * TILE, TILE)], sems.at[0, i]
        )
        for i in range(pieces)
    ]
    for copy in arrivals:
        copy.start()
    leaving = []
    for i, copy in enumerate(arrivals):
        copy.wait()
        part = slice(i * span, (i + 1) * span)
        turned_ref[part] = cot_ref[0, i * TILE : (i + 1) * TILE, :].reshape(span, blocks, features)
        copy = pltpu.make_async_copy(
            turned_ref.at[pl.ds(i * span, span)], out_hbm.at[pl.ds(i * span, span)], sems.at[1, i]
        )
        copy.start()
        leaving.append(copy)
    for copy in leaving:
        copy.wait()


def forward_kernel(
    patches_all, share, place_ref,
    chosen_hbm, gate_hbm, query_hbm, key_hbm, value_hbm, w_in_hbm,
    query_ref, key_ref, value_ref, w_in_ref,
    probs_ref, picked_ref, here_ref, weight_ref, spread_ref,
    chosen_ref, gate_ref, sems,
):
    sources = [chosen_hbm, gate_hbm, query_hbm, key_hbm, value_hbm, w_in_hbm]
    targets = [chosen_ref, gate_ref, query_ref, key_ref, value_ref, w_in_ref]
    copies = [
        pltpu.make_async_copy(source, target, sems.at[i])
        for i, (source, target) in enumerate(zip(sources, targets))
    ]
    for copy in copies:
        copy.start()
    frames, blocks, features = query_ref.shape
    rows = frames * blocks
    scaling = (features // HEADS) ** (-0.5)

    for copy in copies[:2]:
        copy.wait()
    experts, cap = chosen_ref.shape
    myself = place_ref[0]
    before = (
        lax.broadcasted_iota(jnp.int32, (cap, cap), 0)
        < lax.broadcasted_iota(jnp.int32, (cap, cap), 1)
    ).astype(jnp.bfloat16)
    slot = lax.broadcasted_iota(jnp.int32, (SUBLANES, cap), 0)
    row_at = lax.broadcasted_iota(jnp.int32, (rows, cap), 0)
    found = []
    for e in range(experts):
        tokens = chosen_ref[e : e + 1, :]
        gates = gate_ref[e : e + 1, :]
        patch = tokens % patches_all
        owned = jnp.broadcast_to((patch // blocks == myself).astype(jnp.float32), slot.shape)
        rank = dot(owned.astype(jnp.bfloat16), before)
        taken = jnp.where((rank == slot.astype(jnp.float32)) & (owned > 0.0), 1.0, 0.0)
        position = (tokens // patches_all) * blocks + patch % blocks
        at_row = (row_at == position).astype(jnp.bfloat16)
        here = dot_lanes(taken.astype(jnp.bfloat16), at_row)
        weight = jnp.sum(taken * gates, axis=1, keepdims=True)
        here_ref[e * MOST : (e + 1) * MOST, :] = here[:MOST]
        weight_ref[e * MOST : (e + 1) * MOST, :] = jnp.broadcast_to(
            weight[:MOST], (MOST, weight_ref.shape[1])
        )
        found.append(here[:MOST])
    here = jnp.concatenate(found, axis=0).astype(jnp.bfloat16)
    cores, _, returns = spread_ref.shape
    slot_at = lax.broadcasted_iota(jnp.int32, (experts * MOST, returns), 0)
    back_at = lax.broadcasted_iota(jnp.int32, (experts * MOST, returns), 1)
    sender = back_at // MOST
    same = (sender // share == slot_at // MOST) & (back_at % MOST == slot_at % MOST)
    for c in range(cores):
        spread_ref[c] = lax.dot_general(
            here,
            (same & (sender % cores == c)).astype(jnp.bfloat16),
            FIRST_BOTH,
            preferred_element_type=jnp.float32,
        ).astype(jnp.bfloat16)

    for copy in copies[2:5]:
        copy.wait()
    query = query_ref[...].reshape(rows, features)
    key = key_ref[...].reshape(rows, features)
    value = value_ref[...].reshape(rows, features)
    scores = jnp.concatenate(
        [dot_lanes(k, q) for k, q in zip(heads_of(key), heads_of(query))], axis=1
    )
    scores = scores * scaling
    raised = jnp.exp(scores - over_frames(scores, jnp.maximum, blocks))
    probs = raised / over_frames(raised, jnp.add, blocks)
    patch_in = lax.broadcasted_iota(jnp.int32, probs.shape, 0) % blocks
    patch_out = lax.broadcasted_iota(jnp.int32, probs.shape, 1) % blocks
    probs = jnp.where(patch_in == patch_out, probs, 0.0)
    probs_ref[...] = probs
    weights = probs.T.astype(jnp.bfloat16)
    mixed = jnp.concatenate(
        [dot(weights[h * rows : (h + 1) * rows], v) for h, v in enumerate(heads_of(value))],
        axis=1,
    ).astype(jnp.bfloat16)
    picked_ref[...] = dot(here, mixed).astype(jnp.bfloat16)
    for copy in copies[5:]:
        copy.wait()


def pick_kernel(share, here_ref, weight_ref, picked_ref, cot_ref, out_ref):
    frames, blocks, features = cot_ref.shape
    rows = dot(here_ref[...].astype(jnp.bfloat16), cot_ref[...].reshape(frames * blocks, features))
    rows = (rows * weight_ref[:, :1]).astype(jnp.bfloat16)
    part = features // CORES
    picked = picked_ref[...]
    both = [
        jnp.concatenate(
            [half[:, c * part : (c + 1) * part] for half in (picked, rows)], axis=1
        )
        for c in range(CORES)
    ]
    for e in range(out_ref.shape[0] // share):
        for i in range(share):
            out_ref[e * share + i] = both[i % CORES][e * MOST : (e + 1) * MOST]


def in_order(mine, near, far):
    return jnp.where(mine == 0, near, far), jnp.where(mine == 0, far, near)


def first_kernel(place_ref, rows_ref, w_in_ref, w_out_hbm, pre_ref, w_out_ref, sem):
    copy = pltpu.make_async_copy(w_out_hbm.at[0], w_out_ref, sem)
    copy.start()
    rows = rows_ref[...].reshape(pre_ref.shape[0], -1)
    width = rows.shape[1] // 2
    for c in range(CORES):

        @pl.when(place_ref[1] == c)
        def _():
            pre_ref[...] = dot(rows[:, :width], w_in_ref[0, c * width : (c + 1) * width, :])

    copy.wait()


def second_kernel(
    place_ref, near_ref, far_ref, pre_ref, w_in_ref, w_out_ref, kept_ref, sent_ref, sum_ref
):
    near = near_ref[...].reshape(pre_ref.shape[0], -1)
    far = far_ref[...].reshape(pre_ref.shape[0], -1)
    width = near.shape[1] // 2
    mine = place_ref[1]
    for c in range(CORES):

        @pl.when(mine == 1 - c)
        def _():
            sum_ref[...] = dot(far[:, :width], w_in_ref[0, c * width : (c + 1) * width, :])

    cots = jnp.concatenate(in_order(mine, near[:, width:], far[:, width:]), axis=1)
    back_act = dot_lanes(cots, w_out_ref[...])
    slope = back_act * gelu_slope(pre_ref[...] + sum_ref[...])
    product = dot_lanes(slope.astype(jnp.bfloat16), w_in_ref[0])
    kept, sent = in_order(mine, product[:, :width], product[:, width:])
    kept_ref[...] = kept
    sent_ref[...] = sent.astype(jnp.bfloat16)


def sum_kernel(kept_ref, came_ref, out_ref):
    total = kept_ref[...] + came_ref[...].astype(jnp.float32)
    out_ref[...] = total.astype(jnp.bfloat16).reshape(out_ref.shape)


def backward_kernel(
    spread_ref, back_ref, cot_ref, probs_ref, query_ref, key_ref, value_ref,
    grad_query_hbm, grad_key_hbm, grad_value_hbm,
    grad_query_ref, grad_key_ref, grad_value_ref, sems,
):
    frames, blocks, features = query_ref.shape
    rows = frames * blocks
    scaling = (features // HEADS) ** (-0.5)
    query = query_ref[...].reshape(rows, features)
    key = key_ref[...].reshape(rows, features)
    value = value_ref[...].reshape(rows, features)
    back = back_ref[...].reshape(-1, back_ref.shape[2])
    added = jnp.concatenate([dot(spread_ref[c], back) for c in range(CORES)], axis=1)
    cot = cot_ref[...].reshape(rows, features)
    stream = (cot.astype(jnp.float32) + added).astype(jnp.bfloat16)
    probs = probs_ref[...]
    weights = probs.astype(jnp.bfloat16)
    copies = []

    def put(ref, hbm, parts):
        joined = jnp.concatenate(parts, axis=1).astype(jnp.bfloat16)
        ref[...] = joined.reshape(frames, blocks, features)
        copy = pltpu.make_async_copy(ref, hbm, sems.at[len(copies)])
        copy.start()
        copies.append(copy)

    put(
        grad_value_ref,
        grad_value_hbm,
        [dot(w, g) for w, g in zip(heads_of(weights), heads_of(stream))],
    )
    grad_prob = jnp.concatenate(
        [dot_lanes(v, g) for v, g in zip(heads_of(value), heads_of(stream))], axis=1
    )
    centre = over_frames(probs * grad_prob, jnp.add, blocks)
    grad_score = probs * (grad_prob - centre)
    turned = grad_score.T.astype(jnp.bfloat16)
    grad_score = grad_score.astype(jnp.bfloat16)
    put(
        grad_key_ref,
        grad_key_hbm,
        [dot(s, q) * scaling for s, q in zip(heads_of(grad_score), heads_of(query))],
    )
    put(
        grad_query_ref,
        grad_query_hbm,
        [dot(turned[h * rows : (h + 1) * rows], k) * scaling for h, k in enumerate(heads_of(key))],
    )
    for copy in copies:
        copy.wait()


def call(kernel, outs, operands, places, scratch=(), results="v"):
    smem, vmem, hbm = (
        pl.BlockSpec(memory_space=space) for space in (pltpu.SMEM, pltpu.VMEM, pl.ANY)
    )
    spaces = {"s": smem, "v": vmem, "h": hbm}
    return pl.pallas_call(
        kernel,
        out_shape=[jax.ShapeDtypeStruct(shape, dtype) for shape, dtype in outs],
        in_specs=[spaces[place] for place in places],
        out_specs=[spaces[results]] * len(outs),
        scratch_shapes=list(scratch),
        compiler_params=pltpu.CompilerParams(vmem_limit_bytes=32 * 1024 * 1024),
    )(*[
        pltpu.with_memory_space_constraint(operand, pltpu.HBM) if place == "h" else operand
        for operand, place in zip(operands, places)
    ])


def body(query_in, key_in, value_in, cotangent, w_in, w_out, gate_probs, chosen):
    bf16, f32 = jnp.bfloat16, jnp.float32
    frames, blocks, features = query_in.shape
    groups = lax.axis_size("grp")
    columns = lax.axis_size("frm")
    experts = gate_probs.shape[0]
    devices = groups * columns
    share = devices // experts
    rows = frames * blocks
    slots = experts * MOST
    part = features // CORES
    hidden = w_in.shape[2]
    column = lax.axis_index("frm")
    place = jnp.stack([lax.axis_index("grp") * columns + column, column % CORES])
    place = place.astype(jnp.int32)
    everyone = ("grp", "frm")

    def swap(values):
        return lax.ppermute(values, "frm", [(i, i ^ 1) for i in range(columns)])

    (turned,) = call(
        turn_kernel, [((columns, blocks, features), bf16)], [cotangent], "h",
        [
            pltpu.VMEM(cotangent.shape, bf16),
            pltpu.VMEM((columns, blocks, features), bf16),
            pltpu.SemaphoreType.DMA((2, cotangent.shape[1] // TILE)),
        ],
        "h",
    )
    cot = lax.all_to_all(turned, "frm", split_axis=0, concat_axis=0, tiled=True)
    query, key, value, w_in_near, probs, picked, here, weight, spread = call(
        functools.partial(forward_kernel, blocks * devices, share),
        [
            *[(array.shape, bf16) for array in (query_in, key_in, value_in, w_in)],
            ((rows, HEADS * rows), f32),
            ((slots, features), bf16),
            ((slots, rows), f32),
            ((slots, LANES), f32),
            ((CORES, rows, devices * MOST), bf16),
        ],
        [place, chosen, gate_probs, query_in, key_in, value_in, w_in],
        "shhhhhh",
        [
            pltpu.VMEM(chosen.shape, jnp.int32),
            pltpu.VMEM(gate_probs.shape, f32),
            pltpu.SemaphoreType.DMA((6,)),
        ],
    )
    (outgoing,) = call(
        functools.partial(pick_kernel, share),
        [((devices, MOST, 2 * part), bf16)],
        [here, weight, picked, cot],
        "vvvv",
    )
    held = lax.all_to_all(outgoing, everyone, split_axis=0, concat_axis=0, tiled=True)
    other = swap(held)
    acts = (devices * MOST, hidden)
    pre_act, w_out_near = call(
        first_kernel,
        [(acts, f32), (w_out.shape[1:], bf16)],
        [place, held, w_in_near, w_out],
        "svvh",
        [pltpu.SemaphoreType.DMA],
    )
    kept, sent = call(
        second_kernel,
        [((devices * MOST, part), f32), ((devices * MOST, part), bf16)],
        [place, held, other, pre_act, w_in_near, w_out_near],
        "svvvvv",
        [pltpu.VMEM(acts, f32)],
    )
    came = swap(sent)
    (total,) = call(sum_kernel, [((devices, MOST, part), bf16)], [kept, came], "vv")
    back = lax.all_to_all(total, everyone, split_axis=0, concat_axis=0, tiled=True)
    return call(
        backward_kernel,
        [((frames, blocks, features), bf16)] * 3,
        [spread, back, cot, probs, query, key, value],
        "vvvvvvv",
        [pltpu.VMEM((frames, blocks, features), bf16)] * 3 + [pltpu.SemaphoreType.DMA((3,))],
        "h",
    )


def solution(mesh):
    return jax.shard_map(
        body,
        mesh=mesh,
        in_specs=(
            P(None, ("grp", "frm"), None),
            P(None, ("grp", "frm"), None),
            P(None, ("grp", "frm"), None),
            P("frm", "grp", None),
            P("grp", None, "frm"),
            P("grp", "frm", None),
            P(),
            P(),
        ),
        out_specs=(
            P(None, ("grp", "frm"), None),
            P(None, ("grp", "frm"), None),
            P(None, ("grp", "frm"), None),
        ),
        check_vma=False,
    )
```

```python
import functools

import jax
import jax.numpy as jnp
from jax import lax
from jax.experimental import pallas as pl
from jax.experimental.pallas import tpu as pltpu
from jax.sharding import PartitionSpec as P

HEADS = 16
MOST = 2
CORES = 2
SUBLANES = 8
LANES = 128
TILE = 16

root_half = 0.7071067811865476
inv_root_tau = 0.3989422804014327

LANES_BOTH = (((1,), (1,)), ((), ()))
FIRST_BOTH = (((0,), (0,)), ((), ()))


def gelu_slope(pre_act):
    normal_cdf = 0.5 * (1.0 + lax.erf(pre_act * root_half))
    density = jnp.exp(-0.5 * pre_act * pre_act) * inv_root_tau
    return normal_cdf + pre_act * density


def dot(a, b):
    return jnp.dot(a, b, preferred_element_type=jnp.float32)


def dot_lanes(a, b):
    return lax.dot_general(a, b, LANES_BOTH, preferred_element_type=jnp.float32)


def over_frames(values, op, blocks):
    rows = values.shape[0]
    total = values[:SUBLANES]
    for start in range(SUBLANES, rows, SUBLANES):
        total = op(total, values[start : start + SUBLANES])
    step = blocks
    while step < SUBLANES:
        total = op(total, pltpu.roll(total, step, 0))
        step *= 2
    return jnp.concatenate([total] * (rows // SUBLANES), axis=0)


def heads_of(values):
    width = values.shape[1] // HEADS
    return [values[:, h * width : (h + 1) * width] for h in range(HEADS)]


def turn_kernel(cot_hbm, out_hbm, cot_ref, turned_ref, sems):
    _, rows, _ = cot_ref.shape
    columns, blocks, features = turned_ref.shape
    pieces = rows // TILE
    span = columns // pieces
    arrivals = [
        pltpu.make_async_copy(
            cot_hbm.at[:, pl.ds(i * TILE, TILE)], cot_ref.at[:, pl.ds(i * TILE, TILE)], sems.at[0, i]
        )
        for i in range(pieces)
    ]
    for copy in arrivals:
        copy.start()
    leaving = []
    for i, copy in enumerate(arrivals):
        copy.wait()
        part = slice(i * span, (i + 1) * span)
        turned_ref[part] = cot_ref[0, i * TILE : (i + 1) * TILE, :].reshape(span, blocks, features)
        copy = pltpu.make_async_copy(
            turned_ref.at[pl.ds(i * span, span)], out_hbm.at[pl.ds(i * span, span)], sems.at[1, i]
        )
        copy.start()
        leaving.append(copy)
    for copy in leaving:
        copy.wait()


def forward_kernel(
    patches_all, share, place_ref,
    chosen_hbm, gate_hbm, query_hbm, key_hbm, value_hbm, w_in_hbm, w_out_hbm,
    w_in_ref, w_out_ref, probs_ref, picked_ref, here_ref, weight_ref, spread_ref,
    chosen_ref, gate_ref, query_ref, key_ref, value_ref, sems,
):
    upper = w_out_hbm.at[0, pl.ds(0, w_out_ref.shape[0])]
    sources = [chosen_hbm, gate_hbm, query_hbm, key_hbm, value_hbm, w_in_hbm, upper]
    targets = [chosen_ref, gate_ref, query_ref, key_ref, value_ref, w_in_ref, w_out_ref]
    copies = [
        pltpu.make_async_copy(source, target, sems.at[i])
        for i, (source, target) in enumerate(zip(sources, targets))
    ]
    for copy in copies:
        copy.start()
    frames, blocks, features = query_ref.shape
    rows = frames * blocks
    scaling = (features // HEADS) ** (-0.5)

    for copy in copies[:2]:
        copy.wait()
    experts, cap = chosen_ref.shape
    myself = place_ref[0]
    before = (
        lax.broadcasted_iota(jnp.int32, (cap, cap), 0)
        < lax.broadcasted_iota(jnp.int32, (cap, cap), 1)
    ).astype(jnp.bfloat16)
    slot = lax.broadcasted_iota(jnp.int32, (SUBLANES, cap), 0)
    row_at = lax.broadcasted_iota(jnp.int32, (rows, cap), 0)
    found = []
    for e in range(experts):
        tokens = chosen_ref[e : e + 1, :]
        gates = gate_ref[e : e + 1, :]
        patch = tokens % patches_all
        owned = jnp.broadcast_to((patch // blocks == myself).astype(jnp.float32), slot.shape)
        rank = dot(owned.astype(jnp.bfloat16), before)
        taken = jnp.where((rank == slot.astype(jnp.float32)) & (owned > 0.0), 1.0, 0.0)
        position = (tokens // patches_all) * blocks + patch % blocks
        at_row = (row_at == position).astype(jnp.bfloat16)
        here = dot_lanes(taken.astype(jnp.bfloat16), at_row)
        weight = jnp.sum(taken * gates, axis=1, keepdims=True)
        here_ref[e * MOST : (e + 1) * MOST, :] = here[:MOST]
        weight_ref[e * MOST : (e + 1) * MOST, :] = jnp.broadcast_to(
            weight[:MOST], (MOST, weight_ref.shape[1])
        )
        found.append(here[:MOST])
    here = jnp.concatenate(found, axis=0).astype(jnp.bfloat16)
    cores, _, returns = spread_ref.shape
    slot_at = lax.broadcasted_iota(jnp.int32, (experts * MOST, returns), 0)
    back_at = lax.broadcasted_iota(jnp.int32, (experts * MOST, returns), 1)
    sender = back_at // MOST
    same = (sender // share == slot_at // MOST) & (back_at % MOST == slot_at % MOST)
    for c in range(cores):
        spread_ref[c] = lax.dot_general(
            here,
            (same & (sender % cores == c)).astype(jnp.bfloat16),
            FIRST_BOTH,
            preferred_element_type=jnp.float32,
        ).astype(jnp.bfloat16)

    for copy in copies[2:5]:
        copy.wait()
    query = query_ref[...].reshape(rows, features)
    key = key_ref[...].reshape(rows, features)
    value = value_ref[...].reshape(rows, features)
    scores = jnp.concatenate(
        [dot_lanes(k, q) for k, q in zip(heads_of(key), heads_of(query))], axis=1
    )
    scores = scores * scaling
    raised = jnp.exp(scores - over_frames(scores, jnp.maximum, blocks))
    probs = raised / over_frames(raised, jnp.add, blocks)
    patch_in = lax.broadcasted_iota(jnp.int32, probs.shape, 0) % blocks
    patch_out = lax.broadcasted_iota(jnp.int32, probs.shape, 1) % blocks
    probs = jnp.where(patch_in == patch_out, probs, 0.0)
    probs_ref[...] = probs
    weights = probs.T.astype(jnp.bfloat16)
    mixed = jnp.concatenate(
        [dot(weights[h * rows : (h + 1) * rows], v) for h, v in enumerate(heads_of(value))],
        axis=1,
    ).astype(jnp.bfloat16)
    picked_ref[...] = dot(here, mixed).astype(jnp.bfloat16)
    for copy in copies[5:]:
        copy.wait()


def pick_kernel(share, here_ref, weight_ref, picked_ref, cot_ref, out_ref):
    frames, blocks, features = cot_ref.shape
    rows = dot(here_ref[...].astype(jnp.bfloat16), cot_ref[...].reshape(frames * blocks, features))
    rows = (rows * weight_ref[:, :1]).astype(jnp.bfloat16)
    part = features // CORES
    picked = picked_ref[...]
    both = [
        jnp.concatenate(
            [half[:, c * part : (c + 1) * part] for half in (picked, rows)], axis=1
        )
        for c in range(CORES)
    ]
    for e in range(out_ref.shape[0] // share):
        for i in range(share):
            out_ref[e * share + i] = both[i % CORES][e * MOST : (e + 1) * MOST]


def in_order(mine, near, far):
    return jnp.where(mine == 0, near, far), jnp.where(mine == 0, far, near)


def first_kernel(place_ref, near_ref, w_in_ref, w_out_hbm, pre_ref, lower_ref, sem):
    half = lower_ref.shape[0]
    copy = pltpu.make_async_copy(w_out_hbm.at[0, pl.ds(half, half)], lower_ref, sem)
    copy.start()
    width = near_ref.shape[1] // 2
    for c in range(CORES):

        @pl.when(place_ref[1] == c)
        def _():
            pre_ref[...] = dot(near_ref[:, :width], w_in_ref[0, c * width : (c + 1) * width, :])

    copy.wait()


def second_kernel(
    place_ref, near_ref, far_ref, pre_ref, w_in_ref, upper_ref, lower_ref,
    kept_ref, sent_ref, sum_ref,
):
    width = near_ref.shape[1] // 2
    mine = place_ref[1]
    for c in range(CORES):

        @pl.when(mine == 1 - c)
        def _():
            sum_ref[...] = dot(far_ref[:, :width], w_in_ref[0, c * width : (c + 1) * width, :])

    cots = jnp.concatenate(in_order(mine, near_ref[:, width:], far_ref[:, width:]), axis=1)
    back_act = jnp.concatenate(
        [dot_lanes(cots, upper_ref[...]), dot_lanes(cots, lower_ref[...])], axis=1
    )
    slope = back_act * gelu_slope(pre_ref[...] + sum_ref[...])
    product = dot_lanes(slope.astype(jnp.bfloat16), w_in_ref[0])
    kept, sent = in_order(mine, product[:, :width], product[:, width:])
    kept_ref[...] = kept
    sent_ref[...] = sent.astype(jnp.bfloat16)


def sum_kernel(kept_ref, came_ref, out_ref):
    total = kept_ref[...] + came_ref[...].astype(jnp.float32)
    out_ref[...] = total.astype(jnp.bfloat16).reshape(out_ref.shape)


def backward_kernel(
    spread_ref, back_ref, cot_ref, probs_ref, query_ref, key_ref, value_ref,
    grad_query_hbm, grad_key_hbm, grad_value_hbm,
    grad_query_ref, grad_key_ref, grad_value_ref, sems,
):
    frames, blocks, features = query_ref.shape
    rows = frames * blocks
    scaling = (features // HEADS) ** (-0.5)
    query = query_ref[...].reshape(rows, features)
    key = key_ref[...].reshape(rows, features)
    value = value_ref[...].reshape(rows, features)
    added = jnp.concatenate([dot(spread_ref[c], back_ref[...]) for c in range(CORES)], axis=1)
    cot = cot_ref[...].reshape(rows, features)
    stream = (cot.astype(jnp.float32) + added).astype(jnp.bfloat16)
    probs = probs_ref[...]
    weights = probs.astype(jnp.bfloat16)
    copies = []

    def put(ref, hbm, parts):
        joined = jnp.concatenate(parts, axis=1).astype(jnp.bfloat16)
        ref[...] = joined.reshape(frames, blocks, features)
        copy = pltpu.make_async_copy(ref, hbm, sems.at[len(copies)])
        copy.start()
        copies.append(copy)

    put(
        grad_value_ref,
        grad_value_hbm,
        [dot(w, g) for w, g in zip(heads_of(weights), heads_of(stream))],
    )
    grad_prob = jnp.concatenate(
        [dot_lanes(v, g) for v, g in zip(heads_of(value), heads_of(stream))], axis=1
    )
    centre = over_frames(probs * grad_prob, jnp.add, blocks)
    grad_score = probs * (grad_prob - centre)
    turned = grad_score.T.astype(jnp.bfloat16)
    grad_score = grad_score.astype(jnp.bfloat16)
    put(
        grad_key_ref,
        grad_key_hbm,
        [dot(s, q) * scaling for s, q in zip(heads_of(grad_score), heads_of(query))],
    )
    put(
        grad_query_ref,
        grad_query_hbm,
        [dot(turned[h * rows : (h + 1) * rows], k) * scaling for h, k in enumerate(heads_of(key))],
    )
    for copy in copies:
        copy.wait()


def call(kernel, outs, operands, places, scratch=(), results="v"):
    smem, vmem, hbm = (
        pl.BlockSpec(memory_space=space) for space in (pltpu.SMEM, pltpu.VMEM, pl.ANY)
    )
    spaces = {"s": smem, "v": vmem, "h": hbm}
    return pl.pallas_call(
        kernel,
        out_shape=[jax.ShapeDtypeStruct(shape, dtype) for shape, dtype in outs],
        in_specs=[spaces[place] for place in places],
        out_specs=[spaces[results]] * len(outs),
        scratch_shapes=list(scratch),
        compiler_params=pltpu.CompilerParams(vmem_limit_bytes=32 * 1024 * 1024),
    )(*[
        pltpu.with_memory_space_constraint(operand, pltpu.HBM) if place == "h" else operand
        for operand, place in zip(operands, places)
    ])


def body(query_in, key_in, value_in, cotangent, w_in, w_out, gate_probs, chosen):
    bf16, f32 = jnp.bfloat16, jnp.float32
    frames, blocks, features = query_in.shape
    groups = lax.axis_size("grp")
    columns = lax.axis_size("frm")
    experts = gate_probs.shape[0]
    devices = groups * columns
    share = devices // experts
    rows = frames * blocks
    slots = experts * MOST
    part = features // CORES
    hidden = w_in.shape[2]
    column = lax.axis_index("frm")
    place = jnp.stack([lax.axis_index("grp") * columns + column, column % CORES])
    place = place.astype(jnp.int32)
    everyone = ("grp", "frm")

    def swap(values):
        return lax.ppermute(values, "frm", [(i, i ^ 1) for i in range(columns)])

    (turned,) = call(
        turn_kernel, [((columns, blocks, features), bf16)], [cotangent], "h",
        [
            pltpu.VMEM(cotangent.shape, bf16),
            pltpu.VMEM((columns, blocks, features), bf16),
            pltpu.SemaphoreType.DMA((2, cotangent.shape[1] // TILE)),
        ],
        "h",
    )
    cot = lax.all_to_all(turned, "frm", split_axis=0, concat_axis=0, tiled=True)
    w_in_near, upper, probs, picked, here, weight, spread = call(
        functools.partial(forward_kernel, blocks * devices, share),
        [
            (w_in.shape, bf16),
            ((hidden // 2, features), bf16),
            ((rows, HEADS * rows), f32),
            ((slots, features), bf16),
            ((slots, rows), f32),
            ((slots, LANES), f32),
            ((CORES, rows, devices * MOST), bf16),
        ],
        [place, chosen, gate_probs, query_in, key_in, value_in, w_in, w_out],
        "shhhhhhh",
        [
            pltpu.VMEM(chosen.shape, jnp.int32),
            pltpu.VMEM(gate_probs.shape, f32),
            *[pltpu.VMEM(query_in.shape, bf16)] * 3,
            pltpu.SemaphoreType.DMA((7,)),
        ],
    )
    (outgoing,) = call(
        functools.partial(pick_kernel, share),
        [((devices, MOST, 2 * part), bf16)],
        [here, weight, picked, cot],
        "vvvv",
    )
    held = lax.all_to_all(outgoing, everyone, split_axis=0, concat_axis=0, tiled=True)
    held = held.reshape(devices * MOST, 2 * part)
    other = swap(held)
    acts = (devices * MOST, hidden)
    pre_act, lower = call(
        first_kernel,
        [(acts, f32), ((hidden // 2, features), bf16)],
        [place, held, w_in_near, w_out],
        "svvh",
        [pltpu.SemaphoreType.DMA],
    )
    kept, sent = call(
        second_kernel,
        [((devices * MOST, part), f32), ((devices * MOST, part), bf16)],
        [place, held, other, pre_act, w_in_near, upper, lower],
        "svvvvvv",
        [pltpu.VMEM(acts, f32)],
    )
    came = swap(sent)
    (total,) = call(sum_kernel, [((devices, MOST, part), bf16)], [kept, came], "vv")
    back = lax.all_to_all(total, everyone, split_axis=0, concat_axis=0, tiled=True)
    back = back.reshape(devices * MOST, part)
    return call(
        backward_kernel,
        [((frames, blocks, features), bf16)] * 3,
        [spread, back, cot, probs, query_in, key_in, value_in],
        "vvvvvvv",
        [pltpu.VMEM((frames, blocks, features), bf16)] * 3 + [pltpu.SemaphoreType.DMA((3,))],
        "h",
    )


def solution(mesh):
    return jax.shard_map(
        body,
        mesh=mesh,
        in_specs=(
            P(None, ("grp", "frm"), None),
            P(None, ("grp", "frm"), None),
            P(None, ("grp", "frm"), None),
            P("frm", "grp", None),
            P("grp", None, "frm"),
            P("grp", "frm", None),
            P(),
            P(),
        ),
        out_specs=(
            P(None, ("grp", "frm"), None),
            P(None, ("grp", "frm"), None),
            P(None, ("grp", "frm"), None),
        ),
        check_vma=False,
    )
```

```python
import functools

import jax
import jax.numpy as jnp
from jax import lax
from jax.experimental import pallas as pl
from jax.experimental.pallas import tpu as pltpu
from jax.sharding import PartitionSpec as P

HEADS = 16
MOST = 2
CORES = 2
SUBLANES = 8
LANES = 128
TILE = 16

root_half = 0.7071067811865476
inv_root_tau = 0.3989422804014327

LANES_BOTH = (((1,), (1,)), ((), ()))
FIRST_BOTH = (((0,), (0,)), ((), ()))


def gelu_slope(pre_act):
    normal_cdf = 0.5 * (1.0 + lax.erf(pre_act * root_half))
    density = jnp.exp(-0.5 * pre_act * pre_act) * inv_root_tau
    return normal_cdf + pre_act * density


def dot(a, b):
    return jnp.dot(a, b, preferred_element_type=jnp.float32)


def dot_lanes(a, b):
    return lax.dot_general(a, b, LANES_BOTH, preferred_element_type=jnp.float32)


def over_frames(values, op, blocks):
    rows = values.shape[0]
    total = values[:SUBLANES]
    for start in range(SUBLANES, rows, SUBLANES):
        total = op(total, values[start : start + SUBLANES])
    step = blocks
    while step < SUBLANES:
        total = op(total, pltpu.roll(total, step, 0))
        step *= 2
    return jnp.concatenate([total] * (rows // SUBLANES), axis=0)


def heads_of(values):
    width = values.shape[1] // HEADS
    return [values[:, h * width : (h + 1) * width] for h in range(HEADS)]


def turn_kernel(cot_hbm, out_hbm, cot_ref, turned_ref, sems):
    _, rows, _ = cot_ref.shape
    columns, blocks, features = turned_ref.shape
    pieces = rows // TILE
    span = columns // pieces
    arrivals = [
        pltpu.make_async_copy(
            cot_hbm.at[:, pl.ds(i * TILE, TILE)], cot_ref.at[:, pl.ds(i * TILE, TILE)], sems.at[0, i]
        )
        for i in range(pieces)
    ]
    for copy in arrivals:
        copy.start()
    leaving = []
    for i, copy in enumerate(arrivals):
        copy.wait()
        part = slice(i * span, (i + 1) * span)
        turned_ref[part] = cot_ref[0, i * TILE : (i + 1) * TILE, :].reshape(span, blocks, features)
        copy = pltpu.make_async_copy(
            turned_ref.at[pl.ds(i * span, span)], out_hbm.at[pl.ds(i * span, span)], sems.at[1, i]
        )
        copy.start()
        leaving.append(copy)
    for copy in leaving:
        copy.wait()


def forward_kernel(
    patches_all, share,
    chosen_hbm, gate_hbm, query_hbm, key_hbm, value_hbm, w_in_hbm,
    query_ref, key_ref, value_ref, w_in_ref,
    probs_ref, picked_ref, here_ref, weight_ref, spread_ref,
    chosen_ref, gate_ref, sems,
):
    columns = lax.axis_size("frm")
    column = lax.axis_index("frm")
    part = w_in_ref.shape[0] // CORES
    sources = [chosen_hbm, gate_hbm, query_hbm, key_hbm, value_hbm]
    targets = [chosen_ref, gate_ref, query_ref, key_ref, value_ref]
    for i in range(CORES):
        sources.append(w_in_hbm.at[0, part_of(column % CORES ^ i, part)])
        targets.append(w_in_ref.at[pl.ds(i * part, part)])
    copies = [
        pltpu.make_async_copy(source, target, sems.at[i])
        for i, (source, target) in enumerate(zip(sources, targets))
    ]
    for copy in copies:
        copy.start()
    frames, blocks, features = query_ref.shape
    rows = frames * blocks
    scaling = (features // HEADS) ** (-0.5)

    for copy in copies[:2]:
        copy.wait()
    experts, cap = chosen_ref.shape
    myself = lax.axis_index("grp") * columns + column
    before = (
        lax.broadcasted_iota(jnp.int32, (cap, cap), 0)
        < lax.broadcasted_iota(jnp.int32, (cap, cap), 1)
    ).astype(jnp.bfloat16)
    slot = lax.broadcasted_iota(jnp.int32, (SUBLANES, cap), 0)
    row_at = lax.broadcasted_iota(jnp.int32, (rows, cap), 0)
    found = []
    for e in range(experts):
        tokens = chosen_ref[e : e + 1, :]
        gates = gate_ref[e : e + 1, :]
        patch = tokens % patches_all
        owned = jnp.broadcast_to((patch // blocks == myself).astype(jnp.float32), slot.shape)
        rank = dot(owned.astype(jnp.bfloat16), before)
        taken = jnp.where((rank == slot.astype(jnp.float32)) & (owned > 0.0), 1.0, 0.0)
        position = (tokens // patches_all) * blocks + patch % blocks
        at_row = (row_at == position).astype(jnp.bfloat16)
        here = dot_lanes(taken.astype(jnp.bfloat16), at_row)
        weight = jnp.sum(taken * gates, axis=1, keepdims=True)
        here_ref[e * MOST : (e + 1) * MOST, :] = here[:MOST]
        weight_ref[e * MOST : (e + 1) * MOST, :] = jnp.broadcast_to(
            weight[:MOST], (MOST, weight_ref.shape[1])
        )
        found.append(here[:MOST])
    here = jnp.concatenate(found, axis=0).astype(jnp.bfloat16)
    cores, _, returns = spread_ref.shape
    slot_at = lax.broadcasted_iota(jnp.int32, (experts * MOST, returns), 0)
    back_at = lax.broadcasted_iota(jnp.int32, (experts * MOST, returns), 1)
    sender = back_at // MOST
    same = (sender // share == slot_at // MOST) & (back_at % MOST == slot_at % MOST)
    for c in range(cores):
        spread_ref[c] = lax.dot_general(
            here,
            (same & (sender % cores == c)).astype(jnp.bfloat16),
            FIRST_BOTH,
            preferred_element_type=jnp.float32,
        ).astype(jnp.bfloat16)

    for copy in copies[2:5]:
        copy.wait()
    query = query_ref[...].reshape(rows, features)
    key = key_ref[...].reshape(rows, features)
    value = value_ref[...].reshape(rows, features)
    scores = jnp.concatenate(
        [dot_lanes(k, q) for k, q in zip(heads_of(key), heads_of(query))], axis=1
    )
    scores = scores * scaling
    raised = jnp.exp(scores - over_frames(scores, jnp.maximum, blocks))
    probs = raised / over_frames(raised, jnp.add, blocks)
    patch_in = lax.broadcasted_iota(jnp.int32, probs.shape, 0) % blocks
    patch_out = lax.broadcasted_iota(jnp.int32, probs.shape, 1) % blocks
    probs = jnp.where(patch_in == patch_out, probs, 0.0)
    probs_ref[...] = probs
    weights = probs.T.astype(jnp.bfloat16)
    mixed = jnp.concatenate(
        [dot(weights[h * rows : (h + 1) * rows], v) for h, v in enumerate(heads_of(value))],
        axis=1,
    ).astype(jnp.bfloat16)
    picked_ref[...] = dot(here, mixed).astype(jnp.bfloat16)
    for copy in copies[5:]:
        copy.wait()


def pick_kernel(share, here_ref, weight_ref, picked_ref, cot_ref, out_ref):
    frames, blocks, features = cot_ref.shape
    rows = dot(here_ref[...].astype(jnp.bfloat16), cot_ref[...].reshape(frames * blocks, features))
    rows = (rows * weight_ref[:, :1]).astype(jnp.bfloat16)
    part = features // CORES
    picked = picked_ref[...]
    both = [
        jnp.concatenate(
            [half[:, c * part : (c + 1) * part] for half in (picked, rows)], axis=1
        )
        for c in range(CORES)
    ]
    for e in range(out_ref.shape[0] // share):
        for i in range(share):
            out_ref[e * share + i] = both[i % CORES][e * MOST : (e + 1) * MOST]


def part_of(part, width):
    return pl.ds(pl.multiple_of(part * width, width), width)


def first_kernel(near_ref, w_in_ref, w_out_hbm, rows_ref, pre_ref, w_out_ref, sems):
    width = w_in_ref.shape[0] // CORES
    copies = [
        pltpu.make_async_copy(
            w_out_hbm.at[0, :, part_of(lax.axis_index("frm") % CORES ^ i, width)],
            w_out_ref.at[:, pl.ds(i * width, width)],
            sems.at[i],
        )
        for i in range(CORES)
    ]
    for copy in copies:
        copy.start()
    rows = near_ref[...].reshape(rows_ref.shape)
    rows_ref[...] = rows
    pre_ref[...] = dot(rows[:, :width], w_in_ref[:width, :])
    for copy in copies:
        copy.wait()


def second_kernel(near_ref, far_ref, pre_ref, w_in_ref, w_out_ref, slope_ref, sent_ref):
    width = w_in_ref.shape[0] // CORES
    far = far_ref[...].reshape(near_ref.shape)
    pre_act = pre_ref[...] + dot(far[:, :width], w_in_ref[width:, :])
    back_act = dot_lanes(near_ref[:, width:], w_out_ref[:, :width])
    back_act = back_act + dot_lanes(far[:, width:], w_out_ref[:, width:])
    slope = (back_act * gelu_slope(pre_act)).astype(jnp.bfloat16)
    slope_ref[...] = slope
    sent_ref[...] = dot_lanes(slope, w_in_ref[width:, :]).astype(jnp.bfloat16)


def third_kernel(slope_ref, w_in_ref, kept_ref):
    width = kept_ref.shape[1]
    kept_ref[...] = dot_lanes(slope_ref[...], w_in_ref[:width, :])


def sum_kernel(kept_ref, came_ref, out_ref):
    total = kept_ref[...] + came_ref[...].astype(jnp.float32)
    out_ref[...] = total.astype(jnp.bfloat16).reshape(out_ref.shape)


def backward_kernel(
    spread_ref, back_ref, cot_ref, probs_ref, query_ref, key_ref, value_ref,
    grad_query_hbm, grad_key_hbm, grad_value_hbm,
    grad_query_ref, grad_key_ref, grad_value_ref, sems,
):
    frames, blocks, features = query_ref.shape
    rows = frames * blocks
    scaling = (features // HEADS) ** (-0.5)
    query = query_ref[...].reshape(rows, features)
    key = key_ref[...].reshape(rows, features)
    value = value_ref[...].reshape(rows, features)
    back = back_ref[...].reshape(-1, back_ref.shape[2])
    added = jnp.concatenate([dot(spread_ref[c], back) for c in range(CORES)], axis=1)
    cot = cot_ref[...].reshape(rows, features)
    stream = (cot.astype(jnp.float32) + added).astype(jnp.bfloat16)
    probs = probs_ref[...]
    weights = probs.astype(jnp.bfloat16)
    copies = []

    def put(ref, hbm, parts):
        joined = jnp.concatenate(parts, axis=1).astype(jnp.bfloat16)
        ref[...] = joined.reshape(frames, blocks, features)
        copy = pltpu.make_async_copy(ref, hbm, sems.at[len(copies)])
        copy.start()
        copies.append(copy)

    put(
        grad_value_ref,
        grad_value_hbm,
        [dot(w, g) for w, g in zip(heads_of(weights), heads_of(stream))],
    )
    grad_prob = jnp.concatenate(
        [dot_lanes(v, g) for v, g in zip(heads_of(value), heads_of(stream))], axis=1
    )
    centre = over_frames(probs * grad_prob, jnp.add, blocks)
    grad_score = probs * (grad_prob - centre)
    turned = grad_score.T.astype(jnp.bfloat16)
    grad_score = grad_score.astype(jnp.bfloat16)
    put(
        grad_key_ref,
        grad_key_hbm,
        [dot(s, q) * scaling for s, q in zip(heads_of(grad_score), heads_of(query))],
    )
    put(
        grad_query_ref,
        grad_query_hbm,
        [dot(turned[h * rows : (h + 1) * rows], k) * scaling for h, k in enumerate(heads_of(key))],
    )
    for copy in copies:
        copy.wait()


def call(kernel, outs, operands, places, scratch=(), results="v"):
    spaces = {
        "v": pl.BlockSpec(memory_space=pltpu.VMEM),
        "h": pl.BlockSpec(memory_space=pl.ANY),
    }
    return pl.pallas_call(
        kernel,
        out_shape=[jax.ShapeDtypeStruct(shape, dtype) for shape, dtype in outs],
        in_specs=[spaces[place] for place in places],
        out_specs=[spaces[results]] * len(outs),
        scratch_shapes=list(scratch),
        compiler_params=pltpu.CompilerParams(vmem_limit_bytes=32 * 1024 * 1024),
    )(*[
        pltpu.with_memory_space_constraint(operand, pltpu.HBM) if place == "h" else operand
        for operand, place in zip(operands, places)
    ])


def body(query_in, key_in, value_in, cotangent, w_in, w_out, gate_probs, chosen):
    bf16, f32 = jnp.bfloat16, jnp.float32
    frames, blocks, features = query_in.shape
    groups = lax.axis_size("grp")
    columns = lax.axis_size("frm")
    experts = gate_probs.shape[0]
    devices = groups * columns
    share = devices // experts
    rows = frames * blocks
    slots = experts * MOST
    part = features // CORES
    hidden = w_in.shape[2]
    everyone = ("grp", "frm")

    def swap(values):
        return lax.ppermute(values, "frm", [(i, i ^ 1) for i in range(columns)])

    (turned,) = call(
        turn_kernel, [((columns, blocks, features), bf16)], [cotangent], "h",
        [
            pltpu.VMEM(cotangent.shape, bf16),
            pltpu.VMEM((columns, blocks, features), bf16),
            pltpu.SemaphoreType.DMA((2, cotangent.shape[1] // TILE)),
        ],
        "h",
    )
    cot = lax.all_to_all(turned, "frm", split_axis=0, concat_axis=0, tiled=True)
    query, key, value, w_in_near, probs, picked, here, weight, spread = call(
        functools.partial(forward_kernel, blocks * devices, share),
        [
            *[(array.shape, bf16) for array in (query_in, key_in, value_in)],
            (w_in.shape[1:], bf16),
            ((rows, HEADS * rows), f32),
            ((slots, features), bf16),
            ((slots, rows), f32),
            ((slots, LANES), f32),
            ((CORES, rows, devices * MOST), bf16),
        ],
        [chosen, gate_probs, query_in, key_in, value_in, w_in],
        "hhhhhh",
        [
            pltpu.VMEM(chosen.shape, jnp.int32),
            pltpu.VMEM(gate_probs.shape, f32),
            pltpu.SemaphoreType.DMA((5 + CORES,)),
        ],
    )
    (outgoing,) = call(
        functools.partial(pick_kernel, share),
        [((devices, MOST, 2 * part), bf16)],
        [here, weight, picked, cot],
        "vvvv",
    )
    held = lax.all_to_all(outgoing, everyone, split_axis=0, concat_axis=0, tiled=True)
    other = swap(held)
    acts = (devices * MOST, hidden)
    halves = (devices * MOST, part)
    near, pre_act, w_out_near = call(
        first_kernel,
        [((devices * MOST, 2 * part), bf16), (acts, f32), (w_out.shape[1:], bf16)],
        [held, w_in_near, w_out],
        "vvh",
        [pltpu.SemaphoreType.DMA((CORES,))],
    )
    slope, sent = call(
        second_kernel,
        [(acts, bf16), (halves, bf16)],
        [near, other, pre_act, w_in_near, w_out_near],
        "vvvvv",
    )
    came = swap(sent)
    (kept,) = call(third_kernel, [(halves, f32)], [slope, w_in_near], "vv")
    (total,) = call(sum_kernel, [((devices, MOST, part), bf16)], [kept, came], "vv")
    back = lax.all_to_all(total, everyone, split_axis=0, concat_axis=0, tiled=True)
    return call(
        backward_kernel,
        [((frames, blocks, features), bf16)] * 3,
        [spread, back, cot, probs, query, key, value],
        "vvvvvvv",
        [pltpu.VMEM((frames, blocks, features), bf16)] * 3 + [pltpu.SemaphoreType.DMA((3,))],
        "h",
    )


def solution(mesh):
    return jax.shard_map(
        body,
        mesh=mesh,
        in_specs=(
            P(None, ("grp", "frm"), None),
            P(None, ("grp", "frm"), None),
            P(None, ("grp", "frm"), None),
            P("frm", "grp", None),
            P("grp", None, "frm"),
            P("grp", "frm", None),
            P(),
            P(),
        ),
        out_specs=(
            P(None, ("grp", "frm"), None),
            P(None, ("grp", "frm"), None),
            P(None, ("grp", "frm"), None),
        ),
        check_vma=False,
    )
```

```python
import functools

import jax
import jax.numpy as jnp
from jax import lax
from jax.experimental import pallas as pl
from jax.experimental.pallas import tpu as pltpu
from jax.sharding import PartitionSpec as P

HEADS = 16
MOST = 2
CORES = 2
SUBLANES = 8
LANES = 128

root_half = 0.7071067811865476
inv_root_tau = 0.3989422804014327

LANES_BOTH = (((1,), (1,)), ((), ()))
FIRST_BOTH = (((0,), (0,)), ((), ()))


def gelu_slope(pre_act):
    normal_cdf = 0.5 * (1.0 + lax.erf(pre_act * root_half))
    density = jnp.exp(-0.5 * pre_act * pre_act) * inv_root_tau
    return normal_cdf + pre_act * density


def dot(a, b):
    return jnp.dot(a, b, preferred_element_type=jnp.float32)


def dot_lanes(a, b):
    return lax.dot_general(a, b, LANES_BOTH, preferred_element_type=jnp.float32)


def over_frames(values, op, blocks):
    rows = values.shape[0]
    total = values[:SUBLANES]
    for start in range(SUBLANES, rows, SUBLANES):
        total = op(total, values[start : start + SUBLANES])
    step = blocks
    while step < SUBLANES:
        total = op(total, pltpu.roll(total, step, 0))
        step *= 2
    return jnp.concatenate([total] * (rows // SUBLANES), axis=0)


def heads_of(values):
    width = values.shape[1] // HEADS
    return [values[:, h * width : (h + 1) * width] for h in range(HEADS)]


def turn_kernel(cot_hbm, out_ref, cot_ref, sem):
    copy = pltpu.make_async_copy(cot_hbm, cot_ref, sem)
    copy.start()
    copy.wait()
    out_ref[...] = cot_ref[...].reshape(out_ref.shape)


def forward_kernel(
    patches_all, share,
    chosen_hbm, gate_hbm, query_hbm, key_hbm, value_hbm, w_in_hbm,
    query_rows_ref, key_rows_ref, value_rows_ref, w_in_ref,
    probs_ref, picked_ref, here_ref, weight_ref, spread_ref,
    chosen_ref, gate_ref, query_ref, key_ref, value_ref, sems,
):
    columns = lax.axis_size("frm")
    column = lax.axis_index("frm")
    part = w_in_ref.shape[0] // CORES
    sources = [chosen_hbm, gate_hbm, query_hbm, key_hbm, value_hbm]
    targets = [chosen_ref, gate_ref, query_ref, key_ref, value_ref]
    for i in range(CORES):
        sources.append(w_in_hbm.at[0, part_of(column % CORES ^ i, part)])
        targets.append(w_in_ref.at[pl.ds(i * part, part)])
    copies = [
        pltpu.make_async_copy(source, target, sems.at[i])
        for i, (source, target) in enumerate(zip(sources, targets))
    ]
    for copy in copies:
        copy.start()
    frames, blocks, features = query_ref.shape
    rows = frames * blocks
    scaling = (features // HEADS) ** (-0.5)

    for copy in copies[:2]:
        copy.wait()
    experts, cap = chosen_ref.shape
    myself = lax.axis_index("grp") * columns + column
    before = (
        lax.broadcasted_iota(jnp.int32, (cap, cap), 0)
        < lax.broadcasted_iota(jnp.int32, (cap, cap), 1)
    ).astype(jnp.bfloat16)
    slot = lax.broadcasted_iota(jnp.int32, (SUBLANES, cap), 0)
    row_at = lax.broadcasted_iota(jnp.int32, (rows, cap), 0)
    found = []
    for e in range(experts):
        tokens = chosen_ref[e : e + 1, :]
        gates = gate_ref[e : e + 1, :]
        patch = tokens % patches_all
        owned = jnp.broadcast_to((patch // blocks == myself).astype(jnp.float32), slot.shape)
        rank = dot(owned.astype(jnp.bfloat16), before)
        taken = jnp.where((rank == slot.astype(jnp.float32)) & (owned > 0.0), 1.0, 0.0)
        position = (tokens // patches_all) * blocks + patch % blocks
        at_row = (row_at == position).astype(jnp.bfloat16)
        here = dot_lanes(taken.astype(jnp.bfloat16), at_row)
        weight = jnp.sum(taken * gates, axis=1, keepdims=True)
        here_ref[e * MOST : (e + 1) * MOST, :] = here[:MOST]
        weight_ref[e * MOST : (e + 1) * MOST, :] = jnp.broadcast_to(
            weight[:MOST], (MOST, weight_ref.shape[1])
        )
        found.append(here[:MOST])
    here = jnp.concatenate(found, axis=0).astype(jnp.bfloat16)
    cores, _, returns = spread_ref.shape
    slot_at = lax.broadcasted_iota(jnp.int32, (experts * MOST, returns), 0)
    back_at = lax.broadcasted_iota(jnp.int32, (experts * MOST, returns), 1)
    sender = back_at // MOST
    same = (sender // share == slot_at // MOST) & (back_at % MOST == slot_at % MOST)
    for c in range(cores):
        spread_ref[c] = lax.dot_general(
            here,
            (same & (sender % cores == c)).astype(jnp.bfloat16),
            FIRST_BOTH,
            preferred_element_type=jnp.float32,
        ).astype(jnp.bfloat16)

    for copy in copies[2:5]:
        copy.wait()
    query = query_ref[...].reshape(rows, features)
    key = key_ref[...].reshape(rows, features)
    value = value_ref[...].reshape(rows, features)
    query_rows_ref[...] = query
    key_rows_ref[...] = key
    value_rows_ref[...] = value
    scores = jnp.concatenate(
        [dot_lanes(k, q) for k, q in zip(heads_of(key), heads_of(query))], axis=1
    )
    scores = scores * scaling
    raised = jnp.exp(scores - over_frames(scores, jnp.maximum, blocks))
    probs = raised / over_frames(raised, jnp.add, blocks)
    patch_in = lax.broadcasted_iota(jnp.int32, probs.shape, 0) % blocks
    patch_out = lax.broadcasted_iota(jnp.int32, probs.shape, 1) % blocks
    probs = jnp.where(patch_in == patch_out, probs, 0.0)
    probs_ref[...] = probs
    weights = probs.T.astype(jnp.bfloat16)
    mixed = jnp.concatenate(
        [dot(weights[h * rows : (h + 1) * rows], v) for h, v in enumerate(heads_of(value))],
        axis=1,
    ).astype(jnp.bfloat16)
    picked_ref[...] = dot(here, mixed).astype(jnp.bfloat16)
    for copy in copies[5:]:
        copy.wait()


def pick_kernel(share, here_ref, weight_ref, picked_ref, cot_ref, out_ref, cot_rows_ref):
    frames, blocks, features = cot_ref.shape
    cot = cot_ref[...].reshape(frames * blocks, features)
    cot_rows_ref[...] = cot
    rows = dot(here_ref[...].astype(jnp.bfloat16), cot)
    rows = (rows * weight_ref[:, :1]).astype(jnp.bfloat16)
    part = features // CORES
    picked = picked_ref[...]
    both = [
        jnp.concatenate(
            [half[:, c * part : (c + 1) * part] for half in (picked, rows)], axis=1
        )
        for c in range(CORES)
    ]
    for e in range(out_ref.shape[0] // share):
        for i in range(share):
            out_ref[e * share + i] = both[i % CORES][e * MOST : (e + 1) * MOST]


def part_of(part, width):
    return pl.ds(pl.multiple_of(part * width, width), width)


def first_kernel(near_ref, w_in_ref, w_out_hbm, pre_ref, back_ref, w_out_ref, sems):
    width = w_in_ref.shape[0] // CORES
    copies = [
        pltpu.make_async_copy(
            w_out_hbm.at[0, :, part_of(lax.axis_index("frm") % CORES ^ i, width)],
            w_out_ref.at[:, pl.ds(i * width, width)],
            sems.at[i],
        )
        for i in range(CORES)
    ]
    for copy in copies:
        copy.start()
    rows = near_ref[...].reshape(pre_ref.shape[0], CORES * width)
    pre_ref[...] = dot(rows[:, :width], w_in_ref[:width, :])
    copies[0].wait()
    back_ref[...] = dot_lanes(rows[:, width:], w_out_ref[:, :width])
    for copy in copies[1:]:
        copy.wait()


def second_kernel(far_ref, pre_ref, back_ref, w_in_ref, w_out_ref, slope_ref, sent_ref):
    width = w_in_ref.shape[0] // CORES
    far = far_ref[...].reshape(pre_ref.shape[0], CORES * width)
    pre_act = pre_ref[...] + dot(far[:, :width], w_in_ref[width:, :])
    back_act = back_ref[...] + dot_lanes(far[:, width:], w_out_ref[:, width:])
    slope = (back_act * gelu_slope(pre_act)).astype(jnp.bfloat16)
    slope_ref[...] = slope
    sent_ref[...] = dot_lanes(slope, w_in_ref[width:, :]).astype(jnp.bfloat16)


def third_kernel(slope_ref, w_in_ref, kept_ref):
    width = kept_ref.shape[1]
    kept_ref[...] = dot_lanes(slope_ref[...], w_in_ref[:width, :])


def sum_kernel(kept_ref, came_ref, out_ref):
    total = kept_ref[...] + came_ref[...].astype(jnp.float32)
    out_ref[...] = total.astype(jnp.bfloat16).reshape(out_ref.shape)


def backward_kernel(
    spread_ref, back_ref, cot_ref, probs_ref, query_ref, key_ref, value_ref,
    grad_query_hbm, grad_key_hbm, grad_value_hbm,
    grad_query_ref, grad_key_ref, grad_value_ref, sems,
):
    frames, blocks, features = grad_query_ref.shape
    rows = frames * blocks
    scaling = (features // HEADS) ** (-0.5)
    query, key, value = query_ref[...], key_ref[...], value_ref[...]
    back = back_ref[...].reshape(-1, back_ref.shape[2])
    added = jnp.concatenate([dot(spread_ref[c], back) for c in range(CORES)], axis=1)
    stream = (cot_ref[...].astype(jnp.float32) + added).astype(jnp.bfloat16)
    probs = probs_ref[...]
    weights = probs.astype(jnp.bfloat16)
    copies = []

    def put(ref, hbm, parts):
        joined = jnp.concatenate(parts, axis=1).astype(jnp.bfloat16)
        ref[...] = joined.reshape(frames, blocks, features)
        copy = pltpu.make_async_copy(ref, hbm, sems.at[len(copies)])
        copy.start()
        copies.append(copy)

    put(
        grad_value_ref,
        grad_value_hbm,
        [dot(w, g) for w, g in zip(heads_of(weights), heads_of(stream))],
    )
    grad_prob = jnp.concatenate(
        [dot_lanes(v, g) for v, g in zip(heads_of(value), heads_of(stream))], axis=1
    )
    centre = over_frames(probs * grad_prob, jnp.add, blocks)
    grad_score = probs * (grad_prob - centre)
    turned = grad_score.T.astype(jnp.bfloat16)
    grad_score = grad_score.astype(jnp.bfloat16)
    put(
        grad_key_ref,
        grad_key_hbm,
        [dot(s, q) * scaling for s, q in zip(heads_of(grad_score), heads_of(query))],
    )
    put(
        grad_query_ref,
        grad_query_hbm,
        [dot(turned[h * rows : (h + 1) * rows], k) * scaling for h, k in enumerate(heads_of(key))],
    )
    for copy in copies:
        copy.wait()


def call(kernel, outs, operands, places, scratch=(), results="v", pinned=False):
    spaces = {
        "v": pl.BlockSpec(memory_space=pltpu.VMEM),
        "h": pl.BlockSpec(memory_space=pl.ANY),
    }
    return pl.pallas_call(
        kernel,
        out_shape=[
            (pltpu.VMEM if pinned else jax.ShapeDtypeStruct)(shape, dtype) for shape, dtype in outs
        ],
        in_specs=[spaces[place] for place in places],
        out_specs=[spaces[results]] * len(outs),
        scratch_shapes=list(scratch),
        compiler_params=pltpu.CompilerParams(vmem_limit_bytes=32 * 1024 * 1024),
    )(*[
        pltpu.with_memory_space_constraint(operand, pltpu.HBM) if place == "h" else operand
        for operand, place in zip(operands, places)
    ])


def body(query_in, key_in, value_in, cotangent, w_in, w_out, gate_probs, chosen):
    bf16, f32 = jnp.bfloat16, jnp.float32
    frames, blocks, features = query_in.shape
    groups = lax.axis_size("grp")
    columns = lax.axis_size("frm")
    experts = gate_probs.shape[0]
    devices = groups * columns
    share = devices // experts
    rows = frames * blocks
    slots = experts * MOST
    part = features // CORES
    hidden = w_in.shape[2]
    everyone = ("grp", "frm")

    def swap(values):
        return lax.ppermute(values, "frm", [(i, i ^ 1) for i in range(columns)])

    (turned,) = call(
        turn_kernel,
        [((columns, blocks, features), bf16)],
        [cotangent],
        "h",
        [pltpu.VMEM(cotangent.shape, bf16), pltpu.SemaphoreType.DMA],
        pinned=True,
    )
    cot = lax.all_to_all(turned, "frm", split_axis=0, concat_axis=0, tiled=True)
    query, key, value, w_in_near, probs, picked, here, weight, spread = call(
        functools.partial(forward_kernel, blocks * devices, share),
        [
            *[((rows, features), bf16)] * 3,
            (w_in.shape[1:], bf16),
            ((rows, HEADS * rows), f32),
            ((slots, features), bf16),
            ((slots, rows), f32),
            ((slots, LANES), f32),
            ((CORES, rows, devices * MOST), bf16),
        ],
        [chosen, gate_probs, query_in, key_in, value_in, w_in],
        "hhhhhh",
        [
            pltpu.VMEM(chosen.shape, jnp.int32),
            pltpu.VMEM(gate_probs.shape, f32),
            *[pltpu.VMEM(query_in.shape, bf16)] * 3,
            pltpu.SemaphoreType.DMA((5 + CORES,)),
        ],
    )
    outgoing, cot = call(
        functools.partial(pick_kernel, share),
        [((devices, MOST, 2 * part), bf16), ((rows, features), bf16)],
        [here, weight, picked, cot],
        "vvvv",
    )
    held = lax.all_to_all(outgoing, everyone, split_axis=0, concat_axis=0, tiled=True)
    other = swap(held)
    acts = (devices * MOST, hidden)
    halves = (devices * MOST, part)
    pre_act, back_act, w_out_near = call(
        first_kernel,
        [(acts, f32), (acts, f32), (w_out.shape[1:], bf16)],
        [held, w_in_near, w_out],
        "vvh",
        [pltpu.SemaphoreType.DMA((CORES,))],
    )
    slope, sent = call(
        second_kernel,
        [(acts, bf16), (halves, bf16)],
        [other, pre_act, back_act, w_in_near, w_out_near],
        "vvvvv",
    )
    came = swap(sent)
    (kept,) = call(third_kernel, [(halves, f32)], [slope, w_in_near], "vv")
    (total,) = call(sum_kernel, [((devices, MOST, part), bf16)], [kept, came], "vv")
    back = lax.all_to_all(total, everyone, split_axis=0, concat_axis=0, tiled=True)
    return call(
        backward_kernel,
        [((frames, blocks, features), bf16)] * 3,
        [spread, back, cot, probs, query, key, value],
        "vvvvvvv",
        [pltpu.VMEM((frames, blocks, features), bf16)] * 3 + [pltpu.SemaphoreType.DMA((3,))],
        "h",
    )


def solution(mesh):
    return jax.shard_map(
        body,
        mesh=mesh,
        in_specs=(
            P(None, ("grp", "frm"), None),
            P(None, ("grp", "frm"), None),
            P(None, ("grp", "frm"), None),
            P("frm", "grp", None),
            P("grp", None, "frm"),
            P("grp", "frm", None),
            P(),
            P(),
        ),
        out_specs=(
            P(None, ("grp", "frm"), None),
            P(None, ("grp", "frm"), None),
            P(None, ("grp", "frm"), None),
        ),
        check_vma=False,
    )
```

```python
import functools

import jax
import jax.numpy as jnp
from jax import lax
from jax.experimental import pallas as pl
from jax.experimental.pallas import tpu as pltpu
from jax.sharding import Mesh
from jax.sharding import PartitionSpec as P

HEADS = 16
MOST = 2
CORES = 2
SUBLANES = 8
LANES = 128

root_half = 0.7071067811865476
inv_root_tau = 0.3989422804014327

LANES_BOTH = (((1,), (1,)), ((), ()))
FIRST_BOTH = (((0,), (0,)), ((), ()))


def gelu_slope(pre_act):
    normal_cdf = 0.5 * (1.0 + lax.erf(pre_act * root_half))
    density = jnp.exp(-0.5 * pre_act * pre_act) * inv_root_tau
    return normal_cdf + pre_act * density


def dot(a, b):
    return jnp.dot(a, b, preferred_element_type=jnp.float32)


def dot_lanes(a, b):
    return lax.dot_general(a, b, LANES_BOTH, preferred_element_type=jnp.float32)


def over_frames(values, op, blocks):
    rows = values.shape[0]
    total = values[:SUBLANES]
    for start in range(SUBLANES, rows, SUBLANES):
        total = op(total, values[start : start + SUBLANES])
    step = blocks
    while step < SUBLANES:
        total = op(total, pltpu.roll(total, step, 0))
        step *= 2
    return jnp.concatenate([total] * (rows // SUBLANES), axis=0)


def heads_of(values):
    width = values.shape[1] // HEADS
    return [values[:, h * width : (h + 1) * width] for h in range(HEADS)]


def forward_kernel(
    patches_all, share,
    chosen_hbm, gate_hbm, query_hbm, key_hbm, value_hbm, w_in_hbm,
    query_rows_ref, key_rows_ref, value_rows_ref, w_in_ref,
    probs_ref, picked_ref, take_ref, weight_ref, spread_ref,
    chosen_ref, gate_ref, query_ref, key_ref, value_ref, sems,
):
    core = lax.axis_index("core")
    chip = lax.axis_index("grp") * lax.axis_size("z") + lax.axis_index("z")
    part = w_in_ref.shape[0] // CORES
    sources = [chosen_hbm, gate_hbm, query_hbm, key_hbm, value_hbm]
    targets = [chosen_ref, gate_ref, query_ref, key_ref, value_ref]
    for i in range(CORES):
        sources.append(w_in_hbm.at[0, part_of(core ^ i, part)])
        targets.append(w_in_ref.at[pl.ds(i * part, part)])
    copies = [
        pltpu.make_async_copy(source, target, sems.at[i])
        for i, (source, target) in enumerate(zip(sources, targets))
    ]
    for copy in copies:
        copy.start()
    frames, blocks, features = query_ref.shape
    rows = frames * blocks
    scaling = (features // HEADS) ** (-0.5)

    for copy in copies[:2]:
        copy.wait()
    experts, cap = chosen_ref.shape
    before = (
        lax.broadcasted_iota(jnp.int32, (cap, cap), 0)
        < lax.broadcasted_iota(jnp.int32, (cap, cap), 1)
    ).astype(jnp.bfloat16)
    slot = lax.broadcasted_iota(jnp.int32, (SUBLANES, cap), 0)
    row_at = lax.broadcasted_iota(jnp.int32, (rows, cap), 0)
    span = CORES * blocks
    slots = experts * MOST
    found = []
    for e in range(experts):
        tokens = chosen_ref[e : e + 1, :]
        gates = gate_ref[e : e + 1, :]
        patch = tokens % patches_all
        frame = tokens // patches_all
        for i in range(CORES):
            owned = patch // blocks == chip * CORES + (core ^ i)
            owned = jnp.broadcast_to(owned.astype(jnp.float32), slot.shape)
            rank = dot(owned.astype(jnp.bfloat16), before)
            taken = jnp.where((rank == slot.astype(jnp.float32)) & (owned > 0.0), 1.0, 0.0)
            weight = jnp.sum(taken * gates, axis=1, keepdims=True)
            taken = taken.astype(jnp.bfloat16)
            place = jnp.where(
                frame % CORES == core,
                (frame // CORES) * span + (core ^ i) * blocks + patch % blocks,
                -1,
            )
            at = slice(i * slots + e * MOST, i * slots + (e + 1) * MOST)
            take_ref[at] = dot_lanes(taken, (row_at == place).astype(jnp.bfloat16))[:MOST]
            weight_ref[at] = jnp.broadcast_to(weight[:MOST], (MOST, weight_ref.shape[1]))
            if i == 0:
                position = frame * blocks + patch % blocks
                found.append(dot_lanes(taken, (row_at == position).astype(jnp.bfloat16))[:MOST])
    levels = rows // span
    want = lax.broadcasted_iota(jnp.int32, (levels * blocks, rows), 0)
    have = lax.broadcasted_iota(jnp.int32, (levels * blocks, rows), 1)
    source = (want // blocks) * span + (core ^ 1) * blocks + want % blocks
    take_ref[CORES * slots :] = (source == have).astype(jnp.float32)
    here = jnp.concatenate(found, axis=0).astype(jnp.bfloat16)
    _, _, returns = spread_ref.shape
    slot_at = lax.broadcasted_iota(jnp.int32, (experts * MOST, returns), 0)
    back_at = lax.broadcasted_iota(jnp.int32, (experts * MOST, returns), 1)
    sender = back_at // MOST
    same = (sender // share == slot_at // MOST) & (back_at % MOST == slot_at % MOST)
    for c in range(CORES):
        spread_ref[c] = lax.dot_general(
            here,
            (same & (sender % CORES == c)).astype(jnp.bfloat16),
            FIRST_BOTH,
            preferred_element_type=jnp.float32,
        ).astype(jnp.bfloat16)

    for copy in copies[2:5]:
        copy.wait()
    query = query_ref[...].reshape(rows, features)
    key = key_ref[...].reshape(rows, features)
    value = value_ref[...].reshape(rows, features)
    query_rows_ref[...] = query
    key_rows_ref[...] = key
    value_rows_ref[...] = value
    scores = jnp.concatenate(
        [dot_lanes(k, q) for k, q in zip(heads_of(key), heads_of(query))], axis=1
    )
    scores = scores * scaling
    raised = jnp.exp(scores - over_frames(scores, jnp.maximum, blocks))
    probs = raised / over_frames(raised, jnp.add, blocks)
    patch_in = lax.broadcasted_iota(jnp.int32, probs.shape, 0) % blocks
    patch_out = lax.broadcasted_iota(jnp.int32, probs.shape, 1) % blocks
    probs = jnp.where(patch_in == patch_out, probs, 0.0)
    probs_ref[...] = probs
    weights = probs.T.astype(jnp.bfloat16)
    mixed = jnp.concatenate(
        [dot(weights[h * rows : (h + 1) * rows], v) for h, v in enumerate(heads_of(value))],
        axis=1,
    ).astype(jnp.bfloat16)
    picked_ref[...] = dot(here, mixed).astype(jnp.bfloat16)
    for copy in copies[5:]:
        copy.wait()


def pick_kernel(take_ref, weight_ref, cot_ref, mine_ref, sent_ref):
    levels, span, features = cot_ref.shape
    slots = mine_ref.shape[0]
    rows = dot(take_ref[...].astype(jnp.bfloat16), cot_ref[...].reshape(levels * span, features))
    picks = (rows[: CORES * slots] * weight_ref[:, :1]).astype(jnp.bfloat16)
    mine_ref[...] = picks[:slots]
    away = rows[CORES * slots :].astype(jnp.bfloat16)
    sent_ref[...] = jnp.concatenate([away, picks[slots:]], axis=0)


def pack_kernel(share, picked_ref, mine_ref, came_ref, out_ref):
    slots, features = mine_ref.shape
    rows = mine_ref[...] + came_ref[came_ref.shape[0] - slots :, :]
    part = features // CORES
    picked = picked_ref[...]
    both = [
        jnp.concatenate(
            [half[:, c * part : (c + 1) * part] for half in (picked, rows)], axis=1
        )
        for c in range(CORES)
    ]
    for e in range(out_ref.shape[0] // share):
        for i in range(share):
            out_ref[e * share + i] = both[i % CORES][e * MOST : (e + 1) * MOST]


def part_of(part, width):
    return pl.ds(pl.multiple_of(part * width, width), width)


def first_kernel(near_ref, w_in_ref, w_out_hbm, pre_ref, back_ref, w_out_ref, sems):
    width = w_in_ref.shape[0] // CORES
    copies = [
        pltpu.make_async_copy(
            w_out_hbm.at[0, :, part_of(lax.axis_index("core") ^ i, width)],
            w_out_ref.at[:, pl.ds(i * width, width)],
            sems.at[i],
        )
        for i in range(CORES)
    ]
    for copy in copies:
        copy.start()
    rows = near_ref[...].reshape(pre_ref.shape[0], CORES * width)
    pre_ref[...] = dot(rows[:, :width], w_in_ref[:width, :])
    copies[0].wait()
    back_ref[...] = dot_lanes(rows[:, width:], w_out_ref[:, :width])
    for copy in copies[1:]:
        copy.wait()


def second_kernel(far_ref, pre_ref, back_ref, w_in_ref, w_out_ref, slope_ref, sent_ref):
    width = w_in_ref.shape[0] // CORES
    far = far_ref[...].reshape(pre_ref.shape[0], CORES * width)
    pre_act = pre_ref[...] + dot(far[:, :width], w_in_ref[width:, :])
    back_act = back_ref[...] + dot_lanes(far[:, width:], w_out_ref[:, width:])
    slope = (back_act * gelu_slope(pre_act)).astype(jnp.bfloat16)
    slope_ref[...] = slope
    sent_ref[...] = dot_lanes(slope, w_in_ref[width:, :]).astype(jnp.bfloat16)


def third_kernel(slope_ref, w_in_ref, near_ref, came_ref, kept_ref, cot_ref):
    core = lax.axis_index("core")
    levels, span, features = near_ref.shape
    blocks = span // CORES
    rows = levels * span
    want = lax.broadcasted_iota(jnp.int32, (rows, rows), 0)
    have = lax.broadcasted_iota(jnp.int32, (rows, rows), 1)
    frame = want // blocks
    source = (frame // CORES) * span + core * blocks + want % blocks
    own = ((frame % CORES == core) & (source == have)).astype(jnp.bfloat16)
    want, have, frame = (values[:, : levels * blocks] for values in (want, have, frame))
    source = (frame // CORES) * blocks + want % blocks
    others = ((frame % CORES != core) & (source == have)).astype(jnp.bfloat16)
    cot = dot(own, near_ref[...].reshape(rows, features))
    cot = cot + dot(others, came_ref[: levels * blocks, :])
    cot_ref[...] = cot.astype(jnp.bfloat16)
    width = kept_ref.shape[1]
    kept_ref[...] = dot_lanes(slope_ref[...], w_in_ref[:width, :])


def sum_kernel(kept_ref, came_ref, out_ref):
    total = kept_ref[...] + came_ref[...].astype(jnp.float32)
    out_ref[...] = total.astype(jnp.bfloat16).reshape(out_ref.shape)


def backward_kernel(
    spread_ref, back_ref, cot_ref, probs_ref, query_ref, key_ref, value_ref,
    grad_query_hbm, grad_key_hbm, grad_value_hbm,
    grad_query_ref, grad_key_ref, grad_value_ref, sems,
):
    frames, blocks, features = grad_query_ref.shape
    rows = frames * blocks
    scaling = (features // HEADS) ** (-0.5)
    query, key, value = query_ref[...], key_ref[...], value_ref[...]
    back = back_ref[...].reshape(-1, back_ref.shape[2])
    added = jnp.concatenate([dot(spread_ref[c], back) for c in range(CORES)], axis=1)
    stream = (cot_ref[...].astype(jnp.float32) + added).astype(jnp.bfloat16)
    probs = probs_ref[...]
    weights = probs.astype(jnp.bfloat16)
    copies = []

    def put(ref, hbm, parts):
        joined = jnp.concatenate(parts, axis=1).astype(jnp.bfloat16)
        ref[...] = joined.reshape(frames, blocks, features)
        copy = pltpu.make_async_copy(ref, hbm, sems.at[len(copies)])
        copy.start()
        copies.append(copy)

    put(
        grad_value_ref,
        grad_value_hbm,
        [dot(w, g) for w, g in zip(heads_of(weights), heads_of(stream))],
    )
    grad_prob = jnp.concatenate(
        [dot_lanes(v, g) for v, g in zip(heads_of(value), heads_of(stream))], axis=1
    )
    centre = over_frames(probs * grad_prob, jnp.add, blocks)
    grad_score = probs * (grad_prob - centre)
    turned = grad_score.T.astype(jnp.bfloat16)
    grad_score = grad_score.astype(jnp.bfloat16)
    put(
        grad_key_ref,
        grad_key_hbm,
        [dot(s, q) * scaling for s, q in zip(heads_of(grad_score), heads_of(query))],
    )
    put(
        grad_query_ref,
        grad_query_hbm,
        [dot(turned[h * rows : (h + 1) * rows], k) * scaling for h, k in enumerate(heads_of(key))],
    )
    for copy in copies:
        copy.wait()


def call(kernel, outs, operands, places, scratch=(), results="v"):
    spaces = {
        "v": pl.BlockSpec(memory_space=pltpu.VMEM),
        "h": pl.BlockSpec(memory_space=pl.ANY),
    }
    return pl.pallas_call(
        kernel,
        out_shape=[jax.ShapeDtypeStruct(shape, dtype) for shape, dtype in outs],
        in_specs=[spaces[place] for place in places],
        out_specs=[spaces[results]] * len(outs),
        scratch_shapes=list(scratch),
        compiler_params=pltpu.CompilerParams(vmem_limit_bytes=32 * 1024 * 1024),
    )(*[
        pltpu.with_memory_space_constraint(operand, pltpu.HBM) if place == "h" else operand
        for operand, place in zip(operands, places)
    ])


def body(query_in, key_in, value_in, cotangent, w_in, w_out, gate_probs, chosen):
    bf16, f32 = jnp.bfloat16, jnp.float32
    frames, blocks, features = query_in.shape
    groups = lax.axis_size("grp")
    levels = lax.axis_size("z")
    columns = levels * CORES
    experts = gate_probs.shape[0]
    devices = groups * columns
    share = devices // experts
    rows = frames * blocks
    slots = experts * MOST
    part = features // CORES
    hidden = w_in.shape[2]
    everyone = ("grp", "z", "core")

    def swap(values):
        return lax.ppermute(values, "core", [(i, i ^ 1) for i in range(CORES)])

    cot_near = lax.all_to_all(
        cotangent.reshape(levels, CORES * blocks, features),
        "z", split_axis=0, concat_axis=0, tiled=True,
    )
    query, key, value, w_in_near, probs, picked, take, weight, spread = call(
        functools.partial(forward_kernel, blocks * devices, share),
        [
            *[((rows, features), bf16)] * 3,
            (w_in.shape[1:], bf16),
            ((rows, HEADS * rows), f32),
            ((slots, features), bf16),
            ((CORES * slots + levels * blocks, rows), f32),
            ((CORES * slots, LANES), f32),
            ((CORES, rows, devices * MOST), bf16),
        ],
        [chosen, gate_probs, query_in, key_in, value_in, w_in],
        "hhhhhh",
        [
            pltpu.VMEM(chosen.shape, jnp.int32),
            pltpu.VMEM(gate_probs.shape, f32),
            *[pltpu.VMEM(query_in.shape, bf16)] * 3,
            pltpu.SemaphoreType.DMA((5 + CORES,)),
        ],
    )
    mine, sent = call(
        pick_kernel,
        [((slots, features), bf16), ((levels * blocks + slots, features), bf16)],
        [take, weight, cot_near],
        "vvv",
    )
    came_near = swap(sent)
    (outgoing,) = call(
        functools.partial(pack_kernel, share),
        [((devices, MOST, 2 * part), bf16)],
        [picked, mine, came_near],
        "vvv",
    )
    held = lax.all_to_all(outgoing, everyone, split_axis=0, concat_axis=0, tiled=True)
    other = swap(held)
    acts = (devices * MOST, hidden)
    halves = (devices * MOST, part)
    pre_act, back_act, w_out_near = call(
        first_kernel,
        [(acts, f32), (acts, f32), (w_out.shape[1:], bf16)],
        [held, w_in_near, w_out],
        "vvh",
        [pltpu.SemaphoreType.DMA((CORES,))],
    )
    slope, sent = call(
        second_kernel,
        [(acts, bf16), (halves, bf16)],
        [other, pre_act, back_act, w_in_near, w_out_near],
        "vvvvv",
    )
    came = swap(sent)
    kept, cot = call(
        third_kernel,
        [(halves, f32), ((rows, features), bf16)],
        [slope, w_in_near, cot_near, came_near],
        "vvvv",
    )
    (total,) = call(sum_kernel, [((devices, MOST, part), bf16)], [kept, came], "vv")
    back = lax.all_to_all(total, everyone, split_axis=0, concat_axis=0, tiled=True)
    return call(
        backward_kernel,
        [((frames, blocks, features), bf16)] * 3,
        [spread, back, cot, probs, query, key, value],
        "vvvvvvv",
        [pltpu.VMEM((frames, blocks, features), bf16)] * 3 + [pltpu.SemaphoreType.DMA((3,))],
        "h",
    )


def solution(mesh):
    groups, columns = mesh.devices.shape
    split = Mesh(mesh.devices.reshape(groups, columns // CORES, CORES), ("grp", "z", "core"))
    frm = ("z", "core")
    patches = P(None, ("grp",) + frm, None)
    return jax.shard_map(
        body,
        mesh=split,
        in_specs=(
            patches, patches, patches, P(frm, "grp", None), P("grp", None, frm),
            P("grp", frm, None), P(), P(),
        ),
        out_specs=(patches, patches, patches),
        check_vma=False,
    )
```

```python
import functools

import jax
import jax.numpy as jnp
from jax import lax
from jax.experimental import pallas as pl
from jax.experimental.pallas import tpu as pltpu
from jax.sharding import Mesh
from jax.sharding import PartitionSpec as P

HEADS = 16
MOST = 2
CORES = 2
SUBLANES = 8
LANES = 128

root_half = 0.7071067811865476
inv_root_tau = 0.3989422804014327

LANES_BOTH = (((1,), (1,)), ((), ()))
FIRST_BOTH = (((0,), (0,)), ((), ()))


def gelu_slope(pre_act):
    normal_cdf = 0.5 * (1.0 + lax.erf(pre_act * root_half))
    density = jnp.exp(-0.5 * pre_act * pre_act) * inv_root_tau
    return normal_cdf + pre_act * density


def dot(a, b):
    return jnp.dot(a, b, preferred_element_type=jnp.float32)


def dot_lanes(a, b):
    return lax.dot_general(a, b, LANES_BOTH, preferred_element_type=jnp.float32)


def over_frames(values, op, blocks):
    rows = values.shape[0]
    total = values[:SUBLANES]
    for start in range(SUBLANES, rows, SUBLANES):
        total = op(total, values[start : start + SUBLANES])
    step = blocks
    while step < SUBLANES:
        total = op(total, pltpu.roll(total, step, 0))
        step *= 2
    return jnp.concatenate([total] * (rows // SUBLANES), axis=0)


def heads_of(values):
    width = values.shape[1] // HEADS
    return [values[:, h * width : (h + 1) * width] for h in range(HEADS)]


def forward_kernel(
    patches_all, share,
    chosen_hbm, gate_hbm, query_hbm, key_hbm, value_hbm, w_in_hbm,
    query_rows_ref, key_rows_ref, value_rows_ref, w_in_ref,
    probs_ref, picked_ref, take_ref, weight_ref, spread_ref,
    chosen_ref, gate_ref, query_ref, key_ref, value_ref, sems,
):
    core = lax.axis_index("core")
    chip = lax.axis_index("grp") * lax.axis_size("z") + lax.axis_index("z")
    part = w_in_ref.shape[0] // CORES
    sources = [chosen_hbm, gate_hbm, query_hbm, key_hbm, value_hbm]
    targets = [chosen_ref, gate_ref, query_ref, key_ref, value_ref]
    for i in range(CORES):
        sources.append(w_in_hbm.at[0, part_of(core ^ i, part)])
        targets.append(w_in_ref.at[pl.ds(i * part, part)])
    copies = [
        pltpu.make_async_copy(source, target, sems.at[i])
        for i, (source, target) in enumerate(zip(sources, targets))
    ]
    for copy in copies:
        copy.start()
    frames, blocks, features = query_ref.shape
    rows = frames * blocks
    scaling = (features // HEADS) ** (-0.5)

    for copy in copies[:2]:
        copy.wait()
    experts, cap = chosen_ref.shape
    before = (
        lax.broadcasted_iota(jnp.int32, (cap, cap), 0)
        < lax.broadcasted_iota(jnp.int32, (cap, cap), 1)
    ).astype(jnp.bfloat16)
    slot = lax.broadcasted_iota(jnp.int32, (SUBLANES, cap), 0)
    row_at = lax.broadcasted_iota(jnp.int32, (rows, cap), 0)
    span = CORES * blocks
    slots = experts * MOST
    found = []
    for e in range(experts):
        tokens = chosen_ref[e : e + 1, :]
        gates = gate_ref[e : e + 1, :]
        patch = tokens % patches_all
        frame = tokens // patches_all
        for i in range(CORES):
            owned = patch // blocks == chip * CORES + (core ^ i)
            owned = jnp.broadcast_to(owned.astype(jnp.float32), slot.shape)
            rank = dot(owned.astype(jnp.bfloat16), before)
            taken = jnp.where((rank == slot.astype(jnp.float32)) & (owned > 0.0), 1.0, 0.0)
            weight = jnp.sum(taken * gates, axis=1, keepdims=True)
            taken = taken.astype(jnp.bfloat16)
            place = jnp.where(
                frame % CORES == core,
                (frame // CORES) * span + (core ^ i) * blocks + patch % blocks,
                -1,
            )
            at = slice(i * slots + e * MOST, i * slots + (e + 1) * MOST)
            take_ref[at] = dot_lanes(taken, (row_at == place).astype(jnp.bfloat16))[:MOST]
            weight_ref[at] = jnp.broadcast_to(weight[:MOST], (MOST, weight_ref.shape[1]))
            if i == 0:
                position = frame * blocks + patch % blocks
                found.append(dot_lanes(taken, (row_at == position).astype(jnp.bfloat16))[:MOST])
    levels = rows // span
    want = lax.broadcasted_iota(jnp.int32, (levels * blocks, rows), 0)
    have = lax.broadcasted_iota(jnp.int32, (levels * blocks, rows), 1)
    source = (want // blocks) * span + (core ^ 1) * blocks + want % blocks
    take_ref[CORES * slots :] = (source == have).astype(jnp.float32)
    here = jnp.concatenate(found, axis=0).astype(jnp.bfloat16)
    _, _, returns = spread_ref.shape
    slot_at = lax.broadcasted_iota(jnp.int32, (experts * MOST, returns), 0)
    back_at = lax.broadcasted_iota(jnp.int32, (experts * MOST, returns), 1)
    sender = back_at // MOST
    same = (sender // share == slot_at // MOST) & (back_at % MOST == slot_at % MOST)
    for c in range(CORES):
        spread_ref[c] = lax.dot_general(
            here,
            (same & (sender % CORES == c)).astype(jnp.bfloat16),
            FIRST_BOTH,
            preferred_element_type=jnp.float32,
        ).astype(jnp.bfloat16)

    for copy in copies[2:5]:
        copy.wait()
    query = query_ref[...].reshape(rows, features)
    key = key_ref[...].reshape(rows, features)
    value = value_ref[...].reshape(rows, features)
    query_rows_ref[...] = query
    key_rows_ref[...] = key
    value_rows_ref[...] = value
    scores = jnp.concatenate(
        [dot_lanes(k, q) for k, q in zip(heads_of(key), heads_of(query))], axis=1
    )
    scores = scores * scaling
    raised = jnp.exp(scores - over_frames(scores, jnp.maximum, blocks))
    probs = raised / over_frames(raised, jnp.add, blocks)
    patch_in = lax.broadcasted_iota(jnp.int32, probs.shape, 0) % blocks
    patch_out = lax.broadcasted_iota(jnp.int32, probs.shape, 1) % blocks
    probs = jnp.where(patch_in == patch_out, probs, 0.0)
    probs_ref[...] = probs
    weights = probs.T.astype(jnp.bfloat16)
    mixed = jnp.concatenate(
        [dot(weights[h * rows : (h + 1) * rows], v) for h, v in enumerate(heads_of(value))],
        axis=1,
    ).astype(jnp.bfloat16)
    picked_ref[...] = dot(here, mixed).astype(jnp.bfloat16)
    for copy in copies[5:]:
        copy.wait()


def pick_kernel(take_ref, weight_ref, cot_ref, mine_ref, sent_ref):
    levels, span, features = cot_ref.shape
    slots = mine_ref.shape[0]
    rows = dot(take_ref[...].astype(jnp.bfloat16), cot_ref[...].reshape(levels * span, features))
    picks = (rows[: CORES * slots] * weight_ref[:, :1]).astype(jnp.bfloat16)
    mine_ref[...] = picks[:slots]
    away = rows[CORES * slots :].astype(jnp.bfloat16)
    sent_ref[...] = jnp.concatenate([away, picks[slots:]], axis=0)


def pack_kernel(share, picked_ref, mine_ref, came_ref, w_out_near_ref, out_ref):
    slots, features = mine_ref.shape
    rows = mine_ref[...] + came_ref[came_ref.shape[0] - slots :, :]
    part = features // CORES
    picked = picked_ref[...]
    both = [
        jnp.concatenate(
            [half[:, c * part : (c + 1) * part] for half in (picked, rows)], axis=1
        )
        for c in range(CORES)
    ]
    for e in range(out_ref.shape[0] // share):
        for i in range(share):
            out_ref[e * share + i] = both[i % CORES][e * MOST : (e + 1) * MOST]


def part_of(part, width):
    return pl.ds(pl.multiple_of(part * width, width), width)


def half_copy(i, w_out_hbm, half_ref, sem):
    width = half_ref.shape[1]
    return pltpu.make_async_copy(
        w_out_hbm.at[0, :, part_of(lax.axis_index("core") ^ i, width)], half_ref, sem
    )


def load_kernel(after_ref, w_out_hbm, half_ref, sem):
    copy = half_copy(0, w_out_hbm, half_ref, sem)
    copy.start()
    copy.wait()


def first_kernel(
    near_ref, w_in_ref, w_out_near_ref, w_out_hbm, pre_ref, back_ref, w_out_far_ref, sem
):
    copy = half_copy(1, w_out_hbm, w_out_far_ref, sem)
    copy.start()
    width = w_in_ref.shape[0] // CORES
    rows = near_ref[...].reshape(pre_ref.shape[0], CORES * width)
    pre_ref[...] = dot(rows[:, :width], w_in_ref[:width, :])
    back_ref[...] = dot_lanes(rows[:, width:], w_out_near_ref[...])
    copy.wait()


def second_kernel(far_ref, pre_ref, back_ref, w_in_ref, w_out_far_ref, slope_ref, sent_ref):
    width = w_in_ref.shape[0] // CORES
    far = far_ref[...].reshape(pre_ref.shape[0], CORES * width)
    pre_act = pre_ref[...] + dot(far[:, :width], w_in_ref[width:, :])
    back_act = back_ref[...] + dot_lanes(far[:, width:], w_out_far_ref[...])
    slope = (back_act * gelu_slope(pre_act)).astype(jnp.bfloat16)
    slope_ref[...] = slope
    sent_ref[...] = dot_lanes(slope, w_in_ref[width:, :]).astype(jnp.bfloat16)


def third_kernel(slope_ref, w_in_ref, near_ref, came_ref, kept_ref, cot_ref):
    core = lax.axis_index("core")
    levels, span, features = near_ref.shape
    blocks = span // CORES
    rows = levels * span
    want = lax.broadcasted_iota(jnp.int32, (rows, rows), 0)
    have = lax.broadcasted_iota(jnp.int32, (rows, rows), 1)
    frame = want // blocks
    source = (frame // CORES) * span + core * blocks + want % blocks
    own = ((frame % CORES == core) & (source == have)).astype(jnp.bfloat16)
    want, have, frame = (values[:, : levels * blocks] for values in (want, have, frame))
    source = (frame // CORES) * blocks + want % blocks
    others = ((frame % CORES != core) & (source == have)).astype(jnp.bfloat16)
    cot = dot(own, near_ref[...].reshape(rows, features))
    cot = cot + dot(others, came_ref[: levels * blocks, :])
    cot_ref[...] = cot.astype(jnp.bfloat16)
    width = kept_ref.shape[1]
    kept_ref[...] = dot_lanes(slope_ref[...], w_in_ref[:width, :])


def sum_kernel(kept_ref, came_ref, out_ref):
    total = kept_ref[...] + came_ref[...].astype(jnp.float32)
    out_ref[...] = total.astype(jnp.bfloat16).reshape(out_ref.shape)


def backward_kernel(
    spread_ref, back_ref, cot_ref, probs_ref, query_ref, key_ref, value_ref,
    grad_query_hbm, grad_key_hbm, grad_value_hbm,
    grad_query_ref, grad_key_ref, grad_value_ref, sems,
):
    frames, blocks, features = grad_query_ref.shape
    rows = frames * blocks
    scaling = (features // HEADS) ** (-0.5)
    query, key, value = query_ref[...], key_ref[...], value_ref[...]
    back = back_ref[...].reshape(-1, back_ref.shape[2])
    added = jnp.concatenate([dot(spread_ref[c], back) for c in range(CORES)], axis=1)
    stream = (cot_ref[...].astype(jnp.float32) + added).astype(jnp.bfloat16)
    probs = probs_ref[...]
    weights = probs.astype(jnp.bfloat16)
    copies = []

    def put(ref, hbm, parts):
        joined = jnp.concatenate(parts, axis=1).astype(jnp.bfloat16)
        ref[...] = joined.reshape(frames, blocks, features)
        copy = pltpu.make_async_copy(ref, hbm, sems.at[len(copies)])
        copy.start()
        copies.append(copy)

    put(
        grad_value_ref,
        grad_value_hbm,
        [dot(w, g) for w, g in zip(heads_of(weights), heads_of(stream))],
    )
    grad_prob = jnp.concatenate(
        [dot_lanes(v, g) for v, g in zip(heads_of(value), heads_of(stream))], axis=1
    )
    centre = over_frames(probs * grad_prob, jnp.add, blocks)
    grad_score = probs * (grad_prob - centre)
    turned = grad_score.T.astype(jnp.bfloat16)
    grad_score = grad_score.astype(jnp.bfloat16)
    put(
        grad_key_ref,
        grad_key_hbm,
        [dot(s, q) * scaling for s, q in zip(heads_of(grad_score), heads_of(query))],
    )
    put(
        grad_query_ref,
        grad_query_hbm,
        [dot(turned[h * rows : (h + 1) * rows], k) * scaling for h, k in enumerate(heads_of(key))],
    )
    for copy in copies:
        copy.wait()


def call(kernel, outs, operands, places, scratch=(), results="v"):
    spaces = {
        "v": pl.BlockSpec(memory_space=pltpu.VMEM),
        "h": pl.BlockSpec(memory_space=pl.ANY),
    }
    return pl.pallas_call(
        kernel,
        out_shape=[jax.ShapeDtypeStruct(shape, dtype) for shape, dtype in outs],
        in_specs=[spaces[place] for place in places],
        out_specs=[spaces[results]] * len(outs),
        scratch_shapes=list(scratch),
        compiler_params=pltpu.CompilerParams(vmem_limit_bytes=32 * 1024 * 1024),
    )(*[
        pltpu.with_memory_space_constraint(operand, pltpu.HBM) if place == "h" else operand
        for operand, place in zip(operands, places)
    ])


def body(query_in, key_in, value_in, cotangent, w_in, w_out, gate_probs, chosen):
    bf16, f32 = jnp.bfloat16, jnp.float32
    frames, blocks, features = query_in.shape
    groups = lax.axis_size("grp")
    levels = lax.axis_size("z")
    columns = levels * CORES
    experts = gate_probs.shape[0]
    devices = groups * columns
    share = devices // experts
    rows = frames * blocks
    slots = experts * MOST
    part = features // CORES
    hidden = w_in.shape[2]
    everyone = ("grp", "z", "core")

    def swap(values):
        return lax.ppermute(values, "core", [(i, i ^ 1) for i in range(CORES)])

    cot_near = lax.all_to_all(
        cotangent.reshape(levels, CORES * blocks, features),
        "z", split_axis=0, concat_axis=0, tiled=True,
    )
    query, key, value, w_in_near, probs, picked, take, weight, spread = call(
        functools.partial(forward_kernel, blocks * devices, share),
        [
            *[((rows, features), bf16)] * 3,
            (w_in.shape[1:], bf16),
            ((rows, HEADS * rows), f32),
            ((slots, features), bf16),
            ((CORES * slots + levels * blocks, rows), f32),
            ((CORES * slots, LANES), f32),
            ((CORES, rows, devices * MOST), bf16),
        ],
        [chosen, gate_probs, query_in, key_in, value_in, w_in],
        "hhhhhh",
        [
            pltpu.VMEM(chosen.shape, jnp.int32),
            pltpu.VMEM(gate_probs.shape, f32),
            *[pltpu.VMEM(query_in.shape, bf16)] * 3,
            pltpu.SemaphoreType.DMA((5 + CORES,)),
        ],
    )
    mine, sent = call(
        pick_kernel,
        [((slots, features), bf16), ((levels * blocks + slots, features), bf16)],
        [take, weight, cot_near],
        "vvv",
    )
    came_near = swap(sent)
    half = (hidden, part)
    (w_out_near,) = call(
        load_kernel, [(half, bf16)], [mine, w_out], "vh", [pltpu.SemaphoreType.DMA]
    )
    (outgoing,) = call(
        functools.partial(pack_kernel, share),
        [((devices, MOST, 2 * part), bf16)],
        [picked, mine, came_near, w_out_near],
        "vvvv",
    )
    held = lax.all_to_all(outgoing, everyone, split_axis=0, concat_axis=0, tiled=True)
    other = swap(held)
    acts = (devices * MOST, hidden)
    halves = (devices * MOST, part)
    pre_act, back_act, w_out_far = call(
        first_kernel,
        [(acts, f32), (acts, f32), (half, bf16)],
        [held, w_in_near, w_out_near, w_out],
        "vvvh",
        [pltpu.SemaphoreType.DMA],
    )
    slope, sent = call(
        second_kernel,
        [(acts, bf16), (halves, bf16)],
        [other, pre_act, back_act, w_in_near, w_out_far],
        "vvvvv",
    )
    came = swap(sent)
    kept, cot = call(
        third_kernel,
        [(halves, f32), ((rows, features), bf16)],
        [slope, w_in_near, cot_near, came_near],
        "vvvv",
    )
    (total,) = call(sum_kernel, [((devices, MOST, part), bf16)], [kept, came], "vv")
    back = lax.all_to_all(total, everyone, split_axis=0, concat_axis=0, tiled=True)
    return call(
        backward_kernel,
        [((frames, blocks, features), bf16)] * 3,
        [spread, back, cot, probs, query, key, value],
        "vvvvvvv",
        [pltpu.VMEM((frames, blocks, features), bf16)] * 3 + [pltpu.SemaphoreType.DMA((3,))],
        "h",
    )


def solution(mesh):
    groups, columns = mesh.devices.shape
    split = Mesh(mesh.devices.reshape(groups, columns // CORES, CORES), ("grp", "z", "core"))
    frm = ("z", "core")
    patches = P(None, ("grp",) + frm, None)
    return jax.shard_map(
        body,
        mesh=split,
        in_specs=(
            patches, patches, patches, P(frm, "grp", None), P("grp", None, frm),
            P("grp", frm, None), P(), P(),
        ),
        out_specs=(patches, patches, patches),
        check_vma=False,
    )
```

```python
import functools

import jax
import jax.numpy as jnp
from jax import lax
from jax.experimental import pallas as pl
from jax.experimental.pallas import tpu as pltpu
from jax.sharding import Mesh
from jax.sharding import PartitionSpec as P

HEADS = 16
MOST = 2
CORES = 2
SUBLANES = 8
LANES = 128

root_half = 0.7071067811865476
inv_root_tau = 0.3989422804014327

LANES_BOTH = (((1,), (1,)), ((), ()))
FIRST_BOTH = (((0,), (0,)), ((), ()))


def gelu_slope(pre_act):
    normal_cdf = 0.5 * (1.0 + lax.erf(pre_act * root_half))
    density = jnp.exp(-0.5 * pre_act * pre_act) * inv_root_tau
    return normal_cdf + pre_act * density


def dot(a, b):
    return jnp.dot(a, b, preferred_element_type=jnp.float32)


def dot_lanes(a, b):
    return lax.dot_general(a, b, LANES_BOTH, preferred_element_type=jnp.float32)


def over_frames(values, op, blocks):
    rows = values.shape[0]
    total = values[:SUBLANES]
    for start in range(SUBLANES, rows, SUBLANES):
        total = op(total, values[start : start + SUBLANES])
    step = blocks
    while step < SUBLANES:
        total = op(total, pltpu.roll(total, step, 0))
        step *= 2
    return jnp.concatenate([total] * (rows // SUBLANES), axis=0)


def heads_of(values):
    width = values.shape[1] // HEADS
    return [values[:, h * width : (h + 1) * width] for h in range(HEADS)]


def forward_kernel(
    patches_all, share,
    chosen_hbm, gate_hbm, query_hbm, key_hbm, value_hbm, w_in_hbm,
    query_rows_ref, key_rows_ref, value_rows_ref, w_in_ref,
    probs_ref, picked_ref, take_ref, weight_ref, spread_ref,
    chosen_ref, gate_ref, query_ref, key_ref, value_ref, sems,
):
    core = lax.axis_index("core")
    chip = lax.axis_index("grp") * lax.axis_size("z") + lax.axis_index("z")
    part = w_in_ref.shape[0] // CORES
    sources = [chosen_hbm, gate_hbm, query_hbm, key_hbm, value_hbm]
    targets = [chosen_ref, gate_ref, query_ref, key_ref, value_ref]
    for i in range(CORES):
        sources.append(w_in_hbm.at[0, part_of(core ^ i, part)])
        targets.append(w_in_ref.at[pl.ds(i * part, part)])
    copies = [
        pltpu.make_async_copy(source, target, sems.at[i])
        for i, (source, target) in enumerate(zip(sources, targets))
    ]
    for copy in copies:
        copy.start()
    frames, blocks, features = query_ref.shape
    rows = frames * blocks
    scaling = (features // HEADS) ** (-0.5)

    for copy in copies[:2]:
        copy.wait()
    experts, cap = chosen_ref.shape
    before = (
        lax.broadcasted_iota(jnp.int32, (cap, cap), 0)
        < lax.broadcasted_iota(jnp.int32, (cap, cap), 1)
    ).astype(jnp.bfloat16)
    slot = lax.broadcasted_iota(jnp.int32, (SUBLANES, cap), 0)
    row_at = lax.broadcasted_iota(jnp.int32, (rows, cap), 0)
    span = CORES * blocks
    slots = experts * MOST
    found = []
    for e in range(experts):
        tokens = chosen_ref[e : e + 1, :]
        gates = gate_ref[e : e + 1, :]
        patch = tokens % patches_all
        frame = tokens // patches_all
        for i in range(CORES):
            owned = patch // blocks == chip * CORES + (core ^ i)
            owned = jnp.broadcast_to(owned.astype(jnp.float32), slot.shape)
            rank = dot(owned.astype(jnp.bfloat16), before)
            taken = jnp.where((rank == slot.astype(jnp.float32)) & (owned > 0.0), 1.0, 0.0)
            weight = jnp.sum(taken * gates, axis=1, keepdims=True)
            taken = taken.astype(jnp.bfloat16)
            place = jnp.where(
                frame % CORES == core,
                (frame // CORES) * span + (core ^ i) * blocks + patch % blocks,
                -1,
            )
            at = slice(i * slots + e * MOST, i * slots + (e + 1) * MOST)
            take_ref[at] = dot_lanes(taken, (row_at == place).astype(jnp.bfloat16))[:MOST]
            weight_ref[at] = jnp.broadcast_to(weight[:MOST], (MOST, weight_ref.shape[1]))
            if i == 0:
                position = frame * blocks + patch % blocks
                found.append(dot_lanes(taken, (row_at == position).astype(jnp.bfloat16))[:MOST])
    levels = rows // span
    want = lax.broadcasted_iota(jnp.int32, (levels * blocks, rows), 0)
    have = lax.broadcasted_iota(jnp.int32, (levels * blocks, rows), 1)
    source = (want // blocks) * span + (core ^ 1) * blocks + want % blocks
    take_ref[CORES * slots :] = (source == have).astype(jnp.float32)
    here = jnp.concatenate(found, axis=0).astype(jnp.bfloat16)
    _, _, returns = spread_ref.shape
    slot_at = lax.broadcasted_iota(jnp.int32, (experts * MOST, returns), 0)
    back_at = lax.broadcasted_iota(jnp.int32, (experts * MOST, returns), 1)
    sender = back_at // MOST
    same = (sender // share == slot_at // MOST) & (back_at % MOST == slot_at % MOST)
    for c in range(CORES):
        spread_ref[c] = lax.dot_general(
            here,
            (same & (sender % CORES == c)).astype(jnp.bfloat16),
            FIRST_BOTH,
            preferred_element_type=jnp.float32,
        ).astype(jnp.bfloat16)

    for copy in copies[2:5]:
        copy.wait()
    query = query_ref[...].reshape(rows, features)
    key = key_ref[...].reshape(rows, features)
    value = value_ref[...].reshape(rows, features)
    query_rows_ref[...] = query
    key_rows_ref[...] = key
    value_rows_ref[...] = value
    scores = jnp.concatenate(
        [dot_lanes(k, q) for k, q in zip(heads_of(key), heads_of(query))], axis=1
    )
    scores = scores * scaling
    raised = jnp.exp(scores - over_frames(scores, jnp.maximum, blocks))
    probs = raised / over_frames(raised, jnp.add, blocks)
    patch_in = lax.broadcasted_iota(jnp.int32, probs.shape, 0) % blocks
    patch_out = lax.broadcasted_iota(jnp.int32, probs.shape, 1) % blocks
    probs = jnp.where(patch_in == patch_out, probs, 0.0)
    probs_ref[...] = probs
    weights = probs.T.astype(jnp.bfloat16)
    mixed = jnp.concatenate(
        [dot(weights[h * rows : (h + 1) * rows], v) for h, v in enumerate(heads_of(value))],
        axis=1,
    ).astype(jnp.bfloat16)
    picked_ref[...] = dot(here, mixed).astype(jnp.bfloat16)
    for copy in copies[5:]:
        copy.wait()


def pick_kernel(take_ref, weight_ref, picked_ref, cot_ref, mine_ref, sent_ref):
    levels, span, features = cot_ref.shape
    slots = picked_ref.shape[0]
    rows = dot(take_ref[...].astype(jnp.bfloat16), cot_ref[...].reshape(levels * span, features))
    picks = (rows[: CORES * slots] * weight_ref[:, :1]).astype(jnp.bfloat16)
    mine_ref[...] = picks
    away = rows[CORES * slots :].astype(jnp.bfloat16)
    sent_ref[...] = jnp.concatenate([away, picks[slots:], picks[:slots], picked_ref[...]], axis=0)


def pack_kernel(share, picked_ref, mine_ref, came_ref, w_out_near_ref, out_ref):
    core = lax.axis_index("core")
    slots, features = picked_ref.shape
    part = features // CORES
    came = came_ref[came_ref.shape[0] - 3 * slots :, :]
    cots = mine_ref[...] + came[: 2 * slots]
    near = jnp.concatenate([picked_ref[...], cots[:slots]], axis=1)
    far = jnp.concatenate([came[2 * slots :], cots[slots:]], axis=1)

    def columns(values):
        quarters = [values[:, i * part : (i + 1) * part] for i in range(2 * CORES)]
        low = jnp.concatenate(quarters[0::2], axis=1)
        high = jnp.concatenate(quarters[1::2], axis=1)
        return jnp.where(core == 0, low, high)

    near, far = columns(near), columns(far)
    pair = [jnp.where(core == 0, near, far), jnp.where(core == 0, far, near)]
    for e in range(out_ref.shape[0] // share):
        both = jnp.concatenate([rows[e * MOST : (e + 1) * MOST] for rows in pair], axis=0)
        for i in range(share):
            out_ref[e * share + i] = both


def part_of(part, width):
    return pl.ds(pl.multiple_of(part * width, width), width)


def half_copy(i, w_out_hbm, half_ref, sem):
    width = half_ref.shape[1]
    return pltpu.make_async_copy(
        w_out_hbm.at[0, :, part_of(lax.axis_index("core") ^ i, width)], half_ref, sem
    )


def load_kernel(after_ref, w_out_hbm, half_ref, sem):
    copy = half_copy(0, w_out_hbm, half_ref, sem)
    copy.start()
    copy.wait()


def first_kernel(
    near_ref, w_in_ref, w_out_near_ref, w_out_hbm, pre_ref, back_ref, w_out_far_ref, sem
):
    copy = half_copy(1, w_out_hbm, w_out_far_ref, sem)
    copy.start()
    width = w_in_ref.shape[0] // CORES
    rows = near_ref[...].reshape(pre_ref.shape[0], CORES * width)
    pre_ref[...] = dot(rows[:, :width], w_in_ref[:width, :])
    back_ref[...] = dot_lanes(rows[:, width:], w_out_near_ref[...])
    copy.wait()


def second_kernel(far_ref, pre_ref, back_ref, w_in_ref, w_out_far_ref, slope_ref, sent_ref):
    width = w_in_ref.shape[0] // CORES
    far = far_ref[...].reshape(pre_ref.shape[0], CORES * width)
    pre_act = pre_ref[...] + dot(far[:, :width], w_in_ref[width:, :])
    back_act = back_ref[...] + dot_lanes(far[:, width:], w_out_far_ref[...])
    slope = (back_act * gelu_slope(pre_act)).astype(jnp.bfloat16)
    slope_ref[...] = slope
    sent_ref[...] = dot_lanes(slope, w_in_ref[width:, :]).astype(jnp.bfloat16)


def third_kernel(slope_ref, w_in_ref, near_ref, came_ref, kept_ref, cot_ref):
    core = lax.axis_index("core")
    levels, span, features = near_ref.shape
    blocks = span // CORES
    rows = levels * span
    want = lax.broadcasted_iota(jnp.int32, (rows, rows), 0)
    have = lax.broadcasted_iota(jnp.int32, (rows, rows), 1)
    frame = want // blocks
    source = (frame // CORES) * span + core * blocks + want % blocks
    own = ((frame % CORES == core) & (source == have)).astype(jnp.bfloat16)
    want, have, frame = (values[:, : levels * blocks] for values in (want, have, frame))
    source = (frame // CORES) * blocks + want % blocks
    others = ((frame % CORES != core) & (source == have)).astype(jnp.bfloat16)
    cot = dot(own, near_ref[...].reshape(rows, features))
    cot = cot + dot(others, came_ref[: levels * blocks, :])
    cot_ref[...] = cot.astype(jnp.bfloat16)
    width = kept_ref.shape[1]
    kept_ref[...] = dot_lanes(slope_ref[...], w_in_ref[:width, :])


def sum_kernel(kept_ref, came_ref, out_ref):
    total = kept_ref[...] + came_ref[...].astype(jnp.float32)
    out_ref[...] = total.astype(jnp.bfloat16).reshape(out_ref.shape)


def backward_kernel(
    spread_ref, back_ref, cot_ref, probs_ref, query_ref, key_ref, value_ref,
    grad_query_hbm, grad_key_hbm, grad_value_hbm,
    grad_query_ref, grad_key_ref, grad_value_ref, sems,
):
    frames, blocks, features = grad_query_ref.shape
    rows = frames * blocks
    scaling = (features // HEADS) ** (-0.5)
    query, key, value = query_ref[...], key_ref[...], value_ref[...]
    back = back_ref[...].reshape(-1, back_ref.shape[2])
    added = jnp.concatenate([dot(spread_ref[c], back) for c in range(CORES)], axis=1)
    stream = (cot_ref[...].astype(jnp.float32) + added).astype(jnp.bfloat16)
    probs = probs_ref[...]
    weights = probs.astype(jnp.bfloat16)
    copies = []

    def put(ref, hbm, parts):
        joined = jnp.concatenate(parts, axis=1).astype(jnp.bfloat16)
        ref[...] = joined.reshape(frames, blocks, features)
        copy = pltpu.make_async_copy(ref, hbm, sems.at[len(copies)])
        copy.start()
        copies.append(copy)

    put(
        grad_value_ref,
        grad_value_hbm,
        [dot(w, g) for w, g in zip(heads_of(weights), heads_of(stream))],
    )
    grad_prob = jnp.concatenate(
        [dot_lanes(v, g) for v, g in zip(heads_of(value), heads_of(stream))], axis=1
    )
    centre = over_frames(probs * grad_prob, jnp.add, blocks)
    grad_score = probs * (grad_prob - centre)
    turned = grad_score.T.astype(jnp.bfloat16)
    grad_score = grad_score.astype(jnp.bfloat16)
    put(
        grad_key_ref,
        grad_key_hbm,
        [dot(s, q) * scaling for s, q in zip(heads_of(grad_score), heads_of(query))],
    )
    put(
        grad_query_ref,
        grad_query_hbm,
        [dot(turned[h * rows : (h + 1) * rows], k) * scaling for h, k in enumerate(heads_of(key))],
    )
    for copy in copies:
        copy.wait()


def call(kernel, outs, operands, places, scratch=(), results="v"):
    spaces = {
        "v": pl.BlockSpec(memory_space=pltpu.VMEM),
        "h": pl.BlockSpec(memory_space=pl.ANY),
    }
    return pl.pallas_call(
        kernel,
        out_shape=[jax.ShapeDtypeStruct(shape, dtype) for shape, dtype in outs],
        in_specs=[spaces[place] for place in places],
        out_specs=[spaces[results]] * len(outs),
        scratch_shapes=list(scratch),
        compiler_params=pltpu.CompilerParams(vmem_limit_bytes=32 * 1024 * 1024),
    )(*[
        pltpu.with_memory_space_constraint(operand, pltpu.HBM) if place == "h" else operand
        for operand, place in zip(operands, places)
    ])


def body(query_in, key_in, value_in, cotangent, w_in, w_out, gate_probs, chosen):
    bf16, f32 = jnp.bfloat16, jnp.float32
    frames, blocks, features = query_in.shape
    groups = lax.axis_size("grp")
    levels = lax.axis_size("z")
    columns = levels * CORES
    experts = gate_probs.shape[0]
    devices = groups * columns
    share = devices // experts
    rows = frames * blocks
    slots = experts * MOST
    part = features // CORES
    hidden = w_in.shape[2]
    everyone = ("grp", "z", "core")

    def swap(values):
        return lax.ppermute(values, "core", [(i, i ^ 1) for i in range(CORES)])

    cot_near = lax.all_to_all(
        cotangent.reshape(levels, CORES * blocks, features),
        "z", split_axis=0, concat_axis=0, tiled=True,
    )
    query, key, value, w_in_near, probs, picked, take, weight, spread = call(
        functools.partial(forward_kernel, blocks * devices, share),
        [
            *[((rows, features), bf16)] * 3,
            (w_in.shape[1:], bf16),
            ((rows, HEADS * rows), f32),
            ((slots, features), bf16),
            ((CORES * slots + levels * blocks, rows), f32),
            ((CORES * slots, LANES), f32),
            ((CORES, rows, devices * MOST), bf16),
        ],
        [chosen, gate_probs, query_in, key_in, value_in, w_in],
        "hhhhhh",
        [
            pltpu.VMEM(chosen.shape, jnp.int32),
            pltpu.VMEM(gate_probs.shape, f32),
            *[pltpu.VMEM(query_in.shape, bf16)] * 3,
            pltpu.SemaphoreType.DMA((5 + CORES,)),
        ],
    )
    mine, sent = call(
        pick_kernel,
        [((CORES * slots, features), bf16), ((levels * blocks + 3 * slots, features), bf16)],
        [take, weight, picked, cot_near],
        "vvvv",
    )
    came_near = swap(sent)
    half = (hidden, part)
    (w_out_near,) = call(
        load_kernel, [(half, bf16)], [mine, w_out], "vh", [pltpu.SemaphoreType.DMA]
    )
    (outgoing,) = call(
        functools.partial(pack_kernel, share // CORES),
        [((devices // CORES, CORES * MOST, 2 * part), bf16)],
        [picked, mine, came_near, w_out_near],
        "vvvv",
    )
    held = lax.all_to_all(outgoing, ("grp", "z"), split_axis=0, concat_axis=0, tiled=True)
    other = swap(held)
    acts = (devices * MOST, hidden)
    halves = (devices * MOST, part)
    pre_act, back_act, w_out_far = call(
        first_kernel,
        [(acts, f32), (acts, f32), (half, bf16)],
        [held, w_in_near, w_out_near, w_out],
        "vvvh",
        [pltpu.SemaphoreType.DMA],
    )
    slope, sent = call(
        second_kernel,
        [(acts, bf16), (halves, bf16)],
        [other, pre_act, back_act, w_in_near, w_out_far],
        "vvvvv",
    )
    came = swap(sent)
    kept, cot = call(
        third_kernel,
        [(halves, f32), ((rows, features), bf16)],
        [slope, w_in_near, cot_near, came_near],
        "vvvv",
    )
    (total,) = call(sum_kernel, [((devices, MOST, part), bf16)], [kept, came], "vv")
    back = lax.all_to_all(total, everyone, split_axis=0, concat_axis=0, tiled=True)
    return call(
        backward_kernel,
        [((frames, blocks, features), bf16)] * 3,
        [spread, back, cot, probs, query, key, value],
        "vvvvvvv",
        [pltpu.VMEM((frames, blocks, features), bf16)] * 3 + [pltpu.SemaphoreType.DMA((3,))],
        "h",
    )


def solution(mesh):
    groups, columns = mesh.devices.shape
    split = Mesh(mesh.devices.reshape(groups, columns // CORES, CORES), ("grp", "z", "core"))
    frm = ("z", "core")
    patches = P(None, ("grp",) + frm, None)
    return jax.shard_map(
        body,
        mesh=split,
        in_specs=(
            patches, patches, patches, P(frm, "grp", None), P("grp", None, frm),
            P("grp", frm, None), P(), P(),
        ),
        out_specs=(patches, patches, patches),
        check_vma=False,
    )
```

```python
import functools

import jax
import jax.numpy as jnp
from jax import lax
from jax.experimental import pallas as pl
from jax.experimental.pallas import tpu as pltpu
from jax.sharding import Mesh
from jax.sharding import PartitionSpec as P

HEADS = 16
MOST = 2
CORES = 2
SUBLANES = 8
LANES = 128

root_half = 0.7071067811865476
inv_root_tau = 0.3989422804014327

LANES_BOTH = (((1,), (1,)), ((), ()))
FIRST_BOTH = (((0,), (0,)), ((), ()))


def gelu_slope(pre_act):
    normal_cdf = 0.5 * (1.0 + lax.erf(pre_act * root_half))
    density = jnp.exp(-0.5 * pre_act * pre_act) * inv_root_tau
    return normal_cdf + pre_act * density


def dot(a, b):
    return jnp.dot(a, b, preferred_element_type=jnp.float32)


def dot_lanes(a, b):
    return lax.dot_general(a, b, LANES_BOTH, preferred_element_type=jnp.float32)


def over_frames(values, op, blocks):
    rows = values.shape[0]
    total = values[:SUBLANES]
    for start in range(SUBLANES, rows, SUBLANES):
        total = op(total, values[start : start + SUBLANES])
    step = blocks
    while step < SUBLANES:
        total = op(total, pltpu.roll(total, step, 0))
        step *= 2
    return jnp.concatenate([total] * (rows // SUBLANES), axis=0)


def heads_of(values):
    width = values.shape[1] // HEADS
    return [values[:, h * width : (h + 1) * width] for h in range(HEADS)]


def turn_kernel(span, cot_hbm, *refs):
    *part_refs, cot_ref, sem = refs
    copy = pltpu.make_async_copy(cot_hbm, cot_ref, sem)
    copy.start()
    rows = cot_ref.shape[1]
    want = lax.broadcasted_iota(jnp.int32, (rows, rows), 0)
    have = lax.broadcasted_iota(jnp.int32, (rows, rows), 1)
    source = ((want // span) ^ lax.axis_index("z")) * span + want % span
    order = (source == have).astype(jnp.bfloat16)
    copy.wait()
    turned = dot(order, cot_ref[0]).astype(jnp.bfloat16)
    for k, part_ref in enumerate(part_refs):
        part_ref[...] = turned[k * span : (k + 1) * span]


def held_core(level):
    core = lax.axis_index("core")
    return jnp.where(level == 0, core, 1 - core)


def forward_kernel(
    patches_all, share,
    chosen_hbm, gate_hbm, query_hbm, key_hbm, value_hbm, w_in_hbm,
    query_rows_ref, key_rows_ref, value_rows_ref, w_in_ref,
    probs_ref, picked_ref, take_ref, weight_ref, spread_ref,
    chosen_ref, gate_ref, query_ref, key_ref, value_ref, sems,
):
    core = lax.axis_index("core")
    chip = lax.axis_index("grp") * lax.axis_size("z") + lax.axis_index("z")
    part = w_in_ref.shape[0] // CORES
    sources = [chosen_hbm, gate_hbm, query_hbm, key_hbm, value_hbm]
    targets = [chosen_ref, gate_ref, query_ref, key_ref, value_ref]
    for i in range(CORES):
        sources.append(w_in_hbm.at[0, part_of(core ^ i, part)])
        targets.append(w_in_ref.at[pl.ds(i * part, part)])
    copies = [
        pltpu.make_async_copy(source, target, sems.at[i])
        for i, (source, target) in enumerate(zip(sources, targets))
    ]
    for copy in copies:
        copy.start()
    frames, blocks, features = query_ref.shape
    rows = frames * blocks
    scaling = (features // HEADS) ** (-0.5)

    for copy in copies[:2]:
        copy.wait()
    experts, cap = chosen_ref.shape
    before = (
        lax.broadcasted_iota(jnp.int32, (cap, cap), 0)
        < lax.broadcasted_iota(jnp.int32, (cap, cap), 1)
    ).astype(jnp.bfloat16)
    slot = lax.broadcasted_iota(jnp.int32, (SUBLANES, cap), 0)
    row_at = lax.broadcasted_iota(jnp.int32, (rows, cap), 0)
    span = CORES * blocks
    slots = experts * MOST
    found = []
    for e in range(experts):
        tokens = chosen_ref[e : e + 1, :]
        gates = gate_ref[e : e + 1, :]
        patch = tokens % patches_all
        frame = tokens // patches_all
        level = (frame // CORES) ^ lax.axis_index("z")
        for i in range(CORES):
            owned = patch // blocks == chip * CORES + (core ^ i)
            owned = jnp.broadcast_to(owned.astype(jnp.float32), slot.shape)
            rank = dot(owned.astype(jnp.bfloat16), before)
            taken = jnp.where((rank == slot.astype(jnp.float32)) & (owned > 0.0), 1.0, 0.0)
            weight = jnp.sum(taken * gates, axis=1, keepdims=True)
            taken = taken.astype(jnp.bfloat16)
            place = jnp.where(
                frame % CORES == held_core(level),
                level * span + (core ^ i) * blocks + patch % blocks,
                -1,
            )
            at = slice(i * slots + e * MOST, i * slots + (e + 1) * MOST)
            take_ref[at] = dot_lanes(taken, (row_at == place).astype(jnp.bfloat16))[:MOST]
            weight_ref[at] = jnp.broadcast_to(weight[:MOST], (MOST, weight_ref.shape[1]))
            if i == 0:
                position = frame * blocks + patch % blocks
                found.append(dot_lanes(taken, (row_at == position).astype(jnp.bfloat16))[:MOST])
    levels = rows // span
    want = lax.broadcasted_iota(jnp.int32, (levels * blocks, rows), 0)
    have = lax.broadcasted_iota(jnp.int32, (levels * blocks, rows), 1)
    source = (want // blocks) * span + (core ^ 1) * blocks + want % blocks
    take_ref[CORES * slots :] = (source == have).astype(jnp.float32)
    here = jnp.concatenate(found, axis=0).astype(jnp.bfloat16)
    _, _, returns = spread_ref.shape
    slot_at = lax.broadcasted_iota(jnp.int32, (experts * MOST, returns), 0)
    back_at = lax.broadcasted_iota(jnp.int32, (experts * MOST, returns), 1)
    sender = back_at // MOST
    same = (sender // share == slot_at // MOST) & (back_at % MOST == slot_at % MOST)
    for c in range(CORES):
        spread_ref[c] = lax.dot_general(
            here,
            (same & (sender % CORES == c)).astype(jnp.bfloat16),
            FIRST_BOTH,
            preferred_element_type=jnp.float32,
        ).astype(jnp.bfloat16)

    for copy in copies[2:5]:
        copy.wait()
    query = query_ref[...].reshape(rows, features)
    key = key_ref[...].reshape(rows, features)
    value = value_ref[...].reshape(rows, features)
    query_rows_ref[...] = query
    key_rows_ref[...] = key
    value_rows_ref[...] = value
    scores = jnp.concatenate(
        [dot_lanes(k, q) for k, q in zip(heads_of(key), heads_of(query))], axis=1
    )
    scores = scores * scaling
    raised = jnp.exp(scores - over_frames(scores, jnp.maximum, blocks))
    probs = raised / over_frames(raised, jnp.add, blocks)
    patch_in = lax.broadcasted_iota(jnp.int32, probs.shape, 0) % blocks
    patch_out = lax.broadcasted_iota(jnp.int32, probs.shape, 1) % blocks
    probs = jnp.where(patch_in == patch_out, probs, 0.0)
    probs_ref[...] = probs
    weights = probs.T.astype(jnp.bfloat16)
    mixed = jnp.concatenate(
        [dot(weights[h * rows : (h + 1) * rows], v) for h, v in enumerate(heads_of(value))],
        axis=1,
    ).astype(jnp.bfloat16)
    picked_ref[...] = dot(here, mixed).astype(jnp.bfloat16)
    for copy in copies[5:]:
        copy.wait()


def pick_kernel(take_ref, weight_ref, *refs):
    *part_refs, cot_ref, mine_ref, sent_ref = refs
    cot = jnp.concatenate([part_ref[...] for part_ref in part_refs], axis=0)
    cot_ref[...] = cot
    slots = mine_ref.shape[0]
    rows = dot(take_ref[...].astype(jnp.bfloat16), cot)
    picks = (rows[: CORES * slots] * weight_ref[:, :1]).astype(jnp.bfloat16)
    mine_ref[...] = picks[:slots]
    away = rows[CORES * slots :].astype(jnp.bfloat16)
    sent_ref[...] = jnp.concatenate([away, picks[slots:]], axis=0)


def pack_kernel(share, picked_ref, mine_ref, came_ref, w_out_near_ref, out_ref):
    slots, features = mine_ref.shape
    rows = mine_ref[...] + came_ref[came_ref.shape[0] - slots :, :]
    part = features // CORES
    picked = picked_ref[...]
    both = [
        jnp.concatenate(
            [half[:, c * part : (c + 1) * part] for half in (picked, rows)], axis=1
        )
        for c in range(CORES)
    ]
    for e in range(out_ref.shape[0] // share):
        for i in range(share):
            out_ref[e * share + i] = both[i % CORES][e * MOST : (e + 1) * MOST]


def part_of(part, width):
    return pl.ds(pl.multiple_of(part * width, width), width)


def half_copy(i, w_out_hbm, half_ref, sem):
    width = half_ref.shape[1]
    return pltpu.make_async_copy(
        w_out_hbm.at[0, :, part_of(lax.axis_index("core") ^ i, width)], half_ref, sem
    )


def load_kernel(after_ref, w_out_hbm, half_ref, sem):
    copy = half_copy(0, w_out_hbm, half_ref, sem)
    copy.start()
    copy.wait()


def first_kernel(
    near_ref, w_in_ref, w_out_near_ref, w_out_hbm, pre_ref, back_ref, w_out_far_ref, sem
):
    copy = half_copy(1, w_out_hbm, w_out_far_ref, sem)
    copy.start()
    width = w_in_ref.shape[0] // CORES
    rows = near_ref[...].reshape(pre_ref.shape[0], CORES * width)
    pre_ref[...] = dot(rows[:, :width], w_in_ref[:width, :])
    back_ref[...] = dot_lanes(rows[:, width:], w_out_near_ref[...])
    copy.wait()


def second_kernel(far_ref, pre_ref, back_ref, w_in_ref, w_out_far_ref, slope_ref, sent_ref):
    width = w_in_ref.shape[0] // CORES
    far = far_ref[...].reshape(pre_ref.shape[0], CORES * width)
    pre_act = pre_ref[...] + dot(far[:, :width], w_in_ref[width:, :])
    back_act = back_ref[...] + dot_lanes(far[:, width:], w_out_far_ref[...])
    slope = (back_act * gelu_slope(pre_act)).astype(jnp.bfloat16)
    slope_ref[...] = slope
    sent_ref[...] = dot_lanes(slope, w_in_ref[width:, :]).astype(jnp.bfloat16)


def third_kernel(blocks, slope_ref, w_in_ref, near_ref, came_ref, kept_ref, cot_ref):
    rows = near_ref.shape[0]
    span = CORES * blocks
    levels = rows // span
    want = lax.broadcasted_iota(jnp.int32, (rows, rows), 0)
    have = lax.broadcasted_iota(jnp.int32, (rows, rows), 1)
    frame = want // blocks
    level = (frame // CORES) ^ lax.axis_index("z")
    here = frame % CORES == held_core(level)
    source = level * span + lax.axis_index("core") * blocks + want % blocks
    own = (here & (source == have)).astype(jnp.bfloat16)
    source = level * blocks + want % blocks
    others = (jnp.logical_not(here) & (source == have)).astype(jnp.bfloat16)
    others = others[:, : levels * blocks]
    cot = dot(own, near_ref[...])
    cot = cot + dot(others, came_ref[: levels * blocks, :])
    cot_ref[...] = cot.astype(jnp.bfloat16)
    width = kept_ref.shape[1]
    kept_ref[...] = dot_lanes(slope_ref[...], w_in_ref[:width, :])


def sum_kernel(kept_ref, came_ref, out_ref):
    total = kept_ref[...] + came_ref[...].astype(jnp.float32)
    out_ref[...] = total.astype(jnp.bfloat16).reshape(out_ref.shape)


def backward_kernel(
    spread_ref, back_ref, cot_ref, probs_ref, query_ref, key_ref, value_ref,
    grad_query_hbm, grad_key_hbm, grad_value_hbm,
    grad_query_ref, grad_key_ref, grad_value_ref, sems,
):
    frames, blocks, features = grad_query_ref.shape
    rows = frames * blocks
    scaling = (features // HEADS) ** (-0.5)
    query, key, value = query_ref[...], key_ref[...], value_ref[...]
    back = back_ref[...].reshape(-1, back_ref.shape[2])
    added = jnp.concatenate([dot(spread_ref[c], back) for c in range(CORES)], axis=1)
    stream = (cot_ref[...].astype(jnp.float32) + added).astype(jnp.bfloat16)
    probs = probs_ref[...]
    weights = probs.astype(jnp.bfloat16)
    copies = []

    def put(ref, hbm, parts):
        joined = jnp.concatenate(parts, axis=1).astype(jnp.bfloat16)
        ref[...] = joined.reshape(frames, blocks, features)
        copy = pltpu.make_async_copy(ref, hbm, sems.at[len(copies)])
        copy.start()
        copies.append(copy)

    put(
        grad_value_ref,
        grad_value_hbm,
        [dot(w, g) for w, g in zip(heads_of(weights), heads_of(stream))],
    )
    grad_prob = jnp.concatenate(
        [dot_lanes(v, g) for v, g in zip(heads_of(value), heads_of(stream))], axis=1
    )
    centre = over_frames(probs * grad_prob, jnp.add, blocks)
    grad_score = probs * (grad_prob - centre)
    turned = grad_score.T.astype(jnp.bfloat16)
    grad_score = grad_score.astype(jnp.bfloat16)
    put(
        grad_key_ref,
        grad_key_hbm,
        [dot(s, q) * scaling for s, q in zip(heads_of(grad_score), heads_of(query))],
    )
    put(
        grad_query_ref,
        grad_query_hbm,
        [dot(turned[h * rows : (h + 1) * rows], k) * scaling for h, k in enumerate(heads_of(key))],
    )
    for copy in copies:
        copy.wait()


def call(kernel, outs, operands, places, scratch=(), results="v"):
    spaces = {
        "v": pl.BlockSpec(memory_space=pltpu.VMEM),
        "h": pl.BlockSpec(memory_space=pl.ANY),
    }
    return pl.pallas_call(
        kernel,
        out_shape=[jax.ShapeDtypeStruct(shape, dtype) for shape, dtype in outs],
        in_specs=[spaces[place] for place in places],
        out_specs=[spaces[results]] * len(outs),
        scratch_shapes=list(scratch),
        compiler_params=pltpu.CompilerParams(vmem_limit_bytes=32 * 1024 * 1024),
    )(*[
        pltpu.with_memory_space_constraint(operand, pltpu.HBM) if place == "h" else operand
        for operand, place in zip(operands, places)
    ])


def body(query_in, key_in, value_in, cotangent, w_in, w_out, gate_probs, chosen):
    bf16, f32 = jnp.bfloat16, jnp.float32
    frames, blocks, features = query_in.shape
    groups = lax.axis_size("grp")
    levels = lax.axis_size("z")
    columns = levels * CORES
    experts = gate_probs.shape[0]
    devices = groups * columns
    share = devices // experts
    rows = frames * blocks
    slots = experts * MOST
    part = features // CORES
    hidden = w_in.shape[2]
    everyone = ("grp", "z", "core")

    def swap(values):
        return lax.ppermute(values, "core", [(i, i ^ 1) for i in range(CORES)])

    def across(values, step):
        pairs = [(i, i ^ (CORES * step) ^ 1) for i in range(columns)]
        return lax.ppermute(values, ("z", "core"), pairs)

    span = CORES * blocks
    parts = call(
        functools.partial(turn_kernel, span),
        [((span, features), bf16)] * levels,
        [cotangent],
        "h",
        [pltpu.VMEM(cotangent.shape, bf16), pltpu.SemaphoreType.DMA],
    )
    parts = [parts[0]] + [across(parts[k], k) for k in range(1, levels)]
    query, key, value, w_in_near, probs, picked, take, weight, spread = call(
        functools.partial(forward_kernel, blocks * devices, share),
        [
            *[((rows, features), bf16)] * 3,
            (w_in.shape[1:], bf16),
            ((rows, HEADS * rows), f32),
            ((slots, features), bf16),
            ((CORES * slots + levels * blocks, rows), f32),
            ((CORES * slots, LANES), f32),
            ((CORES, rows, devices * MOST), bf16),
        ],
        [chosen, gate_probs, query_in, key_in, value_in, w_in],
        "hhhhhh",
        [
            pltpu.VMEM(chosen.shape, jnp.int32),
            pltpu.VMEM(gate_probs.shape, f32),
            *[pltpu.VMEM(query_in.shape, bf16)] * 3,
            pltpu.SemaphoreType.DMA((5 + CORES,)),
        ],
    )
    cot_near, mine, sent = call(
        pick_kernel,
        [((rows, features), bf16), ((slots, features), bf16), ((levels * blocks + slots, features), bf16)],
        [take, weight, *parts],
        "vv" + "v" * levels,
    )
    came_near = swap(sent)
    half = (hidden, part)
    (w_out_near,) = call(
        load_kernel, [(half, bf16)], [mine, w_out], "vh", [pltpu.SemaphoreType.DMA]
    )
    (outgoing,) = call(
        functools.partial(pack_kernel, share),
        [((devices, MOST, 2 * part), bf16)],
        [picked, mine, came_near, w_out_near],
        "vvvv",
    )
    held = lax.all_to_all(outgoing, everyone, split_axis=0, concat_axis=0, tiled=True)
    other = swap(held)
    acts = (devices * MOST, hidden)
    halves = (devices * MOST, part)
    pre_act, back_act, w_out_far = call(
        first_kernel,
        [(acts, f32), (acts, f32), (half, bf16)],
        [held, w_in_near, w_out_near, w_out],
        "vvvh",
        [pltpu.SemaphoreType.DMA],
    )
    slope, sent = call(
        second_kernel,
        [(acts, bf16), (halves, bf16)],
        [other, pre_act, back_act, w_in_near, w_out_far],
        "vvvvv",
    )
    came = swap(sent)
    kept, cot = call(
        functools.partial(third_kernel, blocks),
        [(halves, f32), ((rows, features), bf16)],
        [slope, w_in_near, cot_near, came_near],
        "vvvv",
    )
    (total,) = call(sum_kernel, [((devices, MOST, part), bf16)], [kept, came], "vv")
    back = lax.all_to_all(total, everyone, split_axis=0, concat_axis=0, tiled=True)
    return call(
        backward_kernel,
        [((frames, blocks, features), bf16)] * 3,
        [spread, back, cot, probs, query, key, value],
        "vvvvvvv",
        [pltpu.VMEM((frames, blocks, features), bf16)] * 3 + [pltpu.SemaphoreType.DMA((3,))],
        "h",
    )


def solution(mesh):
    groups, columns = mesh.devices.shape
    split = Mesh(mesh.devices.reshape(groups, columns // CORES, CORES), ("grp", "z", "core"))
    frm = ("z", "core")
    patches = P(None, ("grp",) + frm, None)
    return jax.shard_map(
        body,
        mesh=split,
        in_specs=(
            patches, patches, patches, P(frm, "grp", None), P("grp", None, frm),
            P("grp", frm, None), P(), P(),
        ),
        out_specs=(patches, patches, patches),
        check_vma=False,
    )
```

```python
import functools

import jax
import jax.numpy as jnp
from jax import lax
from jax.experimental import pallas as pl
from jax.experimental.pallas import tpu as pltpu
from jax.sharding import Mesh
from jax.sharding import PartitionSpec as P

HEADS = 16
MOST = 2
CORES = 2
SUBLANES = 8
LANES = 128

root_half = 0.7071067811865476
inv_root_tau = 0.3989422804014327

LANES_BOTH = (((1,), (1,)), ((), ()))
FIRST_BOTH = (((0,), (0,)), ((), ()))


def gelu_slope(pre_act):
    normal_cdf = 0.5 * (1.0 + lax.erf(pre_act * root_half))
    density = jnp.exp(-0.5 * pre_act * pre_act) * inv_root_tau
    return normal_cdf + pre_act * density


def dot(a, b):
    return jnp.dot(a, b, preferred_element_type=jnp.float32)


def dot_lanes(a, b):
    return lax.dot_general(a, b, LANES_BOTH, preferred_element_type=jnp.float32)


def over_frames(values, op, blocks):
    rows = values.shape[0]
    total = values[:SUBLANES]
    for start in range(SUBLANES, rows, SUBLANES):
        total = op(total, values[start : start + SUBLANES])
    step = blocks
    while step < SUBLANES:
        total = op(total, pltpu.roll(total, step, 0))
        step *= 2
    return jnp.concatenate([total] * (rows // SUBLANES), axis=0)


def heads_of(values):
    width = values.shape[1] // HEADS
    return [values[:, h * width : (h + 1) * width] for h in range(HEADS)]


def turn_kernel(span, cot_hbm, *refs):
    *part_refs, cot_ref, sem = refs
    copy = pltpu.make_async_copy(cot_hbm, cot_ref, sem)
    copy.start()
    rows = cot_ref.shape[1]
    want = lax.broadcasted_iota(jnp.int32, (rows, rows), 0)
    have = lax.broadcasted_iota(jnp.int32, (rows, rows), 1)
    source = ((want // span) ^ lax.axis_index("z")) * span + want % span
    order = (source == have).astype(jnp.bfloat16)
    copy.wait()
    turned = dot(order, cot_ref[0]).astype(jnp.bfloat16)
    for k, part_ref in enumerate(part_refs):
        part_ref[...] = turned[k * span : (k + 1) * span]


def held_core(level):
    core = lax.axis_index("core")
    return jnp.where(level == 0, core, 1 - core)


def forward_kernel(
    patches_all, share,
    chosen_hbm, gate_hbm, query_hbm, key_hbm, value_hbm, w_in_hbm,
    query_rows_ref, key_rows_ref, value_rows_ref, w_in_ref,
    probs_ref, picked_ref, take_ref, weight_ref, spread_ref,
    chosen_ref, gate_ref, query_ref, key_ref, value_ref, sems,
):
    core = lax.axis_index("core")
    chip = lax.axis_index("grp") * lax.axis_size("z") + lax.axis_index("z")
    part = w_in_ref.shape[0] // CORES
    sources = [chosen_hbm, gate_hbm, query_hbm, key_hbm, value_hbm]
    targets = [chosen_ref, gate_ref, query_ref, key_ref, value_ref]
    for i in range(CORES):
        sources.append(w_in_hbm.at[0, part_of(core ^ i, part)])
        targets.append(w_in_ref.at[pl.ds(i * part, part)])
    copies = [
        pltpu.make_async_copy(source, target, sems.at[i])
        for i, (source, target) in enumerate(zip(sources, targets))
    ]
    for copy in copies:
        copy.start()
    frames, blocks, features = query_ref.shape
    rows = frames * blocks
    scaling = (features // HEADS) ** (-0.5)

    for copy in copies[:2]:
        copy.wait()
    experts, cap = chosen_ref.shape
    before = (
        lax.broadcasted_iota(jnp.int32, (cap, cap), 0)
        < lax.broadcasted_iota(jnp.int32, (cap, cap), 1)
    ).astype(jnp.bfloat16)
    slot = lax.broadcasted_iota(jnp.int32, (SUBLANES, cap), 0)
    row_at = lax.broadcasted_iota(jnp.int32, (rows, cap), 0)
    span = CORES * blocks
    slots = experts * MOST
    found = []
    for e in range(experts):
        tokens = chosen_ref[e : e + 1, :]
        gates = gate_ref[e : e + 1, :]
        patch = tokens % patches_all
        frame = tokens // patches_all
        level = (frame // CORES) ^ lax.axis_index("z")
        for i in range(CORES):
            owned = patch // blocks == chip * CORES + (core ^ i)
            owned = jnp.broadcast_to(owned.astype(jnp.float32), slot.shape)
            rank = dot(owned.astype(jnp.bfloat16), before)
            taken = jnp.where((rank == slot.astype(jnp.float32)) & (owned > 0.0), 1.0, 0.0)
            weight = jnp.sum(taken * gates, axis=1, keepdims=True)
            taken = taken.astype(jnp.bfloat16)
            place = jnp.where(
                frame % CORES == held_core(level),
                level * span + (core ^ i) * blocks + patch % blocks,
                -1,
            )
            at = slice(i * slots + e * MOST, i * slots + (e + 1) * MOST)
            take_ref[at] = dot_lanes(taken, (row_at == place).astype(jnp.bfloat16))[:MOST]
            weight_ref[at] = jnp.broadcast_to(weight[:MOST], (MOST, weight_ref.shape[1]))
            if i == 0:
                position = frame * blocks + patch % blocks
                found.append(dot_lanes(taken, (row_at == position).astype(jnp.bfloat16))[:MOST])
    levels = rows // span
    want = lax.broadcasted_iota(jnp.int32, (levels * blocks, rows), 0)
    have = lax.broadcasted_iota(jnp.int32, (levels * blocks, rows), 1)
    source = (want // blocks) * span + (core ^ 1) * blocks + want % blocks
    take_ref[CORES * slots :] = (source == have).astype(jnp.float32)
    here = jnp.concatenate(found, axis=0).astype(jnp.bfloat16)
    _, _, returns = spread_ref.shape
    slot_at = lax.broadcasted_iota(jnp.int32, (experts * MOST, returns), 0)
    back_at = lax.broadcasted_iota(jnp.int32, (experts * MOST, returns), 1)
    sender = back_at // MOST
    same = (sender // share == slot_at // MOST) & (back_at % MOST == slot_at % MOST)
    for c in range(CORES):
        spread_ref[c] = lax.dot_general(
            here,
            (same & (sender % CORES == c)).astype(jnp.bfloat16),
            FIRST_BOTH,
            preferred_element_type=jnp.float32,
        ).astype(jnp.bfloat16)

    for copy in copies[2:5]:
        copy.wait()
    query = query_ref[...].reshape(rows, features)
    key = key_ref[...].reshape(rows, features)
    value = value_ref[...].reshape(rows, features)
    query_rows_ref[...] = query
    key_rows_ref[...] = key
    value_rows_ref[...] = value
    scores = jnp.concatenate(
        [dot_lanes(k, q) for k, q in zip(heads_of(key), heads_of(query))], axis=1
    )
    scores = scores * scaling
    raised = jnp.exp(scores - over_frames(scores, jnp.maximum, blocks))
    probs = raised / over_frames(raised, jnp.add, blocks)
    patch_in = lax.broadcasted_iota(jnp.int32, probs.shape, 0) % blocks
    patch_out = lax.broadcasted_iota(jnp.int32, probs.shape, 1) % blocks
    probs = jnp.where(patch_in == patch_out, probs, 0.0)
    probs_ref[...] = probs
    weights = probs.T.astype(jnp.bfloat16)
    mixed = jnp.concatenate(
        [dot(weights[h * rows : (h + 1) * rows], v) for h, v in enumerate(heads_of(value))],
        axis=1,
    ).astype(jnp.bfloat16)
    picked_ref[...] = dot(here, mixed).astype(jnp.bfloat16)
    for copy in copies[5:]:
        copy.wait()


def pick_kernel(order, take_ref, weight_ref, *refs):
    *part_refs, cot_ref, mine_ref, sent_ref = refs
    parts = [part_refs[order.index(k)][...] for k in range(len(order))]
    cot = jnp.concatenate(parts, axis=0)
    cot_ref[...] = cot
    slots = mine_ref.shape[0]
    rows = dot(take_ref[...].astype(jnp.bfloat16), cot)
    picks = (rows[: CORES * slots] * weight_ref[:, :1]).astype(jnp.bfloat16)
    mine_ref[...] = picks[:slots]
    away = rows[CORES * slots :].astype(jnp.bfloat16)
    sent_ref[...] = jnp.concatenate([away, picks[slots:]], axis=0)


def pack_kernel(share, picked_ref, mine_ref, came_ref, w_out_near_ref, out_ref):
    slots, features = mine_ref.shape
    rows = mine_ref[...] + came_ref[came_ref.shape[0] - slots :, :]
    part = features // CORES
    picked = picked_ref[...]
    both = [
        jnp.concatenate(
            [half[:, c * part : (c + 1) * part] for half in (picked, rows)], axis=1
        )
        for c in range(CORES)
    ]
    for e in range(out_ref.shape[0] // share):
        for i in range(share):
            out_ref[e * share + i] = both[i % CORES][e * MOST : (e + 1) * MOST]


def part_of(part, width):
    return pl.ds(pl.multiple_of(part * width, width), width)


def half_copy(i, w_out_hbm, half_ref, sem):
    width = half_ref.shape[1]
    return pltpu.make_async_copy(
        w_out_hbm.at[0, :, part_of(lax.axis_index("core") ^ i, width)], half_ref, sem
    )


def load_kernel(after_ref, w_out_hbm, half_ref, sem):
    copy = half_copy(0, w_out_hbm, half_ref, sem)
    copy.start()
    copy.wait()


def first_kernel(
    near_ref, w_in_ref, w_out_near_ref, w_out_hbm, pre_ref, back_ref, w_out_far_ref, sem
):
    copy = half_copy(1, w_out_hbm, w_out_far_ref, sem)
    copy.start()
    width = w_in_ref.shape[0] // CORES
    rows = near_ref[...].reshape(pre_ref.shape[0], CORES * width)
    pre_ref[...] = dot(rows[:, :width], w_in_ref[:width, :])
    back_ref[...] = dot_lanes(rows[:, width:], w_out_near_ref[...])
    copy.wait()


def second_kernel(far_ref, pre_ref, back_ref, w_in_ref, w_out_far_ref, slope_ref, sent_ref):
    width = w_in_ref.shape[0] // CORES
    far = far_ref[...].reshape(pre_ref.shape[0], CORES * width)
    pre_act = pre_ref[...] + dot(far[:, :width], w_in_ref[width:, :])
    back_act = back_ref[...] + dot_lanes(far[:, width:], w_out_far_ref[...])
    slope = (back_act * gelu_slope(pre_act)).astype(jnp.bfloat16)
    slope_ref[...] = slope
    sent_ref[...] = dot_lanes(slope, w_in_ref[width:, :]).astype(jnp.bfloat16)


def third_kernel(blocks, slope_ref, w_in_ref, near_ref, came_ref, kept_ref, cot_ref):
    rows = near_ref.shape[0]
    span = CORES * blocks
    levels = rows // span
    want = lax.broadcasted_iota(jnp.int32, (rows, rows), 0)
    have = lax.broadcasted_iota(jnp.int32, (rows, rows), 1)
    frame = want // blocks
    level = (frame // CORES) ^ lax.axis_index("z")
    here = frame % CORES == held_core(level)
    source = level * span + lax.axis_index("core") * blocks + want % blocks
    own = (here & (source == have)).astype(jnp.bfloat16)
    source = level * blocks + want % blocks
    others = (jnp.logical_not(here) & (source == have)).astype(jnp.bfloat16)
    others = others[:, : levels * blocks]
    cot = dot(own, near_ref[...])
    cot = cot + dot(others, came_ref[: levels * blocks, :])
    cot_ref[...] = cot.astype(jnp.bfloat16)
    width = kept_ref.shape[1]
    kept_ref[...] = dot_lanes(slope_ref[...], w_in_ref[:width, :])


def sum_kernel(kept_ref, came_ref, out_ref):
    total = kept_ref[...] + came_ref[...].astype(jnp.float32)
    out_ref[...] = total.astype(jnp.bfloat16).reshape(out_ref.shape)


def backward_kernel(
    spread_ref, back_ref, cot_ref, probs_ref, query_ref, key_ref, value_ref,
    grad_query_hbm, grad_key_hbm, grad_value_hbm,
    grad_query_ref, grad_key_ref, grad_value_ref, sems,
):
    frames, blocks, features = grad_query_ref.shape
    rows = frames * blocks
    scaling = (features // HEADS) ** (-0.5)
    query, key, value = query_ref[...], key_ref[...], value_ref[...]
    back = back_ref[...].reshape(-1, back_ref.shape[2])
    added = jnp.concatenate([dot(spread_ref[c], back) for c in range(CORES)], axis=1)
    stream = (cot_ref[...].astype(jnp.float32) + added).astype(jnp.bfloat16)
    probs = probs_ref[...]
    weights = probs.astype(jnp.bfloat16)
    copies = []

    def put(ref, hbm, parts):
        joined = jnp.concatenate(parts, axis=1).astype(jnp.bfloat16)
        ref[...] = joined.reshape(frames, blocks, features)
        copy = pltpu.make_async_copy(ref, hbm, sems.at[len(copies)])
        copy.start()
        copies.append(copy)

    put(
        grad_value_ref,
        grad_value_hbm,
        [dot(w, g) for w, g in zip(heads_of(weights), heads_of(stream))],
    )
    grad_prob = jnp.concatenate(
        [dot_lanes(v, g) for v, g in zip(heads_of(value), heads_of(stream))], axis=1
    )
    centre = over_frames(probs * grad_prob, jnp.add, blocks)
    grad_score = probs * (grad_prob - centre)
    turned = grad_score.T.astype(jnp.bfloat16)
    grad_score = grad_score.astype(jnp.bfloat16)
    put(
        grad_key_ref,
        grad_key_hbm,
        [dot(s, q) * scaling for s, q in zip(heads_of(grad_score), heads_of(query))],
    )
    put(
        grad_query_ref,
        grad_query_hbm,
        [dot(turned[h * rows : (h + 1) * rows], k) * scaling for h, k in enumerate(heads_of(key))],
    )
    for copy in copies:
        copy.wait()


def call(kernel, outs, operands, places, scratch=(), results="v"):
    spaces = {
        "v": pl.BlockSpec(memory_space=pltpu.VMEM),
        "h": pl.BlockSpec(memory_space=pl.ANY),
    }
    return pl.pallas_call(
        kernel,
        out_shape=[jax.ShapeDtypeStruct(shape, dtype) for shape, dtype in outs],
        in_specs=[spaces[place] for place in places],
        out_specs=[spaces[results]] * len(outs),
        scratch_shapes=list(scratch),
        compiler_params=pltpu.CompilerParams(vmem_limit_bytes=32 * 1024 * 1024),
    )(*[
        pltpu.with_memory_space_constraint(operand, pltpu.HBM) if place == "h" else operand
        for operand, place in zip(operands, places)
    ])


def body(query_in, key_in, value_in, cotangent, w_in, w_out, gate_probs, chosen):
    bf16, f32 = jnp.bfloat16, jnp.float32
    frames, blocks, features = query_in.shape
    groups = lax.axis_size("grp")
    levels = lax.axis_size("z")
    columns = levels * CORES
    experts = gate_probs.shape[0]
    devices = groups * columns
    share = devices // experts
    rows = frames * blocks
    slots = experts * MOST
    part = features // CORES
    hidden = w_in.shape[2]
    everyone = ("grp", "z", "core")

    def swap(values):
        return lax.ppermute(values, "core", [(i, i ^ 1) for i in range(CORES)])

    def across(values, step):
        pairs = [(i, i ^ (CORES * step) ^ 1) for i in range(columns)]
        return lax.ppermute(values, ("z", "core"), pairs)

    span = CORES * blocks
    parts = call(
        functools.partial(turn_kernel, span),
        [((span, features), bf16)] * levels,
        [cotangent],
        "h",
        [pltpu.VMEM(cotangent.shape, bf16), pltpu.SemaphoreType.DMA],
    )
    order = [0] + [i ^ (i >> 1) for i in range(levels - 1, 0, -1)]
    parts = [across(parts[k], k) if k else parts[k] for k in order]
    query, key, value, w_in_near, probs, picked, take, weight, spread = call(
        functools.partial(forward_kernel, blocks * devices, share),
        [
            *[((rows, features), bf16)] * 3,
            (w_in.shape[1:], bf16),
            ((rows, HEADS * rows), f32),
            ((slots, features), bf16),
            ((CORES * slots + levels * blocks, rows), f32),
            ((CORES * slots, LANES), f32),
            ((CORES, rows, devices * MOST), bf16),
        ],
        [chosen, gate_probs, query_in, key_in, value_in, w_in],
        "hhhhhh",
        [
            pltpu.VMEM(chosen.shape, jnp.int32),
            pltpu.VMEM(gate_probs.shape, f32),
            *[pltpu.VMEM(query_in.shape, bf16)] * 3,
            pltpu.SemaphoreType.DMA((5 + CORES,)),
        ],
    )
    cot_near, mine, sent = call(
        functools.partial(pick_kernel, order),
        [((rows, features), bf16), ((slots, features), bf16), ((levels * blocks + slots, features), bf16)],
        [take, weight, *parts],
        "vv" + "v" * levels,
    )
    came_near = swap(sent)
    half = (hidden, part)
    (w_out_near,) = call(
        load_kernel, [(half, bf16)], [mine, w_out], "vh", [pltpu.SemaphoreType.DMA]
    )
    (outgoing,) = call(
        functools.partial(pack_kernel, share),
        [((devices, MOST, 2 * part), bf16)],
        [picked, mine, came_near, w_out_near],
        "vvvv",
    )
    held = lax.all_to_all(outgoing, everyone, split_axis=0, concat_axis=0, tiled=True)
    other = swap(held)
    acts = (devices * MOST, hidden)
    halves = (devices * MOST, part)
    pre_act, back_act, w_out_far = call(
        first_kernel,
        [(acts, f32), (acts, f32), (half, bf16)],
        [held, w_in_near, w_out_near, w_out],
        "vvvh",
        [pltpu.SemaphoreType.DMA],
    )
    slope, sent = call(
        second_kernel,
        [(acts, bf16), (halves, bf16)],
        [other, pre_act, back_act, w_in_near, w_out_far],
        "vvvvv",
    )
    came = swap(sent)
    kept, cot = call(
        functools.partial(third_kernel, blocks),
        [(halves, f32), ((rows, features), bf16)],
        [slope, w_in_near, cot_near, came_near],
        "vvvv",
    )
    (total,) = call(sum_kernel, [((devices, MOST, part), bf16)], [kept, came], "vv")
    back = lax.all_to_all(total, everyone, split_axis=0, concat_axis=0, tiled=True)
    return call(
        backward_kernel,
        [((frames, blocks, features), bf16)] * 3,
        [spread, back, cot, probs, query, key, value],
        "vvvvvvv",
        [pltpu.VMEM((frames, blocks, features), bf16)] * 3 + [pltpu.SemaphoreType.DMA((3,))],
        "h",
    )


def solution(mesh):
    groups, columns = mesh.devices.shape
    split = Mesh(mesh.devices.reshape(groups, columns // CORES, CORES), ("grp", "z", "core"))
    frm = ("z", "core")
    patches = P(None, ("grp",) + frm, None)
    return jax.shard_map(
        body,
        mesh=split,
        in_specs=(
            patches, patches, patches, P(frm, "grp", None), P("grp", None, frm),
            P("grp", frm, None), P(), P(),
        ),
        out_specs=(patches, patches, patches),
        check_vma=False,
    )
```

```python
import functools

import jax
import jax.numpy as jnp
from jax import lax
from jax.experimental import pallas as pl
from jax.experimental.pallas import tpu as pltpu
from jax.sharding import Mesh
from jax.sharding import PartitionSpec as P

HEADS = 16
MOST = 2
CORES = 2
SUBLANES = 8
LANES = 128

root_half = 0.7071067811865476
inv_root_tau = 0.3989422804014327

LANES_BOTH = (((1,), (1,)), ((), ()))
FIRST_BOTH = (((0,), (0,)), ((), ()))


def gelu_slope(pre_act):
    normal_cdf = 0.5 * (1.0 + lax.erf(pre_act * root_half))
    density = jnp.exp(-0.5 * pre_act * pre_act) * inv_root_tau
    return normal_cdf + pre_act * density


def dot(a, b):
    return jnp.dot(a, b, preferred_element_type=jnp.float32)


def dot_lanes(a, b):
    return lax.dot_general(a, b, LANES_BOTH, preferred_element_type=jnp.float32)


def over_frames(values, op, blocks):
    rows = values.shape[0]
    total = values[:SUBLANES]
    for start in range(SUBLANES, rows, SUBLANES):
        total = op(total, values[start : start + SUBLANES])
    step = blocks
    while step < SUBLANES:
        total = op(total, pltpu.roll(total, step, 0))
        step *= 2
    return jnp.concatenate([total] * (rows // SUBLANES), axis=0)


def heads_of(values):
    width = values.shape[1] // HEADS
    return [values[:, h * width : (h + 1) * width] for h in range(HEADS)]


def turn_kernel(span, cot_hbm, *refs):
    *part_refs, cot_ref, sem = refs
    copy = pltpu.make_async_copy(cot_hbm, cot_ref, sem)
    copy.start()
    rows = cot_ref.shape[1]
    want = lax.broadcasted_iota(jnp.int32, (rows, rows), 0)
    have = lax.broadcasted_iota(jnp.int32, (rows, rows), 1)
    source = ((want // span) ^ lax.axis_index("z")) * span + want % span
    order = (source == have).astype(jnp.bfloat16)
    copy.wait()
    turned = dot(order, cot_ref[0]).astype(jnp.bfloat16)
    for k, part_ref in enumerate(part_refs):
        part_ref[...] = turned[k * span : (k + 1) * span]


def held_core(level):
    core = lax.axis_index("core")
    return jnp.where(level == 0, core, 1 - core)


def forward_kernel(
    patches_all, share,
    chosen_hbm, gate_hbm, query_hbm, key_hbm, value_hbm, w_in_hbm, w_out_hbm,
    query_rows_ref, key_rows_ref, value_rows_ref, w_in_ref, w_out_ref,
    probs_ref, picked_ref, take_ref, weight_ref, spread_ref,
    chosen_ref, gate_ref, query_ref, key_ref, value_ref, sems,
):
    core = lax.axis_index("core")
    chip = lax.axis_index("grp") * lax.axis_size("z") + lax.axis_index("z")
    part = w_in_ref.shape[0] // CORES
    sources = [chosen_hbm, gate_hbm, query_hbm, key_hbm, value_hbm]
    targets = [chosen_ref, gate_ref, query_ref, key_ref, value_ref]
    for i in range(CORES):
        sources.append(w_in_hbm.at[0, part_of(core ^ i, part)])
        targets.append(w_in_ref.at[pl.ds(i * part, part)])
        sources.append(w_out_hbm.at[0, :, part_of(core ^ i, part)])
        targets.append(w_out_ref.at[:, pl.ds(i * part, part)])
    copies = [
        pltpu.make_async_copy(source, target, sems.at[i])
        for i, (source, target) in enumerate(zip(sources, targets))
    ]
    for copy in copies:
        copy.start()
    frames, blocks, features = query_ref.shape
    rows = frames * blocks
    scaling = (features // HEADS) ** (-0.5)

    for copy in copies[:2]:
        copy.wait()
    experts, cap = chosen_ref.shape
    before = (
        lax.broadcasted_iota(jnp.int32, (cap, cap), 0)
        < lax.broadcasted_iota(jnp.int32, (cap, cap), 1)
    ).astype(jnp.bfloat16)
    slot = lax.broadcasted_iota(jnp.int32, (SUBLANES, cap), 0)
    row_at = lax.broadcasted_iota(jnp.int32, (rows, cap), 0)
    span = CORES * blocks
    slots = experts * MOST
    found = []
    for e in range(experts):
        tokens = chosen_ref[e : e + 1, :]
        gates = gate_ref[e : e + 1, :]
        patch = tokens % patches_all
        frame = tokens // patches_all
        level = (frame // CORES) ^ lax.axis_index("z")
        for i in range(CORES):
            owned = patch // blocks == chip * CORES + (core ^ i)
            owned = jnp.broadcast_to(owned.astype(jnp.float32), slot.shape)
            rank = dot(owned.astype(jnp.bfloat16), before)
            taken = jnp.where((rank == slot.astype(jnp.float32)) & (owned > 0.0), 1.0, 0.0)
            weight = jnp.sum(taken * gates, axis=1, keepdims=True)
            taken = taken.astype(jnp.bfloat16)
            place = jnp.where(
                frame % CORES == held_core(level),
                level * span + (core ^ i) * blocks + patch % blocks,
                -1,
            )
            at = slice(i * slots + e * MOST, i * slots + (e + 1) * MOST)
            take_ref[at] = dot_lanes(taken, (row_at == place).astype(jnp.bfloat16))[:MOST]
            weight_ref[at] = jnp.broadcast_to(weight[:MOST], (MOST, weight_ref.shape[1]))
            if i == 0:
                position = frame * blocks + patch % blocks
                found.append(dot_lanes(taken, (row_at == position).astype(jnp.bfloat16))[:MOST])
    levels = rows // span
    want = lax.broadcasted_iota(jnp.int32, (levels * blocks, rows), 0)
    have = lax.broadcasted_iota(jnp.int32, (levels * blocks, rows), 1)
    source = (want // blocks) * span + (core ^ 1) * blocks + want % blocks
    take_ref[CORES * slots :] = (source == have).astype(jnp.float32)
    here = jnp.concatenate(found, axis=0).astype(jnp.bfloat16)
    _, _, returns = spread_ref.shape
    slot_at = lax.broadcasted_iota(jnp.int32, (experts * MOST, returns), 0)
    back_at = lax.broadcasted_iota(jnp.int32, (experts * MOST, returns), 1)
    sender = back_at // MOST
    same = (sender // share == slot_at // MOST) & (back_at % MOST == slot_at % MOST)
    for c in range(CORES):
        spread_ref[c] = lax.dot_general(
            here,
            (same & (sender % CORES == c)).astype(jnp.bfloat16),
            FIRST_BOTH,
            preferred_element_type=jnp.float32,
        ).astype(jnp.bfloat16)

    for copy in copies[2:5]:
        copy.wait()
    query = query_ref[...].reshape(rows, features)
    key = key_ref[...].reshape(rows, features)
    value = value_ref[...].reshape(rows, features)
    query_rows_ref[...] = query
    key_rows_ref[...] = key
    value_rows_ref[...] = value
    scores = jnp.concatenate(
        [dot_lanes(k, q) for k, q in zip(heads_of(key), heads_of(query))], axis=1
    )
    scores = scores * scaling
    raised = jnp.exp(scores - over_frames(scores, jnp.maximum, blocks))
    probs = raised / over_frames(raised, jnp.add, blocks)
    patch_in = lax.broadcasted_iota(jnp.int32, probs.shape, 0) % blocks
    patch_out = lax.broadcasted_iota(jnp.int32, probs.shape, 1) % blocks
    probs = jnp.where(patch_in == patch_out, probs, 0.0)
    probs_ref[...] = probs
    weights = probs.T.astype(jnp.bfloat16)
    mixed = jnp.concatenate(
        [dot(weights[h * rows : (h + 1) * rows], v) for h, v in enumerate(heads_of(value))],
        axis=1,
    ).astype(jnp.bfloat16)
    picked_ref[...] = dot(here, mixed).astype(jnp.bfloat16)
    for copy in copies[5:]:
        copy.wait()


def pick_kernel(order, take_ref, weight_ref, *refs):
    *part_refs, cot_ref, mine_ref, sent_ref = refs
    parts = [part_refs[order.index(k)][...] for k in range(len(order))]
    cot = jnp.concatenate(parts, axis=0)
    cot_ref[...] = cot
    slots = mine_ref.shape[0]
    rows = dot(take_ref[...].astype(jnp.bfloat16), cot)
    picks = (rows[: CORES * slots] * weight_ref[:, :1]).astype(jnp.bfloat16)
    mine_ref[...] = picks[:slots]
    away = rows[CORES * slots :].astype(jnp.bfloat16)
    sent_ref[...] = jnp.concatenate([away, picks[slots:]], axis=0)


def pack_kernel(share, picked_ref, mine_ref, came_ref, out_ref):
    slots, features = mine_ref.shape
    rows = mine_ref[...] + came_ref[came_ref.shape[0] - slots :, :]
    part = features // CORES
    picked = picked_ref[...]
    both = [
        jnp.concatenate(
            [half[:, c * part : (c + 1) * part] for half in (picked, rows)], axis=1
        )
        for c in range(CORES)
    ]
    for e in range(out_ref.shape[0] // share):
        for i in range(share):
            out_ref[e * share + i] = both[i % CORES][e * MOST : (e + 1) * MOST]


def part_of(part, width):
    return pl.ds(pl.multiple_of(part * width, width), width)


def first_kernel(near_ref, w_in_ref, w_out_ref, pre_ref, back_ref):
    width = w_in_ref.shape[0] // CORES
    rows = near_ref[...].reshape(pre_ref.shape[0], CORES * width)
    pre_ref[...] = dot(rows[:, :width], w_in_ref[:width, :])
    back_ref[...] = dot_lanes(rows[:, width:], w_out_ref[:, :width])


def second_kernel(far_ref, pre_ref, back_ref, w_in_ref, w_out_ref, slope_ref, sent_ref):
    width = w_in_ref.shape[0] // CORES
    far = far_ref[...].reshape(pre_ref.shape[0], CORES * width)
    pre_act = pre_ref[...] + dot(far[:, :width], w_in_ref[width:, :])
    back_act = back_ref[...] + dot_lanes(far[:, width:], w_out_ref[:, width:])
    slope = (back_act * gelu_slope(pre_act)).astype(jnp.bfloat16)
    slope_ref[...] = slope
    sent_ref[...] = dot_lanes(slope, w_in_ref[width:, :]).astype(jnp.bfloat16)


def third_kernel(blocks, slope_ref, w_in_ref, near_ref, came_ref, kept_ref, cot_ref):
    rows = near_ref.shape[0]
    span = CORES * blocks
    levels = rows // span
    want = lax.broadcasted_iota(jnp.int32, (rows, rows), 0)
    have = lax.broadcasted_iota(jnp.int32, (rows, rows), 1)
    frame = want // blocks
    level = (frame // CORES) ^ lax.axis_index("z")
    here = frame % CORES == held_core(level)
    source = level * span + lax.axis_index("core") * blocks + want % blocks
    own = (here & (source == have)).astype(jnp.bfloat16)
    source = level * blocks + want % blocks
    others = (jnp.logical_not(here) & (source == have)).astype(jnp.bfloat16)
    others = others[:, : levels * blocks]
    cot = dot(own, near_ref[...])
    cot = cot + dot(others, came_ref[: levels * blocks, :])
    cot_ref[...] = cot.astype(jnp.bfloat16)
    width = kept_ref.shape[1]
    kept_ref[...] = dot_lanes(slope_ref[...], w_in_ref[:width, :])


def sum_kernel(kept_ref, came_ref, out_ref):
    total = kept_ref[...] + came_ref[...].astype(jnp.float32)
    out_ref[...] = total.astype(jnp.bfloat16).reshape(out_ref.shape)


def backward_kernel(
    spread_ref, back_ref, cot_ref, probs_ref, query_ref, key_ref, value_ref,
    grad_query_hbm, grad_key_hbm, grad_value_hbm,
    grad_query_ref, grad_key_ref, grad_value_ref, sems,
):
    frames, blocks, features = grad_query_ref.shape
    rows = frames * blocks
    scaling = (features // HEADS) ** (-0.5)
    query, key, value = query_ref[...], key_ref[...], value_ref[...]
    back = back_ref[...].reshape(-1, back_ref.shape[2])
    added = jnp.concatenate([dot(spread_ref[c], back) for c in range(CORES)], axis=1)
    stream = (cot_ref[...].astype(jnp.float32) + added).astype(jnp.bfloat16)
    probs = probs_ref[...]
    weights = probs.astype(jnp.bfloat16)
    copies = []

    def put(ref, hbm, parts):
        joined = jnp.concatenate(parts, axis=1).astype(jnp.bfloat16)
        ref[...] = joined.reshape(frames, blocks, features)
        copy = pltpu.make_async_copy(ref, hbm, sems.at[len(copies)])
        copy.start()
        copies.append(copy)

    put(
        grad_value_ref,
        grad_value_hbm,
        [dot(w, g) for w, g in zip(heads_of(weights), heads_of(stream))],
    )
    grad_prob = jnp.concatenate(
        [dot_lanes(v, g) for v, g in zip(heads_of(value), heads_of(stream))], axis=1
    )
    centre = over_frames(probs * grad_prob, jnp.add, blocks)
    grad_score = probs * (grad_prob - centre)
    turned = grad_score.T.astype(jnp.bfloat16)
    grad_score = grad_score.astype(jnp.bfloat16)
    put(
        grad_key_ref,
        grad_key_hbm,
        [dot(s, q) * scaling for s, q in zip(heads_of(grad_score), heads_of(query))],
    )
    put(
        grad_query_ref,
        grad_query_hbm,
        [dot(turned[h * rows : (h + 1) * rows], k) * scaling for h, k in enumerate(heads_of(key))],
    )
    for copy in copies:
        copy.wait()


def call(kernel, outs, operands, places, scratch=(), results="v"):
    spaces = {
        "v": pl.BlockSpec(memory_space=pltpu.VMEM),
        "h": pl.BlockSpec(memory_space=pl.ANY),
    }
    return pl.pallas_call(
        kernel,
        out_shape=[jax.ShapeDtypeStruct(shape, dtype) for shape, dtype in outs],
        in_specs=[spaces[place] for place in places],
        out_specs=[spaces[results]] * len(outs),
        scratch_shapes=list(scratch),
        compiler_params=pltpu.CompilerParams(vmem_limit_bytes=32 * 1024 * 1024),
    )(*[
        pltpu.with_memory_space_constraint(operand, pltpu.HBM) if place == "h" else operand
        for operand, place in zip(operands, places)
    ])


def body(query_in, key_in, value_in, cotangent, w_in, w_out, gate_probs, chosen):
    bf16, f32 = jnp.bfloat16, jnp.float32
    frames, blocks, features = query_in.shape
    groups = lax.axis_size("grp")
    levels = lax.axis_size("z")
    columns = levels * CORES
    experts = gate_probs.shape[0]
    devices = groups * columns
    share = devices // experts
    rows = frames * blocks
    slots = experts * MOST
    part = features // CORES
    hidden = w_in.shape[2]
    everyone = ("grp", "z", "core")

    def swap(values):
        return lax.ppermute(values, "core", [(i, i ^ 1) for i in range(CORES)])

    def across(values, step):
        pairs = [(i, i ^ (CORES * step) ^ 1) for i in range(columns)]
        return lax.ppermute(values, ("z", "core"), pairs)

    span = CORES * blocks
    parts = call(
        functools.partial(turn_kernel, span),
        [((span, features), bf16)] * levels,
        [cotangent],
        "h",
        [pltpu.VMEM(cotangent.shape, bf16), pltpu.SemaphoreType.DMA],
    )
    order = [0] + [i ^ (i >> 1) for i in range(levels - 1, 0, -1)]
    parts = [across(parts[k], k) if k else parts[k] for k in order]
    query, key, value, w_in_near, w_out_near, probs, picked, take, weight, spread = call(
        functools.partial(forward_kernel, blocks * devices, share),
        [
            *[((rows, features), bf16)] * 3,
            (w_in.shape[1:], bf16),
            (w_out.shape[1:], bf16),
            ((rows, HEADS * rows), f32),
            ((slots, features), bf16),
            ((CORES * slots + levels * blocks, rows), f32),
            ((CORES * slots, LANES), f32),
            ((CORES, rows, devices * MOST), bf16),
        ],
        [chosen, gate_probs, query_in, key_in, value_in, w_in, w_out],
        "hhhhhhh",
        [
            pltpu.VMEM(chosen.shape, jnp.int32),
            pltpu.VMEM(gate_probs.shape, f32),
            *[pltpu.VMEM(query_in.shape, bf16)] * 3,
            pltpu.SemaphoreType.DMA((5 + 2 * CORES,)),
        ],
    )
    cot_near, mine, sent = call(
        functools.partial(pick_kernel, order),
        [((rows, features), bf16), ((slots, features), bf16), ((levels * blocks + slots, features), bf16)],
        [take, weight, *parts],
        "vv" + "v" * levels,
    )
    came_near = swap(sent)
    (outgoing,) = call(
        functools.partial(pack_kernel, share),
        [((devices, MOST, 2 * part), bf16)],
        [picked, mine, came_near],
        "vvv",
    )
    held = lax.all_to_all(outgoing, everyone, split_axis=0, concat_axis=0, tiled=True)
    other = swap(held)
    acts = (devices * MOST, hidden)
    halves = (devices * MOST, part)
    pre_act, back_act = call(
        first_kernel, [(acts, f32), (acts, f32)], [held, w_in_near, w_out_near], "vvv"
    )
    slope, sent = call(
        second_kernel,
        [(acts, bf16), (halves, bf16)],
        [other, pre_act, back_act, w_in_near, w_out_near],
        "vvvvv",
    )
    came = swap(sent)
    kept, cot = call(
        functools.partial(third_kernel, blocks),
        [(halves, f32), ((rows, features), bf16)],
        [slope, w_in_near, cot_near, came_near],
        "vvvv",
    )
    (total,) = call(sum_kernel, [((devices, MOST, part), bf16)], [kept, came], "vv")
    back = lax.all_to_all(total, everyone, split_axis=0, concat_axis=0, tiled=True)
    return call(
        backward_kernel,
        [((frames, blocks, features), bf16)] * 3,
        [spread, back, cot, probs, query, key, value],
        "vvvvvvv",
        [pltpu.VMEM((frames, blocks, features), bf16)] * 3 + [pltpu.SemaphoreType.DMA((3,))],
        "h",
    )


def solution(mesh):
    groups, columns = mesh.devices.shape
    split = Mesh(mesh.devices.reshape(groups, columns // CORES, CORES), ("grp", "z", "core"))
    frm = ("z", "core")
    patches = P(None, ("grp",) + frm, None)
    return jax.shard_map(
        body,
        mesh=split,
        in_specs=(
            patches, patches, patches, P(frm, "grp", None), P("grp", None, frm),
            P("grp", frm, None), P(), P(),
        ),
        out_specs=(patches, patches, patches),
        check_vma=False,
    )
```

```python
import functools

import jax
import jax.numpy as jnp
from jax import lax
from jax.experimental import pallas as pl
from jax.experimental.pallas import tpu as pltpu
from jax.sharding import Mesh
from jax.sharding import PartitionSpec as P

HEADS = 16
MOST = 2
CORES = 2
SUBLANES = 8
LANES = 128

root_half = 0.7071067811865476
inv_root_tau = 0.3989422804014327

LANES_BOTH = (((1,), (1,)), ((), ()))
FIRST_BOTH = (((0,), (0,)), ((), ()))


def gelu_slope(pre_act):
    normal_cdf = 0.5 * (1.0 + lax.erf(pre_act * root_half))
    density = jnp.exp(-0.5 * pre_act * pre_act) * inv_root_tau
    return normal_cdf + pre_act * density


def dot(a, b):
    return jnp.dot(a, b, preferred_element_type=jnp.float32)


def dot_lanes(a, b):
    return lax.dot_general(a, b, LANES_BOTH, preferred_element_type=jnp.float32)


def over_frames(values, op, blocks):
    rows = values.shape[0]
    total = values[:SUBLANES]
    for start in range(SUBLANES, rows, SUBLANES):
        total = op(total, values[start : start + SUBLANES])
    step = blocks
    while step < SUBLANES:
        total = op(total, pltpu.roll(total, step, 0))
        step *= 2
    return jnp.concatenate([total] * (rows // SUBLANES), axis=0)


def heads_of(values):
    width = values.shape[1] // HEADS
    return [values[:, h * width : (h + 1) * width] for h in range(HEADS)]


def turn_kernel(span, cot_hbm, *refs):
    *part_refs, cot_ref, sem = refs
    copy = pltpu.make_async_copy(cot_hbm, cot_ref, sem)
    copy.start()
    rows = cot_ref.shape[1]
    want = lax.broadcasted_iota(jnp.int32, (rows, rows), 0)
    have = lax.broadcasted_iota(jnp.int32, (rows, rows), 1)
    source = ((want // span) ^ lax.axis_index("z")) * span + want % span
    order = (source == have).astype(jnp.bfloat16)
    copy.wait()
    turned = dot(order, cot_ref[0]).astype(jnp.bfloat16)
    for k, part_ref in enumerate(part_refs):
        part_ref[...] = turned[k * span : (k + 1) * span]


def held_core(level):
    core = lax.axis_index("core")
    return jnp.where(level == 0, core, 1 - core)


def forward_kernel(
    patches_all, share,
    chosen_hbm, gate_hbm, query_hbm, key_hbm, value_hbm, w_in_hbm, w_out_hbm,
    query_rows_ref, key_rows_ref, value_rows_ref, w_in_ref, w_out_ref,
    probs_ref, picked_ref, take_ref, weight_ref, spread_ref,
    chosen_ref, gate_ref, query_ref, key_ref, value_ref, sems,
):
    core = lax.axis_index("core")
    chip = lax.axis_index("grp") * lax.axis_size("z") + lax.axis_index("z")
    part = w_in_ref.shape[0] // CORES
    sources = [chosen_hbm, gate_hbm, query_hbm, key_hbm, value_hbm]
    targets = [chosen_ref, gate_ref, query_ref, key_ref, value_ref]
    for i in range(CORES):
        sources.append(w_in_hbm.at[0, part_of(core ^ i, part)])
        targets.append(w_in_ref.at[pl.ds(i * part, part)])
        sources.append(w_out_hbm.at[0, :, part_of(core ^ i, part)])
        targets.append(w_out_ref.at[:, pl.ds(i * part, part)])
    copies = [
        pltpu.make_async_copy(source, target, sems.at[i])
        for i, (source, target) in enumerate(zip(sources, targets))
    ]
    for copy in copies:
        copy.start()
    frames, blocks, features = query_ref.shape
    rows = frames * blocks
    scaling = (features // HEADS) ** (-0.5)

    for copy in copies[:2]:
        copy.wait()
    experts, cap = chosen_ref.shape
    before = (
        lax.broadcasted_iota(jnp.int32, (cap, cap), 0)
        < lax.broadcasted_iota(jnp.int32, (cap, cap), 1)
    ).astype(jnp.bfloat16)
    slot = lax.broadcasted_iota(jnp.int32, (SUBLANES, cap), 0)
    row_at = lax.broadcasted_iota(jnp.int32, (rows, cap), 0)
    span = CORES * blocks
    slots = experts * MOST
    found = []
    for e in range(experts):
        tokens = chosen_ref[e : e + 1, :]
        gates = gate_ref[e : e + 1, :]
        patch = tokens % patches_all
        frame = tokens // patches_all
        level = (frame // CORES) ^ lax.axis_index("z")
        for i in range(CORES):
            owned = patch // blocks == chip * CORES + (core ^ i)
            owned = jnp.broadcast_to(owned.astype(jnp.float32), slot.shape)
            rank = dot(owned.astype(jnp.bfloat16), before)
            taken = jnp.where((rank == slot.astype(jnp.float32)) & (owned > 0.0), 1.0, 0.0)
            weight = jnp.sum(taken * gates, axis=1, keepdims=True)
            taken = taken.astype(jnp.bfloat16)
            place = jnp.where(
                frame % CORES == held_core(level),
                level * span + (core ^ i) * blocks + patch % blocks,
                -1,
            )
            at = slice(i * slots + e * MOST, i * slots + (e + 1) * MOST)
            take_ref[at] = dot_lanes(taken, (row_at == place).astype(jnp.bfloat16))[:MOST]
            weight_ref[at] = jnp.broadcast_to(weight[:MOST], (MOST, weight_ref.shape[1]))
            if i == 0:
                position = frame * blocks + patch % blocks
                found.append(dot_lanes(taken, (row_at == position).astype(jnp.bfloat16))[:MOST])
    levels = rows // span
    want = lax.broadcasted_iota(jnp.int32, (levels * blocks, rows), 0)
    have = lax.broadcasted_iota(jnp.int32, (levels * blocks, rows), 1)
    source = (want // blocks) * span + (core ^ 1) * blocks + want % blocks
    take_ref[CORES * slots :] = (source == have).astype(jnp.float32)
    here = jnp.concatenate(found, axis=0).astype(jnp.bfloat16)
    _, _, returns = spread_ref.shape
    slot_at = lax.broadcasted_iota(jnp.int32, (experts * MOST, returns), 0)
    back_at = lax.broadcasted_iota(jnp.int32, (experts * MOST, returns), 1)
    sender = back_at // MOST
    same = (sender // share == slot_at // MOST) & (back_at % MOST == slot_at % MOST)
    for c in range(CORES):
        spread_ref[c] = lax.dot_general(
            here,
            (same & (sender % CORES == c)).astype(jnp.bfloat16),
            FIRST_BOTH,
            preferred_element_type=jnp.float32,
        ).astype(jnp.bfloat16)

    for copy in copies[2:5]:
        copy.wait()
    query = query_ref[...].reshape(rows, features)
    key = key_ref[...].reshape(rows, features)
    value = value_ref[...].reshape(rows, features)
    query_rows_ref[...] = query
    key_rows_ref[...] = key
    value_rows_ref[...] = value
    scores = jnp.concatenate(
        [dot_lanes(k, q) for k, q in zip(heads_of(key), heads_of(query))], axis=1
    )
    scores = scores * scaling
    raised = jnp.exp(scores - over_frames(scores, jnp.maximum, blocks))
    probs = raised / over_frames(raised, jnp.add, blocks)
    patch_in = lax.broadcasted_iota(jnp.int32, probs.shape, 0) % blocks
    patch_out = lax.broadcasted_iota(jnp.int32, probs.shape, 1) % blocks
    probs = jnp.where(patch_in == patch_out, probs, 0.0)
    probs_ref[...] = probs
    weights = probs.T.astype(jnp.bfloat16)
    mixed = jnp.concatenate(
        [dot(weights[h * rows : (h + 1) * rows], v) for h, v in enumerate(heads_of(value))],
        axis=1,
    ).astype(jnp.bfloat16)
    picked_ref[...] = dot(here, mixed).astype(jnp.bfloat16)
    for copy in copies[5:]:
        copy.wait()


def pick_kernel(order, take_ref, weight_ref, *refs):
    *part_refs, cot_ref, mine_ref, sent_ref = refs
    parts = [part_refs[order.index(k)][...] for k in range(len(order))]
    cot = jnp.concatenate(parts, axis=0)
    cot_ref[...] = cot
    slots = mine_ref.shape[0]
    rows = dot(take_ref[...].astype(jnp.bfloat16), cot)
    picks = (rows[: CORES * slots] * weight_ref[:, :1]).astype(jnp.bfloat16)
    mine_ref[...] = picks[:slots]
    away = rows[CORES * slots :].astype(jnp.bfloat16)
    sent_ref[...] = jnp.concatenate([away, picks[slots:]], axis=0)


def pack_kernel(share, picked_ref, mine_ref, came_ref, out_ref):
    slots, features = mine_ref.shape
    rows = mine_ref[...] + came_ref[came_ref.shape[0] - slots :, :]
    part = features // CORES
    picked = picked_ref[...]
    both = [
        jnp.concatenate(
            [half[:, c * part : (c + 1) * part] for half in (picked, rows)], axis=1
        )
        for c in range(CORES)
    ]
    for e in range(out_ref.shape[0] // share):
        for i in range(share):
            out_ref[e * share + i] = both[i % CORES][e * MOST : (e + 1) * MOST]


def part_of(part, width):
    return pl.ds(pl.multiple_of(part * width, width), width)


def first_kernel(near_ref, w_in_ref, w_out_ref, pre_ref, back_ref):
    width = w_in_ref.shape[0] // CORES
    rows = near_ref[...].reshape(pre_ref.shape[0], CORES * width)
    pre_ref[...] = dot(rows[:, :width], w_in_ref[:width, :])
    back_ref[...] = dot_lanes(rows[:, width:], w_out_ref[:, :width])


def second_kernel(far_ref, pre_ref, back_ref, w_in_ref, w_out_ref, slope_ref, sent_ref):
    width = w_in_ref.shape[0] // CORES
    far = far_ref[...].reshape(pre_ref.shape[0], CORES * width)
    pre_act = pre_ref[...] + dot(far[:, :width], w_in_ref[width:, :])
    back_act = back_ref[...] + dot_lanes(far[:, width:], w_out_ref[:, width:])
    slope = (back_act * gelu_slope(pre_act)).astype(jnp.bfloat16)
    slope_ref[...] = slope
    sent_ref[...] = dot_lanes(slope, w_in_ref[width:, :]).astype(jnp.bfloat16)


def third_kernel(blocks, slope_ref, w_in_ref, near_ref, came_ref, kept_ref, cot_ref):
    rows = near_ref.shape[0]
    span = CORES * blocks
    levels = rows // span
    want = lax.broadcasted_iota(jnp.int32, (rows, rows), 0)
    have = lax.broadcasted_iota(jnp.int32, (rows, rows), 1)
    frame = want // blocks
    level = (frame // CORES) ^ lax.axis_index("z")
    here = frame % CORES == held_core(level)
    source = level * span + lax.axis_index("core") * blocks + want % blocks
    own = (here & (source == have)).astype(jnp.bfloat16)
    source = level * blocks + want % blocks
    others = (jnp.logical_not(here) & (source == have)).astype(jnp.bfloat16)
    others = others[:, : levels * blocks]
    cot = dot(own, near_ref[...])
    cot = cot + dot(others, came_ref[: levels * blocks, :])
    cot_ref[...] = cot.astype(jnp.bfloat16)
    width = kept_ref.shape[1]
    kept_ref[...] = dot_lanes(slope_ref[...], w_in_ref[:width, :])


def sum_kernel(kept_ref, came_ref, out_ref):
    total = kept_ref[...] + came_ref[...].astype(jnp.float32)
    out_ref[...] = total.astype(jnp.bfloat16).reshape(out_ref.shape)


def backward_kernel(
    spread_ref, back_ref, cot_ref, probs_ref, query_ref, key_ref, value_ref,
    grad_query_hbm, grad_key_hbm, grad_value_hbm,
    grad_query_ref, grad_key_ref, grad_value_ref, sems,
):
    frames, blocks, features = grad_query_ref.shape
    rows = frames * blocks
    scaling = (features // HEADS) ** (-0.5)
    query, key, value = query_ref[...], key_ref[...], value_ref[...]
    back = back_ref[...].reshape(-1, back_ref.shape[2])
    added = jnp.concatenate([dot(spread_ref[c], back) for c in range(CORES)], axis=1)
    stream = (cot_ref[...].astype(jnp.float32) + added).astype(jnp.bfloat16)
    probs = probs_ref[...]
    weights = probs.astype(jnp.bfloat16)
    copies = []

    def put(ref, hbm, parts):
        joined = jnp.concatenate(parts, axis=1).astype(jnp.bfloat16)
        ref[...] = joined.reshape(frames, blocks, features)
        copy = pltpu.make_async_copy(ref, hbm, sems.at[len(copies)])
        copy.start()
        copies.append(copy)

    put(
        grad_value_ref,
        grad_value_hbm,
        [dot(w, g) for w, g in zip(heads_of(weights), heads_of(stream))],
    )
    grad_prob = jnp.concatenate(
        [dot_lanes(v, g) for v, g in zip(heads_of(value), heads_of(stream))], axis=1
    )
    centre = over_frames(probs * grad_prob, jnp.add, blocks)
    grad_score = probs * (grad_prob - centre)
    turned = grad_score.T.astype(jnp.bfloat16)
    grad_score = grad_score.astype(jnp.bfloat16)
    put(
        grad_key_ref,
        grad_key_hbm,
        [dot(s, q) * scaling for s, q in zip(heads_of(grad_score), heads_of(query))],
    )
    put(
        grad_query_ref,
        grad_query_hbm,
        [dot(turned[h * rows : (h + 1) * rows], k) * scaling for h, k in enumerate(heads_of(key))],
    )
    for copy in copies:
        copy.wait()


def call(kernel, outs, operands, places, scratch=(), results="v"):
    spaces = {
        "v": pl.BlockSpec(memory_space=pltpu.VMEM),
        "h": pl.BlockSpec(memory_space=pl.ANY),
    }
    return pl.pallas_call(
        kernel,
        out_shape=[jax.ShapeDtypeStruct(shape, dtype) for shape, dtype in outs],
        in_specs=[spaces[place] for place in places],
        out_specs=[spaces[results]] * len(outs),
        scratch_shapes=list(scratch),
        compiler_params=pltpu.CompilerParams(vmem_limit_bytes=32 * 1024 * 1024),
    )(*[
        pltpu.with_memory_space_constraint(operand, pltpu.HBM) if place == "h" else operand
        for operand, place in zip(operands, places)
    ])


def body(query_in, key_in, value_in, cotangent, w_in, w_out, gate_probs, chosen):
    bf16, f32 = jnp.bfloat16, jnp.float32
    frames, blocks, features = query_in.shape
    groups = lax.axis_size("grp")
    levels = lax.axis_size("z")
    columns = levels * CORES
    experts = gate_probs.shape[0]
    devices = groups * columns
    share = devices // experts
    rows = frames * blocks
    slots = experts * MOST
    part = features // CORES
    hidden = w_in.shape[2]
    everyone = ("grp", "z", "core")

    def swap(values):
        return lax.ppermute(values, "core", [(i, i ^ 1) for i in range(CORES)])

    def across(values, step):
        pairs = [(i, i ^ (CORES * step) ^ 1) for i in range(columns)]
        return lax.ppermute(values, ("z", "core"), pairs)

    span = CORES * blocks
    parts = call(
        functools.partial(turn_kernel, span),
        [((span, features), bf16)] * levels,
        [cotangent],
        "h",
        [pltpu.VMEM(cotangent.shape, bf16), pltpu.SemaphoreType.DMA],
    )
    order = [0] + [i ^ (i >> 1) for i in range(1, levels)]
    parts = [across(parts[k], k) if k else parts[k] for k in order]
    query, key, value, w_in_near, w_out_near, probs, picked, take, weight, spread = call(
        functools.partial(forward_kernel, blocks * devices, share),
        [
            *[((rows, features), bf16)] * 3,
            (w_in.shape[1:], bf16),
            (w_out.shape[1:], bf16),
            ((rows, HEADS * rows), f32),
            ((slots, features), bf16),
            ((CORES * slots + levels * blocks, rows), f32),
            ((CORES * slots, LANES), f32),
            ((CORES, rows, devices * MOST), bf16),
        ],
        [chosen, gate_probs, query_in, key_in, value_in, w_in, w_out],
        "hhhhhhh",
        [
            pltpu.VMEM(chosen.shape, jnp.int32),
            pltpu.VMEM(gate_probs.shape, f32),
            *[pltpu.VMEM(query_in.shape, bf16)] * 3,
            pltpu.SemaphoreType.DMA((5 + 2 * CORES,)),
        ],
    )
    cot_near, mine, sent = call(
        functools.partial(pick_kernel, order),
        [((rows, features), bf16), ((slots, features), bf16), ((levels * blocks + slots, features), bf16)],
        [take, weight, *parts],
        "vv" + "v" * levels,
    )
    came_near = swap(sent)
    (outgoing,) = call(
        functools.partial(pack_kernel, share),
        [((devices, MOST, 2 * part), bf16)],
        [picked, mine, came_near],
        "vvv",
    )
    held = lax.all_to_all(outgoing, everyone, split_axis=0, concat_axis=0, tiled=True)
    other = swap(held)
    acts = (devices * MOST, hidden)
    halves = (devices * MOST, part)
    pre_act, back_act = call(
        first_kernel, [(acts, f32), (acts, f32)], [held, w_in_near, w_out_near], "vvv"
    )
    slope, sent = call(
        second_kernel,
        [(acts, bf16), (halves, bf16)],
        [other, pre_act, back_act, w_in_near, w_out_near],
        "vvvvv",
    )
    came = swap(sent)
    kept, cot = call(
        functools.partial(third_kernel, blocks),
        [(halves, f32), ((rows, features), bf16)],
        [slope, w_in_near, cot_near, came_near],
        "vvvv",
    )
    (total,) = call(sum_kernel, [((devices, MOST, part), bf16)], [kept, came], "vv")
    back = lax.all_to_all(total, everyone, split_axis=0, concat_axis=0, tiled=True)
    return call(
        backward_kernel,
        [((frames, blocks, features), bf16)] * 3,
        [spread, back, cot, probs, query, key, value],
        "vvvvvvv",
        [pltpu.VMEM((frames, blocks, features), bf16)] * 3 + [pltpu.SemaphoreType.DMA((3,))],
        "h",
    )


def solution(mesh):
    groups, columns = mesh.devices.shape
    split = Mesh(mesh.devices.reshape(groups, columns // CORES, CORES), ("grp", "z", "core"))
    frm = ("z", "core")
    patches = P(None, ("grp",) + frm, None)
    return jax.shard_map(
        body,
        mesh=split,
        in_specs=(
            patches, patches, patches, P(frm, "grp", None), P("grp", None, frm),
            P("grp", frm, None), P(), P(),
        ),
        out_specs=(patches, patches, patches),
        check_vma=False,
    )
```

```python
import functools

import jax
import jax.numpy as jnp
from jax import lax
from jax.experimental import pallas as pl
from jax.experimental.pallas import tpu as pltpu
from jax.sharding import Mesh
from jax.sharding import PartitionSpec as P

HEADS = 16
MOST = 2
CORES = 2
SUBLANES = 8
LANES = 128
PIECE = 256

root_half = 0.7071067811865476
inv_root_tau = 0.3989422804014327

LANES_BOTH = (((1,), (1,)), ((), ()))
FIRST_BOTH = (((0,), (0,)), ((), ()))


def gelu_slope(pre_act):
    normal_cdf = 0.5 * (1.0 + lax.erf(pre_act * root_half))
    density = jnp.exp(-0.5 * pre_act * pre_act) * inv_root_tau
    return normal_cdf + pre_act * density


def dot(a, b):
    return jnp.dot(a, b, preferred_element_type=jnp.float32)


def dot_lanes(a, b):
    return lax.dot_general(a, b, LANES_BOTH, preferred_element_type=jnp.float32)


def over_frames(values, op, blocks):
    rows = values.shape[0]
    total = values[:SUBLANES]
    for start in range(SUBLANES, rows, SUBLANES):
        total = op(total, values[start : start + SUBLANES])
    step = blocks
    while step < SUBLANES:
        total = op(total, pltpu.roll(total, step, 0))
        step *= 2
    return jnp.concatenate([total] * (rows // SUBLANES), axis=0)


def heads_of(values):
    width = values.shape[1] // HEADS
    return [values[:, h * width : (h + 1) * width] for h in range(HEADS)]


def turn_kernel(span, cot_hbm, *refs):
    *part_refs, cot_ref, sem = refs
    copy = pltpu.make_async_copy(cot_hbm, cot_ref, sem)
    copy.start()
    rows = cot_ref.shape[1]
    want = lax.broadcasted_iota(jnp.int32, (rows, rows), 0)
    have = lax.broadcasted_iota(jnp.int32, (rows, rows), 1)
    source = ((want // span) ^ lax.axis_index("z")) * span + want % span
    order = (source == have).astype(jnp.bfloat16)
    copy.wait()
    turned = dot(order, cot_ref[0]).astype(jnp.bfloat16)
    for k, part_ref in enumerate(part_refs):
        part_ref[...] = turned[k * span : (k + 1) * span]


def held_core(level):
    core = lax.axis_index("core")
    return jnp.where(level == 0, core, 1 - core)


def forward_kernel(
    patches_all, share,
    chosen_hbm, gate_hbm, query_hbm, key_hbm, value_hbm, w_in_hbm, w_out_hbm,
    query_rows_ref, key_rows_ref, value_rows_ref, w_in_ref, w_out_ref,
    probs_ref, picked_ref, take_ref, weight_ref, spread_ref, join_ref,
    chosen_ref, gate_ref, query_ref, key_ref, value_ref, sems,
):
    core = lax.axis_index("core")
    chip = lax.axis_index("grp") * lax.axis_size("z") + lax.axis_index("z")
    sources = [chosen_hbm, gate_hbm, query_hbm, key_hbm, value_hbm]
    sources += [w_in_hbm.at[0], w_out_hbm.at[0]]
    targets = [chosen_ref, gate_ref, query_ref, key_ref, value_ref, w_in_ref, w_out_ref]
    copies = [
        pltpu.make_async_copy(source, target, sems.at[i])
        for i, (source, target) in enumerate(zip(sources, targets))
    ]
    for copy in copies:
        copy.start()
    frames, blocks, features = query_ref.shape
    rows = frames * blocks
    scaling = (features // HEADS) ** (-0.5)

    for copy in copies[:2]:
        copy.wait()
    experts, cap = chosen_ref.shape
    before = (
        lax.broadcasted_iota(jnp.int32, (cap, cap), 0)
        < lax.broadcasted_iota(jnp.int32, (cap, cap), 1)
    ).astype(jnp.bfloat16)
    slot = lax.broadcasted_iota(jnp.int32, (SUBLANES, cap), 0)
    row_at = lax.broadcasted_iota(jnp.int32, (rows, cap), 0)
    span = CORES * blocks
    slots = experts * MOST
    found = []
    for e in range(experts):
        tokens = chosen_ref[e : e + 1, :]
        gates = gate_ref[e : e + 1, :]
        patch = tokens % patches_all
        frame = tokens // patches_all
        level = (frame // CORES) ^ lax.axis_index("z")
        for i in range(CORES):
            owned = patch // blocks == chip * CORES + (core ^ i)
            owned = jnp.broadcast_to(owned.astype(jnp.float32), slot.shape)
            rank = dot(owned.astype(jnp.bfloat16), before)
            taken = jnp.where((rank == slot.astype(jnp.float32)) & (owned > 0.0), 1.0, 0.0)
            weight = jnp.sum(taken * gates, axis=1, keepdims=True)
            taken = taken.astype(jnp.bfloat16)
            place = jnp.where(
                frame % CORES == held_core(level),
                level * span + (core ^ i) * blocks + patch % blocks,
                -1,
            )
            at = slice(i * slots + e * MOST, i * slots + (e + 1) * MOST)
            take_ref[at] = dot_lanes(taken, (row_at == place).astype(jnp.bfloat16))[:MOST]
            weight_ref[at] = jnp.broadcast_to(weight[:MOST], (MOST, weight_ref.shape[1]))
            if i == 0:
                position = frame * blocks + patch % blocks
                found.append(dot_lanes(taken, (row_at == position).astype(jnp.bfloat16))[:MOST])
    levels = rows // span
    want = lax.broadcasted_iota(jnp.int32, (levels * blocks, rows), 0)
    have = lax.broadcasted_iota(jnp.int32, (levels * blocks, rows), 1)
    source = (want // blocks) * span + (core ^ 1) * blocks + want % blocks
    take_ref[CORES * slots :] = (source == have).astype(jnp.float32)
    here = jnp.concatenate(found, axis=0).astype(jnp.bfloat16)
    pieces = spread_ref.shape[0] // rows
    returns = spread_ref.shape[1]
    slot_at = lax.broadcasted_iota(jnp.int32, (slots, returns), 0)
    sender = lax.broadcasted_iota(jnp.int32, (slots, returns), 1) // pieces
    same = (sender // share == slot_at // MOST) & (sender % CORES == slot_at % MOST)
    back = lax.dot_general(
        here, same.astype(jnp.bfloat16), FIRST_BOTH, preferred_element_type=jnp.float32
    )
    piece = lax.broadcasted_iota(jnp.int32, (rows, returns), 1) % pieces
    for j in range(pieces):
        spread_ref[j * rows : (j + 1) * rows, :] = jnp.where(piece == j, back, 0.0).astype(
            jnp.bfloat16
        )
    want = lax.broadcasted_iota(jnp.int32, join_ref.shape, 0)
    have = lax.broadcasted_iota(jnp.int32, join_ref.shape, 1)
    frame = want // blocks
    level = (frame // CORES) ^ lax.axis_index("z")
    mine = level * span + core * blocks + want % blocks
    others = rows + level * blocks + want % blocks
    source = jnp.where(frame % CORES == held_core(level), mine, others)
    join_ref[...] = (source == have).astype(jnp.bfloat16)

    for copy in copies[2:5]:
        copy.wait()
    query = query_ref[...].reshape(rows, features)
    key = key_ref[...].reshape(rows, features)
    value = value_ref[...].reshape(rows, features)
    query_rows_ref[...] = query
    key_rows_ref[...] = key
    value_rows_ref[...] = value
    scores = jnp.concatenate(
        [dot_lanes(k, q) for k, q in zip(heads_of(key), heads_of(query))], axis=1
    )
    scores = scores * scaling
    raised = jnp.exp(scores - over_frames(scores, jnp.maximum, blocks))
    probs = raised / over_frames(raised, jnp.add, blocks)
    patch_in = lax.broadcasted_iota(jnp.int32, probs.shape, 0) % blocks
    patch_out = lax.broadcasted_iota(jnp.int32, probs.shape, 1) % blocks
    probs = jnp.where(patch_in == patch_out, probs, 0.0)
    probs_ref[...] = probs
    weights = probs.T.astype(jnp.bfloat16)
    mixed = jnp.concatenate(
        [dot(weights[h * rows : (h + 1) * rows], v) for h, v in enumerate(heads_of(value))],
        axis=1,
    ).astype(jnp.bfloat16)
    picked_ref[...] = dot(here, mixed).astype(jnp.bfloat16)
    for copy in copies[5:]:
        copy.wait()


def pick_kernel(order, take_ref, weight_ref, *refs):
    *part_refs, cot_ref, mine_ref, sent_ref = refs
    parts = [part_refs[order.index(k)][...] for k in range(len(order))]
    cot = jnp.concatenate(parts, axis=0)
    cot_ref[...] = cot
    slots = mine_ref.shape[0]
    rows = dot(take_ref[...].astype(jnp.bfloat16), cot)
    picks = (rows[: CORES * slots] * weight_ref[:, :1]).astype(jnp.bfloat16)
    mine_ref[...] = picks[:slots]
    away = rows[CORES * slots :].astype(jnp.bfloat16)
    sent_ref[...] = jnp.concatenate([away, picks[slots:]], axis=0)


def pack_kernel(share, picked_ref, mine_ref, came_ref, out_ref):
    slots, features = mine_ref.shape
    rows = mine_ref[...] + came_ref[came_ref.shape[0] - slots :, :]
    rows = [values.astype(jnp.float32) for values in (picked_ref[...], rows)]
    for e in range(out_ref.shape[0] // share):
        for m in range(MOST):
            at = e * MOST + m
            pieces = [
                values[at : at + 1, start : start + PIECE]
                for values in rows
                for start in range(0, features, PIECE)
            ]
            message = jnp.concatenate(pieces, axis=0).astype(jnp.bfloat16)
            for i in range(m, share, CORES):
                out_ref[e * share + i] = message


def expert_kernel(
    held_ref, w_in_ref, w_out_ref, w_in_far_ref, w_out_far_ref, out_ref, came_ref, sent_ref
):
    devices, count, width = held_ref.shape
    held = held_ref[...].reshape(devices * count, width).astype(jnp.float32)
    for i in range(came_ref.shape[0]):
        came_ref[i] = held[:, i * LANES : (i + 1) * LANES]

    def rows_from(first):
        parts = [
            came_ref[i, pl.ds(first + j, devices, stride=count), :]
            for j in range(count // 2)
            for i in range(came_ref.shape[0])
        ]
        return jnp.concatenate(parts, axis=1).astype(jnp.bfloat16)

    rows_in, rows_cot = rows_from(0), rows_from(count // 2)
    product = None
    for w_in, w_out in ((w_in_ref, w_out_ref), (w_in_far_ref, w_out_far_ref)):
        back_act = dot_lanes(rows_cot, w_out[...])
        slope = back_act * gelu_slope(dot(rows_in, w_in[...]))
        part = dot_lanes(slope.astype(jnp.bfloat16), w_in[...])
        product = part if product is None else product + part
    for j in range(count // 2):
        for i in range(sent_ref.shape[0]):
            start = j * width + i * LANES
            sent_ref[i, pl.ds(j, devices, stride=count // 2), :] = product[:, start : start + LANES]
    sent = jnp.concatenate([sent_ref[i] for i in range(sent_ref.shape[0])], axis=1)
    out_ref[...] = sent.astype(jnp.bfloat16).reshape(out_ref.shape)


def backward_kernel(
    spread_ref, back_ref, join_ref, cot_near_ref, came_ref, probs_ref, query_ref, key_ref, value_ref,
    grad_query_hbm, grad_key_hbm, grad_value_hbm,
    grad_query_ref, grad_key_ref, grad_value_ref, sems,
):
    frames, blocks, features = grad_query_ref.shape
    rows = frames * blocks
    scaling = (features // HEADS) ** (-0.5)
    query, key, value = query_ref[...], key_ref[...], value_ref[...]
    back = dot(spread_ref[...], back_ref[...].reshape(-1, back_ref.shape[2]))
    added = jnp.concatenate(
        [back[start : start + rows] for start in range(0, back.shape[0], rows)], axis=1
    )
    cot = jnp.concatenate([cot_near_ref[...], came_ref[: join_ref.shape[1] - rows, :]], axis=0)
    stream = (dot(join_ref[...], cot) + added).astype(jnp.bfloat16)
    probs = probs_ref[...]
    weights = probs.astype(jnp.bfloat16)
    copies = []

    def put(ref, hbm, parts):
        joined = jnp.concatenate(parts, axis=1).astype(jnp.bfloat16)
        ref[...] = joined.reshape(frames, blocks, features)
        copy = pltpu.make_async_copy(ref, hbm, sems.at[len(copies)])
        copy.start()
        copies.append(copy)

    put(
        grad_value_ref,
        grad_value_hbm,
        [dot(w, g) for w, g in zip(heads_of(weights), heads_of(stream))],
    )
    grad_prob = jnp.concatenate(
        [dot_lanes(v, g) for v, g in zip(heads_of(value), heads_of(stream))], axis=1
    )
    centre = over_frames(probs * grad_prob, jnp.add, blocks)
    grad_score = probs * (grad_prob - centre)
    turned = grad_score.T.astype(jnp.bfloat16)
    grad_score = grad_score.astype(jnp.bfloat16)
    put(
        grad_key_ref,
        grad_key_hbm,
        [dot(s, q) * scaling for s, q in zip(heads_of(grad_score), heads_of(query))],
    )
    put(
        grad_query_ref,
        grad_query_hbm,
        [dot(turned[h * rows : (h + 1) * rows], k) * scaling for h, k in enumerate(heads_of(key))],
    )
    for copy in copies:
        copy.wait()


def call(kernel, outs, operands, places, scratch=(), results="v"):
    spaces = {
        "v": pl.BlockSpec(memory_space=pltpu.VMEM),
        "h": pl.BlockSpec(memory_space=pl.ANY),
    }
    return pl.pallas_call(
        kernel,
        out_shape=[jax.ShapeDtypeStruct(shape, dtype) for shape, dtype in outs],
        in_specs=[spaces[place] for place in places],
        out_specs=[spaces[results]] * len(outs),
        scratch_shapes=list(scratch),
        compiler_params=pltpu.CompilerParams(vmem_limit_bytes=32 * 1024 * 1024),
    )(*[
        pltpu.with_memory_space_constraint(operand, pltpu.HBM) if place == "h" else operand
        for operand, place in zip(operands, places)
    ])


def body(query_in, key_in, value_in, cotangent, w_in, w_out, gate_probs, chosen):
    bf16, f32 = jnp.bfloat16, jnp.float32
    frames, blocks, features = query_in.shape
    groups = lax.axis_size("grp")
    levels = lax.axis_size("z")
    columns = levels * CORES
    experts = gate_probs.shape[0]
    devices = groups * columns
    share = devices // experts
    rows = frames * blocks
    slots = experts * MOST
    everyone = ("grp", "z", "core")

    def swap(values):
        return lax.ppermute(values, "core", [(i, i ^ 1) for i in range(CORES)])

    def across(values, step):
        pairs = [(i, i ^ (CORES * step) ^ 1) for i in range(columns)]
        return lax.ppermute(values, ("z", "core"), pairs)

    span = CORES * blocks
    parts = call(
        functools.partial(turn_kernel, span),
        [((span, features), bf16)] * levels,
        [cotangent],
        "h",
        [pltpu.VMEM(cotangent.shape, bf16), pltpu.SemaphoreType.DMA],
    )
    order = [0] + [i ^ (i >> 1) for i in range(levels - 1, 0, -1)]
    parts = [across(parts[k], k) if k else parts[k] for k in order]
    query, key, value, w_in_near, w_out_near, probs, picked, take, weight, spread, join = call(
        functools.partial(forward_kernel, blocks * devices, share),
        [
            *[((rows, features), bf16)] * 3,
            (w_in.shape[1:], bf16),
            (w_out.shape[1:], bf16),
            ((rows, HEADS * rows), f32),
            ((slots, features), bf16),
            ((CORES * slots + levels * blocks, rows), f32),
            ((CORES * slots, LANES), f32),
            ((rows * features // PIECE, devices * features // PIECE), bf16),
            ((rows, rows + levels * blocks), bf16),
        ],
        [chosen, gate_probs, query_in, key_in, value_in, w_in, w_out],
        "hhhhhhh",
        [
            pltpu.VMEM(chosen.shape, jnp.int32),
            pltpu.VMEM(gate_probs.shape, f32),
            *[pltpu.VMEM(query_in.shape, bf16)] * 3,
            pltpu.SemaphoreType.DMA((7,)),
        ],
    )
    cot_near, mine, sent = call(
        functools.partial(pick_kernel, order),
        [((rows, features), bf16), ((slots, features), bf16), ((levels * blocks + slots, features), bf16)],
        [take, weight, *parts],
        "vv" + "v" * levels,
    )
    came_near = swap(sent)
    (outgoing,) = call(
        functools.partial(pack_kernel, share),
        [((devices, 2 * features // PIECE, PIECE), bf16)],
        [picked, mine, came_near],
        "vvv",
    )
    outgoing, w_in_near, w_out_near = lax.optimization_barrier((outgoing, w_in_near, w_out_near))
    w_in_far, w_out_far = swap(w_in_near), swap(w_out_near)
    held = lax.all_to_all(outgoing, everyone, split_axis=0, concat_axis=0, tiled=True)
    (sent_back,) = call(
        expert_kernel,
        [((devices, features // PIECE, PIECE), bf16)],
        [held, w_in_near, w_out_near, w_in_far, w_out_far],
        "vvvvv",
        [
            pltpu.VMEM((PIECE // LANES, devices * 2 * features // PIECE, LANES), f32),
            pltpu.VMEM((PIECE // LANES, devices * features // PIECE, LANES), f32),
        ],
    )
    back = lax.all_to_all(sent_back, everyone, split_axis=0, concat_axis=0, tiled=True)
    return call(
        backward_kernel,
        [((frames, blocks, features), bf16)] * 3,
        [spread, back, join, cot_near, came_near, probs, query, key, value],
        "vvvvvvvvv",
        [pltpu.VMEM((frames, blocks, features), bf16)] * 3 + [pltpu.SemaphoreType.DMA((3,))],
        "h",
    )


def solution(mesh):
    groups, columns = mesh.devices.shape
    split = Mesh(mesh.devices.reshape(groups, columns // CORES, CORES), ("grp", "z", "core"))
    frm = ("z", "core")
    patches = P(None, ("grp",) + frm, None)
    return jax.shard_map(
        body,
        mesh=split,
        in_specs=(
            patches, patches, patches, P(frm, "grp", None), P("grp", None, frm),
            P("grp", frm, None), P(), P(),
        ),
        out_specs=(patches, patches, patches),
        check_vma=False,
    )
```

```python
import functools

import jax
import jax.numpy as jnp
from jax import lax
from jax.experimental import pallas as pl
from jax.experimental.pallas import tpu as pltpu
from jax.sharding import Mesh
from jax.sharding import PartitionSpec as P

HEADS = 16
MOST = 2
CORES = 2
SUBLANES = 8
LANES = 128
PIECE = 256

root_half = 0.7071067811865476
inv_root_tau = 0.3989422804014327

LANES_BOTH = (((1,), (1,)), ((), ()))
FIRST_BOTH = (((0,), (0,)), ((), ()))


def gelu_slope(pre_act):
    normal_cdf = 0.5 * (1.0 + lax.erf(pre_act * root_half))
    density = jnp.exp(-0.5 * pre_act * pre_act) * inv_root_tau
    return normal_cdf + pre_act * density


def dot(a, b):
    return jnp.dot(a, b, preferred_element_type=jnp.float32)


def dot_lanes(a, b):
    return lax.dot_general(a, b, LANES_BOTH, preferred_element_type=jnp.float32)


def over_frames(values, op, blocks):
    rows = values.shape[0]
    total = values[:SUBLANES]
    for start in range(SUBLANES, rows, SUBLANES):
        total = op(total, values[start : start + SUBLANES])
    step = blocks
    while step < SUBLANES:
        total = op(total, pltpu.roll(total, step, 0))
        step *= 2
    return jnp.concatenate([total] * (rows // SUBLANES), axis=0)


def heads_of(values):
    width = values.shape[1] // HEADS
    return [values[:, h * width : (h + 1) * width] for h in range(HEADS)]


def turn_kernel(span, cot_hbm, *refs):
    *part_refs, cot_ref, sem = refs
    copy = pltpu.make_async_copy(cot_hbm, cot_ref, sem)
    copy.start()
    level = lax.axis_index("z")
    copy.wait()
    parts = [cot_ref[0, k * span : (k + 1) * span, :] for k in range(len(part_refs))]
    bit = 1
    while bit < len(parts):
        turn = (level // bit) % 2 == 1
        parts = [jnp.where(turn, parts[k ^ bit], parts[k]) for k in range(len(parts))]
        bit *= 2
    for part_ref, part in zip(part_refs, parts):
        part_ref[...] = part


def held_core(level):
    core = lax.axis_index("core")
    return jnp.where(level == 0, core, 1 - core)


def forward_kernel(
    patches_all, share,
    chosen_hbm, gate_hbm, query_hbm, key_hbm, value_hbm, w_in_hbm, w_out_hbm,
    query_rows_ref, key_rows_ref, value_rows_ref, w_in_ref, w_out_ref,
    probs_ref, picked_ref, take_ref, weight_ref, spread_ref,
    chosen_ref, gate_ref, query_ref, key_ref, value_ref, sems,
):
    core = lax.axis_index("core")
    chip = lax.axis_index("grp") * lax.axis_size("z") + lax.axis_index("z")
    part = w_in_ref.shape[0] // CORES
    sources = [chosen_hbm, gate_hbm, query_hbm, key_hbm, value_hbm]
    targets = [chosen_ref, gate_ref, query_ref, key_ref, value_ref]
    for i in range(CORES):
        sources.append(w_in_hbm.at[0, part_of(core ^ i, part)])
        targets.append(w_in_ref.at[pl.ds(i * part, part)])
        sources.append(w_out_hbm.at[0, :, part_of(core ^ i, part)])
        targets.append(w_out_ref.at[:, pl.ds(i * part, part)])
    copies = [
        pltpu.make_async_copy(source, target, sems.at[i])
        for i, (source, target) in enumerate(zip(sources, targets))
    ]
    for copy in copies:
        copy.start()
    frames, blocks, features = query_ref.shape
    rows = frames * blocks
    scaling = (features // HEADS) ** (-0.5)

    for copy in copies[:2]:
        copy.wait()
    experts, cap = chosen_ref.shape
    before = (
        lax.broadcasted_iota(jnp.int32, (cap, cap), 0)
        < lax.broadcasted_iota(jnp.int32, (cap, cap), 1)
    ).astype(jnp.bfloat16)
    slot = lax.broadcasted_iota(jnp.int32, (SUBLANES, cap), 0)
    row_at = lax.broadcasted_iota(jnp.int32, (rows, cap), 0)
    span = CORES * blocks
    slots = experts * MOST
    found = []
    for e in range(experts):
        tokens = chosen_ref[e : e + 1, :]
        gates = gate_ref[e : e + 1, :]
        patch = tokens % patches_all
        frame = tokens // patches_all
        level = (frame // CORES) ^ lax.axis_index("z")
        for i in range(CORES):
            owned = patch // blocks == chip * CORES + (core ^ i)
            owned = jnp.broadcast_to(owned.astype(jnp.float32), slot.shape)
            rank = dot(owned.astype(jnp.bfloat16), before)
            taken = jnp.where((rank == slot.astype(jnp.float32)) & (owned > 0.0), 1.0, 0.0)
            weight = jnp.sum(taken * gates, axis=1, keepdims=True)
            taken = taken.astype(jnp.bfloat16)
            place = jnp.where(
                frame % CORES == held_core(level),
                level * span + (core ^ i) * blocks + patch % blocks,
                -1,
            )
            at = slice(i * slots + e * MOST, i * slots + (e + 1) * MOST)
            take_ref[at] = dot_lanes(taken, (row_at == place).astype(jnp.bfloat16))[:MOST]
            weight_ref[at] = jnp.broadcast_to(weight[:MOST], (MOST, weight_ref.shape[1]))
            if i == 0:
                position = frame * blocks + patch % blocks
                found.append(dot_lanes(taken, (row_at == position).astype(jnp.bfloat16))[:MOST])
    levels = rows // span
    want = lax.broadcasted_iota(jnp.int32, (levels * blocks, rows), 0)
    have = lax.broadcasted_iota(jnp.int32, (levels * blocks, rows), 1)
    source = (want // blocks) * span + (core ^ 1) * blocks + want % blocks
    take_ref[CORES * slots :] = (source == have).astype(jnp.float32)
    here = jnp.concatenate(found, axis=0).astype(jnp.bfloat16)
    pieces = spread_ref.shape[0] // (rows * CORES)
    returns = spread_ref.shape[1]
    slot_at = lax.broadcasted_iota(jnp.int32, (slots, returns), 0)
    back_at = lax.broadcasted_iota(jnp.int32, (slots, returns), 1) // pieces
    same = (back_at // MOST // share == slot_at // MOST) & (back_at % MOST == slot_at % MOST)
    back = lax.dot_general(
        here, same.astype(jnp.bfloat16), FIRST_BOTH, preferred_element_type=jnp.float32
    )
    back_at = lax.broadcasted_iota(jnp.int32, (rows, returns), 1)
    piece = back_at // (MOST * pieces) % CORES * pieces + back_at % pieces
    for j in range(CORES * pieces):
        spread_ref[j * rows : (j + 1) * rows, :] = jnp.where(piece == j, back, 0.0).astype(
            jnp.bfloat16
        )

    for copy in copies[2:5]:
        copy.wait()
    query = query_ref[...].reshape(rows, features)
    key = key_ref[...].reshape(rows, features)
    value = value_ref[...].reshape(rows, features)
    query_rows_ref[...] = query
    key_rows_ref[...] = key
    value_rows_ref[...] = value
    scores = jnp.concatenate(
        [dot_lanes(k, q) for k, q in zip(heads_of(key), heads_of(query))], axis=1
    )
    scores = scores * scaling
    raised = jnp.exp(scores - over_frames(scores, jnp.maximum, blocks))
    probs = raised / over_frames(raised, jnp.add, blocks)
    patch_in = lax.broadcasted_iota(jnp.int32, probs.shape, 0) % blocks
    patch_out = lax.broadcasted_iota(jnp.int32, probs.shape, 1) % blocks
    probs = jnp.where(patch_in == patch_out, probs, 0.0)
    probs_ref[...] = probs
    weights = probs.T.astype(jnp.bfloat16)
    mixed = jnp.concatenate(
        [dot(weights[h * rows : (h + 1) * rows], v) for h, v in enumerate(heads_of(value))],
        axis=1,
    ).astype(jnp.bfloat16)
    picked_ref[...] = dot(here, mixed).astype(jnp.bfloat16)
    for copy in copies[5:]:
        copy.wait()


def pick_kernel(order, take_ref, weight_ref, *refs):
    *part_refs, cot_ref, mine_ref, sent_ref = refs
    parts = [part_refs[order.index(k)][...] for k in range(len(order))]
    cot = jnp.concatenate(parts, axis=0)
    cot_ref[...] = cot
    slots = mine_ref.shape[0]
    rows = dot(take_ref[...].astype(jnp.bfloat16), cot)
    picks = (rows[: CORES * slots] * weight_ref[:, :1]).astype(jnp.bfloat16)
    mine_ref[...] = picks[:slots]
    away = rows[CORES * slots :].astype(jnp.bfloat16)
    sent_ref[...] = jnp.concatenate([away, picks[slots:]], axis=0)


def pack_kernel(share, picked_ref, mine_ref, came_ref, out_ref):
    slots, features = mine_ref.shape
    rows = mine_ref[...] + came_ref[came_ref.shape[0] - slots :, :]
    part = features // CORES
    picked = picked_ref[...]
    both = [
        jnp.concatenate(
            [half[:, c * part : (c + 1) * part] for half in (picked, rows)], axis=1
        )
        for c in range(CORES)
    ]
    for e in range(out_ref.shape[0] // share):
        for i in range(share):
            out_ref[e * share + i] = both[i % CORES][e * MOST : (e + 1) * MOST]


def part_of(part, width):
    return pl.ds(pl.multiple_of(part * width, width), width)


def first_kernel(near_ref, w_in_ref, w_out_ref, pre_ref, back_ref):
    width = w_in_ref.shape[0] // CORES
    rows = near_ref[...].reshape(pre_ref.shape[0], CORES * width)
    pre_ref[...] = dot(rows[:, :width], w_in_ref[:width, :])
    back_ref[...] = dot_lanes(rows[:, width:], w_out_ref[:, :width])


def second_kernel(far_ref, pre_ref, back_ref, w_in_ref, w_out_ref, slope_ref, sent_ref):
    width = w_in_ref.shape[0] // CORES
    far = far_ref[...].reshape(pre_ref.shape[0], CORES * width)
    pre_act = pre_ref[...] + dot(far[:, :width], w_in_ref[width:, :])
    back_act = back_ref[...] + dot_lanes(far[:, width:], w_out_ref[:, width:])
    slope = (back_act * gelu_slope(pre_act)).astype(jnp.bfloat16)
    slope_ref[...] = slope
    sent_ref[...] = dot_lanes(slope, w_in_ref[width:, :]).astype(jnp.bfloat16)


def third_kernel(blocks, slope_ref, w_in_ref, near_ref, came_ref, kept_ref, cot_ref):
    rows = near_ref.shape[0]
    span = CORES * blocks
    levels = rows // span
    want = lax.broadcasted_iota(jnp.int32, (rows, rows), 0)
    have = lax.broadcasted_iota(jnp.int32, (rows, rows), 1)
    frame = want // blocks
    level = (frame // CORES) ^ lax.axis_index("z")
    here = frame % CORES == held_core(level)
    source = level * span + lax.axis_index("core") * blocks + want % blocks
    own = (here & (source == have)).astype(jnp.bfloat16)
    source = level * blocks + want % blocks
    others = (jnp.logical_not(here) & (source == have)).astype(jnp.bfloat16)
    others = others[:, : levels * blocks]
    cot = dot(own, near_ref[...])
    cot = cot + dot(others, came_ref[: levels * blocks, :])
    cot_ref[...] = cot.astype(jnp.bfloat16)
    width = kept_ref.shape[1]
    kept_ref[...] = dot_lanes(slope_ref[...], w_in_ref[:width, :])


def sum_kernel(kept_ref, came_ref, out_ref, piece_ref):
    total = kept_ref[...] + came_ref[...].astype(jnp.float32)
    count, width = total.shape
    pieces = width // PIECE
    parts = piece_ref.shape[0]
    for j in range(pieces):
        for i in range(parts):
            start = j * PIECE + i * LANES
            piece_ref[i, pl.ds(j, count, stride=pieces), :] = total[:, start : start + LANES]
    total = jnp.concatenate([piece_ref[i] for i in range(parts)], axis=1)
    out_ref[...] = total.astype(jnp.bfloat16).reshape(out_ref.shape)


def backward_kernel(
    spread_ref, back_ref, cot_ref, probs_ref, query_ref, key_ref, value_ref,
    grad_query_hbm, grad_key_hbm, grad_value_hbm,
    grad_query_ref, grad_key_ref, grad_value_ref, sems,
):
    frames, blocks, features = grad_query_ref.shape
    rows = frames * blocks
    scaling = (features // HEADS) ** (-0.5)
    query, key, value = query_ref[...], key_ref[...], value_ref[...]
    back = dot(spread_ref[...], back_ref[...].reshape(-1, PIECE))
    added = jnp.concatenate(
        [back[start : start + rows] for start in range(0, back.shape[0], rows)], axis=1
    )
    stream = (cot_ref[...].astype(jnp.float32) + added).astype(jnp.bfloat16)
    probs = probs_ref[...]
    weights = probs.astype(jnp.bfloat16)
    copies = []

    def put(ref, hbm, parts):
        joined = jnp.concatenate(parts, axis=1).astype(jnp.bfloat16)
        ref[...] = joined.reshape(frames, blocks, features)
        copy = pltpu.make_async_copy(ref, hbm, sems.at[len(copies)])
        copy.start()
        copies.append(copy)

    put(
        grad_value_ref,
        grad_value_hbm,
        [dot(w, g) for w, g in zip(heads_of(weights), heads_of(stream))],
    )
    grad_prob = jnp.concatenate(
        [dot_lanes(v, g) for v, g in zip(heads_of(value), heads_of(stream))], axis=1
    )
    centre = over_frames(probs * grad_prob, jnp.add, blocks)
    grad_score = probs * (grad_prob - centre)
    turned = grad_score.T.astype(jnp.bfloat16)
    grad_score = grad_score.astype(jnp.bfloat16)
    put(
        grad_key_ref,
        grad_key_hbm,
        [dot(s, q) * scaling for s, q in zip(heads_of(grad_score), heads_of(query))],
    )
    put(
        grad_query_ref,
        grad_query_hbm,
        [dot(turned[h * rows : (h + 1) * rows], k) * scaling for h, k in enumerate(heads_of(key))],
    )
    for copy in copies:
        copy.wait()


def call(kernel, outs, operands, places, scratch=(), results="v"):
    spaces = {
        "v": pl.BlockSpec(memory_space=pltpu.VMEM),
        "h": pl.BlockSpec(memory_space=pl.ANY),
    }
    return pl.pallas_call(
        kernel,
        out_shape=[jax.ShapeDtypeStruct(shape, dtype) for shape, dtype in outs],
        in_specs=[spaces[place] for place in places],
        out_specs=[spaces[results]] * len(outs),
        scratch_shapes=list(scratch),
        compiler_params=pltpu.CompilerParams(vmem_limit_bytes=32 * 1024 * 1024),
    )(*[
        pltpu.with_memory_space_constraint(operand, pltpu.HBM) if place == "h" else operand
        for operand, place in zip(operands, places)
    ])


def body(query_in, key_in, value_in, cotangent, w_in, w_out, gate_probs, chosen):
    bf16, f32 = jnp.bfloat16, jnp.float32
    frames, blocks, features = query_in.shape
    groups = lax.axis_size("grp")
    levels = lax.axis_size("z")
    columns = levels * CORES
    experts = gate_probs.shape[0]
    devices = groups * columns
    share = devices // experts
    rows = frames * blocks
    slots = experts * MOST
    part = features // CORES
    hidden = w_in.shape[2]
    everyone = ("grp", "z", "core")

    def swap(values):
        return lax.ppermute(values, "core", [(i, i ^ 1) for i in range(CORES)])

    def across(values, step):
        pairs = [(i, i ^ (CORES * step) ^ 1) for i in range(columns)]
        return lax.ppermute(values, ("z", "core"), pairs)

    span = CORES * blocks
    parts = call(
        functools.partial(turn_kernel, span),
        [((span, features), bf16)] * levels,
        [cotangent],
        "h",
        [pltpu.VMEM(cotangent.shape, bf16), pltpu.SemaphoreType.DMA],
    )
    order = [0] + [i ^ (i >> 1) for i in range(levels - 1, 0, -1)]
    parts = [across(parts[k], k) if k else parts[k] for k in order]
    query, key, value, w_in_near, w_out_near, probs, picked, take, weight, spread = call(
        functools.partial(forward_kernel, blocks * devices, share),
        [
            *[((rows, features), bf16)] * 3,
            (w_in.shape[1:], bf16),
            (w_out.shape[1:], bf16),
            ((rows, HEADS * rows), f32),
            ((slots, features), bf16),
            ((CORES * slots + levels * blocks, rows), f32),
            ((CORES * slots, LANES), f32),
            ((rows * features // PIECE, devices * MOST * part // PIECE), bf16),
        ],
        [chosen, gate_probs, query_in, key_in, value_in, w_in, w_out],
        "hhhhhhh",
        [
            pltpu.VMEM(chosen.shape, jnp.int32),
            pltpu.VMEM(gate_probs.shape, f32),
            *[pltpu.VMEM(query_in.shape, bf16)] * 3,
            pltpu.SemaphoreType.DMA((5 + 2 * CORES,)),
        ],
    )
    cot_near, mine, sent = call(
        functools.partial(pick_kernel, order),
        [((rows, features), bf16), ((slots, features), bf16), ((levels * blocks + slots, features), bf16)],
        [take, weight, *parts],
        "vv" + "v" * levels,
    )
    came_near = swap(sent)
    (outgoing,) = call(
        functools.partial(pack_kernel, share),
        [((devices, MOST, 2 * part), bf16)],
        [picked, mine, came_near],
        "vvv",
    )
    held = lax.all_to_all(outgoing, everyone, split_axis=0, concat_axis=0, tiled=True)
    other = swap(held)
    acts = (devices * MOST, hidden)
    halves = (devices * MOST, part)
    pre_act, back_act = call(
        first_kernel, [(acts, f32), (acts, f32)], [held, w_in_near, w_out_near], "vvv"
    )
    slope, sent = call(
        second_kernel,
        [(acts, bf16), (halves, bf16)],
        [other, pre_act, back_act, w_in_near, w_out_near],
        "vvvvv",
    )
    came = swap(sent)
    kept, cot = call(
        functools.partial(third_kernel, blocks),
        [(halves, f32), ((rows, features), bf16)],
        [slope, w_in_near, cot_near, came_near],
        "vvvv",
    )
    pieces = MOST * part // PIECE
    (total,) = call(
        sum_kernel,
        [((devices, pieces, PIECE), bf16)],
        [kept, came],
        "vv",
        [pltpu.VMEM((PIECE // LANES, devices * pieces, LANES), f32)],
    )
    back = lax.all_to_all(total, everyone, split_axis=0, concat_axis=0, tiled=True)
    return call(
        backward_kernel,
        [((frames, blocks, features), bf16)] * 3,
        [spread, back, cot, probs, query, key, value],
        "vvvvvvv",
        [pltpu.VMEM((frames, blocks, features), bf16)] * 3 + [pltpu.SemaphoreType.DMA((3,))],
        "h",
    )


def solution(mesh):
    groups, columns = mesh.devices.shape
    split = Mesh(mesh.devices.reshape(groups, columns // CORES, CORES), ("grp", "z", "core"))
    frm = ("z", "core")
    patches = P(None, ("grp",) + frm, None)
    return jax.shard_map(
        body,
        mesh=split,
        in_specs=(
            patches, patches, patches, P(frm, "grp", None), P("grp", None, frm),
            P("grp", frm, None), P(), P(),
        ),
        out_specs=(patches, patches, patches),
        check_vma=False,
    )
```

```python
import functools

import jax
import jax.numpy as jnp
from jax import lax
from jax.experimental import pallas as pl
from jax.experimental.pallas import tpu as pltpu
from jax.sharding import Mesh
from jax.sharding import PartitionSpec as P

HEADS = 16
MOST = 2
CORES = 2
SUBLANES = 8
LANES = 128
PIECE = 256

root_half = 0.7071067811865476
inv_root_tau = 0.3989422804014327

LANES_BOTH = (((1,), (1,)), ((), ()))
FIRST_BOTH = (((0,), (0,)), ((), ()))


def gelu_slope(pre_act):
    normal_cdf = 0.5 * (1.0 + lax.erf(pre_act * root_half))
    density = jnp.exp(-0.5 * pre_act * pre_act) * inv_root_tau
    return normal_cdf + pre_act * density


def dot(a, b):
    return jnp.dot(a, b, preferred_element_type=jnp.float32)


def dot_lanes(a, b):
    return lax.dot_general(a, b, LANES_BOTH, preferred_element_type=jnp.float32)


def over_frames(values, op, blocks):
    rows = values.shape[0]
    total = values[:SUBLANES]
    for start in range(SUBLANES, rows, SUBLANES):
        total = op(total, values[start : start + SUBLANES])
    step = blocks
    while step < SUBLANES:
        total = op(total, pltpu.roll(total, step, 0))
        step *= 2
    return jnp.concatenate([total] * (rows // SUBLANES), axis=0)


def heads_of(values):
    width = values.shape[1] // HEADS
    return [values[:, h * width : (h + 1) * width] for h in range(HEADS)]


def turn_kernel(blocks, cot_hbm, *refs):
    *part_refs, cot_ref, sem = refs
    copy = pltpu.make_async_copy(cot_hbm, cot_ref, sem)
    copy.start()
    column = lax.axis_index("z") * CORES + lax.axis_index("core")
    copy.wait()
    parts = [cot_ref[0, k * blocks : (k + 1) * blocks, :] for k in range(len(part_refs))]
    bit = 1
    while bit < len(parts):
        turn = (column // bit) % 2 == 1
        parts = [jnp.where(turn, parts[k ^ bit], parts[k]) for k in range(len(parts))]
        bit *= 2
    for part_ref, part in zip(part_refs, parts):
        part_ref[...] = part


def forward_kernel(
    patches_all, share,
    chosen_hbm, gate_hbm, query_hbm, key_hbm, value_hbm, w_in_hbm, w_out_hbm,
    query_rows_ref, key_rows_ref, value_rows_ref, w_in_ref, w_out_ref,
    probs_ref, picked_ref, take_ref, weight_ref, spread_ref,
    chosen_ref, gate_ref, query_ref, key_ref, value_ref, sems,
):
    core = lax.axis_index("core")
    chip = lax.axis_index("grp") * lax.axis_size("z") + lax.axis_index("z")
    part = w_in_ref.shape[0] // CORES
    sources = [chosen_hbm, gate_hbm, query_hbm, key_hbm, value_hbm]
    targets = [chosen_ref, gate_ref, query_ref, key_ref, value_ref]
    for i in range(CORES):
        sources.append(w_in_hbm.at[0, part_of(core ^ i, part)])
        targets.append(w_in_ref.at[pl.ds(i * part, part)])
        sources.append(w_out_hbm.at[0, :, part_of(core ^ i, part)])
        targets.append(w_out_ref.at[:, pl.ds(i * part, part)])
    copies = [
        pltpu.make_async_copy(source, target, sems.at[i])
        for i, (source, target) in enumerate(zip(sources, targets))
    ]
    for copy in copies:
        copy.start()
    frames, blocks, features = query_ref.shape
    rows = frames * blocks
    scaling = (features // HEADS) ** (-0.5)

    for copy in copies[:2]:
        copy.wait()
    experts, cap = chosen_ref.shape
    before = (
        lax.broadcasted_iota(jnp.int32, (cap, cap), 0)
        < lax.broadcasted_iota(jnp.int32, (cap, cap), 1)
    ).astype(jnp.bfloat16)
    slot = lax.broadcasted_iota(jnp.int32, (SUBLANES, cap), 0)
    row_at = lax.broadcasted_iota(jnp.int32, (rows, cap), 0)
    column = lax.axis_index("z") * CORES + core
    slots = experts * MOST
    found = []
    for e in range(experts):
        tokens = chosen_ref[e : e + 1, :]
        gates = gate_ref[e : e + 1, :]
        patch = tokens % patches_all
        frame = tokens // patches_all
        owned = patch // blocks == chip * CORES + core
        owned = jnp.broadcast_to(owned.astype(jnp.float32), slot.shape)
        rank = dot(owned.astype(jnp.bfloat16), before)
        taken = jnp.where((rank == slot.astype(jnp.float32)) & (owned > 0.0), 1.0, 0.0)
        weight = jnp.sum(taken * gates, axis=1, keepdims=True)
        taken = taken.astype(jnp.bfloat16)
        at = slice(e * MOST, (e + 1) * MOST)
        place = (frame ^ column) * blocks + patch % blocks
        take_ref[at] = dot_lanes(taken, (row_at == place).astype(jnp.bfloat16))[:MOST]
        weight_ref[at] = jnp.broadcast_to(weight[:MOST], (MOST, weight_ref.shape[1]))
        position = frame * blocks + patch % blocks
        found.append(dot_lanes(taken, (row_at == position).astype(jnp.bfloat16))[:MOST])
    here = jnp.concatenate(found, axis=0).astype(jnp.bfloat16)
    pieces = spread_ref.shape[0] // (rows * CORES)
    returns = spread_ref.shape[1]
    slot_at = lax.broadcasted_iota(jnp.int32, (slots, returns), 0)
    back_at = lax.broadcasted_iota(jnp.int32, (slots, returns), 1) // pieces
    same = (back_at // MOST // share == slot_at // MOST) & (back_at % MOST == slot_at % MOST)
    back = lax.dot_general(
        here, same.astype(jnp.bfloat16), FIRST_BOTH, preferred_element_type=jnp.float32
    )
    back_at = lax.broadcasted_iota(jnp.int32, (rows, returns), 1)
    piece = back_at // (MOST * pieces) % CORES * pieces + back_at % pieces
    for j in range(CORES * pieces):
        spread_ref[j * rows : (j + 1) * rows, :] = jnp.where(piece == j, back, 0.0).astype(
            jnp.bfloat16
        )

    for copy in copies[2:5]:
        copy.wait()
    query = query_ref[...].reshape(rows, features)
    key = key_ref[...].reshape(rows, features)
    value = value_ref[...].reshape(rows, features)
    query_rows_ref[...] = query
    key_rows_ref[...] = key
    value_rows_ref[...] = value
    scores = jnp.concatenate(
        [dot_lanes(k, q) for k, q in zip(heads_of(key), heads_of(query))], axis=1
    )
    scores = scores * scaling
    raised = jnp.exp(scores - over_frames(scores, jnp.maximum, blocks))
    probs = raised / over_frames(raised, jnp.add, blocks)
    patch_in = lax.broadcasted_iota(jnp.int32, probs.shape, 0) % blocks
    patch_out = lax.broadcasted_iota(jnp.int32, probs.shape, 1) % blocks
    probs = jnp.where(patch_in == patch_out, probs, 0.0)
    probs_ref[...] = probs
    weights = probs.T.astype(jnp.bfloat16)
    mixed = jnp.concatenate(
        [dot(weights[h * rows : (h + 1) * rows], v) for h, v in enumerate(heads_of(value))],
        axis=1,
    ).astype(jnp.bfloat16)
    picked_ref[...] = dot(here, mixed).astype(jnp.bfloat16)
    for copy in copies[5:]:
        copy.wait()


def pick_kernel(share, order, take_ref, weight_ref, picked_ref, *refs):
    *part_refs, cot_ref, out_ref = refs
    parts = [part_refs[order.index(k)][...] for k in range(len(order))]
    cot = jnp.concatenate(parts, axis=0)
    cot_ref[...] = cot
    rows = dot(take_ref[...].astype(jnp.bfloat16), cot)
    rows = (rows * weight_ref[:, :1]).astype(jnp.bfloat16)
    part = rows.shape[1] // CORES
    picked = picked_ref[...]
    both = [
        jnp.concatenate(
            [half[:, c * part : (c + 1) * part] for half in (picked, rows)], axis=1
        )
        for c in range(CORES)
    ]
    for e in range(out_ref.shape[0] // share):
        for i in range(share):
            out_ref[e * share + i] = both[i % CORES][e * MOST : (e + 1) * MOST]


def part_of(part, width):
    return pl.ds(pl.multiple_of(part * width, width), width)


def first_kernel(near_ref, w_in_ref, w_out_ref, pre_ref, back_ref):
    width = w_in_ref.shape[0] // CORES
    rows = near_ref[...].reshape(pre_ref.shape[0], CORES * width)
    pre_ref[...] = dot(rows[:, :width], w_in_ref[:width, :])
    back_ref[...] = dot_lanes(rows[:, width:], w_out_ref[:, :width])


def second_kernel(far_ref, pre_ref, back_ref, w_in_ref, w_out_ref, slope_ref, sent_ref):
    width = w_in_ref.shape[0] // CORES
    far = far_ref[...].reshape(pre_ref.shape[0], CORES * width)
    pre_act = pre_ref[...] + dot(far[:, :width], w_in_ref[width:, :])
    back_act = back_ref[...] + dot_lanes(far[:, width:], w_out_ref[:, width:])
    slope = (back_act * gelu_slope(pre_act)).astype(jnp.bfloat16)
    slope_ref[...] = slope
    sent_ref[...] = dot_lanes(slope, w_in_ref[width:, :]).astype(jnp.bfloat16)


def third_kernel(blocks, slope_ref, w_in_ref, near_ref, kept_ref, cot_ref):
    rows = near_ref.shape[0]
    want = lax.broadcasted_iota(jnp.int32, (rows, rows), 0)
    have = lax.broadcasted_iota(jnp.int32, (rows, rows), 1)
    column = lax.axis_index("z") * CORES + lax.axis_index("core")
    source = ((want // blocks) ^ column) * blocks + want % blocks
    cot = dot((source == have).astype(jnp.bfloat16), near_ref[...])
    cot_ref[...] = cot.astype(jnp.bfloat16)
    width = kept_ref.shape[1]
    kept_ref[...] = dot_lanes(slope_ref[...], w_in_ref[:width, :])


def sum_kernel(kept_ref, came_ref, out_ref, piece_ref):
    total = kept_ref[...] + came_ref[...].astype(jnp.float32)
    count, width = total.shape
    pieces = width // PIECE
    parts = piece_ref.shape[0]
    for j in range(pieces):
        for i in range(parts):
            start = j * PIECE + i * LANES
            piece_ref[i, pl.ds(j, count, stride=pieces), :] = total[:, start : start + LANES]
    total = jnp.concatenate([piece_ref[i] for i in range(parts)], axis=1)
    out_ref[...] = total.astype(jnp.bfloat16).reshape(out_ref.shape)


def backward_kernel(
    spread_ref, back_ref, cot_ref, probs_ref, query_ref, key_ref, value_ref,
    grad_query_hbm, grad_key_hbm, grad_value_hbm,
    grad_query_ref, grad_key_ref, grad_value_ref, sems,
):
    frames, blocks, features = grad_query_ref.shape
    rows = frames * blocks
    scaling = (features // HEADS) ** (-0.5)
    query, key, value = query_ref[...], key_ref[...], value_ref[...]
    back = dot(spread_ref[...], back_ref[...].reshape(-1, PIECE))
    added = jnp.concatenate(
        [back[start : start + rows] for start in range(0, back.shape[0], rows)], axis=1
    )
    stream = (cot_ref[...].astype(jnp.float32) + added).astype(jnp.bfloat16)
    probs = probs_ref[...]
    weights = probs.astype(jnp.bfloat16)
    copies = []

    def put(ref, hbm, parts):
        joined = jnp.concatenate(parts, axis=1).astype(jnp.bfloat16)
        ref[...] = joined.reshape(frames, blocks, features)
        copy = pltpu.make_async_copy(ref, hbm, sems.at[len(copies)])
        copy.start()
        copies.append(copy)

    put(
        grad_value_ref,
        grad_value_hbm,
        [dot(w, g) for w, g in zip(heads_of(weights), heads_of(stream))],
    )
    grad_prob = jnp.concatenate(
        [dot_lanes(v, g) for v, g in zip(heads_of(value), heads_of(stream))], axis=1
    )
    centre = over_frames(probs * grad_prob, jnp.add, blocks)
    grad_score = probs * (grad_prob - centre)
    turned = grad_score.T.astype(jnp.bfloat16)
    grad_score = grad_score.astype(jnp.bfloat16)
    put(
        grad_key_ref,
        grad_key_hbm,
        [dot(s, q) * scaling for s, q in zip(heads_of(grad_score), heads_of(query))],
    )
    put(
        grad_query_ref,
        grad_query_hbm,
        [dot(turned[h * rows : (h + 1) * rows], k) * scaling for h, k in enumerate(heads_of(key))],
    )
    for copy in copies:
        copy.wait()


def call(kernel, outs, operands, places, scratch=(), results="v"):
    spaces = {
        "v": pl.BlockSpec(memory_space=pltpu.VMEM),
        "h": pl.BlockSpec(memory_space=pl.ANY),
    }
    return pl.pallas_call(
        kernel,
        out_shape=[jax.ShapeDtypeStruct(shape, dtype) for shape, dtype in outs],
        in_specs=[spaces[place] for place in places],
        out_specs=[spaces[results]] * len(outs),
        scratch_shapes=list(scratch),
        compiler_params=pltpu.CompilerParams(vmem_limit_bytes=32 * 1024 * 1024),
    )(*[
        pltpu.with_memory_space_constraint(operand, pltpu.HBM) if place == "h" else operand
        for operand, place in zip(operands, places)
    ])


def body(query_in, key_in, value_in, cotangent, w_in, w_out, gate_probs, chosen):
    bf16, f32 = jnp.bfloat16, jnp.float32
    frames, blocks, features = query_in.shape
    groups = lax.axis_size("grp")
    levels = lax.axis_size("z")
    columns = levels * CORES
    experts = gate_probs.shape[0]
    devices = groups * columns
    share = devices // experts
    rows = frames * blocks
    slots = experts * MOST
    part = features // CORES
    hidden = w_in.shape[2]
    everyone = ("grp", "z", "core")

    def swap(values):
        return lax.ppermute(values, "core", [(i, i ^ 1) for i in range(CORES)])

    def across(values, step):
        pairs = [(i, i ^ step) for i in range(columns)]
        return lax.ppermute(values, ("z", "core"), pairs)

    parts = call(
        functools.partial(turn_kernel, blocks),
        [((blocks, features), bf16)] * columns,
        [cotangent],
        "h",
        [pltpu.VMEM(cotangent.shape, bf16), pltpu.SemaphoreType.DMA],
    )
    order = [i ^ (i >> 1) for i in range(levels - 1, 0, -1)]
    order = [0] + [CORES * k + c for k in order for c in (1, 0)] + [1]
    parts = [across(parts[k], k) if k else parts[k] for k in order]
    query, key, value, w_in_near, w_out_near, probs, picked, take, weight, spread = call(
        functools.partial(forward_kernel, blocks * devices, share),
        [
            *[((rows, features), bf16)] * 3,
            (w_in.shape[1:], bf16),
            (w_out.shape[1:], bf16),
            ((rows, HEADS * rows), f32),
            ((slots, features), bf16),
            ((slots, rows), f32),
            ((slots, LANES), f32),
            ((rows * features // PIECE, devices * MOST * part // PIECE), bf16),
        ],
        [chosen, gate_probs, query_in, key_in, value_in, w_in, w_out],
        "hhhhhhh",
        [
            pltpu.VMEM(chosen.shape, jnp.int32),
            pltpu.VMEM(gate_probs.shape, f32),
            *[pltpu.VMEM(query_in.shape, bf16)] * 3,
            pltpu.SemaphoreType.DMA((5 + 2 * CORES,)),
        ],
    )
    cot_near, outgoing = call(
        functools.partial(pick_kernel, share, order),
        [((rows, features), bf16), ((devices, MOST, 2 * part), bf16)],
        [take, weight, picked, *parts],
        "vvv" + "v" * columns,
    )
    held = lax.all_to_all(outgoing, everyone, split_axis=0, concat_axis=0, tiled=True)
    other = swap(held)
    acts = (devices * MOST, hidden)
    halves = (devices * MOST, part)
    pre_act, back_act = call(
        first_kernel, [(acts, f32), (acts, f32)], [held, w_in_near, w_out_near], "vvv"
    )
    slope, sent = call(
        second_kernel,
        [(acts, bf16), (halves, bf16)],
        [other, pre_act, back_act, w_in_near, w_out_near],
        "vvvvv",
    )
    came = swap(sent)
    kept, cot = call(
        functools.partial(third_kernel, blocks),
        [(halves, f32), ((rows, features), bf16)],
        [slope, w_in_near, cot_near],
        "vvv",
    )
    pieces = MOST * part // PIECE
    (total,) = call(
        sum_kernel,
        [((devices, pieces, PIECE), bf16)],
        [kept, came],
        "vv",
        [pltpu.VMEM((PIECE // LANES, devices * pieces, LANES), f32)],
    )
    back = lax.all_to_all(total, everyone, split_axis=0, concat_axis=0, tiled=True)
    return call(
        backward_kernel,
        [((frames, blocks, features), bf16)] * 3,
        [spread, back, cot, probs, query, key, value],
        "vvvvvvv",
        [pltpu.VMEM((frames, blocks, features), bf16)] * 3 + [pltpu.SemaphoreType.DMA((3,))],
        "h",
    )


def solution(mesh):
    groups, columns = mesh.devices.shape
    split = Mesh(mesh.devices.reshape(groups, columns // CORES, CORES), ("grp", "z", "core"))
    frm = ("z", "core")
    patches = P(None, ("grp",) + frm, None)
    return jax.shard_map(
        body,
        mesh=split,
        in_specs=(
            patches, patches, patches, P(frm, "grp", None), P("grp", None, frm),
            P("grp", frm, None), P(), P(),
        ),
        out_specs=(patches, patches, patches),
        check_vma=False,
    )
```

```python
import functools

import jax
import jax.numpy as jnp
from jax import lax
from jax.experimental import pallas as pl
from jax.experimental.pallas import tpu as pltpu
from jax.sharding import Mesh
from jax.sharding import PartitionSpec as P

HEADS = 16
MOST = 2
CORES = 2
SUBLANES = 8
LANES = 128
PIECE = 256

root_half = 0.7071067811865476
inv_root_tau = 0.3989422804014327

LANES_BOTH = (((1,), (1,)), ((), ()))
FIRST_BOTH = (((0,), (0,)), ((), ()))


def gelu_slope(pre_act):
    normal_cdf = 0.5 * (1.0 + lax.erf(pre_act * root_half))
    density = jnp.exp(-0.5 * pre_act * pre_act) * inv_root_tau
    return normal_cdf + pre_act * density


def dot(a, b):
    return jnp.dot(a, b, preferred_element_type=jnp.float32)


def dot_lanes(a, b):
    return lax.dot_general(a, b, LANES_BOTH, preferred_element_type=jnp.float32)


def over_frames(values, op, blocks):
    rows = values.shape[0]
    total = values[:SUBLANES]
    for start in range(SUBLANES, rows, SUBLANES):
        total = op(total, values[start : start + SUBLANES])
    step = blocks
    while step < SUBLANES:
        total = op(total, pltpu.roll(total, step, 0))
        step *= 2
    return jnp.concatenate([total] * (rows // SUBLANES), axis=0)


def heads_of(values):
    width = values.shape[1] // HEADS
    return [values[:, h * width : (h + 1) * width] for h in range(HEADS)]


def turn_kernel(span, cot_hbm, *refs):
    *part_refs, cot_ref, sem = refs
    copy = pltpu.make_async_copy(cot_hbm, cot_ref, sem)
    copy.start()
    level = lax.axis_index("z")
    copy.wait()
    parts = [cot_ref[0, k * span : (k + 1) * span, :] for k in range(len(part_refs))]
    bit = 1
    while bit < len(parts):
        turn = (level // bit) % 2 == 1
        parts = [jnp.where(turn, parts[k ^ bit], parts[k]) for k in range(len(parts))]
        bit *= 2
    for part_ref, part in zip(part_refs, parts):
        part_ref[...] = part


def held_core(level):
    core = lax.axis_index("core")
    return jnp.where(level == 0, core, 1 - core)


def forward_kernel(
    patches_all, share,
    chosen_hbm, gate_hbm, query_hbm, key_hbm, value_hbm, w_in_hbm, w_out_hbm,
    query_rows_ref, key_rows_ref, value_rows_ref, w_in_ref, w_out_ref,
    probs_ref, picked_ref, take_ref, weight_ref, spread_ref,
    chosen_ref, gate_ref, query_ref, key_ref, value_ref, sems,
):
    core = lax.axis_index("core")
    chip = lax.axis_index("grp") * lax.axis_size("z") + lax.axis_index("z")
    part = w_in_ref.shape[0] // CORES
    sources = [chosen_hbm, gate_hbm, query_hbm, key_hbm, value_hbm]
    targets = [chosen_ref, gate_ref, query_ref, key_ref, value_ref]
    for i in range(CORES):
        sources.append(w_in_hbm.at[0, part_of(core ^ i, part)])
        targets.append(w_in_ref.at[pl.ds(i * part, part)])
        sources.append(w_out_hbm.at[0, :, part_of(core ^ i, part)])
        targets.append(w_out_ref.at[:, pl.ds(i * part, part)])
    copies = [
        pltpu.make_async_copy(source, target, sems.at[i])
        for i, (source, target) in enumerate(zip(sources, targets))
    ]
    for copy in copies:
        copy.start()
    frames, blocks, features = query_ref.shape
    rows = frames * blocks
    scaling = (features // HEADS) ** (-0.5)

    for copy in copies[:2]:
        copy.wait()
    experts, cap = chosen_ref.shape
    before = (
        lax.broadcasted_iota(jnp.int32, (cap, cap), 0)
        < lax.broadcasted_iota(jnp.int32, (cap, cap), 1)
    ).astype(jnp.bfloat16)
    slot = lax.broadcasted_iota(jnp.int32, (SUBLANES, cap), 0)
    row_at = lax.broadcasted_iota(jnp.int32, (rows, cap), 0)
    span = CORES * blocks
    slots = experts * MOST
    found = []
    for e in range(experts):
        tokens = chosen_ref[e : e + 1, :]
        gates = gate_ref[e : e + 1, :]
        patch = tokens % patches_all
        frame = tokens // patches_all
        level = (frame // CORES) ^ lax.axis_index("z")
        for i in range(CORES):
            owned = patch // blocks == chip * CORES + (core ^ i)
            owned = jnp.broadcast_to(owned.astype(jnp.float32), slot.shape)
            rank = dot(owned.astype(jnp.bfloat16), before)
            taken = jnp.where((rank == slot.astype(jnp.float32)) & (owned > 0.0), 1.0, 0.0)
            weight = jnp.sum(taken * gates, axis=1, keepdims=True)
            taken = taken.astype(jnp.bfloat16)
            place = jnp.where(
                frame % CORES == held_core(level),
                level * span + (core ^ i) * blocks + patch % blocks,
                -1,
            )
            at = slice(i * slots + e * MOST, i * slots + (e + 1) * MOST)
            take_ref[at] = dot_lanes(taken, (row_at == place).astype(jnp.bfloat16))[:MOST]
            weight_ref[at] = jnp.broadcast_to(weight[:MOST], (MOST, weight_ref.shape[1]))
            if i == 0:
                position = frame * blocks + patch % blocks
                found.append(dot_lanes(taken, (row_at == position).astype(jnp.bfloat16))[:MOST])
    levels = rows // span
    want = lax.broadcasted_iota(jnp.int32, (levels * blocks, rows), 0)
    have = lax.broadcasted_iota(jnp.int32, (levels * blocks, rows), 1)
    source = (want // blocks) * span + (core ^ 1) * blocks + want % blocks
    take_ref[CORES * slots :] = (source == have).astype(jnp.float32)
    here = jnp.concatenate(found, axis=0).astype(jnp.bfloat16)
    pieces = spread_ref.shape[0] // (rows * CORES)
    returns = spread_ref.shape[1]
    slot_at = lax.broadcasted_iota(jnp.int32, (slots, returns), 0)
    back_at = lax.broadcasted_iota(jnp.int32, (slots, returns), 1) // pieces
    same = (back_at // MOST // share == slot_at // MOST) & (back_at % MOST == slot_at % MOST)
    back = lax.dot_general(
        here, same.astype(jnp.bfloat16), FIRST_BOTH, preferred_element_type=jnp.float32
    )
    back_at = lax.broadcasted_iota(jnp.int32, (rows, returns), 1)
    piece = back_at // (MOST * pieces) % CORES * pieces + back_at % pieces
    for j in range(CORES * pieces):
        spread_ref[j * rows : (j + 1) * rows, :] = jnp.where(piece == j, back, 0.0).astype(
            jnp.bfloat16
        )

    for copy in copies[2:5]:
        copy.wait()
    query = query_ref[...].reshape(rows, features)
    key = key_ref[...].reshape(rows, features)
    value = value_ref[...].reshape(rows, features)
    query_rows_ref[...] = query
    key_rows_ref[...] = key
    value_rows_ref[...] = value
    scores = jnp.concatenate(
        [dot_lanes(k, q) for k, q in zip(heads_of(key), heads_of(query))], axis=1
    )
    scores = scores * scaling
    raised = jnp.exp(scores - over_frames(scores, jnp.maximum, blocks))
    probs = raised / over_frames(raised, jnp.add, blocks)
    patch_in = lax.broadcasted_iota(jnp.int32, probs.shape, 0) % blocks
    patch_out = lax.broadcasted_iota(jnp.int32, probs.shape, 1) % blocks
    probs = jnp.where(patch_in == patch_out, probs, 0.0)
    probs_ref[...] = probs
    weights = probs.T.astype(jnp.bfloat16)
    mixed = jnp.concatenate(
        [dot(weights[h * rows : (h + 1) * rows], v) for h, v in enumerate(heads_of(value))],
        axis=1,
    ).astype(jnp.bfloat16)
    picked_ref[...] = dot(here, mixed).astype(jnp.bfloat16)
    for copy in copies[5:]:
        copy.wait()


def pick_kernel(order, take_ref, weight_ref, *refs):
    *part_refs, cot_ref, mine_ref, sent_ref = refs
    parts = [part_refs[order.index(k)][...] for k in range(len(order))]
    cot = jnp.concatenate(parts, axis=0)
    cot_ref[...] = cot
    slots = mine_ref.shape[0]
    rows = dot(take_ref[...].astype(jnp.bfloat16), cot)
    picks = (rows[: CORES * slots] * weight_ref[:, :1]).astype(jnp.bfloat16)
    mine_ref[...] = picks[:slots]
    away = rows[CORES * slots :].astype(jnp.bfloat16)
    sent_ref[...] = jnp.concatenate([away, picks[slots:]], axis=0)


def pack_kernel(share, picked_ref, mine_ref, came_ref, out_ref):
    slots, features = mine_ref.shape
    rows = mine_ref[...] + came_ref[came_ref.shape[0] - slots :, :]
    part = features // CORES
    picked = picked_ref[...]
    both = [
        jnp.concatenate(
            [half[:, c * part : (c + 1) * part] for half in (picked, rows)], axis=1
        )
        for c in range(CORES)
    ]
    for e in range(out_ref.shape[0] // share):
        for i in range(share):
            out_ref[e * share + i] = both[i % CORES][e * MOST : (e + 1) * MOST]


def part_of(part, width):
    return pl.ds(pl.multiple_of(part * width, width), width)


def first_kernel(near_ref, w_in_ref, w_out_ref, pre_ref, back_ref):
    width = w_in_ref.shape[0] // CORES
    rows = near_ref[...].reshape(pre_ref.shape[0], CORES * width)
    pre_ref[...] = dot(rows[:, :width], w_in_ref[:width, :])
    back_ref[...] = dot_lanes(rows[:, width:], w_out_ref[:, :width])


def second_kernel(far_ref, pre_ref, back_ref, w_in_ref, w_out_ref, slope_ref, sent_ref):
    width = w_in_ref.shape[0] // CORES
    far = far_ref[...].reshape(pre_ref.shape[0], CORES * width)
    pre_act = pre_ref[...] + dot(far[:, :width], w_in_ref[width:, :])
    back_act = back_ref[...] + dot_lanes(far[:, width:], w_out_ref[:, width:])
    slope = (back_act * gelu_slope(pre_act)).astype(jnp.bfloat16)
    slope_ref[...] = slope
    sent_ref[...] = dot_lanes(slope, w_in_ref[width:, :]).astype(jnp.bfloat16)


def third_kernel(blocks, slope_ref, w_in_ref, near_ref, came_ref, kept_ref, cot_ref):
    rows = near_ref.shape[0]
    span = CORES * blocks
    levels = rows // span
    want = lax.broadcasted_iota(jnp.int32, (rows, rows), 0)
    have = lax.broadcasted_iota(jnp.int32, (rows, rows), 1)
    frame = want // blocks
    level = (frame // CORES) ^ lax.axis_index("z")
    here = frame % CORES == held_core(level)
    source = level * span + lax.axis_index("core") * blocks + want % blocks
    own = (here & (source == have)).astype(jnp.bfloat16)
    source = level * blocks + want % blocks
    others = (jnp.logical_not(here) & (source == have)).astype(jnp.bfloat16)
    others = others[:, : levels * blocks]
    cot = dot(own, near_ref[...])
    cot = cot + dot(others, came_ref[: levels * blocks, :])
    cot_ref[...] = cot.astype(jnp.bfloat16)
    width = kept_ref.shape[1]
    kept_ref[...] = dot_lanes(slope_ref[...], w_in_ref[:width, :])


def sum_kernel(kept_ref, came_ref, out_ref, piece_ref):
    total = kept_ref[...] + came_ref[...].astype(jnp.float32)
    count, width = total.shape
    pieces = width // PIECE
    parts = piece_ref.shape[0]
    for j in range(pieces):
        for i in range(parts):
            start = j * PIECE + i * LANES
            piece_ref[i, pl.ds(j, count, stride=pieces), :] = total[:, start : start + LANES]
    total = jnp.concatenate([piece_ref[i] for i in range(parts)], axis=1)
    out_ref[...] = total.astype(jnp.bfloat16).reshape(out_ref.shape)


def backward_kernel(
    spread_ref, back_ref, cot_ref, probs_ref, query_ref, key_ref, value_ref,
    grad_query_hbm, grad_key_hbm, grad_value_hbm,
    grad_query_ref, grad_key_ref, grad_value_ref, sems,
):
    frames, blocks, features = grad_query_ref.shape
    rows = frames * blocks
    scaling = (features // HEADS) ** (-0.5)
    query, key, value = query_ref[...], key_ref[...], value_ref[...]
    back = dot(spread_ref[...], back_ref[...].reshape(-1, PIECE))
    added = jnp.concatenate(
        [back[start : start + rows] for start in range(0, back.shape[0], rows)], axis=1
    )
    stream = (cot_ref[...].astype(jnp.float32) + added).astype(jnp.bfloat16)
    probs = probs_ref[...]
    weights = probs.astype(jnp.bfloat16)
    copies = []

    def put(ref, hbm, parts):
        joined = jnp.concatenate(parts, axis=1).astype(jnp.bfloat16)
        ref[...] = joined.reshape(frames, blocks, features)
        copy = pltpu.make_async_copy(ref, hbm, sems.at[len(copies)])
        copy.start()
        copies.append(copy)

    grad_prob = jnp.concatenate(
        [dot_lanes(v, g) for v, g in zip(heads_of(value), heads_of(stream))], axis=1
    )
    put(
        grad_value_ref,
        grad_value_hbm,
        [dot(w, g) for w, g in zip(heads_of(weights), heads_of(stream))],
    )
    centre = over_frames(probs * grad_prob, jnp.add, blocks)
    grad_score = probs * (grad_prob - centre)
    turned = grad_score.T.astype(jnp.bfloat16)
    grad_score = grad_score.astype(jnp.bfloat16)
    put(
        grad_key_ref,
        grad_key_hbm,
        [dot(s, q) * scaling for s, q in zip(heads_of(grad_score), heads_of(query))],
    )
    put(
        grad_query_ref,
        grad_query_hbm,
        [dot(turned[h * rows : (h + 1) * rows], k) * scaling for h, k in enumerate(heads_of(key))],
    )
    for copy in copies:
        copy.wait()


def call(kernel, outs, operands, places, scratch=(), results="v"):
    spaces = {
        "v": pl.BlockSpec(memory_space=pltpu.VMEM),
        "h": pl.BlockSpec(memory_space=pl.ANY),
    }
    return pl.pallas_call(
        kernel,
        out_shape=[jax.ShapeDtypeStruct(shape, dtype) for shape, dtype in outs],
        in_specs=[spaces[place] for place in places],
        out_specs=[spaces[results]] * len(outs),
        scratch_shapes=list(scratch),
        compiler_params=pltpu.CompilerParams(vmem_limit_bytes=32 * 1024 * 1024),
    )(*[
        pltpu.with_memory_space_constraint(operand, pltpu.HBM) if place == "h" else operand
        for operand, place in zip(operands, places)
    ])


def body(query_in, key_in, value_in, cotangent, w_in, w_out, gate_probs, chosen):
    bf16, f32 = jnp.bfloat16, jnp.float32
    frames, blocks, features = query_in.shape
    groups = lax.axis_size("grp")
    levels = lax.axis_size("z")
    columns = levels * CORES
    experts = gate_probs.shape[0]
    devices = groups * columns
    share = devices // experts
    rows = frames * blocks
    slots = experts * MOST
    part = features // CORES
    hidden = w_in.shape[2]
    everyone = ("grp", "z", "core")

    def swap(values):
        return lax.ppermute(values, "core", [(i, i ^ 1) for i in range(CORES)])

    def across(values, step):
        pairs = [(i, i ^ (CORES * step) ^ 1) for i in range(columns)]
        return lax.ppermute(values, ("z", "core"), pairs)

    span = CORES * blocks
    parts = call(
        functools.partial(turn_kernel, span),
        [((span, features), bf16)] * levels,
        [cotangent],
        "h",
        [pltpu.VMEM(cotangent.shape, bf16), pltpu.SemaphoreType.DMA],
    )
    order = [0] + [i ^ (i >> 1) for i in range(levels - 1, 0, -1)]
    parts = [across(parts[k], k) if k else parts[k] for k in order]
    query, key, value, w_in_near, w_out_near, probs, picked, take, weight, spread = call(
        functools.partial(forward_kernel, blocks * devices, share),
        [
            *[((rows, features), bf16)] * 3,
            (w_in.shape[1:], bf16),
            (w_out.shape[1:], bf16),
            ((rows, HEADS * rows), f32),
            ((slots, features), bf16),
            ((CORES * slots + levels * blocks, rows), f32),
            ((CORES * slots, LANES), f32),
            ((rows * features // PIECE, devices * MOST * part // PIECE), bf16),
        ],
        [chosen, gate_probs, query_in, key_in, value_in, w_in, w_out],
        "hhhhhhh",
        [
            pltpu.VMEM(chosen.shape, jnp.int32),
            pltpu.VMEM(gate_probs.shape, f32),
            *[pltpu.VMEM(query_in.shape, bf16)] * 3,
            pltpu.SemaphoreType.DMA((5 + 2 * CORES,)),
        ],
    )
    cot_near, mine, sent = call(
        functools.partial(pick_kernel, order),
        [((rows, features), bf16), ((slots, features), bf16), ((levels * blocks + slots, features), bf16)],
        [take, weight, *parts],
        "vv" + "v" * levels,
    )
    came_near = swap(sent)
    (outgoing,) = call(
        functools.partial(pack_kernel, share),
        [((devices, MOST, 2 * part), bf16)],
        [picked, mine, came_near],
        "vvv",
    )
    held = lax.all_to_all(outgoing, everyone, split_axis=0, concat_axis=0, tiled=True)
    other = swap(held)
    acts = (devices * MOST, hidden)
    halves = (devices * MOST, part)
    pre_act, back_act = call(
        first_kernel, [(acts, f32), (acts, f32)], [held, w_in_near, w_out_near], "vvv"
    )
    slope, sent = call(
        second_kernel,
        [(acts, bf16), (halves, bf16)],
        [other, pre_act, back_act, w_in_near, w_out_near],
        "vvvvv",
    )
    came = swap(sent)
    kept, cot = call(
        functools.partial(third_kernel, blocks),
        [(halves, f32), ((rows, features), bf16)],
        [slope, w_in_near, cot_near, came_near],
        "vvvv",
    )
    pieces = MOST * part // PIECE
    (total,) = call(
        sum_kernel,
        [((devices, pieces, PIECE), bf16)],
        [kept, came],
        "vv",
        [pltpu.VMEM((PIECE // LANES, devices * pieces, LANES), f32)],
    )
    back = lax.all_to_all(total, everyone, split_axis=0, concat_axis=0, tiled=True)
    return call(
        backward_kernel,
        [((frames, blocks, features), bf16)] * 3,
        [spread, back, cot, probs, query, key, value],
        "vvvvvvv",
        [pltpu.VMEM((frames, blocks, features), bf16)] * 3 + [pltpu.SemaphoreType.DMA((3,))],
        "h",
    )


def solution(mesh):
    groups, columns = mesh.devices.shape
    split = Mesh(mesh.devices.reshape(groups, columns // CORES, CORES), ("grp", "z", "core"))
    frm = ("z", "core")
    patches = P(None, ("grp",) + frm, None)
    return jax.shard_map(
        body,
        mesh=split,
        in_specs=(
            patches, patches, patches, P(frm, "grp", None), P("grp", None, frm),
            P("grp", frm, None), P(), P(),
        ),
        out_specs=(patches, patches, patches),
        check_vma=False,
    )
```

```python
import functools

import jax
import jax.numpy as jnp
from jax import lax
from jax.experimental import pallas as pl
from jax.experimental.pallas import tpu as pltpu
from jax.sharding import Mesh
from jax.sharding import PartitionSpec as P

HEADS = 16
MOST = 2
CORES = 2
SUBLANES = 8
LANES = 128
PIECE = 256

root_half = 0.7071067811865476
inv_root_tau = 0.3989422804014327

LANES_BOTH = (((1,), (1,)), ((), ()))
FIRST_BOTH = (((0,), (0,)), ((), ()))


def gelu_slope(pre_act):
    normal_cdf = 0.5 * (1.0 + lax.erf(pre_act * root_half))
    density = jnp.exp(-0.5 * pre_act * pre_act) * inv_root_tau
    return normal_cdf + pre_act * density


def dot(a, b):
    return jnp.dot(a, b, preferred_element_type=jnp.float32)


def dot_lanes(a, b):
    return lax.dot_general(a, b, LANES_BOTH, preferred_element_type=jnp.float32)


def over_frames(values, op, blocks):
    rows = values.shape[0]
    total = values[:SUBLANES]
    for start in range(SUBLANES, rows, SUBLANES):
        total = op(total, values[start : start + SUBLANES])
    step = blocks
    while step < SUBLANES:
        total = op(total, pltpu.roll(total, step, 0))
        step *= 2
    return jnp.concatenate([total] * (rows // SUBLANES), axis=0)


def heads_of(values):
    width = values.shape[1] // HEADS
    return [values[:, h * width : (h + 1) * width] for h in range(HEADS)]


def turn_kernel(span, cot_hbm, *refs):
    *part_refs, cot_ref, sem = refs
    copy = pltpu.make_async_copy(cot_hbm, cot_ref, sem)
    copy.start()
    level = lax.axis_index("z")
    copy.wait()
    parts = [cot_ref[0, k * span : (k + 1) * span, :] for k in range(len(part_refs))]
    bit = 1
    while bit < len(parts):
        turn = (level // bit) % 2 == 1
        parts = [jnp.where(turn, parts[k ^ bit], parts[k]) for k in range(len(parts))]
        bit *= 2
    for part_ref, part in zip(part_refs, parts):
        part_ref[...] = part


def held_core(level):
    core = lax.axis_index("core")
    return jnp.where(level == 0, core, 1 - core)


def forward_kernel(
    patches_all, share,
    chosen_hbm, gate_hbm, query_hbm, key_hbm, value_hbm, w_in_hbm, w_out_hbm,
    query_rows_ref, key_rows_ref, value_rows_ref, w_in_ref, w_out_ref,
    probs_ref, picked_ref, take_ref, weight_ref, spread_ref,
    chosen_ref, gate_ref, query_ref, key_ref, value_ref, sems,
):
    core = lax.axis_index("core")
    chip = lax.axis_index("grp") * lax.axis_size("z") + lax.axis_index("z")
    part = w_in_ref.shape[0] // CORES
    sources = [chosen_hbm, gate_hbm, query_hbm, key_hbm, value_hbm]
    targets = [chosen_ref, gate_ref, query_ref, key_ref, value_ref]
    for i in range(CORES):
        sources.append(w_in_hbm.at[0, part_of(core ^ i, part)])
        targets.append(w_in_ref.at[pl.ds(i * part, part)])
        sources.append(w_out_hbm.at[0, :, part_of(core ^ i, part)])
        targets.append(w_out_ref.at[:, pl.ds(i * part, part)])
    copies = [
        pltpu.make_async_copy(source, target, sems.at[i])
        for i, (source, target) in enumerate(zip(sources, targets))
    ]
    for copy in copies:
        copy.start()
    frames, blocks, features = query_ref.shape
    rows = frames * blocks
    scaling = (features // HEADS) ** (-0.5)

    for copy in copies[:2]:
        copy.wait()
    experts, cap = chosen_ref.shape
    before = (
        lax.broadcasted_iota(jnp.int32, (cap, cap), 0)
        < lax.broadcasted_iota(jnp.int32, (cap, cap), 1)
    ).astype(jnp.bfloat16)
    slot = lax.broadcasted_iota(jnp.int32, (SUBLANES, cap), 0)
    row_at = lax.broadcasted_iota(jnp.int32, (rows, cap), 0)
    span = CORES * blocks
    slots = experts * MOST
    found = []
    for e in range(experts):
        tokens = chosen_ref[e : e + 1, :]
        gates = gate_ref[e : e + 1, :]
        patch = tokens % patches_all
        frame = tokens // patches_all
        level = (frame // CORES) ^ lax.axis_index("z")
        for i in range(CORES):
            owned = patch // blocks == chip * CORES + (core ^ i)
            owned = jnp.broadcast_to(owned.astype(jnp.float32), slot.shape)
            rank = dot(owned.astype(jnp.bfloat16), before)
            taken = jnp.where((rank == slot.astype(jnp.float32)) & (owned > 0.0), 1.0, 0.0)
            weight = jnp.sum(taken * gates, axis=1, keepdims=True)
            taken = taken.astype(jnp.bfloat16)
            place = jnp.where(
                frame % CORES == held_core(level),
                level * span + (core ^ i) * blocks + patch % blocks,
                -1,
            )
            at = slice(i * slots + e * MOST, i * slots + (e + 1) * MOST)
            take_ref[at] = dot_lanes(taken, (row_at == place).astype(jnp.bfloat16))[:MOST]
            weight_ref[at] = jnp.broadcast_to(weight[:MOST], (MOST, weight_ref.shape[1]))
            if i == 0:
                position = frame * blocks + patch % blocks
                found.append(dot_lanes(taken, (row_at == position).astype(jnp.bfloat16))[:MOST])
    levels = rows // span
    want = lax.broadcasted_iota(jnp.int32, (levels * blocks, rows), 0)
    have = lax.broadcasted_iota(jnp.int32, (levels * blocks, rows), 1)
    source = (want // blocks) * span + (core ^ 1) * blocks + want % blocks
    take_ref[CORES * slots :] = (source == have).astype(jnp.float32)
    here = jnp.concatenate(found, axis=0).astype(jnp.bfloat16)
    pieces = spread_ref.shape[0] // (rows * CORES)
    returns = spread_ref.shape[1]
    slot_at = lax.broadcasted_iota(jnp.int32, (slots, returns), 0)
    back_at = lax.broadcasted_iota(jnp.int32, (slots, returns), 1) // pieces
    same = (back_at // MOST // share == slot_at // MOST) & (back_at % MOST == slot_at % MOST)
    back = lax.dot_general(
        here, same.astype(jnp.bfloat16), FIRST_BOTH, preferred_element_type=jnp.float32
    )
    back_at = lax.broadcasted_iota(jnp.int32, (rows, returns), 1)
    sender = back_at // (MOST * pieces)
    piece = sender // lax.axis_size("z") % CORES * pieces + back_at % pieces
    for j in range(CORES * pieces):
        spread_ref[j * rows : (j + 1) * rows, :] = jnp.where(piece == j, back, 0.0).astype(
            jnp.bfloat16
        )

    for copy in copies[2:5]:
        copy.wait()
    query = query_ref[...].reshape(rows, features)
    key = key_ref[...].reshape(rows, features)
    value = value_ref[...].reshape(rows, features)
    query_rows_ref[...] = query
    key_rows_ref[...] = key
    value_rows_ref[...] = value
    scores = jnp.concatenate(
        [dot_lanes(k, q) for k, q in zip(heads_of(key), heads_of(query))], axis=1
    )
    scores = scores * scaling
    raised = jnp.exp(scores - over_frames(scores, jnp.maximum, blocks))
    probs = raised / over_frames(raised, jnp.add, blocks)
    patch_in = lax.broadcasted_iota(jnp.int32, probs.shape, 0) % blocks
    patch_out = lax.broadcasted_iota(jnp.int32, probs.shape, 1) % blocks
    probs = jnp.where(patch_in == patch_out, probs, 0.0)
    probs_ref[...] = probs
    weights = probs.T.astype(jnp.bfloat16)
    mixed = jnp.concatenate(
        [dot(weights[h * rows : (h + 1) * rows], v) for h, v in enumerate(heads_of(value))],
        axis=1,
    ).astype(jnp.bfloat16)
    picked_ref[...] = dot(here, mixed).astype(jnp.bfloat16)
    for copy in copies[5:]:
        copy.wait()


def pick_kernel(order, take_ref, weight_ref, *refs):
    *part_refs, cot_ref, mine_ref, sent_ref = refs
    parts = [part_refs[order.index(k)][...] for k in range(len(order))]
    cot = jnp.concatenate(parts, axis=0)
    cot_ref[...] = cot
    slots = mine_ref.shape[0]
    rows = dot(take_ref[...].astype(jnp.bfloat16), cot)
    picks = (rows[: CORES * slots] * weight_ref[:, :1]).astype(jnp.bfloat16)
    mine_ref[...] = picks[:slots]
    away = rows[CORES * slots :].astype(jnp.bfloat16)
    sent_ref[...] = jnp.concatenate([away, picks[slots:]], axis=0)


def pack_kernel(share, picked_ref, mine_ref, came_ref, out_ref):
    levels = lax.axis_size("z")
    slots, features = mine_ref.shape
    rows = mine_ref[...] + came_ref[came_ref.shape[0] - slots :, :]
    part = features // CORES
    picked = picked_ref[...]
    both = [
        jnp.concatenate(
            [half[:, c * part : (c + 1) * part] for half in (picked, rows)], axis=1
        )
        for c in range(CORES)
    ]
    for e in range(out_ref.shape[0] // share):
        for i in range(share):
            core = i // levels % CORES
            out_ref[e * share + i] = both[core][e * MOST : (e + 1) * MOST]


def part_of(part, width):
    return pl.ds(pl.multiple_of(part * width, width), width)


def first_kernel(near_ref, w_in_ref, w_out_ref, pre_ref, back_ref):
    width = w_in_ref.shape[0] // CORES
    rows = near_ref[...].reshape(pre_ref.shape[0], CORES * width)
    pre_ref[...] = dot(rows[:, :width], w_in_ref[:width, :])
    back_ref[...] = dot_lanes(rows[:, width:], w_out_ref[:, :width])


def second_kernel(far_ref, pre_ref, back_ref, w_in_ref, w_out_ref, slope_ref, sent_ref):
    width = w_in_ref.shape[0] // CORES
    far = far_ref[...].reshape(pre_ref.shape[0], CORES * width)
    pre_act = pre_ref[...] + dot(far[:, :width], w_in_ref[width:, :])
    back_act = back_ref[...] + dot_lanes(far[:, width:], w_out_ref[:, width:])
    slope = (back_act * gelu_slope(pre_act)).astype(jnp.bfloat16)
    slope_ref[...] = slope
    sent_ref[...] = dot_lanes(slope, w_in_ref[width:, :]).astype(jnp.bfloat16)


def third_kernel(blocks, slope_ref, w_in_ref, near_ref, came_ref, kept_ref, cot_ref):
    rows = near_ref.shape[0]
    span = CORES * blocks
    levels = rows // span
    want = lax.broadcasted_iota(jnp.int32, (rows, rows), 0)
    have = lax.broadcasted_iota(jnp.int32, (rows, rows), 1)
    frame = want // blocks
    level = (frame // CORES) ^ lax.axis_index("z")
    here = frame % CORES == held_core(level)
    source = level * span + lax.axis_index("core") * blocks + want % blocks
    own = (here & (source == have)).astype(jnp.bfloat16)
    source = level * blocks + want % blocks
    others = (jnp.logical_not(here) & (source == have)).astype(jnp.bfloat16)
    others = others[:, : levels * blocks]
    cot = dot(own, near_ref[...])
    cot = cot + dot(others, came_ref[: levels * blocks, :])
    cot_ref[...] = cot.astype(jnp.bfloat16)
    width = kept_ref.shape[1]
    kept_ref[...] = dot_lanes(slope_ref[...], w_in_ref[:width, :])


def sum_kernel(kept_ref, came_ref, out_ref, piece_ref):
    total = kept_ref[...] + came_ref[...].astype(jnp.float32)
    count, width = total.shape
    pieces = width // PIECE
    parts = piece_ref.shape[0]
    for j in range(pieces):
        for i in range(parts):
            start = j * PIECE + i * LANES
            piece_ref[i, pl.ds(j, count, stride=pieces), :] = total[:, start : start + LANES]
    total = jnp.concatenate([piece_ref[i] for i in range(parts)], axis=1)
    out_ref[...] = total.astype(jnp.bfloat16).reshape(out_ref.shape)


def backward_kernel(
    spread_ref, back_ref, cot_ref, probs_ref, query_ref, key_ref, value_ref,
    grad_query_hbm, grad_key_hbm, grad_value_hbm,
    grad_query_ref, grad_key_ref, grad_value_ref, sems,
):
    frames, blocks, features = grad_query_ref.shape
    rows = frames * blocks
    scaling = (features // HEADS) ** (-0.5)
    query, key, value = query_ref[...], key_ref[...], value_ref[...]
    back = dot(spread_ref[...], back_ref[...].reshape(-1, PIECE))
    added = jnp.concatenate(
        [back[start : start + rows] for start in range(0, back.shape[0], rows)], axis=1
    )
    stream = (cot_ref[...].astype(jnp.float32) + added).astype(jnp.bfloat16)
    probs = probs_ref[...]
    weights = probs.astype(jnp.bfloat16)
    copies = []

    def put(ref, hbm, parts):
        joined = jnp.concatenate(parts, axis=1).astype(jnp.bfloat16)
        ref[...] = joined.reshape(frames, blocks, features)
        copy = pltpu.make_async_copy(ref, hbm, sems.at[len(copies)])
        copy.start()
        copies.append(copy)

    grad_prob = jnp.concatenate(
        [dot_lanes(v, g) for v, g in zip(heads_of(value), heads_of(stream))], axis=1
    )
    put(
        grad_value_ref,
        grad_value_hbm,
        [dot(w, g) for w, g in zip(heads_of(weights), heads_of(stream))],
    )
    centre = over_frames(probs * grad_prob, jnp.add, blocks)
    grad_score = probs * (grad_prob - centre)
    turned = grad_score.T.astype(jnp.bfloat16)
    grad_score = grad_score.astype(jnp.bfloat16)
    put(
        grad_key_ref,
        grad_key_hbm,
        [dot(s, q) * scaling for s, q in zip(heads_of(grad_score), heads_of(query))],
    )
    put(
        grad_query_ref,
        grad_query_hbm,
        [dot(turned[h * rows : (h + 1) * rows], k) * scaling for h, k in enumerate(heads_of(key))],
    )
    for copy in copies:
        copy.wait()


def call(kernel, outs, operands, places, scratch=(), results="v"):
    spaces = {
        "v": pl.BlockSpec(memory_space=pltpu.VMEM),
        "h": pl.BlockSpec(memory_space=pl.ANY),
    }
    return pl.pallas_call(
        kernel,
        out_shape=[jax.ShapeDtypeStruct(shape, dtype) for shape, dtype in outs],
        in_specs=[spaces[place] for place in places],
        out_specs=[spaces[results]] * len(outs),
        scratch_shapes=list(scratch),
        compiler_params=pltpu.CompilerParams(vmem_limit_bytes=32 * 1024 * 1024),
    )(*[
        pltpu.with_memory_space_constraint(operand, pltpu.HBM) if place == "h" else operand
        for operand, place in zip(operands, places)
    ])


def body(query_in, key_in, value_in, cotangent, w_in, w_out, gate_probs, chosen):
    bf16, f32 = jnp.bfloat16, jnp.float32
    frames, blocks, features = query_in.shape
    groups = lax.axis_size("grp")
    levels = lax.axis_size("z")
    columns = levels * CORES
    experts = gate_probs.shape[0]
    devices = groups * columns
    share = devices // experts
    rows = frames * blocks
    slots = experts * MOST
    part = features // CORES
    hidden = w_in.shape[2]
    everyone = ("grp", "core", "z")

    def swap(values):
        return lax.ppermute(values, "core", [(i, i ^ 1) for i in range(CORES)])

    def across(values, step):
        pairs = [(i, i ^ (CORES * step) ^ 1) for i in range(columns)]
        return lax.ppermute(values, ("z", "core"), pairs)

    span = CORES * blocks
    parts = call(
        functools.partial(turn_kernel, span),
        [((span, features), bf16)] * levels,
        [cotangent],
        "h",
        [pltpu.VMEM(cotangent.shape, bf16), pltpu.SemaphoreType.DMA],
    )
    order = [0] + [i ^ (i >> 1) for i in range(levels - 1, 0, -1)]
    parts = [across(parts[k], k) if k else parts[k] for k in order]
    query, key, value, w_in_near, w_out_near, probs, picked, take, weight, spread = call(
        functools.partial(forward_kernel, blocks * devices, share),
        [
            *[((rows, features), bf16)] * 3,
            (w_in.shape[1:], bf16),
            (w_out.shape[1:], bf16),
            ((rows, HEADS * rows), f32),
            ((slots, features), bf16),
            ((CORES * slots + levels * blocks, rows), f32),
            ((CORES * slots, LANES), f32),
            ((rows * features // PIECE, devices * MOST * part // PIECE), bf16),
        ],
        [chosen, gate_probs, query_in, key_in, value_in, w_in, w_out],
        "hhhhhhh",
        [
            pltpu.VMEM(chosen.shape, jnp.int32),
            pltpu.VMEM(gate_probs.shape, f32),
            *[pltpu.VMEM(query_in.shape, bf16)] * 3,
            pltpu.SemaphoreType.DMA((5 + 2 * CORES,)),
        ],
    )
    cot_near, mine, sent = call(
        functools.partial(pick_kernel, order),
        [((rows, features), bf16), ((slots, features), bf16), ((levels * blocks + slots, features), bf16)],
        [take, weight, *parts],
        "vv" + "v" * levels,
    )
    came_near = swap(sent)
    (outgoing,) = call(
        functools.partial(pack_kernel, share),
        [((devices, MOST, 2 * part), bf16)],
        [picked, mine, came_near],
        "vvv",
    )
    held = lax.all_to_all(outgoing, everyone, split_axis=0, concat_axis=0, tiled=True)
    other = swap(held)
    acts = (devices * MOST, hidden)
    halves = (devices * MOST, part)
    pre_act, back_act = call(
        first_kernel, [(acts, f32), (acts, f32)], [held, w_in_near, w_out_near], "vvv"
    )
    slope, sent = call(
        second_kernel,
        [(acts, bf16), (halves, bf16)],
        [other, pre_act, back_act, w_in_near, w_out_near],
        "vvvvv",
    )
    came = swap(sent)
    kept, cot = call(
        functools.partial(third_kernel, blocks),
        [(halves, f32), ((rows, features), bf16)],
        [slope, w_in_near, cot_near, came_near],
        "vvvv",
    )
    pieces = MOST * part // PIECE
    (total,) = call(
        sum_kernel,
        [((devices, pieces, PIECE), bf16)],
        [kept, came],
        "vv",
        [pltpu.VMEM((PIECE // LANES, devices * pieces, LANES), f32)],
    )
    back = lax.all_to_all(total, everyone, split_axis=0, concat_axis=0, tiled=True)
    return call(
        backward_kernel,
        [((frames, blocks, features), bf16)] * 3,
        [spread, back, cot, probs, query, key, value],
        "vvvvvvv",
        [pltpu.VMEM((frames, blocks, features), bf16)] * 3 + [pltpu.SemaphoreType.DMA((3,))],
        "h",
    )


def solution(mesh):
    groups, columns = mesh.devices.shape
    split = Mesh(mesh.devices.reshape(groups, columns // CORES, CORES), ("grp", "z", "core"))
    frm = ("z", "core")
    patches = P(None, ("grp",) + frm, None)
    return jax.shard_map(
        body,
        mesh=split,
        in_specs=(
            patches, patches, patches, P(frm, "grp", None), P("grp", None, frm),
            P("grp", frm, None), P(), P(),
        ),
        out_specs=(patches, patches, patches),
        check_vma=False,
    )
```

```python
import functools

import jax
import jax.numpy as jnp
from jax import lax
from jax.experimental import pallas as pl
from jax.experimental.pallas import tpu as pltpu
from jax.sharding import Mesh
from jax.sharding import PartitionSpec as P

HEADS = 16
MOST = 2
CORES = 2
SUBLANES = 8
LANES = 128
PIECE = 256

root_half = 0.7071067811865476
inv_root_tau = 0.3989422804014327

LANES_BOTH = (((1,), (1,)), ((), ()))
FIRST_BOTH = (((0,), (0,)), ((), ()))


def gelu_slope(pre_act):
    normal_cdf = 0.5 * (1.0 + lax.erf(pre_act * root_half))
    density = jnp.exp(-0.5 * pre_act * pre_act) * inv_root_tau
    return normal_cdf + pre_act * density


def dot(a, b):
    return jnp.dot(a, b, preferred_element_type=jnp.float32)


def dot_lanes(a, b):
    return lax.dot_general(a, b, LANES_BOTH, preferred_element_type=jnp.float32)


def over_frames(values, op, blocks):
    rows = values.shape[0]
    total = values[:SUBLANES]
    for start in range(SUBLANES, rows, SUBLANES):
        total = op(total, values[start : start + SUBLANES])
    step = blocks
    while step < SUBLANES:
        total = op(total, pltpu.roll(total, step, 0))
        step *= 2
    return jnp.concatenate([total] * (rows // SUBLANES), axis=0)


def heads_of(values):
    width = values.shape[1] // HEADS
    return [values[:, h * width : (h + 1) * width] for h in range(HEADS)]


def turn_kernel(span, cot_hbm, *refs):
    *part_refs, cot_ref, sem = refs
    copy = pltpu.make_async_copy(cot_hbm, cot_ref, sem)
    copy.start()
    level = lax.axis_index("z")
    copy.wait()
    parts = [cot_ref[0, k * span : (k + 1) * span, :] for k in range(len(part_refs))]
    bit = 1
    while bit < len(parts):
        turn = (level // bit) % 2 == 1
        parts = [jnp.where(turn, parts[k ^ bit], parts[k]) for k in range(len(parts))]
        bit *= 2
    for part_ref, part in zip(part_refs, parts):
        part_ref[...] = part


def held_core(level):
    core = lax.axis_index("core")
    return jnp.where(level == 0, core, 1 - core)


def forward_kernel(
    patches_all, share,
    chosen_hbm, gate_hbm, query_hbm, key_hbm, value_hbm, w_in_hbm, w_out_hbm,
    query_rows_ref, key_rows_ref, value_rows_ref, w_in_ref, w_out_ref,
    probs_ref, picked_ref, take_ref, weight_ref, spread_ref,
    chosen_ref, gate_ref, query_ref, key_ref, value_ref, sems,
):
    core = lax.axis_index("core")
    chip = lax.axis_index("grp") * lax.axis_size("z") + lax.axis_index("z")
    part = w_in_ref.shape[0] // CORES
    sources = [chosen_hbm, gate_hbm, query_hbm, key_hbm, value_hbm]
    targets = [chosen_ref, gate_ref, query_ref, key_ref, value_ref]
    for i in range(CORES):
        sources.append(w_in_hbm.at[0, part_of(core ^ i, part)])
        targets.append(w_in_ref.at[pl.ds(i * part, part)])
        sources.append(w_out_hbm.at[0, :, part_of(core ^ i, part)])
        targets.append(w_out_ref.at[:, pl.ds(i * part, part)])
    copies = [
        pltpu.make_async_copy(source, target, sems.at[i])
        for i, (source, target) in enumerate(zip(sources, targets))
    ]
    for copy in copies:
        copy.start()
    frames, blocks, features = query_ref.shape
    rows = frames * blocks
    scaling = (features // HEADS) ** (-0.5)

    for copy in copies[:2]:
        copy.wait()
    experts, cap = chosen_ref.shape
    before = (
        lax.broadcasted_iota(jnp.int32, (cap, cap), 0)
        < lax.broadcasted_iota(jnp.int32, (cap, cap), 1)
    ).astype(jnp.bfloat16)
    slot = lax.broadcasted_iota(jnp.int32, (SUBLANES, cap), 0)
    row_at = lax.broadcasted_iota(jnp.int32, (rows, cap), 0)
    span = CORES * blocks
    slots = experts * MOST
    found = []
    for e in range(experts):
        tokens = chosen_ref[e : e + 1, :]
        gates = gate_ref[e : e + 1, :]
        patch = tokens % patches_all
        frame = tokens // patches_all
        level = (frame // CORES) ^ lax.axis_index("z")
        for i in range(CORES):
            owned = patch // blocks == chip * CORES + (core ^ i)
            owned = jnp.broadcast_to(owned.astype(jnp.float32), slot.shape)
            rank = dot(owned.astype(jnp.bfloat16), before)
            taken = jnp.where((rank == slot.astype(jnp.float32)) & (owned > 0.0), 1.0, 0.0)
            weight = jnp.sum(taken * gates, axis=1, keepdims=True)
            taken = taken.astype(jnp.bfloat16)
            place = jnp.where(
                frame % CORES == held_core(level),
                level * span + (core ^ i) * blocks + patch % blocks,
                -1,
            )
            at = slice(i * slots + e * MOST, i * slots + (e + 1) * MOST)
            take_ref[at] = dot_lanes(taken, (row_at == place).astype(jnp.bfloat16))[:MOST]
            weight_ref[at] = jnp.broadcast_to(weight[:MOST], (MOST, weight_ref.shape[1]))
            if i == 0:
                position = frame * blocks + patch % blocks
                found.append(dot_lanes(taken, (row_at == position).astype(jnp.bfloat16))[:MOST])
    levels = rows // span
    want = lax.broadcasted_iota(jnp.int32, (levels * blocks, rows), 0)
    have = lax.broadcasted_iota(jnp.int32, (levels * blocks, rows), 1)
    source = (want // blocks) * span + (core ^ 1) * blocks + want % blocks
    take_ref[CORES * slots :] = (source == have).astype(jnp.float32)
    here = jnp.concatenate(found, axis=0).astype(jnp.bfloat16)
    pieces = spread_ref.shape[0] // (rows * CORES)
    returns = spread_ref.shape[1]
    slot_at = lax.broadcasted_iota(jnp.int32, (slots, returns), 0)
    back_at = lax.broadcasted_iota(jnp.int32, (slots, returns), 1) // pieces
    levels, groups = lax.axis_size("z"), lax.axis_size("grp")
    expert_of = back_at // MOST // levels % groups // share
    same = (expert_of == slot_at // MOST) & (back_at % MOST == slot_at % MOST)
    back = lax.dot_general(
        here, same.astype(jnp.bfloat16), FIRST_BOTH, preferred_element_type=jnp.float32
    )
    back_at = lax.broadcasted_iota(jnp.int32, (rows, returns), 1)
    piece = back_at // (MOST * pieces * levels * groups) * pieces + back_at % pieces
    for j in range(CORES * pieces):
        spread_ref[j * rows : (j + 1) * rows, :] = jnp.where(piece == j, back, 0.0).astype(
            jnp.bfloat16
        )

    for copy in copies[2:5]:
        copy.wait()
    query = query_ref[...].reshape(rows, features)
    key = key_ref[...].reshape(rows, features)
    value = value_ref[...].reshape(rows, features)
    query_rows_ref[...] = query
    key_rows_ref[...] = key
    value_rows_ref[...] = value
    scores = jnp.concatenate(
        [dot_lanes(k, q) for k, q in zip(heads_of(key), heads_of(query))], axis=1
    )
    scores = scores * scaling
    raised = jnp.exp(scores - over_frames(scores, jnp.maximum, blocks))
    probs = raised / over_frames(raised, jnp.add, blocks)
    patch_in = lax.broadcasted_iota(jnp.int32, probs.shape, 0) % blocks
    patch_out = lax.broadcasted_iota(jnp.int32, probs.shape, 1) % blocks
    probs = jnp.where(patch_in == patch_out, probs, 0.0)
    probs_ref[...] = probs
    weights = probs.T.astype(jnp.bfloat16)
    mixed = jnp.concatenate(
        [dot(weights[h * rows : (h + 1) * rows], v) for h, v in enumerate(heads_of(value))],
        axis=1,
    ).astype(jnp.bfloat16)
    picked_ref[...] = dot(here, mixed).astype(jnp.bfloat16)
    for copy in copies[5:]:
        copy.wait()


def pick_kernel(order, take_ref, weight_ref, *refs):
    *part_refs, cot_ref, mine_ref, sent_ref = refs
    parts = [part_refs[order.index(k)][...] for k in range(len(order))]
    cot = jnp.concatenate(parts, axis=0)
    cot_ref[...] = cot
    slots = mine_ref.shape[0]
    rows = dot(take_ref[...].astype(jnp.bfloat16), cot)
    picks = (rows[: CORES * slots] * weight_ref[:, :1]).astype(jnp.bfloat16)
    mine_ref[...] = picks[:slots]
    away = rows[CORES * slots :].astype(jnp.bfloat16)
    sent_ref[...] = jnp.concatenate([away, picks[slots:]], axis=0)


def pack_kernel(share, picked_ref, mine_ref, came_ref, out_ref):
    levels, groups = lax.axis_size("z"), lax.axis_size("grp")
    slots, features = mine_ref.shape
    rows = mine_ref[...] + came_ref[came_ref.shape[0] - slots :, :]
    part = features // CORES
    picked = picked_ref[...]
    both = [
        jnp.concatenate(
            [half[:, c * part : (c + 1) * part] for half in (picked, rows)], axis=1
        )
        for c in range(CORES)
    ]
    for i in range(out_ref.shape[0]):
        e = i // levels % groups // share
        out_ref[i] = both[i // (levels * groups)][e * MOST : (e + 1) * MOST]


def part_of(part, width):
    return pl.ds(pl.multiple_of(part * width, width), width)


def first_kernel(near_ref, w_in_ref, w_out_ref, pre_ref, back_ref):
    width = w_in_ref.shape[0] // CORES
    rows = near_ref[...].reshape(pre_ref.shape[0], CORES * width)
    pre_ref[...] = dot(rows[:, :width], w_in_ref[:width, :])
    back_ref[...] = dot_lanes(rows[:, width:], w_out_ref[:, :width])


def second_kernel(far_ref, pre_ref, back_ref, w_in_ref, w_out_ref, slope_ref, sent_ref):
    width = w_in_ref.shape[0] // CORES
    far = far_ref[...].reshape(pre_ref.shape[0], CORES * width)
    pre_act = pre_ref[...] + dot(far[:, :width], w_in_ref[width:, :])
    back_act = back_ref[...] + dot_lanes(far[:, width:], w_out_ref[:, width:])
    slope = (back_act * gelu_slope(pre_act)).astype(jnp.bfloat16)
    slope_ref[...] = slope
    sent_ref[...] = dot_lanes(slope, w_in_ref[width:, :]).astype(jnp.bfloat16)


def third_kernel(blocks, slope_ref, w_in_ref, near_ref, came_ref, kept_ref, cot_ref):
    rows = near_ref.shape[0]
    span = CORES * blocks
    levels = rows // span
    want = lax.broadcasted_iota(jnp.int32, (rows, rows), 0)
    have = lax.broadcasted_iota(jnp.int32, (rows, rows), 1)
    frame = want // blocks
    level = (frame // CORES) ^ lax.axis_index("z")
    here = frame % CORES == held_core(level)
    source = level * span + lax.axis_index("core") * blocks + want % blocks
    own = (here & (source == have)).astype(jnp.bfloat16)
    source = level * blocks + want % blocks
    others = (jnp.logical_not(here) & (source == have)).astype(jnp.bfloat16)
    others = others[:, : levels * blocks]
    cot = dot(own, near_ref[...])
    cot = cot + dot(others, came_ref[: levels * blocks, :])
    cot_ref[...] = cot.astype(jnp.bfloat16)
    width = kept_ref.shape[1]
    kept_ref[...] = dot_lanes(slope_ref[...], w_in_ref[:width, :])


def sum_kernel(kept_ref, came_ref, out_ref, piece_ref):
    total = kept_ref[...] + came_ref[...].astype(jnp.float32)
    count, width = total.shape
    pieces = width // PIECE
    parts = piece_ref.shape[0]
    for j in range(pieces):
        for i in range(parts):
            start = j * PIECE + i * LANES
            piece_ref[i, pl.ds(j, count, stride=pieces), :] = total[:, start : start + LANES]
    total = jnp.concatenate([piece_ref[i] for i in range(parts)], axis=1)
    out_ref[...] = total.astype(jnp.bfloat16).reshape(out_ref.shape)


def backward_kernel(
    spread_ref, back_ref, cot_ref, probs_ref, query_ref, key_ref, value_ref,
    grad_query_hbm, grad_key_hbm, grad_value_hbm,
    grad_query_ref, grad_key_ref, grad_value_ref, sems,
):
    frames, blocks, features = grad_query_ref.shape
    rows = frames * blocks
    scaling = (features // HEADS) ** (-0.5)
    query, key, value = query_ref[...], key_ref[...], value_ref[...]
    back = dot(spread_ref[...], back_ref[...].reshape(-1, PIECE))
    added = jnp.concatenate(
        [back[start : start + rows] for start in range(0, back.shape[0], rows)], axis=1
    )
    stream = (cot_ref[...].astype(jnp.float32) + added).astype(jnp.bfloat16)
    probs = probs_ref[...]
    weights = probs.astype(jnp.bfloat16)
    copies = []

    def put(ref, hbm, parts):
        joined = jnp.concatenate(parts, axis=1).astype(jnp.bfloat16)
        ref[...] = joined.reshape(frames, blocks, features)
        copy = pltpu.make_async_copy(ref, hbm, sems.at[len(copies)])
        copy.start()
        copies.append(copy)

    grad_prob = jnp.concatenate(
        [dot_lanes(v, g) for v, g in zip(heads_of(value), heads_of(stream))], axis=1
    )
    put(
        grad_value_ref,
        grad_value_hbm,
        [dot(w, g) for w, g in zip(heads_of(weights), heads_of(stream))],
    )
    centre = over_frames(probs * grad_prob, jnp.add, blocks)
    grad_score = probs * (grad_prob - centre)
    turned = grad_score.T.astype(jnp.bfloat16)
    grad_score = grad_score.astype(jnp.bfloat16)
    put(
        grad_key_ref,
        grad_key_hbm,
        [dot(s, q) * scaling for s, q in zip(heads_of(grad_score), heads_of(query))],
    )
    put(
        grad_query_ref,
        grad_query_hbm,
        [dot(turned[h * rows : (h + 1) * rows], k) * scaling for h, k in enumerate(heads_of(key))],
    )
    for copy in copies:
        copy.wait()


def call(kernel, outs, operands, places, scratch=(), results="v"):
    spaces = {
        "v": pl.BlockSpec(memory_space=pltpu.VMEM),
        "h": pl.BlockSpec(memory_space=pl.ANY),
    }
    return pl.pallas_call(
        kernel,
        out_shape=[jax.ShapeDtypeStruct(shape, dtype) for shape, dtype in outs],
        in_specs=[spaces[place] for place in places],
        out_specs=[spaces[results]] * len(outs),
        scratch_shapes=list(scratch),
        compiler_params=pltpu.CompilerParams(vmem_limit_bytes=32 * 1024 * 1024),
    )(*[
        pltpu.with_memory_space_constraint(operand, pltpu.HBM) if place == "h" else operand
        for operand, place in zip(operands, places)
    ])


def body(query_in, key_in, value_in, cotangent, w_in, w_out, gate_probs, chosen):
    bf16, f32 = jnp.bfloat16, jnp.float32
    frames, blocks, features = query_in.shape
    groups = lax.axis_size("grp")
    levels = lax.axis_size("z")
    columns = levels * CORES
    experts = gate_probs.shape[0]
    devices = groups * columns
    share = groups // experts
    rows = frames * blocks
    slots = experts * MOST
    part = features // CORES
    hidden = w_in.shape[2]
    everyone = ("core", "grp", "z")

    def swap(values):
        return lax.ppermute(values, "core", [(i, i ^ 1) for i in range(CORES)])

    def across(values, step):
        pairs = [(i, i ^ (CORES * step) ^ 1) for i in range(columns)]
        return lax.ppermute(values, ("z", "core"), pairs)

    span = CORES * blocks
    parts = call(
        functools.partial(turn_kernel, span),
        [((span, features), bf16)] * levels,
        [cotangent],
        "h",
        [pltpu.VMEM(cotangent.shape, bf16), pltpu.SemaphoreType.DMA],
    )
    order = [0] + [i ^ (i >> 1) for i in range(levels - 1, 0, -1)]
    parts = [across(parts[k], k) if k else parts[k] for k in order]
    query, key, value, w_in_near, w_out_near, probs, picked, take, weight, spread = call(
        functools.partial(forward_kernel, blocks * devices, share),
        [
            *[((rows, features), bf16)] * 3,
            (w_in.shape[1:], bf16),
            (w_out.shape[1:], bf16),
            ((rows, HEADS * rows), f32),
            ((slots, features), bf16),
            ((CORES * slots + levels * blocks, rows), f32),
            ((CORES * slots, LANES), f32),
            ((rows * features // PIECE, devices * MOST * part // PIECE), bf16),
        ],
        [chosen, gate_probs, query_in, key_in, value_in, w_in, w_out],
        "hhhhhhh",
        [
            pltpu.VMEM(chosen.shape, jnp.int32),
            pltpu.VMEM(gate_probs.shape, f32),
            *[pltpu.VMEM(query_in.shape, bf16)] * 3,
            pltpu.SemaphoreType.DMA((5 + 2 * CORES,)),
        ],
    )
    cot_near, mine, sent = call(
        functools.partial(pick_kernel, order),
        [((rows, features), bf16), ((slots, features), bf16), ((levels * blocks + slots, features), bf16)],
        [take, weight, *parts],
        "vv" + "v" * levels,
    )
    came_near = swap(sent)
    (outgoing,) = call(
        functools.partial(pack_kernel, share),
        [((devices, MOST, 2 * part), bf16)],
        [picked, mine, came_near],
        "vvv",
    )
    held = lax.all_to_all(outgoing, everyone, split_axis=0, concat_axis=0, tiled=True)
    other = swap(held)
    acts = (devices * MOST, hidden)
    halves = (devices * MOST, part)
    pre_act, back_act = call(
        first_kernel, [(acts, f32), (acts, f32)], [held, w_in_near, w_out_near], "vvv"
    )
    slope, sent = call(
        second_kernel,
        [(acts, bf16), (halves, bf16)],
        [other, pre_act, back_act, w_in_near, w_out_near],
        "vvvvv",
    )
    came = swap(sent)
    kept, cot = call(
        functools.partial(third_kernel, blocks),
        [(halves, f32), ((rows, features), bf16)],
        [slope, w_in_near, cot_near, came_near],
        "vvvv",
    )
    pieces = MOST * part // PIECE
    (total,) = call(
        sum_kernel,
        [((devices, pieces, PIECE), bf16)],
        [kept, came],
        "vv",
        [pltpu.VMEM((PIECE // LANES, devices * pieces, LANES), f32)],
    )
    back = lax.all_to_all(total, everyone, split_axis=0, concat_axis=0, tiled=True)
    return call(
        backward_kernel,
        [((frames, blocks, features), bf16)] * 3,
        [spread, back, cot, probs, query, key, value],
        "vvvvvvv",
        [pltpu.VMEM((frames, blocks, features), bf16)] * 3 + [pltpu.SemaphoreType.DMA((3,))],
        "h",
    )


def solution(mesh):
    groups, columns = mesh.devices.shape
    split = Mesh(mesh.devices.reshape(groups, columns // CORES, CORES), ("grp", "z", "core"))
    frm = ("z", "core")
    patches = P(None, ("grp",) + frm, None)
    return jax.shard_map(
        body,
        mesh=split,
        in_specs=(
            patches, patches, patches, P(frm, "grp", None), P("grp", None, frm),
            P("grp", frm, None), P(), P(),
        ),
        out_specs=(patches, patches, patches),
        check_vma=False,
    )
```

```python
import functools

import jax
import jax.numpy as jnp
from jax import lax
from jax.experimental import pallas as pl
from jax.experimental.pallas import tpu as pltpu
from jax.sharding import Mesh
from jax.sharding import PartitionSpec as P

HEADS = 16
MOST = 2
CORES = 2
SUBLANES = 8
LANES = 128
PIECE = 256

root_half = 0.7071067811865476
inv_root_tau = 0.3989422804014327

LANES_BOTH = (((1,), (1,)), ((), ()))
FIRST_BOTH = (((0,), (0,)), ((), ()))


def gelu_slope(pre_act):
    normal_cdf = 0.5 * (1.0 + lax.erf(pre_act * root_half))
    density = jnp.exp(-0.5 * pre_act * pre_act) * inv_root_tau
    return normal_cdf + pre_act * density


def dot(a, b):
    return jnp.dot(a, b, preferred_element_type=jnp.float32)


def dot_lanes(a, b):
    return lax.dot_general(a, b, LANES_BOTH, preferred_element_type=jnp.float32)


def over_frames(values, op, blocks):
    rows = values.shape[0]
    total = values[:SUBLANES]
    for start in range(SUBLANES, rows, SUBLANES):
        total = op(total, values[start : start + SUBLANES])
    step = blocks
    while step < SUBLANES:
        total = op(total, pltpu.roll(total, step, 0))
        step *= 2
    return jnp.concatenate([total] * (rows // SUBLANES), axis=0)


def heads_of(values):
    width = values.shape[1] // HEADS
    return [values[:, h * width : (h + 1) * width] for h in range(HEADS)]


def turn_kernel(span, cot_hbm, *refs):
    *part_refs, cot_ref, sem = refs
    copy = pltpu.make_async_copy(cot_hbm, cot_ref, sem)
    copy.start()
    level = lax.axis_index("z")
    copy.wait()
    parts = [cot_ref[0, k * span : (k + 1) * span, :] for k in range(len(part_refs))]
    bit = 1
    while bit < len(parts):
        turn = (level // bit) % 2 == 1
        parts = [jnp.where(turn, parts[k ^ bit], parts[k]) for k in range(len(parts))]
        bit *= 2
    for part_ref, part in zip(part_refs, parts):
        part_ref[...] = part


def held_core(level):
    core = lax.axis_index("core")
    return jnp.where(level == 0, core, 1 - core)


def forward_kernel(
    patches_all, share,
    chosen_hbm, gate_hbm, query_hbm, key_hbm, value_hbm, w_in_hbm, w_out_hbm,
    query_rows_ref, key_rows_ref, value_rows_ref, w_in_ref, w_out_ref,
    probs_ref, picked_ref, take_ref, weight_ref, spread_ref,
    chosen_ref, gate_ref, query_ref, key_ref, value_ref, sems,
):
    core = lax.axis_index("core")
    chip = lax.axis_index("grp") * lax.axis_size("z") + lax.axis_index("z")
    part = w_in_ref.shape[0] // CORES
    sources = [chosen_hbm, gate_hbm, query_hbm, key_hbm, value_hbm]
    targets = [chosen_ref, gate_ref, query_ref, key_ref, value_ref]
    for i in range(CORES):
        sources.append(w_in_hbm.at[0, part_of(core ^ i, part)])
        targets.append(w_in_ref.at[pl.ds(i * part, part)])
        sources.append(w_out_hbm.at[0, :, part_of(core ^ i, part)])
        targets.append(w_out_ref.at[:, pl.ds(i * part, part)])
    copies = [
        pltpu.make_async_copy(source, target, sems.at[i])
        for i, (source, target) in enumerate(zip(sources, targets))
    ]
    for copy in copies:
        copy.start()
    frames, blocks, features = query_ref.shape
    rows = frames * blocks
    scaling = (features // HEADS) ** (-0.5)

    for copy in copies[:2]:
        copy.wait()
    experts, cap = chosen_ref.shape
    before = (
        lax.broadcasted_iota(jnp.int32, (cap, cap), 0)
        < lax.broadcasted_iota(jnp.int32, (cap, cap), 1)
    ).astype(jnp.bfloat16)
    slot = lax.broadcasted_iota(jnp.int32, (SUBLANES, cap), 0)
    row_at = lax.broadcasted_iota(jnp.int32, (rows, cap), 0)
    span = CORES * blocks
    slots = experts * MOST
    found = []
    for e in range(experts):
        tokens = chosen_ref[e : e + 1, :]
        gates = gate_ref[e : e + 1, :]
        patch = tokens % patches_all
        frame = tokens // patches_all
        level = (frame // CORES) ^ lax.axis_index("z")
        for i in range(CORES):
            owned = patch // blocks == chip * CORES + (core ^ i)
            owned = jnp.broadcast_to(owned.astype(jnp.float32), slot.shape)
            rank = dot(owned.astype(jnp.bfloat16), before)
            taken = jnp.where((rank == slot.astype(jnp.float32)) & (owned > 0.0), 1.0, 0.0)
            weight = jnp.sum(taken * gates, axis=1, keepdims=True)
            taken = taken.astype(jnp.bfloat16)
            place = jnp.where(
                frame % CORES == held_core(level),
                level * span + (core ^ i) * blocks + patch % blocks,
                -1,
            )
            at = slice(i * slots + e * MOST, i * slots + (e + 1) * MOST)
            take_ref[at] = dot_lanes(taken, (row_at == place).astype(jnp.bfloat16))[:MOST]
            weight_ref[at] = jnp.broadcast_to(weight[:MOST], (MOST, weight_ref.shape[1]))
            if i == 0:
                position = frame * blocks + patch % blocks
                found.append(dot_lanes(taken, (row_at == position).astype(jnp.bfloat16))[:MOST])
    levels = rows // span
    want = lax.broadcasted_iota(jnp.int32, (levels * blocks, rows), 0)
    have = lax.broadcasted_iota(jnp.int32, (levels * blocks, rows), 1)
    source = (want // blocks) * span + (core ^ 1) * blocks + want % blocks
    take_ref[CORES * slots :] = (source == have).astype(jnp.float32)
    here = jnp.concatenate(found, axis=0).astype(jnp.bfloat16)
    pieces = spread_ref.shape[0] // (rows * CORES)
    returns = spread_ref.shape[1]
    slot_at = lax.broadcasted_iota(jnp.int32, (slots, returns), 0)
    back_at = lax.broadcasted_iota(jnp.int32, (slots, returns), 1) // pieces
    levels, groups = lax.axis_size("z"), lax.axis_size("grp")
    expert_of = back_at // MOST % groups // share
    same = (expert_of == slot_at // MOST) & (back_at % MOST == slot_at % MOST)
    back = lax.dot_general(
        here, same.astype(jnp.bfloat16), FIRST_BOTH, preferred_element_type=jnp.float32
    )
    back_at = lax.broadcasted_iota(jnp.int32, (rows, returns), 1)
    piece = back_at // (MOST * pieces * levels * groups) * pieces + back_at % pieces
    for j in range(CORES * pieces):
        spread_ref[j * rows : (j + 1) * rows, :] = jnp.where(piece == j, back, 0.0).astype(
            jnp.bfloat16
        )

    for copy in copies[2:5]:
        copy.wait()
    query = query_ref[...].reshape(rows, features)
    key = key_ref[...].reshape(rows, features)
    value = value_ref[...].reshape(rows, features)
    query_rows_ref[...] = query
    key_rows_ref[...] = key
    value_rows_ref[...] = value
    scores = jnp.concatenate(
        [dot_lanes(k, q) for k, q in zip(heads_of(key), heads_of(query))], axis=1
    )
    scores = scores * scaling
    raised = jnp.exp(scores - over_frames(scores, jnp.maximum, blocks))
    probs = raised / over_frames(raised, jnp.add, blocks)
    patch_in = lax.broadcasted_iota(jnp.int32, probs.shape, 0) % blocks
    patch_out = lax.broadcasted_iota(jnp.int32, probs.shape, 1) % blocks
    probs = jnp.where(patch_in == patch_out, probs, 0.0)
    probs_ref[...] = probs
    weights = probs.T.astype(jnp.bfloat16)
    mixed = jnp.concatenate(
        [dot(weights[h * rows : (h + 1) * rows], v) for h, v in enumerate(heads_of(value))],
        axis=1,
    ).astype(jnp.bfloat16)
    picked_ref[...] = dot(here, mixed).astype(jnp.bfloat16)
    for copy in copies[5:]:
        copy.wait()


def pick_kernel(order, take_ref, weight_ref, *refs):
    *part_refs, cot_ref, mine_ref, sent_ref = refs
    parts = [part_refs[order.index(k)][...] for k in range(len(order))]
    cot = jnp.concatenate(parts, axis=0)
    cot_ref[...] = cot
    slots = mine_ref.shape[0]
    rows = dot(take_ref[...].astype(jnp.bfloat16), cot)
    picks = (rows[: CORES * slots] * weight_ref[:, :1]).astype(jnp.bfloat16)
    mine_ref[...] = picks[:slots]
    away = rows[CORES * slots :].astype(jnp.bfloat16)
    sent_ref[...] = jnp.concatenate([away, picks[slots:]], axis=0)


def pack_kernel(share, picked_ref, mine_ref, came_ref, out_ref):
    levels, groups = lax.axis_size("z"), lax.axis_size("grp")
    slots, features = mine_ref.shape
    rows = mine_ref[...] + came_ref[came_ref.shape[0] - slots :, :]
    part = features // CORES
    picked = picked_ref[...]
    both = [
        jnp.concatenate(
            [half[:, c * part : (c + 1) * part] for half in (picked, rows)], axis=1
        )
        for c in range(CORES)
    ]
    for i in range(out_ref.shape[0]):
        e = i % groups // share
        out_ref[i] = both[i // (levels * groups)][e * MOST : (e + 1) * MOST]


def part_of(part, width):
    return pl.ds(pl.multiple_of(part * width, width), width)


def first_kernel(near_ref, w_in_ref, w_out_ref, pre_ref, back_ref):
    width = w_in_ref.shape[0] // CORES
    rows = near_ref[...].reshape(pre_ref.shape[0], CORES * width)
    pre_ref[...] = dot(rows[:, :width], w_in_ref[:width, :])
    back_ref[...] = dot_lanes(rows[:, width:], w_out_ref[:, :width])


def second_kernel(far_ref, pre_ref, back_ref, w_in_ref, w_out_ref, slope_ref, sent_ref):
    width = w_in_ref.shape[0] // CORES
    far = far_ref[...].reshape(pre_ref.shape[0], CORES * width)
    pre_act = pre_ref[...] + dot(far[:, :width], w_in_ref[width:, :])
    back_act = back_ref[...] + dot_lanes(far[:, width:], w_out_ref[:, width:])
    slope = (back_act * gelu_slope(pre_act)).astype(jnp.bfloat16)
    slope_ref[...] = slope
    sent_ref[...] = dot_lanes(slope, w_in_ref[width:, :]).astype(jnp.bfloat16)


def third_kernel(blocks, slope_ref, w_in_ref, near_ref, came_ref, kept_ref, cot_ref):
    rows = near_ref.shape[0]
    span = CORES * blocks
    levels = rows // span
    want = lax.broadcasted_iota(jnp.int32, (rows, rows), 0)
    have = lax.broadcasted_iota(jnp.int32, (rows, rows), 1)
    frame = want // blocks
    level = (frame // CORES) ^ lax.axis_index("z")
    here = frame % CORES == held_core(level)
    source = level * span + lax.axis_index("core") * blocks + want % blocks
    own = (here & (source == have)).astype(jnp.bfloat16)
    source = level * blocks + want % blocks
    others = (jnp.logical_not(here) & (source == have)).astype(jnp.bfloat16)
    others = others[:, : levels * blocks]
    cot = dot(own, near_ref[...])
    cot = cot + dot(others, came_ref[: levels * blocks, :])
    cot_ref[...] = cot.astype(jnp.bfloat16)
    width = kept_ref.shape[1]
    kept_ref[...] = dot_lanes(slope_ref[...], w_in_ref[:width, :])


def sum_kernel(kept_ref, came_ref, out_ref, piece_ref):
    total = kept_ref[...] + came_ref[...].astype(jnp.float32)
    count, width = total.shape
    pieces = width // PIECE
    parts = piece_ref.shape[0]
    for j in range(pieces):
        for i in range(parts):
            start = j * PIECE + i * LANES
            piece_ref[i, pl.ds(j, count, stride=pieces), :] = total[:, start : start + LANES]
    total = jnp.concatenate([piece_ref[i] for i in range(parts)], axis=1)
    out_ref[...] = total.astype(jnp.bfloat16).reshape(out_ref.shape)


def backward_kernel(
    spread_ref, back_ref, cot_ref, probs_ref, query_ref, key_ref, value_ref,
    grad_query_hbm, grad_key_hbm, grad_value_hbm,
    grad_query_ref, grad_key_ref, grad_value_ref, sems,
):
    frames, blocks, features = grad_query_ref.shape
    rows = frames * blocks
    scaling = (features // HEADS) ** (-0.5)
    query, key, value = query_ref[...], key_ref[...], value_ref[...]
    back = dot(spread_ref[...], back_ref[...].reshape(-1, PIECE))
    added = jnp.concatenate(
        [back[start : start + rows] for start in range(0, back.shape[0], rows)], axis=1
    )
    stream = (cot_ref[...].astype(jnp.float32) + added).astype(jnp.bfloat16)
    probs = probs_ref[...]
    weights = probs.astype(jnp.bfloat16)
    copies = []

    def put(ref, hbm, parts):
        joined = jnp.concatenate(parts, axis=1).astype(jnp.bfloat16)
        ref[...] = joined.reshape(frames, blocks, features)
        copy = pltpu.make_async_copy(ref, hbm, sems.at[len(copies)])
        copy.start()
        copies.append(copy)

    grad_prob = jnp.concatenate(
        [dot_lanes(v, g) for v, g in zip(heads_of(value), heads_of(stream))], axis=1
    )
    put(
        grad_value_ref,
        grad_value_hbm,
        [dot(w, g) for w, g in zip(heads_of(weights), heads_of(stream))],
    )
    centre = over_frames(probs * grad_prob, jnp.add, blocks)
    grad_score = probs * (grad_prob - centre)
    turned = grad_score.T.astype(jnp.bfloat16)
    grad_score = grad_score.astype(jnp.bfloat16)
    put(
        grad_key_ref,
        grad_key_hbm,
        [dot(s, q) * scaling for s, q in zip(heads_of(grad_score), heads_of(query))],
    )
    put(
        grad_query_ref,
        grad_query_hbm,
        [dot(turned[h * rows : (h + 1) * rows], k) * scaling for h, k in enumerate(heads_of(key))],
    )
    for copy in copies:
        copy.wait()


def call(kernel, outs, operands, places, scratch=(), results="v"):
    spaces = {
        "v": pl.BlockSpec(memory_space=pltpu.VMEM),
        "h": pl.BlockSpec(memory_space=pl.ANY),
    }
    return pl.pallas_call(
        kernel,
        out_shape=[jax.ShapeDtypeStruct(shape, dtype) for shape, dtype in outs],
        in_specs=[spaces[place] for place in places],
        out_specs=[spaces[results]] * len(outs),
        scratch_shapes=list(scratch),
        compiler_params=pltpu.CompilerParams(vmem_limit_bytes=32 * 1024 * 1024),
    )(*[
        pltpu.with_memory_space_constraint(operand, pltpu.HBM) if place == "h" else operand
        for operand, place in zip(operands, places)
    ])


def body(query_in, key_in, value_in, cotangent, w_in, w_out, gate_probs, chosen):
    bf16, f32 = jnp.bfloat16, jnp.float32
    frames, blocks, features = query_in.shape
    groups = lax.axis_size("grp")
    levels = lax.axis_size("z")
    columns = levels * CORES
    experts = gate_probs.shape[0]
    devices = groups * columns
    share = groups // experts
    rows = frames * blocks
    slots = experts * MOST
    part = features // CORES
    hidden = w_in.shape[2]
    everyone = ("core", "z", "grp")

    def swap(values):
        return lax.ppermute(values, "core", [(i, i ^ 1) for i in range(CORES)])

    def across(values, step):
        pairs = [(i, i ^ (CORES * step) ^ 1) for i in range(columns)]
        return lax.ppermute(values, ("z", "core"), pairs)

    span = CORES * blocks
    parts = call(
        functools.partial(turn_kernel, span),
        [((span, features), bf16)] * levels,
        [cotangent],
        "h",
        [pltpu.VMEM(cotangent.shape, bf16), pltpu.SemaphoreType.DMA],
    )
    order = [0] + [i ^ (i >> 1) for i in range(levels - 1, 0, -1)]
    parts = [across(parts[k], k) if k else parts[k] for k in order]
    query, key, value, w_in_near, w_out_near, probs, picked, take, weight, spread = call(
        functools.partial(forward_kernel, blocks * devices, share),
        [
            *[((rows, features), bf16)] * 3,
            (w_in.shape[1:], bf16),
            (w_out.shape[1:], bf16),
            ((rows, HEADS * rows), f32),
            ((slots, features), bf16),
            ((CORES * slots + levels * blocks, rows), f32),
            ((CORES * slots, LANES), f32),
            ((rows * features // PIECE, devices * MOST * part // PIECE), bf16),
        ],
        [chosen, gate_probs, query_in, key_in, value_in, w_in, w_out],
        "hhhhhhh",
        [
            pltpu.VMEM(chosen.shape, jnp.int32),
            pltpu.VMEM(gate_probs.shape, f32),
            *[pltpu.VMEM(query_in.shape, bf16)] * 3,
            pltpu.SemaphoreType.DMA((5 + 2 * CORES,)),
        ],
    )
    cot_near, mine, sent = call(
        functools.partial(pick_kernel, order),
        [((rows, features), bf16), ((slots, features), bf16), ((levels * blocks + slots, features), bf16)],
        [take, weight, *parts],
        "vv" + "v" * levels,
    )
    came_near = swap(sent)
    (outgoing,) = call(
        functools.partial(pack_kernel, share),
        [((devices, MOST, 2 * part), bf16)],
        [picked, mine, came_near],
        "vvv",
    )
    held = lax.all_to_all(outgoing, everyone, split_axis=0, concat_axis=0, tiled=True)
    other = swap(held)
    acts = (devices * MOST, hidden)
    halves = (devices * MOST, part)
    pre_act, back_act = call(
        first_kernel, [(acts, f32), (acts, f32)], [held, w_in_near, w_out_near], "vvv"
    )
    slope, sent = call(
        second_kernel,
        [(acts, bf16), (halves, bf16)],
        [other, pre_act, back_act, w_in_near, w_out_near],
        "vvvvv",
    )
    came = swap(sent)
    kept, cot = call(
        functools.partial(third_kernel, blocks),
        [(halves, f32), ((rows, features), bf16)],
        [slope, w_in_near, cot_near, came_near],
        "vvvv",
    )
    pieces = MOST * part // PIECE
    (total,) = call(
        sum_kernel,
        [((devices, pieces, PIECE), bf16)],
        [kept, came],
        "vv",
        [pltpu.VMEM((PIECE // LANES, devices * pieces, LANES), f32)],
    )
    back = lax.all_to_all(total, everyone, split_axis=0, concat_axis=0, tiled=True)
    return call(
        backward_kernel,
        [((frames, blocks, features), bf16)] * 3,
        [spread, back, cot, probs, query, key, value],
        "vvvvvvv",
        [pltpu.VMEM((frames, blocks, features), bf16)] * 3 + [pltpu.SemaphoreType.DMA((3,))],
        "h",
    )


def solution(mesh):
    groups, columns = mesh.devices.shape
    split = Mesh(mesh.devices.reshape(groups, columns // CORES, CORES), ("grp", "z", "core"))
    frm = ("z", "core")
    patches = P(None, ("grp",) + frm, None)
    return jax.shard_map(
        body,
        mesh=split,
        in_specs=(
            patches, patches, patches, P(frm, "grp", None), P("grp", None, frm),
            P("grp", frm, None), P(), P(),
        ),
        out_specs=(patches, patches, patches),
        check_vma=False,
    )
```

```python
import functools

import jax
import jax.numpy as jnp
from jax import lax
from jax.experimental import pallas as pl
from jax.experimental.pallas import tpu as pltpu
from jax.sharding import Mesh
from jax.sharding import PartitionSpec as P

HEADS = 16
MOST = 2
CORES = 2
SUBLANES = 8
LANES = 128
PIECE = 256

root_half = 0.7071067811865476
inv_root_tau = 0.3989422804014327

LANES_BOTH = (((1,), (1,)), ((), ()))
FIRST_BOTH = (((0,), (0,)), ((), ()))


def gelu_slope(pre_act):
    normal_cdf = 0.5 * (1.0 + lax.erf(pre_act * root_half))
    density = jnp.exp(-0.5 * pre_act * pre_act) * inv_root_tau
    return normal_cdf + pre_act * density


def dot(a, b):
    return jnp.dot(a, b, preferred_element_type=jnp.float32)


def dot_lanes(a, b):
    return lax.dot_general(a, b, LANES_BOTH, preferred_element_type=jnp.float32)


def over_frames(values, op, blocks):
    rows = values.shape[0]
    total = values[:SUBLANES]
    for start in range(SUBLANES, rows, SUBLANES):
        total = op(total, values[start : start + SUBLANES])
    step = blocks
    while step < SUBLANES:
        total = op(total, pltpu.roll(total, step, 0))
        step *= 2
    return jnp.concatenate([total] * (rows // SUBLANES), axis=0)


def heads_of(values):
    width = values.shape[1] // HEADS
    return [values[:, h * width : (h + 1) * width] for h in range(HEADS)]


def turn_kernel(span, cot_hbm, *refs):
    *part_refs, cot_ref, sem = refs
    copy = pltpu.make_async_copy(cot_hbm, cot_ref, sem)
    copy.start()
    level = lax.axis_index("z")
    copy.wait()
    parts = [cot_ref[0, k * span : (k + 1) * span, :] for k in range(len(part_refs))]
    bit = 1
    while bit < len(parts):
        turn = (level // bit) % 2 == 1
        parts = [jnp.where(turn, parts[k ^ bit], parts[k]) for k in range(len(parts))]
        bit *= 2
    for part_ref, part in zip(part_refs, parts):
        part_ref[...] = part


def held_core(level):
    core = lax.axis_index("core")
    return jnp.where(level == 0, core, 1 - core)


def forward_kernel(
    patches_all, share,
    chosen_hbm, gate_hbm, query_hbm, key_hbm, value_hbm, w_in_hbm, w_out_hbm,
    query_rows_ref, key_rows_ref, value_rows_ref, w_in_ref, w_out_ref,
    probs_ref, picked_ref, take_ref, weight_ref, spread_ref,
    chosen_ref, gate_ref, query_ref, key_ref, value_ref, sems,
):
    core = lax.axis_index("core")
    chip = lax.axis_index("grp") * lax.axis_size("z") + lax.axis_index("z")
    part = w_in_ref.shape[0] // CORES
    sources = [chosen_hbm, gate_hbm, query_hbm, key_hbm, value_hbm]
    targets = [chosen_ref, gate_ref, query_ref, key_ref, value_ref]
    for i in range(CORES):
        sources.append(w_in_hbm.at[0, part_of(core ^ i, part)])
        targets.append(w_in_ref.at[pl.ds(i * part, part)])
        sources.append(w_out_hbm.at[0, :, part_of(core ^ i, part)])
        targets.append(w_out_ref.at[:, pl.ds(i * part, part)])
    copies = [
        pltpu.make_async_copy(source, target, sems.at[i])
        for i, (source, target) in enumerate(zip(sources, targets))
    ]
    for copy in copies:
        copy.start()
    frames, blocks, features = query_ref.shape
    rows = frames * blocks
    scaling = (features // HEADS) ** (-0.5)

    for copy in copies[:2]:
        copy.wait()
    experts, cap = chosen_ref.shape
    before = (
        lax.broadcasted_iota(jnp.int32, (cap, cap), 0)
        < lax.broadcasted_iota(jnp.int32, (cap, cap), 1)
    ).astype(jnp.bfloat16)
    slot = lax.broadcasted_iota(jnp.int32, (SUBLANES, cap), 0)
    row_at = lax.broadcasted_iota(jnp.int32, (rows, cap), 0)
    span = CORES * blocks
    slots = experts * MOST
    found = []
    for e in range(experts):
        tokens = chosen_ref[e : e + 1, :]
        gates = gate_ref[e : e + 1, :]
        patch = tokens % patches_all
        frame = tokens // patches_all
        level = (frame // CORES) ^ lax.axis_index("z")
        for i in range(CORES):
            owned = patch // blocks == chip * CORES + (core ^ i)
            owned = jnp.broadcast_to(owned.astype(jnp.float32), slot.shape)
            rank = dot(owned.astype(jnp.bfloat16), before)
            taken = jnp.where((rank == slot.astype(jnp.float32)) & (owned > 0.0), 1.0, 0.0)
            weight = jnp.sum(taken * gates, axis=1, keepdims=True)
            taken = taken.astype(jnp.bfloat16)
            place = jnp.where(
                frame % CORES == held_core(level),
                level * span + (core ^ i) * blocks + patch % blocks,
                -1,
            )
            at = slice(i * slots + e * MOST, i * slots + (e + 1) * MOST)
            take_ref[at] = dot_lanes(taken, (row_at == place).astype(jnp.bfloat16))[:MOST]
            weight_ref[at] = jnp.broadcast_to(weight[:MOST], (MOST, weight_ref.shape[1]))
            if i == 0:
                position = frame * blocks + patch % blocks
                found.append(dot_lanes(taken, (row_at == position).astype(jnp.bfloat16))[:MOST])
    levels = rows // span
    want = lax.broadcasted_iota(jnp.int32, (levels * blocks, rows), 0)
    have = lax.broadcasted_iota(jnp.int32, (levels * blocks, rows), 1)
    source = (want // blocks) * span + (core ^ 1) * blocks + want % blocks
    take_ref[CORES * slots :] = (source == have).astype(jnp.float32)
    here = jnp.concatenate(found, axis=0).astype(jnp.bfloat16)
    pieces = spread_ref.shape[0] // (rows * CORES)
    returns = spread_ref.shape[1]
    slot_at = lax.broadcasted_iota(jnp.int32, (slots, returns), 0)
    back_at = lax.broadcasted_iota(jnp.int32, (slots, returns), 1) // pieces
    levels, groups = lax.axis_size("z"), lax.axis_size("grp")
    expert_of = back_at // MOST // levels % groups // share
    same = (expert_of == slot_at // MOST) & (back_at % MOST == slot_at % MOST)
    back = lax.dot_general(
        here, same.astype(jnp.bfloat16), FIRST_BOTH, preferred_element_type=jnp.float32
    )
    back_at = lax.broadcasted_iota(jnp.int32, (rows, returns), 1)
    piece = back_at // (MOST * pieces * levels * groups) * pieces + back_at % pieces
    for j in range(CORES * pieces):
        spread_ref[j * rows : (j + 1) * rows, :] = jnp.where(piece == j, back, 0.0).astype(
            jnp.bfloat16
        )

    for copy in copies[2:5]:
        copy.wait()
    query = query_ref[...].reshape(rows, features)
    key = key_ref[...].reshape(rows, features)
    value = value_ref[...].reshape(rows, features)
    query_rows_ref[...] = query
    key_rows_ref[...] = key
    value_rows_ref[...] = value
    scores = jnp.concatenate(
        [dot_lanes(k, q) for k, q in zip(heads_of(key), heads_of(query))], axis=1
    )
    scores = scores * scaling
    raised = jnp.exp(scores - over_frames(scores, jnp.maximum, blocks))
    probs = raised / over_frames(raised, jnp.add, blocks)
    patch_in = lax.broadcasted_iota(jnp.int32, probs.shape, 0) % blocks
    patch_out = lax.broadcasted_iota(jnp.int32, probs.shape, 1) % blocks
    probs = jnp.where(patch_in == patch_out, probs, 0.0)
    probs_ref[...] = probs
    weights = probs.T.astype(jnp.bfloat16)
    mixed = jnp.concatenate(
        [dot(weights[h * rows : (h + 1) * rows], v) for h, v in enumerate(heads_of(value))],
        axis=1,
    ).astype(jnp.bfloat16)
    picked_ref[...] = dot(here, mixed).astype(jnp.bfloat16)
    for copy in copies[5:]:
        copy.wait()


def pick_kernel(order, take_ref, weight_ref, *refs):
    *part_refs, cot_ref, mine_ref, sent_ref = refs
    parts = [part_refs[order.index(k)][...] for k in range(len(order))]
    cot = jnp.concatenate(parts, axis=0)
    cot_ref[...] = cot
    slots = mine_ref.shape[0]
    rows = dot(take_ref[...].astype(jnp.bfloat16), cot)
    picks = (rows[: CORES * slots] * weight_ref[:, :1]).astype(jnp.bfloat16)
    mine_ref[...] = picks[:slots]
    away = rows[CORES * slots :].astype(jnp.bfloat16)
    sent_ref[...] = jnp.concatenate([away, picks[slots:]], axis=0)


def pack_kernel(share, picked_ref, mine_ref, came_ref, out_ref):
    levels = lax.axis_size("z")
    slots, features = mine_ref.shape
    rows = mine_ref[...] + came_ref[came_ref.shape[0] - slots :, :]
    part = features // CORES
    picked = picked_ref[...]
    both = [
        jnp.concatenate(
            [half[:, c * part : (c + 1) * part] for half in (picked, rows)], axis=1
        )
        for c in range(CORES)
    ]
    for i in range(out_ref.shape[0]):
        e = i // (CORES * levels) // share
        out_ref[i] = both[i % CORES][e * MOST : (e + 1) * MOST]


def part_of(part, width):
    return pl.ds(pl.multiple_of(part * width, width), width)


def first_kernel(near_ref, w_in_ref, w_out_ref, pre_ref, back_ref):
    width = w_in_ref.shape[0] // CORES
    rows = near_ref[...].reshape(pre_ref.shape[0], CORES * width)
    pre_ref[...] = dot(rows[:, :width], w_in_ref[:width, :])
    back_ref[...] = dot_lanes(rows[:, width:], w_out_ref[:, :width])


def second_kernel(far_ref, pre_ref, back_ref, w_in_ref, w_out_ref, slope_ref, sent_ref):
    width = w_in_ref.shape[0] // CORES
    far = far_ref[...].reshape(pre_ref.shape[0], CORES * width)
    pre_act = pre_ref[...] + dot(far[:, :width], w_in_ref[width:, :])
    back_act = back_ref[...] + dot_lanes(far[:, width:], w_out_ref[:, width:])
    slope = (back_act * gelu_slope(pre_act)).astype(jnp.bfloat16)
    slope_ref[...] = slope
    sent_ref[...] = dot_lanes(slope, w_in_ref[width:, :]).astype(jnp.bfloat16)


def third_kernel(blocks, slope_ref, w_in_ref, near_ref, came_ref, kept_ref, cot_ref):
    rows = near_ref.shape[0]
    span = CORES * blocks
    levels = rows // span
    want = lax.broadcasted_iota(jnp.int32, (rows, rows), 0)
    have = lax.broadcasted_iota(jnp.int32, (rows, rows), 1)
    frame = want // blocks
    level = (frame // CORES) ^ lax.axis_index("z")
    here = frame % CORES == held_core(level)
    source = level * span + lax.axis_index("core") * blocks + want % blocks
    own = (here & (source == have)).astype(jnp.bfloat16)
    source = level * blocks + want % blocks
    others = (jnp.logical_not(here) & (source == have)).astype(jnp.bfloat16)
    others = others[:, : levels * blocks]
    cot = dot(own, near_ref[...])
    cot = cot + dot(others, came_ref[: levels * blocks, :])
    cot_ref[...] = cot.astype(jnp.bfloat16)
    width = kept_ref.shape[1]
    kept_ref[...] = dot_lanes(slope_ref[...], w_in_ref[:width, :])


def sum_kernel(kept_ref, came_ref, out_ref, piece_ref):
    total = kept_ref[...] + came_ref[...].astype(jnp.float32)
    count, width = total.shape
    pieces = width // PIECE
    parts = piece_ref.shape[0]
    for j in range(pieces):
        for i in range(parts):
            start = j * PIECE + i * LANES
            piece_ref[i, pl.ds(j, count, stride=pieces), :] = total[:, start : start + LANES]
    total = jnp.concatenate([piece_ref[i] for i in range(parts)], axis=1)
    devices, pieces, _ = out_ref.shape
    total = total.astype(jnp.bfloat16).reshape(devices // CORES, CORES, pieces, PIECE)
    for c in range(CORES):
        out_ref[c * (devices // CORES) : (c + 1) * (devices // CORES)] = total[:, c]


def backward_kernel(
    spread_ref, back_ref, cot_ref, probs_ref, query_ref, key_ref, value_ref,
    grad_query_hbm, grad_key_hbm, grad_value_hbm,
    grad_query_ref, grad_key_ref, grad_value_ref, sems,
):
    frames, blocks, features = grad_query_ref.shape
    rows = frames * blocks
    scaling = (features // HEADS) ** (-0.5)
    query, key, value = query_ref[...], key_ref[...], value_ref[...]
    back = dot(spread_ref[...], back_ref[...].reshape(-1, PIECE))
    added = jnp.concatenate(
        [back[start : start + rows] for start in range(0, back.shape[0], rows)], axis=1
    )
    stream = (cot_ref[...].astype(jnp.float32) + added).astype(jnp.bfloat16)
    probs = probs_ref[...]
    weights = probs.astype(jnp.bfloat16)
    copies = []

    def put(ref, hbm, parts):
        joined = jnp.concatenate(parts, axis=1).astype(jnp.bfloat16)
        ref[...] = joined.reshape(frames, blocks, features)
        copy = pltpu.make_async_copy(ref, hbm, sems.at[len(copies)])
        copy.start()
        copies.append(copy)

    grad_prob = jnp.concatenate(
        [dot_lanes(v, g) for v, g in zip(heads_of(value), heads_of(stream))], axis=1
    )
    put(
        grad_value_ref,
        grad_value_hbm,
        [dot(w, g) for w, g in zip(heads_of(weights), heads_of(stream))],
    )
    centre = over_frames(probs * grad_prob, jnp.add, blocks)
    grad_score = probs * (grad_prob - centre)
    turned = grad_score.T.astype(jnp.bfloat16)
    grad_score = grad_score.astype(jnp.bfloat16)
    put(
        grad_key_ref,
        grad_key_hbm,
        [dot(s, q) * scaling for s, q in zip(heads_of(grad_score), heads_of(query))],
    )
    put(
        grad_query_ref,
        grad_query_hbm,
        [dot(turned[h * rows : (h + 1) * rows], k) * scaling for h, k in enumerate(heads_of(key))],
    )
    for copy in copies:
        copy.wait()


def call(kernel, outs, operands, places, scratch=(), results="v"):
    spaces = {
        "v": pl.BlockSpec(memory_space=pltpu.VMEM),
        "h": pl.BlockSpec(memory_space=pl.ANY),
    }
    return pl.pallas_call(
        kernel,
        out_shape=[jax.ShapeDtypeStruct(shape, dtype) for shape, dtype in outs],
        in_specs=[spaces[place] for place in places],
        out_specs=[spaces[results]] * len(outs),
        scratch_shapes=list(scratch),
        compiler_params=pltpu.CompilerParams(vmem_limit_bytes=32 * 1024 * 1024),
    )(*[
        pltpu.with_memory_space_constraint(operand, pltpu.HBM) if place == "h" else operand
        for operand, place in zip(operands, places)
    ])


def body(query_in, key_in, value_in, cotangent, w_in, w_out, gate_probs, chosen):
    bf16, f32 = jnp.bfloat16, jnp.float32
    frames, blocks, features = query_in.shape
    groups = lax.axis_size("grp")
    levels = lax.axis_size("z")
    columns = levels * CORES
    experts = gate_probs.shape[0]
    devices = groups * columns
    share = groups // experts
    rows = frames * blocks
    slots = experts * MOST
    part = features // CORES
    hidden = w_in.shape[2]

    def swap(values):
        return lax.ppermute(values, "core", [(i, i ^ 1) for i in range(CORES)])

    def across(values, step):
        pairs = [(i, i ^ (CORES * step) ^ 1) for i in range(columns)]
        return lax.ppermute(values, ("z", "core"), pairs)

    span = CORES * blocks
    parts = call(
        functools.partial(turn_kernel, span),
        [((span, features), bf16)] * levels,
        [cotangent],
        "h",
        [pltpu.VMEM(cotangent.shape, bf16), pltpu.SemaphoreType.DMA],
    )
    order = [0] + [i ^ (i >> 1) for i in range(levels - 1, 0, -1)]
    parts = [across(parts[k], k) if k else parts[k] for k in order]
    query, key, value, w_in_near, w_out_near, probs, picked, take, weight, spread = call(
        functools.partial(forward_kernel, blocks * devices, share),
        [
            *[((rows, features), bf16)] * 3,
            (w_in.shape[1:], bf16),
            (w_out.shape[1:], bf16),
            ((rows, HEADS * rows), f32),
            ((slots, features), bf16),
            ((CORES * slots + levels * blocks, rows), f32),
            ((CORES * slots, LANES), f32),
            ((rows * features // PIECE, devices * MOST * part // PIECE), bf16),
        ],
        [chosen, gate_probs, query_in, key_in, value_in, w_in, w_out],
        "hhhhhhh",
        [
            pltpu.VMEM(chosen.shape, jnp.int32),
            pltpu.VMEM(gate_probs.shape, f32),
            *[pltpu.VMEM(query_in.shape, bf16)] * 3,
            pltpu.SemaphoreType.DMA((5 + 2 * CORES,)),
        ],
    )
    cot_near, mine, sent = call(
        functools.partial(pick_kernel, order),
        [((rows, features), bf16), ((slots, features), bf16), ((levels * blocks + slots, features), bf16)],
        [take, weight, *parts],
        "vv" + "v" * levels,
    )
    came_near = swap(sent)
    (outgoing,) = call(
        functools.partial(pack_kernel, share),
        [((devices, MOST, 2 * part), bf16)],
        [picked, mine, came_near],
        "vvv",
    )
    held = lax.all_to_all(outgoing, ("grp", "z", "core"), split_axis=0, concat_axis=0, tiled=True)
    other = swap(held)
    acts = (devices * MOST, hidden)
    halves = (devices * MOST, part)
    pre_act, back_act = call(
        first_kernel, [(acts, f32), (acts, f32)], [held, w_in_near, w_out_near], "vvv"
    )
    slope, sent = call(
        second_kernel,
        [(acts, bf16), (halves, bf16)],
        [other, pre_act, back_act, w_in_near, w_out_near],
        "vvvvv",
    )
    came = swap(sent)
    kept, cot = call(
        functools.partial(third_kernel, blocks),
        [(halves, f32), ((rows, features), bf16)],
        [slope, w_in_near, cot_near, came_near],
        "vvvv",
    )
    pieces = MOST * part // PIECE
    (total,) = call(
        sum_kernel,
        [((devices, pieces, PIECE), bf16)],
        [kept, came],
        "vv",
        [pltpu.VMEM((PIECE // LANES, devices * pieces, LANES), f32)],
    )
    back = lax.all_to_all(total, ("core", "grp", "z"), split_axis=0, concat_axis=0, tiled=True)
    return call(
        backward_kernel,
        [((frames, blocks, features), bf16)] * 3,
        [spread, back, cot, probs, query, key, value],
        "vvvvvvv",
        [pltpu.VMEM((frames, blocks, features), bf16)] * 3 + [pltpu.SemaphoreType.DMA((3,))],
        "h",
    )


def solution(mesh):
    groups, columns = mesh.devices.shape
    split = Mesh(mesh.devices.reshape(groups, columns // CORES, CORES), ("grp", "z", "core"))
    frm = ("z", "core")
    patches = P(None, ("grp",) + frm, None)
    return jax.shard_map(
        body,
        mesh=split,
        in_specs=(
            patches, patches, patches, P(frm, "grp", None), P("grp", None, frm),
            P("grp", frm, None), P(), P(),
        ),
        out_specs=(patches, patches, patches),
        check_vma=False,
    )
```

```python
import functools

import jax
import jax.numpy as jnp
from jax import lax
from jax.experimental import pallas as pl
from jax.experimental.pallas import tpu as pltpu
from jax.sharding import Mesh
from jax.sharding import PartitionSpec as P

HEADS = 16
MOST = 2
CORES = 2
SUBLANES = 8
LANES = 128
PIECE = 256

root_half = 0.7071067811865476
inv_root_tau = 0.3989422804014327

LANES_BOTH = (((1,), (1,)), ((), ()))
FIRST_BOTH = (((0,), (0,)), ((), ()))


def gelu_slope(pre_act):
    normal_cdf = 0.5 * (1.0 + lax.erf(pre_act * root_half))
    density = jnp.exp(-0.5 * pre_act * pre_act) * inv_root_tau
    return normal_cdf + pre_act * density


def dot(a, b):
    return jnp.dot(a, b, preferred_element_type=jnp.float32)


def dot_lanes(a, b):
    return lax.dot_general(a, b, LANES_BOTH, preferred_element_type=jnp.float32)


def over_frames(values, op, blocks):
    rows = values.shape[0]
    total = values[:SUBLANES]
    for start in range(SUBLANES, rows, SUBLANES):
        total = op(total, values[start : start + SUBLANES])
    step = blocks
    while step < SUBLANES:
        total = op(total, pltpu.roll(total, step, 0))
        step *= 2
    return jnp.concatenate([total] * (rows // SUBLANES), axis=0)


def heads_of(values):
    width = values.shape[1] // HEADS
    return [values[:, h * width : (h + 1) * width] for h in range(HEADS)]


def turn_kernel(span, cot_hbm, *refs):
    *part_refs, cot_ref, sem = refs
    copy = pltpu.make_async_copy(cot_hbm, cot_ref, sem)
    copy.start()
    level = lax.axis_index("z")
    copy.wait()
    parts = [cot_ref[0, k * span : (k + 1) * span, :] for k in range(len(part_refs))]
    bit = 1
    while bit < len(parts):
        turn = (level // bit) % 2 == 1
        parts = [jnp.where(turn, parts[k ^ bit], parts[k]) for k in range(len(parts))]
        bit *= 2
    for part_ref, part in zip(part_refs, parts):
        part_ref[...] = part


def held_core(level):
    core = lax.axis_index("core")
    return jnp.where(level == 0, core, 1 - core)


def forward_kernel(
    patches_all, share,
    chosen_hbm, gate_hbm, query_hbm, key_hbm, value_hbm, w_in_hbm, w_out_hbm,
    query_rows_ref, key_rows_ref, value_rows_ref, w_in_ref, w_out_ref,
    probs_ref, picked_ref, take_ref, weight_ref, spread_ref,
    chosen_ref, gate_ref, query_ref, key_ref, value_ref, sems,
):
    core = lax.axis_index("core")
    chip = lax.axis_index("grp") * lax.axis_size("z") + lax.axis_index("z")
    part = w_in_ref.shape[0] // CORES
    sources = [chosen_hbm, gate_hbm, query_hbm, key_hbm, value_hbm]
    targets = [chosen_ref, gate_ref, query_ref, key_ref, value_ref]
    for i in range(CORES):
        sources.append(w_in_hbm.at[0, part_of(core ^ i, part)])
        targets.append(w_in_ref.at[pl.ds(i * part, part)])
        sources.append(w_out_hbm.at[0, :, part_of(core ^ i, part)])
        targets.append(w_out_ref.at[:, pl.ds(i * part, part)])
    copies = [
        pltpu.make_async_copy(source, target, sems.at[i])
        for i, (source, target) in enumerate(zip(sources, targets))
    ]
    for copy in copies:
        copy.start()
    frames, blocks, features = query_ref.shape
    rows = frames * blocks
    scaling = (features // HEADS) ** (-0.5)

    for copy in copies[:2]:
        copy.wait()
    experts, cap = chosen_ref.shape
    before = (
        lax.broadcasted_iota(jnp.int32, (cap, cap), 0)
        < lax.broadcasted_iota(jnp.int32, (cap, cap), 1)
    ).astype(jnp.bfloat16)
    slot = lax.broadcasted_iota(jnp.int32, (SUBLANES, cap), 0)
    row_at = lax.broadcasted_iota(jnp.int32, (rows, cap), 0)
    span = CORES * blocks
    slots = experts * MOST
    found = []
    for e in range(experts):
        tokens = chosen_ref[e : e + 1, :]
        gates = gate_ref[e : e + 1, :]
        patch = tokens % patches_all
        frame = tokens // patches_all
        level = (frame // CORES) ^ lax.axis_index("z")
        for i in range(CORES):
            owned = patch // blocks == chip * CORES + (core ^ i)
            owned = jnp.broadcast_to(owned.astype(jnp.float32), slot.shape)
            rank = dot(owned.astype(jnp.bfloat16), before)
            taken = jnp.where((rank == slot.astype(jnp.float32)) & (owned > 0.0), 1.0, 0.0)
            weight = jnp.sum(taken * gates, axis=1, keepdims=True)
            taken = taken.astype(jnp.bfloat16)
            place = jnp.where(
                frame % CORES == held_core(level),
                level * span + (core ^ i) * blocks + patch % blocks,
                -1,
            )
            at = slice(i * slots + e * MOST, i * slots + (e + 1) * MOST)
            take_ref[at] = dot_lanes(taken, (row_at == place).astype(jnp.bfloat16))[:MOST]
            weight_ref[at] = jnp.broadcast_to(weight[:MOST], (MOST, weight_ref.shape[1]))
            if i == 0:
                position = frame * blocks + patch % blocks
                found.append(dot_lanes(taken, (row_at == position).astype(jnp.bfloat16))[:MOST])
    levels = rows // span
    want = lax.broadcasted_iota(jnp.int32, (levels * blocks, rows), 0)
    have = lax.broadcasted_iota(jnp.int32, (levels * blocks, rows), 1)
    source = (want // blocks) * span + (core ^ 1) * blocks + want % blocks
    take_ref[CORES * slots :] = (source == have).astype(jnp.float32)
    here = jnp.concatenate(found, axis=0).astype(jnp.bfloat16)
    pieces = spread_ref.shape[0] // (rows * CORES)
    returns = spread_ref.shape[1]
    slot_at = lax.broadcasted_iota(jnp.int32, (slots, returns), 0)
    back_at = lax.broadcasted_iota(jnp.int32, (slots, returns), 1) // pieces
    levels, groups = lax.axis_size("z"), lax.axis_size("grp")
    expert_of = back_at // MOST // levels % groups // share
    same = (expert_of == slot_at // MOST) & (back_at % MOST == slot_at % MOST)
    back = lax.dot_general(
        here, same.astype(jnp.bfloat16), FIRST_BOTH, preferred_element_type=jnp.float32
    )
    back_at = lax.broadcasted_iota(jnp.int32, (rows, returns), 1)
    piece = back_at // (MOST * pieces * levels * groups) * pieces + back_at % pieces
    for j in range(CORES * pieces):
        spread_ref[j * rows : (j + 1) * rows, :] = jnp.where(piece == j, back, 0.0).astype(
            jnp.bfloat16
        )

    for copy in copies[2:5]:
        copy.wait()
    query = query_ref[...].reshape(rows, features)
    key = key_ref[...].reshape(rows, features)
    value = value_ref[...].reshape(rows, features)
    query_rows_ref[...] = query
    key_rows_ref[...] = key
    value_rows_ref[...] = value
    scores = jnp.concatenate(
        [dot_lanes(k, q) for k, q in zip(heads_of(key), heads_of(query))], axis=1
    )
    scores = scores * scaling
    raised = jnp.exp(scores - over_frames(scores, jnp.maximum, blocks))
    probs = raised / over_frames(raised, jnp.add, blocks)
    patch_in = lax.broadcasted_iota(jnp.int32, probs.shape, 0) % blocks
    patch_out = lax.broadcasted_iota(jnp.int32, probs.shape, 1) % blocks
    probs = jnp.where(patch_in == patch_out, probs, 0.0)
    probs_ref[...] = probs
    weights = probs.T.astype(jnp.bfloat16)
    mixed = jnp.concatenate(
        [dot(weights[h * rows : (h + 1) * rows], v) for h, v in enumerate(heads_of(value))],
        axis=1,
    ).astype(jnp.bfloat16)
    picked_ref[...] = dot(here, mixed).astype(jnp.bfloat16)
    for copy in copies[5:]:
        copy.wait()


def pick_kernel(order, take_ref, weight_ref, *refs):
    *part_refs, cot_ref, mine_ref, sent_ref, away_ref = refs
    parts = [part_refs[order.index(k)][...] for k in range(len(order))]
    cot = jnp.concatenate(parts, axis=0)
    cot_ref[...] = cot
    slots = mine_ref.shape[0]
    rows = dot(take_ref[...].astype(jnp.bfloat16), cot)
    picks = (rows[: CORES * slots] * weight_ref[:, :1]).astype(jnp.bfloat16)
    mine_ref[...] = picks[:slots]
    sent_ref[...] = picks[slots:]
    away_ref[...] = rows[CORES * slots :].astype(jnp.bfloat16)


def pack_kernel(share, picked_ref, mine_ref, came_ref, out_ref):
    levels, groups = lax.axis_size("z"), lax.axis_size("grp")
    slots, features = mine_ref.shape
    rows = mine_ref[...] + came_ref[...]
    part = features // CORES
    picked = picked_ref[...]
    both = [
        jnp.concatenate(
            [half[:, c * part : (c + 1) * part] for half in (picked, rows)], axis=1
        )
        for c in range(CORES)
    ]
    for i in range(out_ref.shape[0]):
        e = i // levels % groups // share
        out_ref[i] = both[i // (levels * groups)][e * MOST : (e + 1) * MOST]


def part_of(part, width):
    return pl.ds(pl.multiple_of(part * width, width), width)


def first_kernel(near_ref, w_in_ref, w_out_ref, away_ref, pre_ref, back_ref, later_ref):
    later_ref[...] = away_ref[...]
    width = w_in_ref.shape[0] // CORES
    rows = near_ref[...].reshape(pre_ref.shape[0], CORES * width)
    pre_ref[...] = dot(rows[:, :width], w_in_ref[:width, :])
    back_ref[...] = dot_lanes(rows[:, width:], w_out_ref[:, :width])


def second_kernel(far_ref, pre_ref, back_ref, w_in_ref, w_out_ref, slope_ref, sent_ref):
    width = w_in_ref.shape[0] // CORES
    far = far_ref[...].reshape(pre_ref.shape[0], CORES * width)
    pre_act = pre_ref[...] + dot(far[:, :width], w_in_ref[width:, :])
    back_act = back_ref[...] + dot_lanes(far[:, width:], w_out_ref[:, width:])
    slope = (back_act * gelu_slope(pre_act)).astype(jnp.bfloat16)
    slope_ref[...] = slope
    sent_ref[...] = dot_lanes(slope, w_in_ref[width:, :]).astype(jnp.bfloat16)


def cot_kernel(blocks, near_ref, came_ref, after_ref, cot_ref):
    rows = near_ref.shape[0]
    span = CORES * blocks
    levels = rows // span
    want = lax.broadcasted_iota(jnp.int32, (rows, rows), 0)
    have = lax.broadcasted_iota(jnp.int32, (rows, rows), 1)
    frame = want // blocks
    level = (frame // CORES) ^ lax.axis_index("z")
    here = frame % CORES == held_core(level)
    source = level * span + lax.axis_index("core") * blocks + want % blocks
    own = (here & (source == have)).astype(jnp.bfloat16)
    source = level * blocks + want % blocks
    others = (jnp.logical_not(here) & (source == have)).astype(jnp.bfloat16)
    others = others[:, : levels * blocks]
    cot = dot(own, near_ref[...])
    cot = cot + dot(others, came_ref[: levels * blocks, :])
    cot_ref[...] = cot.astype(jnp.bfloat16)


def third_kernel(slope_ref, w_in_ref, kept_ref):
    width = kept_ref.shape[1]
    kept_ref[...] = dot_lanes(slope_ref[...], w_in_ref[:width, :])


def sum_kernel(kept_ref, came_ref, out_ref, piece_ref):
    total = kept_ref[...] + came_ref[...].astype(jnp.float32)
    count, width = total.shape
    pieces = width // PIECE
    parts = piece_ref.shape[0]
    for j in range(pieces):
        for i in range(parts):
            start = j * PIECE + i * LANES
            piece_ref[i, pl.ds(j, count, stride=pieces), :] = total[:, start : start + LANES]
    total = jnp.concatenate([piece_ref[i] for i in range(parts)], axis=1)
    out_ref[...] = total.astype(jnp.bfloat16).reshape(out_ref.shape)


def backward_kernel(
    spread_ref, back_ref, cot_ref, probs_ref, query_ref, key_ref, value_ref,
    grad_query_hbm, grad_key_hbm, grad_value_hbm,
    grad_query_ref, grad_key_ref, grad_value_ref, sems,
):
    frames, blocks, features = grad_query_ref.shape
    rows = frames * blocks
    scaling = (features // HEADS) ** (-0.5)
    query, key, value = query_ref[...], key_ref[...], value_ref[...]
    back = dot(spread_ref[...], back_ref[...].reshape(-1, PIECE))
    added = jnp.concatenate(
        [back[start : start + rows] for start in range(0, back.shape[0], rows)], axis=1
    )
    stream = (cot_ref[...].astype(jnp.float32) + added).astype(jnp.bfloat16)
    probs = probs_ref[...]
    weights = probs.astype(jnp.bfloat16)
    copies = []

    def put(ref, hbm, parts):
        joined = jnp.concatenate(parts, axis=1).astype(jnp.bfloat16)
        ref[...] = joined.reshape(frames, blocks, features)
        copy = pltpu.make_async_copy(ref, hbm, sems.at[len(copies)])
        copy.start()
        copies.append(copy)

    grad_prob = jnp.concatenate(
        [dot_lanes(v, g) for v, g in zip(heads_of(value), heads_of(stream))], axis=1
    )
    put(
        grad_value_ref,
        grad_value_hbm,
        [dot(w, g) for w, g in zip(heads_of(weights), heads_of(stream))],
    )
    centre = over_frames(probs * grad_prob, jnp.add, blocks)
    grad_score = probs * (grad_prob - centre)
    turned = grad_score.T.astype(jnp.bfloat16)
    grad_score = grad_score.astype(jnp.bfloat16)
    put(
        grad_key_ref,
        grad_key_hbm,
        [dot(s, q) * scaling for s, q in zip(heads_of(grad_score), heads_of(query))],
    )
    put(
        grad_query_ref,
        grad_query_hbm,
        [dot(turned[h * rows : (h + 1) * rows], k) * scaling for h, k in enumerate(heads_of(key))],
    )
    for copy in copies:
        copy.wait()


def call(kernel, outs, operands, places, scratch=(), results="v"):
    spaces = {
        "v": pl.BlockSpec(memory_space=pltpu.VMEM),
        "h": pl.BlockSpec(memory_space=pl.ANY),
    }
    return pl.pallas_call(
        kernel,
        out_shape=[jax.ShapeDtypeStruct(shape, dtype) for shape, dtype in outs],
        in_specs=[spaces[place] for place in places],
        out_specs=[spaces[results]] * len(outs),
        scratch_shapes=list(scratch),
        compiler_params=pltpu.CompilerParams(vmem_limit_bytes=32 * 1024 * 1024),
    )(*[
        pltpu.with_memory_space_constraint(operand, pltpu.HBM) if place == "h" else operand
        for operand, place in zip(operands, places)
    ])


def body(query_in, key_in, value_in, cotangent, w_in, w_out, gate_probs, chosen):
    bf16, f32 = jnp.bfloat16, jnp.float32
    frames, blocks, features = query_in.shape
    groups = lax.axis_size("grp")
    levels = lax.axis_size("z")
    columns = levels * CORES
    experts = gate_probs.shape[0]
    devices = groups * columns
    share = groups // experts
    rows = frames * blocks
    slots = experts * MOST
    part = features // CORES
    hidden = w_in.shape[2]
    everyone = ("core", "grp", "z")

    def swap(values):
        return lax.ppermute(values, "core", [(i, i ^ 1) for i in range(CORES)])

    def across(values, step):
        pairs = [(i, i ^ (CORES * step) ^ 1) for i in range(columns)]
        return lax.ppermute(values, ("z", "core"), pairs)

    span = CORES * blocks
    parts = call(
        functools.partial(turn_kernel, span),
        [((span, features), bf16)] * levels,
        [cotangent],
        "h",
        [pltpu.VMEM(cotangent.shape, bf16), pltpu.SemaphoreType.DMA],
    )
    order = [0] + [i ^ (i >> 1) for i in range(levels - 1, 0, -1)]
    parts = [across(parts[k], k) if k else parts[k] for k in order]
    query, key, value, w_in_near, w_out_near, probs, picked, take, weight, spread = call(
        functools.partial(forward_kernel, blocks * devices, share),
        [
            *[((rows, features), bf16)] * 3,
            (w_in.shape[1:], bf16),
            (w_out.shape[1:], bf16),
            ((rows, HEADS * rows), f32),
            ((slots, features), bf16),
            ((CORES * slots + levels * blocks, rows), f32),
            ((CORES * slots, LANES), f32),
            ((rows * features // PIECE, devices * MOST * part // PIECE), bf16),
        ],
        [chosen, gate_probs, query_in, key_in, value_in, w_in, w_out],
        "hhhhhhh",
        [
            pltpu.VMEM(chosen.shape, jnp.int32),
            pltpu.VMEM(gate_probs.shape, f32),
            *[pltpu.VMEM(query_in.shape, bf16)] * 3,
            pltpu.SemaphoreType.DMA((5 + 2 * CORES,)),
        ],
    )
    cot_near, mine, sent, away = call(
        functools.partial(pick_kernel, order),
        [
            ((rows, features), bf16),
            ((slots, features), bf16),
            ((slots, features), bf16),
            ((levels * blocks, features), bf16),
        ],
        [take, weight, *parts],
        "vv" + "v" * levels,
    )
    came_picks = swap(sent)
    (outgoing,) = call(
        functools.partial(pack_kernel, share),
        [((devices, MOST, 2 * part), bf16)],
        [picked, mine, came_picks],
        "vvv",
    )
    held = lax.all_to_all(outgoing, everyone, split_axis=0, concat_axis=0, tiled=True)
    other = swap(held)
    acts = (devices * MOST, hidden)
    halves = (devices * MOST, part)
    pre_act, back_act, away = call(
        first_kernel,
        [(acts, f32), (acts, f32), ((levels * blocks, features), bf16)],
        [held, w_in_near, w_out_near, away],
        "vvvv",
    )
    came_near = swap(away)
    slope, sent = call(
        second_kernel,
        [(acts, bf16), (halves, bf16)],
        [other, pre_act, back_act, w_in_near, w_out_near],
        "vvvvv",
    )
    came = swap(sent)
    (kept,) = call(third_kernel, [(halves, f32)], [slope, w_in_near], "vv")
    (cot,) = call(
        functools.partial(cot_kernel, blocks),
        [((rows, features), bf16)],
        [cot_near, came_near, kept],
        "vvv",
    )
    pieces = MOST * part // PIECE
    (total,) = call(
        sum_kernel,
        [((devices, pieces, PIECE), bf16)],
        [kept, came],
        "vv",
        [pltpu.VMEM((PIECE // LANES, devices * pieces, LANES), f32)],
    )
    back = lax.all_to_all(total, everyone, split_axis=0, concat_axis=0, tiled=True)
    return call(
        backward_kernel,
        [((frames, blocks, features), bf16)] * 3,
        [spread, back, cot, probs, query, key, value],
        "vvvvvvv",
        [pltpu.VMEM((frames, blocks, features), bf16)] * 3 + [pltpu.SemaphoreType.DMA((3,))],
        "h",
    )


def solution(mesh):
    groups, columns = mesh.devices.shape
    split = Mesh(mesh.devices.reshape(groups, columns // CORES, CORES), ("grp", "z", "core"))
    frm = ("z", "core")
    patches = P(None, ("grp",) + frm, None)
    return jax.shard_map(
        body,
        mesh=split,
        in_specs=(
            patches, patches, patches, P(frm, "grp", None), P("grp", None, frm),
            P("grp", frm, None), P(), P(),
        ),
        out_specs=(patches, patches, patches),
        check_vma=False,
    )
```

```python
import functools

import jax
import jax.numpy as jnp
from jax import lax
from jax.experimental import pallas as pl
from jax.experimental.pallas import tpu as pltpu
from jax.sharding import Mesh
from jax.sharding import PartitionSpec as P

HEADS = 16
MOST = 2
CORES = 2
SUBLANES = 8
LANES = 128
PIECE = 256
TILE = 16

root_half = 0.7071067811865476
inv_root_tau = 0.3989422804014327

LANES_BOTH = (((1,), (1,)), ((), ()))
FIRST_BOTH = (((0,), (0,)), ((), ()))


def gelu_slope(pre_act):
    normal_cdf = 0.5 * (1.0 + lax.erf(pre_act * root_half))
    density = jnp.exp(-0.5 * pre_act * pre_act) * inv_root_tau
    return normal_cdf + pre_act * density


def dot(a, b):
    return jnp.dot(a, b, preferred_element_type=jnp.float32)


def dot_lanes(a, b):
    return lax.dot_general(a, b, LANES_BOTH, preferred_element_type=jnp.float32)


def over_frames(values, op, blocks):
    rows = values.shape[0]
    total = values[:SUBLANES]
    for start in range(SUBLANES, rows, SUBLANES):
        total = op(total, values[start : start + SUBLANES])
    step = blocks
    while step < SUBLANES:
        total = op(total, pltpu.roll(total, step, 0))
        step *= 2
    return jnp.concatenate([total] * (rows // SUBLANES), axis=0)


def heads_of(values):
    width = values.shape[1] // HEADS
    return [values[:, h * width : (h + 1) * width] for h in range(HEADS)]


def turn_kernel(span, cot_hbm, *refs):
    *part_refs, cot_ref, sems = refs
    copies = [
        pltpu.make_async_copy(
            cot_hbm.at[:, pl.ds(i * TILE, TILE)], cot_ref.at[:, pl.ds(i * TILE, TILE)], sems.at[i]
        )
        for i in range(cot_ref.shape[1] // TILE)
    ]
    for copy in copies:
        copy.start()
    level = lax.axis_index("z")
    for copy in copies:
        copy.wait()
    parts = [cot_ref[0, k * span : (k + 1) * span, :] for k in range(len(part_refs))]
    bit = 1
    while bit < len(parts):
        turn = (level // bit) % 2 == 1
        parts = [jnp.where(turn, parts[k ^ bit], parts[k]) for k in range(len(parts))]
        bit *= 2
    for part_ref, part in zip(part_refs, parts):
        part_ref[...] = part


def held_core(level):
    core = lax.axis_index("core")
    return jnp.where(level == 0, core, 1 - core)


def forward_kernel(
    patches_all, share,
    chosen_hbm, gate_hbm, query_hbm, key_hbm, value_hbm, w_in_hbm, w_out_hbm,
    query_rows_ref, key_rows_ref, value_rows_ref, w_in_ref, w_out_ref,
    probs_ref, picked_ref, take_ref, weight_ref, spread_ref,
    chosen_ref, gate_ref, query_ref, key_ref, value_ref, sems,
):
    core = lax.axis_index("core")
    chip = lax.axis_index("grp") * lax.axis_size("z") + lax.axis_index("z")
    part = w_in_ref.shape[0] // CORES
    sources = [chosen_hbm, gate_hbm, query_hbm, key_hbm, value_hbm]
    targets = [chosen_ref, gate_ref, query_ref, key_ref, value_ref]
    for i in range(CORES):
        sources.append(w_in_hbm.at[0, part_of(core ^ i, part)])
        targets.append(w_in_ref.at[pl.ds(i * part, part)])
        sources.append(w_out_hbm.at[0, :, part_of(core ^ i, part)])
        targets.append(w_out_ref.at[:, pl.ds(i * part, part)])
    copies = [
        pltpu.make_async_copy(source, target, sems.at[i])
        for i, (source, target) in enumerate(zip(sources, targets))
    ]
    for copy in copies:
        copy.start()
    frames, blocks, features = query_ref.shape
    rows = frames * blocks
    scaling = (features // HEADS) ** (-0.5)

    for copy in copies[:2]:
        copy.wait()
    experts, cap = chosen_ref.shape
    before = (
        lax.broadcasted_iota(jnp.int32, (cap, cap), 0)
        < lax.broadcasted_iota(jnp.int32, (cap, cap), 1)
    ).astype(jnp.bfloat16)
    slot = lax.broadcasted_iota(jnp.int32, (SUBLANES, cap), 0)
    row_at = lax.broadcasted_iota(jnp.int32, (rows, cap), 0)
    span = CORES * blocks
    slots = experts * MOST
    found = []
    for e in range(experts):
        tokens = chosen_ref[e : e + 1, :]
        gates = gate_ref[e : e + 1, :]
        patch = tokens % patches_all
        frame = tokens // patches_all
        level = (frame // CORES) ^ lax.axis_index("z")
        for i in range(CORES):
            owned = patch // blocks == chip * CORES + (core ^ i)
            owned = jnp.broadcast_to(owned.astype(jnp.float32), slot.shape)
            rank = dot(owned.astype(jnp.bfloat16), before)
            taken = jnp.where((rank == slot.astype(jnp.float32)) & (owned > 0.0), 1.0, 0.0)
            weight = jnp.sum(taken * gates, axis=1, keepdims=True)
            taken = taken.astype(jnp.bfloat16)
            place = jnp.where(
                frame % CORES == held_core(level),
                level * span + (core ^ i) * blocks + patch % blocks,
                -1,
            )
            at = slice(i * slots + e * MOST, i * slots + (e + 1) * MOST)
            take_ref[at] = dot_lanes(taken, (row_at == place).astype(jnp.bfloat16))[:MOST]
            weight_ref[at] = jnp.broadcast_to(weight[:MOST], (MOST, weight_ref.shape[1]))
            if i == 0:
                position = frame * blocks + patch % blocks
                found.append(dot_lanes(taken, (row_at == position).astype(jnp.bfloat16))[:MOST])
    levels = rows // span
    want = lax.broadcasted_iota(jnp.int32, (levels * blocks, rows), 0)
    have = lax.broadcasted_iota(jnp.int32, (levels * blocks, rows), 1)
    source = (want // blocks) * span + (core ^ 1) * blocks + want % blocks
    take_ref[CORES * slots :] = (source == have).astype(jnp.float32)
    here = jnp.concatenate(found, axis=0).astype(jnp.bfloat16)
    pieces = spread_ref.shape[0] // (rows * CORES)
    returns = spread_ref.shape[1]
    slot_at = lax.broadcasted_iota(jnp.int32, (slots, returns), 0)
    back_at = lax.broadcasted_iota(jnp.int32, (slots, returns), 1) // pieces
    levels, groups = lax.axis_size("z"), lax.axis_size("grp")
    expert_of = back_at // MOST // levels % groups // share
    same = (expert_of == slot_at // MOST) & (back_at % MOST == slot_at % MOST)
    back = lax.dot_general(
        here, same.astype(jnp.bfloat16), FIRST_BOTH, preferred_element_type=jnp.float32
    )
    back_at = lax.broadcasted_iota(jnp.int32, (rows, returns), 1)
    piece = back_at // (MOST * pieces * levels * groups) * pieces + back_at % pieces
    for j in range(CORES * pieces):
        spread_ref[j * rows : (j + 1) * rows, :] = jnp.where(piece == j, back, 0.0).astype(
            jnp.bfloat16
        )

    for copy in copies[2:5]:
        copy.wait()
    query = query_ref[...].reshape(rows, features)
    key = key_ref[...].reshape(rows, features)
    value = value_ref[...].reshape(rows, features)
    query_rows_ref[...] = query
    key_rows_ref[...] = key
    value_rows_ref[...] = value
    scores = jnp.concatenate(
        [dot_lanes(k, q) for k, q in zip(heads_of(key), heads_of(query))], axis=1
    )
    scores = scores * scaling
    raised = jnp.exp(scores - over_frames(scores, jnp.maximum, blocks))
    probs = raised / over_frames(raised, jnp.add, blocks)
    patch_in = lax.broadcasted_iota(jnp.int32, probs.shape, 0) % blocks
    patch_out = lax.broadcasted_iota(jnp.int32, probs.shape, 1) % blocks
    probs = jnp.where(patch_in == patch_out, probs, 0.0)
    probs_ref[...] = probs
    weights = probs.T.astype(jnp.bfloat16)
    mixed = jnp.concatenate(
        [dot(weights[h * rows : (h + 1) * rows], v) for h, v in enumerate(heads_of(value))],
        axis=1,
    ).astype(jnp.bfloat16)
    picked_ref[...] = dot(here, mixed).astype(jnp.bfloat16)
    for copy in copies[5:]:
        copy.wait()


def pick_kernel(order, take_ref, weight_ref, *refs):
    *part_refs, cot_ref, mine_ref, sent_ref = refs
    parts = [part_refs[order.index(k)][...] for k in range(len(order))]
    cot = jnp.concatenate(parts, axis=0)
    cot_ref[...] = cot
    slots = mine_ref.shape[0]
    rows = dot(take_ref[...].astype(jnp.bfloat16), cot)
    picks = (rows[: CORES * slots] * weight_ref[:, :1]).astype(jnp.bfloat16)
    mine_ref[...] = picks[:slots]
    away = rows[CORES * slots :].astype(jnp.bfloat16)
    sent_ref[...] = jnp.concatenate([away, picks[slots:]], axis=0)


def pack_kernel(share, picked_ref, mine_ref, came_ref, out_ref):
    levels, groups = lax.axis_size("z"), lax.axis_size("grp")
    slots, features = mine_ref.shape
    rows = mine_ref[...] + came_ref[came_ref.shape[0] - slots :, :]
    part = features // CORES
    picked = picked_ref[...]
    both = [
        jnp.concatenate(
            [half[:, c * part : (c + 1) * part] for half in (picked, rows)], axis=1
        )
        for c in range(CORES)
    ]
    for i in range(out_ref.shape[0]):
        e = i // levels % groups // share
        out_ref[i] = both[i // (levels * groups)][e * MOST : (e + 1) * MOST]


def part_of(part, width):
    return pl.ds(pl.multiple_of(part * width, width), width)


def first_kernel(near_ref, w_in_ref, w_out_ref, pre_ref, back_ref):
    width = w_in_ref.shape[0] // CORES
    rows = near_ref[...].reshape(pre_ref.shape[0], CORES * width)
    pre_ref[...] = dot(rows[:, :width], w_in_ref[:width, :])
    back_ref[...] = dot_lanes(rows[:, width:], w_out_ref[:, :width])


def second_kernel(far_ref, pre_ref, back_ref, w_in_ref, w_out_ref, slope_ref, sent_ref):
    width = w_in_ref.shape[0] // CORES
    far = far_ref[...].reshape(pre_ref.shape[0], CORES * width)
    pre_act = pre_ref[...] + dot(far[:, :width], w_in_ref[width:, :])
    back_act = back_ref[...] + dot_lanes(far[:, width:], w_out_ref[:, width:])
    slope = (back_act * gelu_slope(pre_act)).astype(jnp.bfloat16)
    slope_ref[...] = slope
    sent_ref[...] = dot_lanes(slope, w_in_ref[width:, :]).astype(jnp.bfloat16)


def third_kernel(blocks, slope_ref, w_in_ref, near_ref, came_ref, kept_ref, cot_ref):
    rows = near_ref.shape[0]
    span = CORES * blocks
    levels = rows // span
    want = lax.broadcasted_iota(jnp.int32, (rows, rows), 0)
    have = lax.broadcasted_iota(jnp.int32, (rows, rows), 1)
    frame = want // blocks
    level = (frame // CORES) ^ lax.axis_index("z")
    here = frame % CORES == held_core(level)
    source = level * span + lax.axis_index("core") * blocks + want % blocks
    own = (here & (source == have)).astype(jnp.bfloat16)
    source = level * blocks + want % blocks
    others = (jnp.logical_not(here) & (source == have)).astype(jnp.bfloat16)
    others = others[:, : levels * blocks]
    cot = dot(own, near_ref[...])
    cot = cot + dot(others, came_ref[: levels * blocks, :])
    cot_ref[...] = cot.astype(jnp.bfloat16)
    width = kept_ref.shape[1]
    kept_ref[...] = dot_lanes(slope_ref[...], w_in_ref[:width, :])


def sum_kernel(kept_ref, came_ref, out_ref, piece_ref):
    total = kept_ref[...] + came_ref[...].astype(jnp.float32)
    count, width = total.shape
    pieces = width // PIECE
    parts = piece_ref.shape[0]
    for j in range(pieces):
        for i in range(parts):
            start = j * PIECE + i * LANES
            piece_ref[i, pl.ds(j, count, stride=pieces), :] = total[:, start : start + LANES]
    total = jnp.concatenate([piece_ref[i] for i in range(parts)], axis=1)
    out_ref[...] = total.astype(jnp.bfloat16).reshape(out_ref.shape)


def backward_kernel(
    spread_ref, back_ref, cot_ref, probs_ref, query_ref, key_ref, value_ref,
    grad_query_hbm, grad_key_hbm, grad_value_hbm,
    grad_query_ref, grad_key_ref, grad_value_ref, sems,
):
    frames, blocks, features = grad_query_ref.shape
    rows = frames * blocks
    scaling = (features // HEADS) ** (-0.5)
    query, key, value = query_ref[...], key_ref[...], value_ref[...]
    back = dot(spread_ref[...], back_ref[...].reshape(-1, PIECE))
    added = jnp.concatenate(
        [back[start : start + rows] for start in range(0, back.shape[0], rows)], axis=1
    )
    stream = (cot_ref[...].astype(jnp.float32) + added).astype(jnp.bfloat16)
    probs = probs_ref[...]
    weights = probs.astype(jnp.bfloat16)
    copies = []

    def put(ref, hbm, parts):
        joined = jnp.concatenate(parts, axis=1).astype(jnp.bfloat16)
        half = frames // 2
        for i in range(2):
            part = joined[i * half * blocks : (i + 1) * half * blocks]
            ref[i * half : (i + 1) * half] = part.reshape(half, blocks, features)
            at = pl.ds(i * half, half)
            copy = pltpu.make_async_copy(ref.at[at], hbm.at[at], sems.at[len(copies)])
            copy.start()
            copies.append(copy)

    grad_prob = jnp.concatenate(
        [dot_lanes(v, g) for v, g in zip(heads_of(value), heads_of(stream))], axis=1
    )
    put(
        grad_value_ref,
        grad_value_hbm,
        [dot(w, g) for w, g in zip(heads_of(weights), heads_of(stream))],
    )
    centre = over_frames(probs * grad_prob, jnp.add, blocks)
    grad_score = probs * (grad_prob - centre)
    turned = grad_score.T.astype(jnp.bfloat16)
    grad_score = grad_score.astype(jnp.bfloat16)
    put(
        grad_key_ref,
        grad_key_hbm,
        [dot(s, q) * scaling for s, q in zip(heads_of(grad_score), heads_of(query))],
    )
    put(
        grad_query_ref,
        grad_query_hbm,
        [dot(turned[h * rows : (h + 1) * rows], k) * scaling for h, k in enumerate(heads_of(key))],
    )
    for copy in copies:
        copy.wait()


def call(kernel, outs, operands, places, scratch=(), results="v"):
    spaces = {
        "v": pl.BlockSpec(memory_space=pltpu.VMEM),
        "h": pl.BlockSpec(memory_space=pl.ANY),
    }
    return pl.pallas_call(
        kernel,
        out_shape=[jax.ShapeDtypeStruct(shape, dtype) for shape, dtype in outs],
        in_specs=[spaces[place] for place in places],
        out_specs=[spaces[results]] * len(outs),
        scratch_shapes=list(scratch),
        compiler_params=pltpu.CompilerParams(vmem_limit_bytes=32 * 1024 * 1024),
    )(*[
        pltpu.with_memory_space_constraint(operand, pltpu.HBM) if place == "h" else operand
        for operand, place in zip(operands, places)
    ])


def body(query_in, key_in, value_in, cotangent, w_in, w_out, gate_probs, chosen):
    bf16, f32 = jnp.bfloat16, jnp.float32
    frames, blocks, features = query_in.shape
    groups = lax.axis_size("grp")
    levels = lax.axis_size("z")
    columns = levels * CORES
    experts = gate_probs.shape[0]
    devices = groups * columns
    share = groups // experts
    rows = frames * blocks
    slots = experts * MOST
    part = features // CORES
    hidden = w_in.shape[2]
    everyone = ("core", "grp", "z")

    def swap(values):
        return lax.ppermute(values, "core", [(i, i ^ 1) for i in range(CORES)])

    def across(values, step):
        pairs = [(i, i ^ (CORES * step) ^ 1) for i in range(columns)]
        return lax.ppermute(values, ("z", "core"), pairs)

    span = CORES * blocks
    parts = call(
        functools.partial(turn_kernel, span),
        [((span, features), bf16)] * levels,
        [cotangent],
        "h",
        [
            pltpu.VMEM(cotangent.shape, bf16),
            pltpu.SemaphoreType.DMA((cotangent.shape[1] // TILE,)),
        ],
    )
    order = [0] + [i ^ (i >> 1) for i in range(levels - 1, 0, -1)]
    parts = [across(parts[k], k) if k else parts[k] for k in order]
    query, key, value, w_in_near, w_out_near, probs, picked, take, weight, spread = call(
        functools.partial(forward_kernel, blocks * devices, share),
        [
            *[((rows, features), bf16)] * 3,
            (w_in.shape[1:], bf16),
            (w_out.shape[1:], bf16),
            ((rows, HEADS * rows), f32),
            ((slots, features), bf16),
            ((CORES * slots + levels * blocks, rows), f32),
            ((CORES * slots, LANES), f32),
            ((rows * features // PIECE, devices * MOST * part // PIECE), bf16),
        ],
        [chosen, gate_probs, query_in, key_in, value_in, w_in, w_out],
        "hhhhhhh",
        [
            pltpu.VMEM(chosen.shape, jnp.int32),
            pltpu.VMEM(gate_probs.shape, f32),
            *[pltpu.VMEM(query_in.shape, bf16)] * 3,
            pltpu.SemaphoreType.DMA((5 + 2 * CORES,)),
        ],
    )
    cot_near, mine, sent = call(
        functools.partial(pick_kernel, order),
        [((rows, features), bf16), ((slots, features), bf16), ((levels * blocks + slots, features), bf16)],
        [take, weight, *parts],
        "vv" + "v" * levels,
    )
    came_near = swap(sent)
    (outgoing,) = call(
        functools.partial(pack_kernel, share),
        [((devices, MOST, 2 * part), bf16)],
        [picked, mine, came_near],
        "vvv",
    )
    held = lax.all_to_all(outgoing, everyone, split_axis=0, concat_axis=0, tiled=True)
    other = swap(held)
    acts = (devices * MOST, hidden)
    halves = (devices * MOST, part)
    pre_act, back_act = call(
        first_kernel, [(acts, f32), (acts, f32)], [held, w_in_near, w_out_near], "vvv"
    )
    slope, sent = call(
        second_kernel,
        [(acts, bf16), (halves, bf16)],
        [other, pre_act, back_act, w_in_near, w_out_near],
        "vvvvv",
    )
    came = swap(sent)
    kept, cot = call(
        functools.partial(third_kernel, blocks),
        [(halves, f32), ((rows, features), bf16)],
        [slope, w_in_near, cot_near, came_near],
        "vvvv",
    )
    pieces = MOST * part // PIECE
    (total,) = call(
        sum_kernel,
        [((devices, pieces, PIECE), bf16)],
        [kept, came],
        "vv",
        [pltpu.VMEM((PIECE // LANES, devices * pieces, LANES), f32)],
    )
    back = lax.all_to_all(total, everyone, split_axis=0, concat_axis=0, tiled=True)
    return call(
        backward_kernel,
        [((frames, blocks, features), bf16)] * 3,
        [spread, back, cot, probs, query, key, value],
        "vvvvvvv",
        [pltpu.VMEM((frames, blocks, features), bf16)] * 3 + [pltpu.SemaphoreType.DMA((6,))],
        "h",
    )


def solution(mesh):
    groups, columns = mesh.devices.shape
    split = Mesh(mesh.devices.reshape(groups, columns // CORES, CORES), ("grp", "z", "core"))
    frm = ("z", "core")
    patches = P(None, ("grp",) + frm, None)
    return jax.shard_map(
        body,
        mesh=split,
        in_specs=(
            patches, patches, patches, P(frm, "grp", None), P("grp", None, frm),
            P("grp", frm, None), P(), P(),
        ),
        out_specs=(patches, patches, patches),
        check_vma=False,
    )
```

```python
import functools

import jax
import jax.numpy as jnp
from jax import lax
from jax.experimental import pallas as pl
from jax.experimental.pallas import tpu as pltpu
from jax.sharding import Mesh
from jax.sharding import PartitionSpec as P

HEADS = 16
MOST = 2
CORES = 2
SUBLANES = 8
LANES = 128
PIECE = 256
TILE = 16

root_half = 0.7071067811865476
inv_root_tau = 0.3989422804014327

LANES_BOTH = (((1,), (1,)), ((), ()))
FIRST_BOTH = (((0,), (0,)), ((), ()))


def gelu_slope(pre_act):
    normal_cdf = 0.5 * (1.0 + lax.erf(pre_act * root_half))
    density = jnp.exp(-0.5 * pre_act * pre_act) * inv_root_tau
    return normal_cdf + pre_act * density


def dot(a, b):
    return jnp.dot(a, b, preferred_element_type=jnp.float32)


def dot_lanes(a, b):
    return lax.dot_general(a, b, LANES_BOTH, preferred_element_type=jnp.float32)


def over_frames(values, op, blocks):
    rows = values.shape[0]
    total = values[:SUBLANES]
    for start in range(SUBLANES, rows, SUBLANES):
        total = op(total, values[start : start + SUBLANES])
    step = blocks
    while step < SUBLANES:
        total = op(total, pltpu.roll(total, step, 0))
        step *= 2
    return jnp.concatenate([total] * (rows // SUBLANES), axis=0)


def heads_of(values):
    width = values.shape[1] // HEADS
    return [values[:, h * width : (h + 1) * width] for h in range(HEADS)]


def turn_kernel(span, cot_hbm, *refs):
    *part_refs, cot_ref, sems = refs
    copies = [
        pltpu.make_async_copy(
            cot_hbm.at[:, pl.ds(i * TILE, TILE)], cot_ref.at[:, pl.ds(i * TILE, TILE)], sems.at[i]
        )
        for i in range(cot_ref.shape[1] // TILE)
    ]
    for copy in copies:
        copy.start()
    level = lax.axis_index("z")
    for copy in copies:
        copy.wait()
    parts = [cot_ref[0, k * span : (k + 1) * span, :] for k in range(len(part_refs))]
    bit = 1
    while bit < len(parts):
        turn = (level // bit) % 2 == 1
        parts = [jnp.where(turn, parts[k ^ bit], parts[k]) for k in range(len(parts))]
        bit *= 2
    for part_ref, part in zip(part_refs, parts):
        part_ref[...] = part


def held_core(level):
    core = lax.axis_index("core")
    return jnp.where(level == 0, core, 1 - core)


def forward_kernel(
    patches_all, share,
    chosen_hbm, gate_hbm, query_hbm, key_hbm, value_hbm, w_in_hbm, w_out_hbm,
    query_rows_ref, key_rows_ref, value_rows_ref, w_in_ref, w_out_ref,
    probs_ref, picked_ref, take_ref, weight_ref, spread_ref,
    chosen_ref, gate_ref, query_ref, key_ref, value_ref, sems,
):
    core = lax.axis_index("core")
    chip = lax.axis_index("grp") * lax.axis_size("z") + lax.axis_index("z")
    part = w_in_ref.shape[0] // CORES
    sources = [chosen_hbm, gate_hbm, query_hbm, key_hbm, value_hbm]
    targets = [chosen_ref, gate_ref, query_ref, key_ref, value_ref]
    for i in range(CORES):
        sources.append(w_in_hbm.at[0, part_of(core ^ i, part)])
        targets.append(w_in_ref.at[pl.ds(i * part, part)])
        sources.append(w_out_hbm.at[0, :, part_of(core ^ i, part)])
        targets.append(w_out_ref.at[:, pl.ds(i * part, part)])
    copies = [
        pltpu.make_async_copy(source, target, sems.at[i])
        for i, (source, target) in enumerate(zip(sources, targets))
    ]
    for copy in copies:
        copy.start()
    frames, blocks, features = query_ref.shape
    rows = frames * blocks
    scaling = (features // HEADS) ** (-0.5)

    for copy in copies[:2]:
        copy.wait()
    experts, cap = chosen_ref.shape
    before = (
        lax.broadcasted_iota(jnp.int32, (cap, cap), 0)
        < lax.broadcasted_iota(jnp.int32, (cap, cap), 1)
    ).astype(jnp.bfloat16)
    slot = lax.broadcasted_iota(jnp.int32, (SUBLANES, cap), 0)
    row_at = lax.broadcasted_iota(jnp.int32, (rows, cap), 0)
    span = CORES * blocks
    slots = experts * MOST
    found = []
    for e in range(experts):
        tokens = chosen_ref[e : e + 1, :]
        gates = gate_ref[e : e + 1, :]
        patch = tokens % patches_all
        frame = tokens // patches_all
        level = (frame // CORES) ^ lax.axis_index("z")
        for i in range(CORES):
            owned = patch // blocks == chip * CORES + (core ^ i)
            owned = jnp.broadcast_to(owned.astype(jnp.float32), slot.shape)
            rank = dot(owned.astype(jnp.bfloat16), before)
            taken = jnp.where((rank == slot.astype(jnp.float32)) & (owned > 0.0), 1.0, 0.0)
            weight = jnp.sum(taken * gates, axis=1, keepdims=True)
            taken = taken.astype(jnp.bfloat16)
            place = jnp.where(
                frame % CORES == held_core(level),
                level * span + (core ^ i) * blocks + patch % blocks,
                -1,
            )
            at = slice(i * slots + e * MOST, i * slots + (e + 1) * MOST)
            take_ref[at] = dot_lanes(taken, (row_at == place).astype(jnp.bfloat16))[:MOST]
            weight_ref[at] = jnp.broadcast_to(weight[:MOST], (MOST, weight_ref.shape[1]))
            if i == 0:
                position = frame * blocks + patch % blocks
                found.append(dot_lanes(taken, (row_at == position).astype(jnp.bfloat16))[:MOST])
    levels = rows // span
    want = lax.broadcasted_iota(jnp.int32, (levels * blocks, rows), 0)
    have = lax.broadcasted_iota(jnp.int32, (levels * blocks, rows), 1)
    source = (want // blocks) * span + (core ^ 1) * blocks + want % blocks
    take_ref[CORES * slots :] = (source == have).astype(jnp.float32)
    here = jnp.concatenate(found, axis=0).astype(jnp.bfloat16)
    pieces = spread_ref.shape[0] // (rows * CORES)
    returns = spread_ref.shape[1]
    slot_at = lax.broadcasted_iota(jnp.int32, (slots, returns), 0)
    back_at = lax.broadcasted_iota(jnp.int32, (slots, returns), 1) // pieces
    levels, groups = lax.axis_size("z"), lax.axis_size("grp")
    expert_of = back_at // MOST // levels % groups // share
    same = (expert_of == slot_at // MOST) & (back_at % MOST == slot_at % MOST)
    back = lax.dot_general(
        here, same.astype(jnp.bfloat16), FIRST_BOTH, preferred_element_type=jnp.float32
    )
    back_at = lax.broadcasted_iota(jnp.int32, (rows, returns), 1)
    piece = back_at // (MOST * pieces * levels * groups) * pieces + back_at % pieces
    for j in range(CORES * pieces):
        spread_ref[j * rows : (j + 1) * rows, :] = jnp.where(piece == j, back, 0.0).astype(
            jnp.bfloat16
        )

    for copy in copies[2:5]:
        copy.wait()
    query = query_ref[...].reshape(rows, features)
    key = key_ref[...].reshape(rows, features)
    value = value_ref[...].reshape(rows, features)
    query_rows_ref[...] = query
    key_rows_ref[...] = key
    value_rows_ref[...] = value
    scores = jnp.concatenate(
        [dot_lanes(k, q) for k, q in zip(heads_of(key), heads_of(query))], axis=1
    )
    scores = scores * scaling
    raised = jnp.exp(scores - over_frames(scores, jnp.maximum, blocks))
    probs = raised / over_frames(raised, jnp.add, blocks)
    patch_in = lax.broadcasted_iota(jnp.int32, probs.shape, 0) % blocks
    patch_out = lax.broadcasted_iota(jnp.int32, probs.shape, 1) % blocks
    probs = jnp.where(patch_in == patch_out, probs, 0.0)
    probs_ref[...] = probs
    weights = probs.T.astype(jnp.bfloat16)
    mixed = jnp.concatenate(
        [dot(weights[h * rows : (h + 1) * rows], v) for h, v in enumerate(heads_of(value))],
        axis=1,
    ).astype(jnp.bfloat16)
    picked_ref[...] = dot(here, mixed).astype(jnp.bfloat16)
    for copy in copies[5:]:
        copy.wait()


def pick_kernel(order, take_ref, weight_ref, *refs):
    *part_refs, cot_ref, mine_ref, sent_ref = refs
    parts = [part_refs[order.index(k)][...] for k in range(len(order))]
    cot = jnp.concatenate(parts, axis=0)
    cot_ref[...] = cot
    slots = mine_ref.shape[0]
    rows = dot(take_ref[...].astype(jnp.bfloat16), cot)
    picks = (rows[: CORES * slots] * weight_ref[:, :1]).astype(jnp.bfloat16)
    mine_ref[...] = picks[:slots]
    away = rows[CORES * slots :].astype(jnp.bfloat16)
    sent_ref[...] = jnp.concatenate([away, picks[slots:]], axis=0)


def pack_kernel(share, picked_ref, mine_ref, came_ref, out_ref):
    levels = lax.axis_size("z")
    slots, features = mine_ref.shape
    rows = mine_ref[...] + came_ref[came_ref.shape[0] - slots :, :]
    part = features // CORES
    picked = picked_ref[...]
    both = [
        jnp.concatenate(
            [half[:, c * part : (c + 1) * part] for half in (picked, rows)], axis=1
        )
        for c in range(CORES)
    ]
    for i in range(out_ref.shape[0]):
        e = i // (CORES * levels) // share
        out_ref[i] = both[i // levels % CORES][e * MOST : (e + 1) * MOST]


def part_of(part, width):
    return pl.ds(pl.multiple_of(part * width, width), width)


def first_kernel(near_ref, w_in_ref, w_out_ref, pre_ref, back_ref):
    width = w_in_ref.shape[0] // CORES
    rows = near_ref[...].reshape(pre_ref.shape[0], CORES * width)
    pre_ref[...] = dot(rows[:, :width], w_in_ref[:width, :])
    back_ref[...] = dot_lanes(rows[:, width:], w_out_ref[:, :width])


def second_kernel(far_ref, pre_ref, back_ref, w_in_ref, w_out_ref, slope_ref, sent_ref):
    width = w_in_ref.shape[0] // CORES
    far = far_ref[...].reshape(pre_ref.shape[0], CORES * width)
    pre_act = pre_ref[...] + dot(far[:, :width], w_in_ref[width:, :])
    back_act = back_ref[...] + dot_lanes(far[:, width:], w_out_ref[:, width:])
    slope = (back_act * gelu_slope(pre_act)).astype(jnp.bfloat16)
    slope_ref[...] = slope
    sent_ref[...] = dot_lanes(slope, w_in_ref[width:, :]).astype(jnp.bfloat16)


def third_kernel(blocks, slope_ref, w_in_ref, near_ref, came_ref, kept_ref, cot_ref):
    rows = near_ref.shape[0]
    span = CORES * blocks
    levels = rows // span
    want = lax.broadcasted_iota(jnp.int32, (rows, rows), 0)
    have = lax.broadcasted_iota(jnp.int32, (rows, rows), 1)
    frame = want // blocks
    level = (frame // CORES) ^ lax.axis_index("z")
    here = frame % CORES == held_core(level)
    source = level * span + lax.axis_index("core") * blocks + want % blocks
    own = (here & (source == have)).astype(jnp.bfloat16)
    source = level * blocks + want % blocks
    others = (jnp.logical_not(here) & (source == have)).astype(jnp.bfloat16)
    others = others[:, : levels * blocks]
    cot = dot(own, near_ref[...])
    cot = cot + dot(others, came_ref[: levels * blocks, :])
    cot_ref[...] = cot.astype(jnp.bfloat16)
    width = kept_ref.shape[1]
    kept_ref[...] = dot_lanes(slope_ref[...], w_in_ref[:width, :])


def sum_kernel(kept_ref, came_ref, out_ref, piece_ref):
    total = kept_ref[...] + came_ref[...].astype(jnp.float32)
    count, width = total.shape
    pieces = width // PIECE
    parts = piece_ref.shape[0]
    for j in range(pieces):
        for i in range(parts):
            start = j * PIECE + i * LANES
            piece_ref[i, pl.ds(j, count, stride=pieces), :] = total[:, start : start + LANES]
    total = jnp.concatenate([piece_ref[i] for i in range(parts)], axis=1)
    devices, pieces, _ = out_ref.shape
    levels = lax.axis_size("z")
    total = total.astype(jnp.bfloat16).reshape(-1, CORES, levels, pieces, PIECE)
    for c in range(CORES):
        out_ref[c * (devices // CORES) : (c + 1) * (devices // CORES)] = (
            total[:, c].reshape(devices // CORES, pieces, PIECE)
        )


def backward_kernel(
    spread_ref, back_ref, cot_ref, probs_ref, query_ref, key_ref, value_ref,
    grad_query_hbm, grad_key_hbm, grad_value_hbm,
    grad_query_ref, grad_key_ref, grad_value_ref, sems,
):
    frames, blocks, features = grad_query_ref.shape
    rows = frames * blocks
    scaling = (features // HEADS) ** (-0.5)
    query, key, value = query_ref[...], key_ref[...], value_ref[...]
    back = dot(spread_ref[...], back_ref[...].reshape(-1, PIECE))
    added = jnp.concatenate(
        [back[start : start + rows] for start in range(0, back.shape[0], rows)], axis=1
    )
    stream = (cot_ref[...].astype(jnp.float32) + added).astype(jnp.bfloat16)
    probs = probs_ref[...]
    weights = probs.astype(jnp.bfloat16)
    copies = []

    def put(ref, hbm, parts):
        joined = jnp.concatenate(parts, axis=1).astype(jnp.bfloat16)
        ref[...] = joined.reshape(frames, blocks, features)
        copy = pltpu.make_async_copy(ref, hbm, sems.at[len(copies)])
        copy.start()
        copies.append(copy)

    grad_prob = jnp.concatenate(
        [dot_lanes(v, g) for v, g in zip(heads_of(value), heads_of(stream))], axis=1
    )
    put(
        grad_value_ref,
        grad_value_hbm,
        [dot(w, g) for w, g in zip(heads_of(weights), heads_of(stream))],
    )
    centre = over_frames(probs * grad_prob, jnp.add, blocks)
    grad_score = probs * (grad_prob - centre)
    turned = grad_score.T.astype(jnp.bfloat16)
    grad_score = grad_score.astype(jnp.bfloat16)
    put(
        grad_key_ref,
        grad_key_hbm,
        [dot(s, q) * scaling for s, q in zip(heads_of(grad_score), heads_of(query))],
    )
    put(
        grad_query_ref,
        grad_query_hbm,
        [dot(turned[h * rows : (h + 1) * rows], k) * scaling for h, k in enumerate(heads_of(key))],
    )
    for copy in copies:
        copy.wait()


def call(kernel, outs, operands, places, scratch=(), results="v"):
    spaces = {
        "v": pl.BlockSpec(memory_space=pltpu.VMEM),
        "h": pl.BlockSpec(memory_space=pl.ANY),
    }
    return pl.pallas_call(
        kernel,
        out_shape=[jax.ShapeDtypeStruct(shape, dtype) for shape, dtype in outs],
        in_specs=[spaces[place] for place in places],
        out_specs=[spaces[results]] * len(outs),
        scratch_shapes=list(scratch),
        compiler_params=pltpu.CompilerParams(vmem_limit_bytes=32 * 1024 * 1024),
    )(*[
        pltpu.with_memory_space_constraint(operand, pltpu.HBM) if place == "h" else operand
        for operand, place in zip(operands, places)
    ])


def body(query_in, key_in, value_in, cotangent, w_in, w_out, gate_probs, chosen):
    bf16, f32 = jnp.bfloat16, jnp.float32
    frames, blocks, features = query_in.shape
    groups = lax.axis_size("grp")
    levels = lax.axis_size("z")
    columns = levels * CORES
    experts = gate_probs.shape[0]
    devices = groups * columns
    share = groups // experts
    rows = frames * blocks
    slots = experts * MOST
    part = features // CORES
    hidden = w_in.shape[2]

    def swap(values):
        return lax.ppermute(values, "core", [(i, i ^ 1) for i in range(CORES)])

    def across(values, step):
        pairs = [(i, i ^ (CORES * step) ^ 1) for i in range(columns)]
        return lax.ppermute(values, ("z", "core"), pairs)

    span = CORES * blocks
    parts = call(
        functools.partial(turn_kernel, span),
        [((span, features), bf16)] * levels,
        [cotangent],
        "h",
        [
            pltpu.VMEM(cotangent.shape, bf16),
            pltpu.SemaphoreType.DMA((cotangent.shape[1] // TILE,)),
        ],
    )
    order = [0] + [i ^ (i >> 1) for i in range(levels - 1, 0, -1)]
    parts = [across(parts[k], k) if k else parts[k] for k in order]
    query, key, value, w_in_near, w_out_near, probs, picked, take, weight, spread = call(
        functools.partial(forward_kernel, blocks * devices, share),
        [
            *[((rows, features), bf16)] * 3,
            (w_in.shape[1:], bf16),
            (w_out.shape[1:], bf16),
            ((rows, HEADS * rows), f32),
            ((slots, features), bf16),
            ((CORES * slots + levels * blocks, rows), f32),
            ((CORES * slots, LANES), f32),
            ((rows * features // PIECE, devices * MOST * part // PIECE), bf16),
        ],
        [chosen, gate_probs, query_in, key_in, value_in, w_in, w_out],
        "hhhhhhh",
        [
            pltpu.VMEM(chosen.shape, jnp.int32),
            pltpu.VMEM(gate_probs.shape, f32),
            *[pltpu.VMEM(query_in.shape, bf16)] * 3,
            pltpu.SemaphoreType.DMA((5 + 2 * CORES,)),
        ],
    )
    cot_near, mine, sent = call(
        functools.partial(pick_kernel, order),
        [((rows, features), bf16), ((slots, features), bf16), ((levels * blocks + slots, features), bf16)],
        [take, weight, *parts],
        "vv" + "v" * levels,
    )
    came_near = swap(sent)
    (outgoing,) = call(
        functools.partial(pack_kernel, share),
        [((devices, MOST, 2 * part), bf16)],
        [picked, mine, came_near],
        "vvv",
    )
    held = lax.all_to_all(outgoing, ("grp", "core", "z"), split_axis=0, concat_axis=0, tiled=True)
    other = swap(held)
    acts = (devices * MOST, hidden)
    halves = (devices * MOST, part)
    pre_act, back_act = call(
        first_kernel, [(acts, f32), (acts, f32)], [held, w_in_near, w_out_near], "vvv"
    )
    slope, sent = call(
        second_kernel,
        [(acts, bf16), (halves, bf16)],
        [other, pre_act, back_act, w_in_near, w_out_near],
        "vvvvv",
    )
    came = swap(sent)
    kept, cot = call(
        functools.partial(third_kernel, blocks),
        [(halves, f32), ((rows, features), bf16)],
        [slope, w_in_near, cot_near, came_near],
        "vvvv",
    )
    pieces = MOST * part // PIECE
    (total,) = call(
        sum_kernel,
        [((devices, pieces, PIECE), bf16)],
        [kept, came],
        "vv",
        [pltpu.VMEM((PIECE // LANES, devices * pieces, LANES), f32)],
    )
    back = lax.all_to_all(total, ("core", "grp", "z"), split_axis=0, concat_axis=0, tiled=True)
    return call(
        backward_kernel,
        [((frames, blocks, features), bf16)] * 3,
        [spread, back, cot, probs, query, key, value],
        "vvvvvvv",
        [pltpu.VMEM((frames, blocks, features), bf16)] * 3 + [pltpu.SemaphoreType.DMA((3,))],
        "h",
    )


def solution(mesh):
    groups, columns = mesh.devices.shape
    split = Mesh(mesh.devices.reshape(groups, columns // CORES, CORES), ("grp", "z", "core"))
    frm = ("z", "core")
    patches = P(None, ("grp",) + frm, None)
    return jax.shard_map(
        body,
        mesh=split,
        in_specs=(
            patches, patches, patches, P(frm, "grp", None), P("grp", None, frm),
            P("grp", frm, None), P(), P(),
        ),
        out_specs=(patches, patches, patches),
        check_vma=False,
    )
```

```python
import functools

import jax
import jax.numpy as jnp
from jax import lax
from jax.experimental import pallas as pl
from jax.experimental.pallas import tpu as pltpu
from jax.sharding import Mesh
from jax.sharding import PartitionSpec as P

HEADS = 16
MOST = 2
CORES = 2
SUBLANES = 8
LANES = 128
PIECE = 256
TILE = 16

root_half = 0.7071067811865476
inv_root_tau = 0.3989422804014327

LANES_BOTH = (((1,), (1,)), ((), ()))
FIRST_BOTH = (((0,), (0,)), ((), ()))


def gelu_slope(pre_act):
    normal_cdf = 0.5 * (1.0 + lax.erf(pre_act * root_half))
    density = jnp.exp(-0.5 * pre_act * pre_act) * inv_root_tau
    return normal_cdf + pre_act * density


def dot(a, b):
    return jnp.dot(a, b, preferred_element_type=jnp.float32)


def dot_lanes(a, b):
    return lax.dot_general(a, b, LANES_BOTH, preferred_element_type=jnp.float32)


def over_frames(values, op, blocks):
    rows = values.shape[0]
    total = values[:SUBLANES]
    for start in range(SUBLANES, rows, SUBLANES):
        total = op(total, values[start : start + SUBLANES])
    step = blocks
    while step < SUBLANES:
        total = op(total, pltpu.roll(total, step, 0))
        step *= 2
    return jnp.concatenate([total] * (rows // SUBLANES), axis=0)


def heads_of(values):
    width = values.shape[1] // HEADS
    return [values[:, h * width : (h + 1) * width] for h in range(HEADS)]


def turn_kernel(span, cot_hbm, *refs):
    *part_refs, cot_ref, sems = refs
    copies = [
        pltpu.make_async_copy(
            cot_hbm.at[:, pl.ds(i * TILE, TILE)], cot_ref.at[:, pl.ds(i * TILE, TILE)], sems.at[i]
        )
        for i in range(cot_ref.shape[1] // TILE)
    ]
    for copy in copies:
        copy.start()
    level = lax.axis_index("z")
    for copy in copies:
        copy.wait()
    parts = [cot_ref[0, k * span : (k + 1) * span, :] for k in range(len(part_refs))]
    bit = 1
    while bit < len(parts):
        turn = (level // bit) % 2 == 1
        parts = [jnp.where(turn, parts[k ^ bit], parts[k]) for k in range(len(parts))]
        bit *= 2
    for part_ref, part in zip(part_refs, parts):
        part_ref[...] = part


def held_core(level):
    core = lax.axis_index("core")
    return jnp.where(level == 0, core, 1 - core)


def forward_kernel(
    patches_all, share,
    chosen_hbm, gate_hbm, query_hbm, key_hbm, value_hbm, w_in_hbm, w_out_hbm,
    query_rows_ref, key_rows_ref, value_rows_ref, w_in_ref, w_out_ref,
    probs_ref, picked_ref, take_ref, weight_ref, spread_ref,
    chosen_ref, gate_ref, query_ref, key_ref, value_ref, sems,
):
    core = lax.axis_index("core")
    chip = lax.axis_index("grp") * lax.axis_size("z") + lax.axis_index("z")
    part = w_in_ref.shape[0] // CORES
    sources = [chosen_hbm, gate_hbm, query_hbm, key_hbm, value_hbm]
    targets = [chosen_ref, gate_ref, query_ref, key_ref, value_ref]
    for i in range(CORES):
        sources.append(w_in_hbm.at[0, part_of(core ^ i, part)])
        targets.append(w_in_ref.at[pl.ds(i * part, part)])
        sources.append(w_out_hbm.at[0, :, part_of(core ^ i, part)])
        targets.append(w_out_ref.at[:, pl.ds(i * part, part)])
    copies = [
        pltpu.make_async_copy(source, target, sems.at[i])
        for i, (source, target) in enumerate(zip(sources, targets))
    ]
    for copy in copies:
        copy.start()
    frames, blocks, features = query_ref.shape
    rows = frames * blocks
    scaling = (features // HEADS) ** (-0.5)

    for copy in copies[:2]:
        copy.wait()
    experts, cap = chosen_ref.shape
    before = (
        lax.broadcasted_iota(jnp.int32, (cap, cap), 0)
        < lax.broadcasted_iota(jnp.int32, (cap, cap), 1)
    ).astype(jnp.bfloat16)
    slot = lax.broadcasted_iota(jnp.int32, (SUBLANES, cap), 0)
    row_at = lax.broadcasted_iota(jnp.int32, (rows, cap), 0)
    span = CORES * blocks
    slots = experts * MOST
    found = []
    for e in range(experts):
        tokens = chosen_ref[e : e + 1, :]
        gates = gate_ref[e : e + 1, :]
        patch = tokens % patches_all
        frame = tokens // patches_all
        level = (frame // CORES) ^ lax.axis_index("z")
        for i in range(CORES):
            owned = patch // blocks == chip * CORES + (core ^ i)
            owned = jnp.broadcast_to(owned.astype(jnp.float32), slot.shape)
            rank = dot(owned.astype(jnp.bfloat16), before)
            taken = jnp.where((rank == slot.astype(jnp.float32)) & (owned > 0.0), 1.0, 0.0)
            weight = jnp.sum(taken * gates, axis=1, keepdims=True)
            taken = taken.astype(jnp.bfloat16)
            place = jnp.where(
                frame % CORES == held_core(level),
                level * span + (core ^ i) * blocks + patch % blocks,
                -1,
            )
            at = slice(i * slots + e * MOST, i * slots + (e + 1) * MOST)
            take_ref[at] = dot_lanes(taken, (row_at == place).astype(jnp.bfloat16))[:MOST]
            weight_ref[at] = jnp.broadcast_to(weight[:MOST], (MOST, weight_ref.shape[1]))
            if i == 0:
                position = frame * blocks + patch % blocks
                found.append(dot_lanes(taken, (row_at == position).astype(jnp.bfloat16))[:MOST])
    levels = rows // span
    want = lax.broadcasted_iota(jnp.int32, (levels * blocks, rows), 0)
    have = lax.broadcasted_iota(jnp.int32, (levels * blocks, rows), 1)
    source = (want // blocks) * span + (core ^ 1) * blocks + want % blocks
    take_ref[CORES * slots :] = (source == have).astype(jnp.float32)
    here = jnp.concatenate(found, axis=0).astype(jnp.bfloat16)
    pieces = spread_ref.shape[0] // (rows * CORES)
    returns = spread_ref.shape[1]
    slot_at = lax.broadcasted_iota(jnp.int32, (slots, returns), 0)
    back_at = lax.broadcasted_iota(jnp.int32, (slots, returns), 1) // pieces
    levels, groups = lax.axis_size("z"), lax.axis_size("grp")
    expert_of = back_at // MOST // levels % groups // share
    same = (expert_of == slot_at // MOST) & (back_at % MOST == slot_at % MOST)
    back = lax.dot_general(
        here, same.astype(jnp.bfloat16), FIRST_BOTH, preferred_element_type=jnp.float32
    )
    back_at = lax.broadcasted_iota(jnp.int32, (rows, returns), 1)
    piece = back_at // (MOST * pieces * levels * groups) * pieces + back_at % pieces
    for j in range(CORES * pieces):
        spread_ref[j * rows : (j + 1) * rows, :] = jnp.where(piece == j, back, 0.0).astype(
            jnp.bfloat16
        )

    for copy in copies[2:5]:
        copy.wait()
    query = query_ref[...].reshape(rows, features)
    key = key_ref[...].reshape(rows, features)
    value = value_ref[...].reshape(rows, features)
    query_rows_ref[...] = query
    key_rows_ref[...] = key
    value_rows_ref[...] = value
    scores = jnp.concatenate(
        [dot_lanes(k, q) for k, q in zip(heads_of(key), heads_of(query))], axis=1
    )
    scores = scores * scaling
    raised = jnp.exp(scores - over_frames(scores, jnp.maximum, blocks))
    probs = raised / over_frames(raised, jnp.add, blocks)
    patch_in = lax.broadcasted_iota(jnp.int32, probs.shape, 0) % blocks
    patch_out = lax.broadcasted_iota(jnp.int32, probs.shape, 1) % blocks
    probs = jnp.where(patch_in == patch_out, probs, 0.0)
    probs_ref[...] = probs
    weights = probs.T.astype(jnp.bfloat16)
    mixed = jnp.concatenate(
        [dot(weights[h * rows : (h + 1) * rows], v) for h, v in enumerate(heads_of(value))],
        axis=1,
    ).astype(jnp.bfloat16)
    picked_ref[...] = dot(here, mixed).astype(jnp.bfloat16)
    for copy in copies[5:]:
        copy.wait()


def pick_kernel(order, take_ref, weight_ref, *refs):
    *part_refs, cot_ref, mine_ref, sent_ref = refs
    parts = [part_refs[order.index(k)][...] for k in range(len(order))]
    cot = jnp.concatenate(parts, axis=0)
    cot_ref[...] = cot
    slots = mine_ref.shape[0]
    rows = dot(take_ref[...].astype(jnp.bfloat16), cot)
    picks = (rows[: CORES * slots] * weight_ref[:, :1]).astype(jnp.bfloat16)
    mine_ref[...] = picks[:slots]
    away = rows[CORES * slots :].astype(jnp.bfloat16)
    sent_ref[...] = jnp.concatenate([away, picks[slots:]], axis=0)


def pack_kernel(share, picked_ref, mine_ref, came_ref, out_ref):
    levels, groups = lax.axis_size("z"), lax.axis_size("grp")
    slots, features = mine_ref.shape
    rows = mine_ref[...] + came_ref[came_ref.shape[0] - slots :, :]
    part = features // CORES
    picked = picked_ref[...]
    both = [
        jnp.concatenate(
            [half[:, c * part : (c + 1) * part] for half in (picked, rows)], axis=1
        )
        for c in range(CORES)
    ]
    for i in range(out_ref.shape[0]):
        e = i // levels % groups // share
        out_ref[i] = both[i // (levels * groups)][e * MOST : (e + 1) * MOST]


def part_of(part, width):
    return pl.ds(pl.multiple_of(part * width, width), width)


def first_kernel(near_ref, w_in_ref, w_out_ref, pre_ref, back_ref):
    width = w_in_ref.shape[0] // CORES
    rows = near_ref[...].reshape(pre_ref.shape[0], CORES * width)
    pre_ref[...] = dot(rows[:, :width], w_in_ref[:width, :])
    back_ref[...] = dot_lanes(rows[:, width:], w_out_ref[:, :width])


def second_kernel(far_ref, pre_ref, back_ref, w_in_ref, w_out_ref, slope_ref, sent_ref):
    width = w_in_ref.shape[0] // CORES
    far = far_ref[...].reshape(pre_ref.shape[0], CORES * width)
    pre_act = pre_ref[...] + dot(far[:, :width], w_in_ref[width:, :])
    back_act = back_ref[...] + dot_lanes(far[:, width:], w_out_ref[:, width:])
    slope = (back_act * gelu_slope(pre_act)).astype(jnp.bfloat16)
    slope_ref[...] = slope
    sent_ref[...] = dot_lanes(slope, w_in_ref[width:, :]).astype(jnp.bfloat16)


def third_kernel(blocks, slope_ref, w_in_ref, near_ref, came_ref, kept_ref, cot_ref):
    rows = near_ref.shape[0]
    span = CORES * blocks
    levels = rows // span
    want = lax.broadcasted_iota(jnp.int32, (rows, rows), 0)
    have = lax.broadcasted_iota(jnp.int32, (rows, rows), 1)
    frame = want // blocks
    level = (frame // CORES) ^ lax.axis_index("z")
    here = frame % CORES == held_core(level)
    source = level * span + lax.axis_index("core") * blocks + want % blocks
    own = (here & (source == have)).astype(jnp.bfloat16)
    source = level * blocks + want % blocks
    others = (jnp.logical_not(here) & (source == have)).astype(jnp.bfloat16)
    others = others[:, : levels * blocks]
    cot = dot(own, near_ref[...])
    cot = cot + dot(others, came_ref[: levels * blocks, :])
    cot_ref[...] = cot.astype(jnp.bfloat16)
    width = kept_ref.shape[1]
    kept_ref[...] = dot_lanes(slope_ref[...], w_in_ref[:width, :])


def sum_kernel(kept_ref, came_ref, out_ref, piece_ref):
    total = kept_ref[...] + came_ref[...].astype(jnp.float32)
    count, width = total.shape
    pieces = width // PIECE
    parts = piece_ref.shape[0]
    for j in range(pieces):
        for i in range(parts):
            start = j * PIECE + i * LANES
            piece_ref[i, pl.ds(j, count, stride=pieces), :] = total[:, start : start + LANES]
    total = jnp.concatenate([piece_ref[i] for i in range(parts)], axis=1)
    out_ref[...] = total.astype(jnp.bfloat16).reshape(out_ref.shape)


def backward_kernel(
    spread_ref, back_ref, cot_ref, probs_ref, query_ref, key_ref, value_ref,
    grad_query_hbm, grad_key_hbm, grad_value_hbm,
    grad_query_ref, grad_key_ref, grad_value_ref, sems,
):
    frames, blocks, features = grad_query_ref.shape
    rows = frames * blocks
    scaling = (features // HEADS) ** (-0.5)
    query, key, value = query_ref[...], key_ref[...], value_ref[...]
    back = dot(spread_ref[...], back_ref[...].reshape(-1, PIECE))
    added = jnp.concatenate(
        [back[start : start + rows] for start in range(0, back.shape[0], rows)], axis=1
    )
    stream = (cot_ref[...].astype(jnp.float32) + added).astype(jnp.bfloat16)
    probs = probs_ref[...]
    weights = probs.astype(jnp.bfloat16)
    copies = []

    def put(ref, hbm, parts):
        joined = jnp.concatenate(parts, axis=1).astype(jnp.bfloat16)
        ref[...] = joined.reshape(frames, blocks, features)
        copy = pltpu.make_async_copy(ref, hbm, sems.at[len(copies)])
        copy.start()
        copies.append(copy)

    grad_prob = jnp.concatenate(
        [dot_lanes(v, g) for v, g in zip(heads_of(value), heads_of(stream))], axis=1
    )
    put(
        grad_value_ref,
        grad_value_hbm,
        [dot(w, g) for w, g in zip(heads_of(weights), heads_of(stream))],
    )
    centre = over_frames(probs * grad_prob, jnp.add, blocks)
    grad_score = probs * (grad_prob - centre)
    turned = grad_score.T.astype(jnp.bfloat16)
    grad_score = grad_score.astype(jnp.bfloat16)
    put(
        grad_key_ref,
        grad_key_hbm,
        [dot(s, q) * scaling for s, q in zip(heads_of(grad_score), heads_of(query))],
    )
    put(
        grad_query_ref,
        grad_query_hbm,
        [dot(turned[h * rows : (h + 1) * rows], k) * scaling for h, k in enumerate(heads_of(key))],
    )
    for copy in copies:
        copy.wait()


def call(kernel, outs, operands, places, scratch=(), results="v"):
    spaces = {
        "v": pl.BlockSpec(memory_space=pltpu.VMEM),
        "h": pl.BlockSpec(memory_space=pl.ANY),
    }
    return pl.pallas_call(
        kernel,
        out_shape=[jax.ShapeDtypeStruct(shape, dtype) for shape, dtype in outs],
        in_specs=[spaces[place] for place in places],
        out_specs=[spaces[results]] * len(outs),
        scratch_shapes=list(scratch),
        compiler_params=pltpu.CompilerParams(vmem_limit_bytes=32 * 1024 * 1024),
    )(*[
        pltpu.with_memory_space_constraint(operand, pltpu.HBM) if place == "h" else operand
        for operand, place in zip(operands, places)
    ])


def body(query_in, key_in, value_in, cotangent, w_in, w_out, gate_probs, chosen):
    bf16, f32 = jnp.bfloat16, jnp.float32
    frames, blocks, features = query_in.shape
    groups = lax.axis_size("grp")
    levels = lax.axis_size("z")
    columns = levels * CORES
    experts = gate_probs.shape[0]
    devices = groups * columns
    share = groups // experts
    rows = frames * blocks
    slots = experts * MOST
    part = features // CORES
    hidden = w_in.shape[2]
    everyone = ("core", "grp", "z")

    def swap(values):
        return lax.ppermute(values, "core", [(i, i ^ 1) for i in range(CORES)])

    def across(values, step):
        pairs = [(i, i ^ (CORES * step) ^ 1) for i in range(columns)]
        return lax.ppermute(values, ("z", "core"), pairs)

    span = CORES * blocks
    parts = call(
        functools.partial(turn_kernel, span),
        [((span, features), bf16)] * levels,
        [cotangent],
        "h",
        [
            pltpu.VMEM(cotangent.shape, bf16),
            pltpu.SemaphoreType.DMA((cotangent.shape[1] // TILE,)),
        ],
    )
    order = [0] + [i ^ (i >> 1) for i in range(levels - 1, 0, -1)]
    parts = [across(parts[k], k) if k else parts[k] for k in order]
    query, key, value, w_in_near, w_out_near, probs, picked, take, weight, spread = call(
        functools.partial(forward_kernel, blocks * devices, share),
        [
            *[((rows, features), bf16)] * 3,
            (w_in.shape[1:], bf16),
            (w_out.shape[1:], bf16),
            ((rows, HEADS * rows), f32),
            ((slots, features), bf16),
            ((CORES * slots + levels * blocks, rows), f32),
            ((CORES * slots, LANES), f32),
            ((rows * features // PIECE, devices * MOST * part // PIECE), bf16),
        ],
        [chosen, gate_probs, query_in, key_in, value_in, w_in, w_out],
        "hhhhhhh",
        [
            pltpu.VMEM(chosen.shape, jnp.int32),
            pltpu.VMEM(gate_probs.shape, f32),
            *[pltpu.VMEM(query_in.shape, bf16)] * 3,
            pltpu.SemaphoreType.DMA((5 + 2 * CORES,)),
        ],
    )
    cot_near, mine, sent = call(
        functools.partial(pick_kernel, order),
        [((rows, features), bf16), ((slots, features), bf16), ((levels * blocks + slots, features), bf16)],
        [take, weight, *parts],
        "vv" + "v" * levels,
    )
    came_near = swap(sent)
    (outgoing,) = call(
        functools.partial(pack_kernel, share),
        [((devices, MOST, 2 * part), bf16)],
        [picked, mine, came_near],
        "vvv",
    )
    held = lax.all_to_all(outgoing, everyone, split_axis=0, concat_axis=0, tiled=True)
    other = swap(held)
    acts = (devices * MOST, hidden)
    halves = (devices * MOST, part)
    pre_act, back_act = call(
        first_kernel, [(acts, f32), (acts, f32)], [held, w_in_near, w_out_near], "vvv"
    )
    slope, sent = call(
        second_kernel,
        [(acts, bf16), (halves, bf16)],
        [other, pre_act, back_act, w_in_near, w_out_near],
        "vvvvv",
    )
    came = swap(sent)
    kept, cot = call(
        functools.partial(third_kernel, blocks),
        [(halves, f32), ((rows, features), bf16)],
        [slope, w_in_near, cot_near, came_near],
        "vvvv",
    )
    pieces = MOST * part // PIECE
    (total,) = call(
        sum_kernel,
        [((devices, pieces, PIECE), bf16)],
        [kept, came],
        "vv",
        [pltpu.VMEM((PIECE // LANES, devices * pieces, LANES), f32)],
    )
    back = lax.all_to_all(total, everyone, split_axis=0, concat_axis=0, tiled=True)
    return call(
        backward_kernel,
        [((frames, blocks, features), bf16)] * 3,
        [spread, back, cot, probs, query, key, value],
        "vvvvvvv",
        [pltpu.VMEM((frames, blocks, features), bf16)] * 3 + [pltpu.SemaphoreType.DMA((3,))],
        "h",
    )


def solution(mesh):
    groups, columns = mesh.devices.shape
    split = Mesh(mesh.devices.reshape(groups, columns // CORES, CORES), ("grp", "z", "core"))
    frm = ("z", "core")
    patches = P(None, ("grp",) + frm, None)
    return jax.shard_map(
        body,
        mesh=split,
        in_specs=(
            patches, patches, patches, P(frm, "grp", None), P("grp", None, frm),
            P("grp", frm, None), P(), P(),
        ),
        out_specs=(patches, patches, patches),
        check_vma=False,
    )
```
